32 devices in a mesh: shard: 4 (over z), ctx: 4 (over y, x), tp: 2 (over core).
Axes of the slice: x: 2, y: 2, z: 4, core: 2. Of those that a mesh axis runs over, the one named last changes fastest.
Arguments:
- images: bfloat16 [4, 1024, 768], P('shard', 'ctx'), may hold values from -6 to 6
- cotangent: bfloat16 [4, 1024, 768], P('shard', 'ctx'), may hold values from -6 to 6
- ln1_gain: bfloat16 [768], P('shard'), may hold values from 0.5 to 1.5
- ln1_bias: bfloat16 [768], P('shard'), may hold values from -1.75 to 1.75
- ln2_gain: bfloat16 [768], P('shard'), may hold values from 0.5 to 1.5
- ln2_bias: bfloat16 [768], P('shard'), may hold values from -1.75 to 1.75
- q_gain: bfloat16 [12, 64], P('tp', 'shard'), may hold values from 0.7 to 2.2
- k_gain: bfloat16 [12, 64], P('tp', 'shard'), may hold values from 0.7 to 2.2
- w_query: bfloat16 [768, 768], P('shard', 'tp'), may hold values from -6 to 6
- w_key: bfloat16 [768, 768], P('shard', 'tp'), may hold values from -6 to 6
- w_value: bfloat16 [768, 768], P('shard', 'tp'), may hold values from -0.21875 to 0.21875
- w_out: bfloat16 [768, 768], P('tp', 'shard'), may hold values from -1.75 to 1.75
- w_up: bfloat16 [768, 3072], P('shard', 'tp'), may hold values from -0.21875 to 0.21875
- w_down: bfloat16 [3072, 768], P('tp', 'shard'), may hold values from -0.109375 to 0.109375
Outputs:
- block_out: bfloat16 [4, 1024, 768], P('shard', 'ctx')
- input_grad: bfloat16 [4, 1024, 768], P('shard', 'ctx')
- ln1_gain_grad: float32 [768], P('shard')
- ln1_bias_grad: float32 [768], P('shard')
- ln2_gain_grad: float32 [768], P('shard')
- ln2_bias_grad: float32 [768], P('shard')
- q_gain_grad: float32 [12, 64], P('tp', 'shard')
- k_gain_grad: float32 [12, 64], P('tp', 'shard')
- w_query_grad: float32 [768, 768], P('shard', 'tp')
- w_key_grad: float32 [768, 768], P('shard', 'tp')
- w_value_grad: float32 [768, 768], P('shard', 'tp')
- w_out_grad: float32 [768, 768], P('tp', 'shard')
- w_up_grad: float32 [768, 3072], P('shard', 'tp')
- w_down_grad: float32 [3072, 768], P('tp', 'shard')
- w_query_clipped: bfloat16 [768, 768], P('shard', 'tp')
- w_key_clipped: bfloat16 [768, 768], P('shard', 'tp')
The draws below stay inside these ranges and needn't reach their ends.
All inputs are finite; a program needn't handle non-finite values.
Results may differ from the reference program's by a relative error of at most 0.013.
The reference program's roundings to bfloat16 on the way count: a program that leaves them out, or rounds other values in their place, can miss the bound.
Values may be sent and summed in bfloat16 or wider, within the bound.
A program may use at most 128 MiB of HBM per device.

```python
import math
from functools import partial
import jax
import jax.numpy as jnp
from jax import lax

D = 768
HEADS = 12
HD = 64
FF = 3072
LEN = 1024
IMAGES = 4


def head_gains(key):
    per_head = jax.random.uniform(jax.random.fold_in(key, 1), (HEADS, 1), jnp.float32, 0.0, 1.0)
    factor = jnp.exp(jnp.log(0.9) + per_head * (jnp.log(1.8) - jnp.log(0.9)))
    element = jax.random.uniform(jax.random.fold_in(key, 2), (HEADS, HD), jnp.float32, 0.8, 1.2)
    return factor * element


def draw_q_gain(key, part):
    return head_gains(jax.random.fold_in(key, 11)).astype(jnp.bfloat16)


def draw_k_gain(key, part):
    return head_gains(jax.random.fold_in(key, 23)).astype(jnp.bfloat16)


def level_of(key, shape, cuts, least, top_value):
    def one(dim, shards_of):
        steps = jax.random.uniform(jax.random.fold_in(jax.random.fold_in(key, 6), dim), (shards_of,), jnp.float32, least / len(cuts), top_value / len(cuts))
        return jnp.repeat(jnp.exp(steps), shape[dim] // shards_of).reshape((-1,) + (1,) * (len(shape) - dim - 1))

    level = one(*cuts[0])
    for cut in cuts[1:]:
        level = level * one(*cut)
    return level


def noise(rng, extent, width, bound, cuts=(), kind=jnp.bfloat16):
    level = level_of(rng, extent, cuts, -0.22, 0.18) if cuts else 1.0
    values = jax.random.normal(rng, extent, jnp.float32) * width * level
    return jnp.minimum(jnp.maximum(values, -bound), bound).astype(kind)


def setup_inputs(seed: int = 0) -> dict:
    key_of = jax.random.split(jax.random.key(seed), 15)
    images = noise(key_of[0], (IMAGES, LEN, D), 1.0, 6.0, ((0, 4), (1, 4)))
    cotangent = noise(key_of[1], (IMAGES, LEN, D), 1.0, 6.0, ((0, 4), (1, 4)))
    ln1_gain = jnp.clip(1.0 + 0.1 * jax.random.normal(key_of[2], (D,), jnp.float32), 0.5, 1.5).astype(jnp.bfloat16)
    ln1_bias = noise(key_of[3], (D,), 0.3, 1.75, ((0, 4),))
    ln2_gain = jnp.clip(1.0 + 0.1 * jax.random.normal(key_of[4], (D,), jnp.float32), 0.5, 1.5).astype(jnp.bfloat16)
    ln2_bias = noise(key_of[5], (D,), 0.3, 1.75, ((0, 4),))
    q_gain = draw_q_gain(jax.random.fold_in(key_of[14], 71), 0)
    k_gain = draw_k_gain(jax.random.fold_in(key_of[14], 71), 0)
    w_query = noise(key_of[8], (D, D), 1.0, 6.0, ((0, 4), (1, 2)))
    w_key = noise(key_of[9], (D, D), 1.0, 6.0, ((0, 4), (1, 2)))
    w_value = noise(key_of[10], (D, D), D ** -0.5, 0.21875, ((0, 4), (1, 2)))
    w_out = noise(key_of[11], (D, D), (D // 64) ** -0.5, 1.75, ((0, 2), (1, 4)))
    w_up = noise(key_of[12], (D, FF), D ** -0.5, 0.21875, ((0, 4), (1, 2)))
    w_down = noise(key_of[13], (FF, D), FF ** -0.5, 0.109375, ((0, 2), (1, 4)))
    return {"images": images, "cotangent": cotangent, "ln1_gain": ln1_gain, "ln1_bias": ln1_bias, "ln2_gain": ln2_gain, "ln2_bias": ln2_bias, "q_gain": q_gain, "k_gain": k_gain, "w_query": w_query, "w_key": w_key, "w_value": w_value, "w_out": w_out, "w_up": w_up, "w_down": w_down}


@jax.custom_vjp
def low(v):
    return lax.optimization_barrier(v.astype(jnp.bfloat16)).astype(jnp.float32)

@jax.custom_vjp
def low_back(v):
    return v

def low_keep(v):
    return (low(v), None)

def low_pass(kept, grad):
    return (grad,)

def back_keep(v):
    return (v, None)

def back_low(kept, grad):
    return (low(grad),)
low.defvjp(low_keep, low_pass)
low_back.defvjp(back_keep, back_low)
norm_eps = 1e-06
clip_level = 0.5

def exact(left, right):
    return jnp.matmul(left, right, precision=lax.Precision.HIGHEST)

def layer_norm(values, gain, shift):
    center = values - lax.optimization_barrier(jnp.mean(values, axis=-1, keepdims=True))
    inverse = lax.rsqrt(lax.optimization_barrier(jnp.mean(center * center, axis=-1, keepdims=True)) + norm_eps)
    return center * inverse * gain + shift

def head_scale(values, gain):
    shaped = values.reshape(values.shape[:-1] + (HEADS, HD))
    inverse = lax.rsqrt(lax.optimization_barrier(jnp.mean(shaped * shaped, axis=-1, keepdims=True)) + norm_eps)
    return shaped * inverse * gain

def block(params, pictures):
    gain_one, shift_one, gain_two, shift_two, query_gain, key_gain, w_query, w_key, w_value, w_out, w_up, w_down = params
    hidden_one = low(layer_norm(pictures, gain_one, shift_one))
    queries = low(head_scale(low_back(exact(hidden_one, w_query)), query_gain))
    keyset = low(head_scale(low_back(exact(hidden_one, w_key)), key_gain))
    valueset = low(low_back(exact(hidden_one, w_value))).reshape(pictures.shape[:-1] + (HEADS, HD))
    scores = low_back(jnp.einsum('gqhd,gkhd->ghqk', queries, keyset, precision=lax.Precision.HIGHEST) * HD ** (-0.5))
    peaks = lax.optimization_barrier(jnp.max(scores, axis=(0, 2, 3)))
    probs = low(jax.nn.softmax(scores, axis=-1))
    mixed = jnp.einsum('ghqk,gkhd->gqhd', probs, valueset, precision=lax.Precision.HIGHEST).reshape(pictures.shape)
    attended = low(low_back(mixed))
    resid = pictures + low_back(exact(attended, w_out))
    hidden_two = low(layer_norm(resid, gain_two, shift_two))
    active = low(jax.nn.gelu(low_back(exact(hidden_two, w_up)), approximate=False))
    return (resid + low_back(exact(active, w_down)), peaks)

def forward(params, pictures):
    per_step = math.gcd(IMAGES, 2)
    grouped = pictures.reshape(IMAGES // per_step, per_step, LEN, D)
    outputs, peaks = lax.map(jax.checkpoint(partial(block, params)), grouped)
    return (outputs.reshape(IMAGES, LEN, D), lax.optimization_barrier(jnp.max(peaks, axis=0)))

def reference(images, cotangent, ln1_gain, ln1_bias, ln2_gain, ln2_bias, q_gain, k_gain, w_query, w_key, w_value, w_out, w_up, w_down):
    params = tuple((array.astype(jnp.float32) for array in (ln1_gain, ln1_bias, ln2_gain, ln2_bias, q_gain, k_gain, w_query, w_key, w_value, w_out, w_up, w_down)))
    pictures = images.astype(jnp.float32)
    block_out, pull, peaks = jax.vjp(forward, params, pictures, has_aux=True)
    param_grads, input_grad = pull(cotangent.astype(jnp.float32))
    factor = jnp.sqrt(clip_level / jnp.maximum(peaks, clip_level))
    columns = jnp.repeat(factor, HD)
    query_clip = (w_query.astype(jnp.float32) * columns).astype(jnp.bfloat16)
    key_clip = (w_key.astype(jnp.float32) * columns).astype(jnp.bfloat16)
    return (block_out.astype(jnp.bfloat16), input_grad.astype(jnp.bfloat16), param_grads[0], param_grads[1], param_grads[2], param_grads[3], param_grads[4], param_grads[5], param_grads[6], param_grads[7], param_grads[8], param_grads[9], param_grads[10], param_grads[11], query_clip, key_clip)
```

```python
import functools
import jax
import jax.numpy as jnp
from jax import lax
from jax.experimental import pallas as pl
from jax.experimental.pallas import tpu as pltpu
from jax.sharding import PartitionSpec as P

norm_eps = 1e-06
clip_level = 0.5


def matmul(left, right):
    return jnp.dot(left, right, preferred_element_type=jnp.float32)


def norm_parts(values):
    center = values - jnp.mean(values, axis=-1, keepdims=True)
    inverse = lax.rsqrt(jnp.mean(center * center, axis=-1, keepdims=True) + norm_eps)
    return (center * inverse, inverse)


def norm_back(grad_hat, normed, inverse):
    return inverse * (
        grad_hat
        - jnp.mean(grad_hat, axis=-1, keepdims=True)
        - normed * jnp.mean(grad_hat * normed, axis=-1, keepdims=True)
    )


def head_scale(values, gain):
    inverse = lax.rsqrt(jnp.mean(values * values, axis=-1, keepdims=True) + norm_eps)
    return values * inverse * gain


def gelu_exact(values):
    return jax.nn.gelu(values, approximate=False)


def general_layer(
    images,
    cotangent,
    ln1_gain,
    ln1_bias,
    ln2_gain,
    ln2_bias,
    q_gain,
    k_gain,
    w_query,
    w_key,
    w_value,
    w_out,
    w_up,
    w_down,
):
    (
        full_query,
        full_key,
        full_value,
        full_up,
        full_out,
        full_down,
        gain_low_one,
        shift_low_one,
        gain_low_two,
        shift_low_two,
        query_gain_low,
        key_gain_low,
    ) = (
        lax.all_gather(w_query, "shard", axis=0, tiled=True),
        lax.all_gather(w_key, "shard", axis=0, tiled=True),
        lax.all_gather(w_value, "shard", axis=0, tiled=True),
        lax.all_gather(w_up, "shard", axis=0, tiled=True),
        lax.all_gather(w_out, "shard", axis=1, tiled=True),
        lax.all_gather(w_down, "shard", axis=1, tiled=True),
        lax.all_gather(ln1_gain, "shard", axis=0, tiled=True),
        lax.all_gather(ln1_bias, "shard", axis=0, tiled=True),
        lax.all_gather(ln2_gain, "shard", axis=0, tiled=True),
        lax.all_gather(ln2_bias, "shard", axis=0, tiled=True),
        lax.all_gather(q_gain, "shard", axis=1, tiled=True),
        lax.all_gather(k_gain, "shard", axis=1, tiled=True),
    )
    gain_one = gain_low_one.astype(jnp.float32)
    shift_one = shift_low_one.astype(jnp.float32)
    gain_two = gain_low_two.astype(jnp.float32)
    shift_two = shift_low_two.astype(jnp.float32)
    query_gain = query_gain_low.astype(jnp.float32)
    key_gain = key_gain_low.astype(jnp.float32)
    count_img, local_len, width = images.shape
    tokens = count_img * local_len
    heads_here, head_size = query_gain.shape
    local_width = heads_here * head_size
    full_len = local_len * lax.axis_size("ctx")
    group = 1
    groups = count_img // group
    scale = head_size ** (-0.5)
    flat = images.reshape(tokens, width).astype(jnp.float32)
    normed_one, inverse_one = norm_parts(flat)
    hidden_one = (normed_one * gain_one + shift_one).astype(jnp.bfloat16)
    query_raw = matmul(hidden_one, full_query).reshape(tokens, heads_here, head_size)
    key_raw = matmul(hidden_one, full_key).reshape(tokens, heads_here, head_size)
    query_norm = head_scale(query_raw, query_gain).astype(jnp.bfloat16)
    key_norm = head_scale(key_raw, key_gain).astype(jnp.bfloat16)
    value_low = matmul(hidden_one, full_value).astype(jnp.bfloat16)
    key_all, value_all = (
        lax.all_gather(
            key_norm.reshape(count_img, local_len, local_width), "ctx", axis=1, tiled=True
        ),
        lax.all_gather(
            value_low.reshape(count_img, local_len, local_width), "ctx", axis=1, tiled=True
        ),
    )
    query_grp = query_norm.reshape(groups, group, local_len, heads_here, head_size)
    key_grp = key_all.reshape(groups, group, full_len, heads_here, head_size)
    value_grp = value_all.reshape(groups, group, full_len, heads_here, head_size)

    def attend(pieces):
        query_blk, key_blk, value_blk = pieces
        scores = (
            jnp.einsum("gqhd,gkhd->ghqk", query_blk, key_blk, preferred_element_type=jnp.float32)
            * scale
        )
        top = jnp.max(scores, axis=-1, keepdims=True)
        expo = jnp.exp(scores - top)
        total = jnp.sum(expo, axis=-1, keepdims=True)
        probs = (expo / total).astype(jnp.bfloat16)
        mixed_blk = jnp.einsum(
            "ghqk,gkhd->gqhd", probs, value_blk, preferred_element_type=jnp.float32
        )
        return (mixed_blk, top + jnp.log(total), jnp.max(top, axis=(0, 2, 3)))

    mixed, log_total, group_peaks = lax.map(attend, (query_grp, key_grp, value_grp))
    local_peak = jnp.max(group_peaks, axis=0)
    peak_all = lax.pmax(local_peak, ("shard", "ctx"))
    attended = mixed.reshape(tokens, local_width).astype(jnp.bfloat16)
    branch_attn = lax.psum(matmul(attended, full_out), "tp")
    resid = flat + branch_attn
    normed_two, inverse_two = norm_parts(resid)
    hidden_two = (normed_two * gain_two + shift_two).astype(jnp.bfloat16)
    up_raw = matmul(hidden_two, full_up)
    active = gelu_exact(up_raw).astype(jnp.bfloat16)
    branch_mlp = lax.psum(matmul(active, full_down).astype(jnp.bfloat16), "tp").astype(jnp.float32)
    block_out = (resid + branch_mlp).astype(jnp.bfloat16).reshape(images.shape)
    grad_out = cotangent.reshape(tokens, width).astype(jnp.float32)
    grad_down = cotangent.reshape(tokens, width)
    grad_w_down = jnp.dot(active.T, grad_down, preferred_element_type=jnp.float32)
    grad_active = matmul(grad_down, full_down.T)
    unused_up, gelu_pull = jax.vjp(gelu_exact, up_raw)
    grad_up = gelu_pull(grad_active)[0].astype(jnp.bfloat16)
    grad_w_up = jnp.dot(hidden_two.T, grad_up, preferred_element_type=jnp.float32)
    grad_two = lax.psum(matmul(grad_up, full_up.T), "tp")
    grad_gain_two = jnp.sum(grad_two * normed_two, axis=0)
    grad_shift_two = jnp.sum(grad_two, axis=0)
    grad_resid = grad_out + norm_back(grad_two * gain_two, normed_two, inverse_two)
    grad_branch = grad_resid.astype(jnp.bfloat16)
    grad_w_out = jnp.dot(attended.T, grad_branch, preferred_element_type=jnp.float32)
    grad_mixed = matmul(grad_branch, full_out.T).astype(jnp.bfloat16)
    grad_grp = grad_mixed.reshape(groups, group, local_len, heads_here, head_size)

    def attend_back(pieces):
        query_blk, key_blk, value_blk, log_blk, grad_blk = pieces
        scores = (
            jnp.einsum("gqhd,gkhd->ghqk", query_blk, key_blk, preferred_element_type=jnp.float32)
            * scale
        )
        probs = jnp.exp(scores - log_blk)
        grad_probs = jnp.einsum(
            "gqhd,gkhd->ghqk", grad_blk, value_blk, preferred_element_type=jnp.float32
        )
        grad_scores = (
            probs * (grad_probs - jnp.sum(probs * grad_probs, axis=-1, keepdims=True))
        ).astype(jnp.bfloat16)
        grad_val = jnp.einsum(
            "ghqk,gqhd->gkhd",
            probs.astype(jnp.bfloat16),
            grad_blk,
            preferred_element_type=jnp.float32,
        )
        grad_qry = (
            jnp.einsum("ghqk,gkhd->gqhd", grad_scores, key_blk, preferred_element_type=jnp.float32)
            * scale
        )
        grad_kys = (
            jnp.einsum(
                "ghqk,gqhd->gkhd", grad_scores, query_blk, preferred_element_type=jnp.float32
            )
            * scale
        )
        return (grad_qry, grad_kys, grad_val)

    grad_query_n, grad_key_full, grad_value_full = lax.map(
        attend_back, (query_grp, key_grp, value_grp, log_total, grad_grp)
    )
    grad_key_n, grad_value_n = (
        lax.psum_scatter(
            grad_key_full.reshape(count_img, full_len, local_width),
            "ctx",
            scatter_dimension=1,
            tiled=True,
        ),
        lax.psum_scatter(
            grad_value_full.reshape(count_img, full_len, local_width),
            "ctx",
            scatter_dimension=1,
            tiled=True,
        ),
    )
    unused_query, query_pull = jax.vjp(head_scale, query_raw, query_gain)
    grad_query_raw, grad_query_gain = query_pull(
        grad_query_n.reshape(tokens, heads_here, head_size)
    )
    unused_key, key_pull = jax.vjp(head_scale, key_raw, key_gain)
    grad_key_raw, grad_key_gain = key_pull(grad_key_n.reshape(tokens, heads_here, head_size))
    grad_query_low = grad_query_raw.reshape(tokens, local_width).astype(jnp.bfloat16)
    grad_key_low = grad_key_raw.reshape(tokens, local_width).astype(jnp.bfloat16)
    grad_value_low = grad_value_n.reshape(tokens, local_width).astype(jnp.bfloat16)
    grad_w_query = jnp.dot(hidden_one.T, grad_query_low, preferred_element_type=jnp.float32)
    grad_w_key = jnp.dot(hidden_one.T, grad_key_low, preferred_element_type=jnp.float32)
    grad_w_value = jnp.dot(hidden_one.T, grad_value_low, preferred_element_type=jnp.float32)
    grad_one_part = (
        matmul(grad_query_low, full_query.T)
        + matmul(grad_key_low, full_key.T)
        + matmul(grad_value_low, full_value.T)
    )
    grad_one = lax.psum(grad_one_part, "tp")
    grad_gain_one = jnp.sum(grad_one * normed_one, axis=0)
    grad_shift_one = jnp.sum(grad_one, axis=0)
    input_grad = (
        (grad_resid + norm_back(grad_one * gain_one, normed_one, inverse_one))
        .astype(jnp.bfloat16)
        .reshape(images.shape)
    )
    (
        sum_query,
        sum_key,
        sum_value,
        sum_up,
        sum_out,
        sum_down,
        sum_gain_one,
        sum_shift_one,
        sum_gain_two,
        sum_shift_two,
        sum_qgain,
        sum_kgain,
    ) = lax.psum(
        (
            grad_w_query,
            grad_w_key,
            grad_w_value,
            grad_w_up,
            grad_w_out,
            grad_w_down,
            grad_gain_one,
            grad_shift_one,
            grad_gain_two,
            grad_shift_two,
            grad_query_gain,
            grad_key_gain,
        ),
        "ctx",
    )
    (
        part_query,
        part_key,
        part_value,
        part_up,
        part_out,
        part_down,
        part_gain_one,
        part_shift_one,
        part_gain_two,
        part_shift_two,
        part_qgain,
        part_kgain,
    ) = (
        lax.psum_scatter(sum_query, "shard", scatter_dimension=0, tiled=True),
        lax.psum_scatter(sum_key, "shard", scatter_dimension=0, tiled=True),
        lax.psum_scatter(sum_value, "shard", scatter_dimension=0, tiled=True),
        lax.psum_scatter(sum_up, "shard", scatter_dimension=0, tiled=True),
        lax.psum_scatter(sum_out, "shard", scatter_dimension=1, tiled=True),
        lax.psum_scatter(sum_down, "shard", scatter_dimension=1, tiled=True),
        lax.psum_scatter(sum_gain_one, "shard", scatter_dimension=0, tiled=True),
        lax.psum_scatter(sum_shift_one, "shard", scatter_dimension=0, tiled=True),
        lax.psum_scatter(sum_gain_two, "shard", scatter_dimension=0, tiled=True),
        lax.psum_scatter(sum_shift_two, "shard", scatter_dimension=0, tiled=True),
        lax.psum_scatter(sum_qgain, "shard", scatter_dimension=1, tiled=True),
        lax.psum_scatter(sum_kgain, "shard", scatter_dimension=1, tiled=True),
    )
    factor = jnp.sqrt(clip_level / jnp.maximum(peak_all, clip_level))
    columns = jnp.repeat(factor, head_size)
    query_clip = (w_query.astype(jnp.float32) * columns).astype(jnp.bfloat16)
    key_clip = (w_key.astype(jnp.float32) * columns).astype(jnp.bfloat16)
    return (
        block_out,
        input_grad,
        part_gain_one,
        part_shift_one,
        part_gain_two,
        part_shift_two,
        part_qgain,
        part_kgain,
        part_query,
        part_key,
        part_value,
        part_out,
        part_up,
        part_down,
        query_clip,
        key_clip,
    )


MESH = pl.DeviceIdType.MESH
NN = (((1,), (0,)), ((), ()))
NT = (((1,), (1,)), ((), ()))
TN = (((0,), (0,)), ((), ()))
low_type = jnp.bfloat16
full_type = jnp.float32


def dot(left, right, dims=NN):
    return lax.dot_general(left, right, dims, preferred_element_type=full_type)


def flip(place, bits, count):
    result = 0
    unit = 1
    while unit < count:
        result = result + ((place // unit + bits // unit) % 2) * unit
        unit *= 2
    return result


def fits_fused(images, w_query, w_up, q_gain):
    count_img, local_len, width = images.shape
    ctx, shard, tp = lax.axis_size("ctx"), lax.axis_size("shard"), lax.axis_size("tp")
    rows = w_query.shape[0]
    return (
        count_img == 1
        and tp == 2
        and ctx == 4
        and shard == 4
        and rows % (16 * ctx) == 0
        and local_len % 32 == 0
        and q_gain.shape[0] % 2 == 0
        and w_up.shape[1] % (128 * ctx) == 0
    )


def fused_kernel(
    sizes,
    img_h, cot_h, small_h, wq_h, wk_h, wv_h, wo_h, wup_h, wdn_h,
    bo_o, ig_o, upo, dno, qkvo, lnr_o, qkr_o, peak_o,
    xg, ctg, smalls, wl, wol, wdl, wqkv, wot, wup, wdt, wtmp,
    xh1, h1, nq, nk, sq, sk, qs, kall, vall, pst, sbuf, attq, attr, pks,
    h2, ga, act, gu, g2s, g2r, g2own, bos, bor, boown,
    gsib_s, gsib_r, gown, gz_s, gz_r, gfin,
    gres, gbg, gms, gm, dqb, dkt, dvt, dks_s, dks_r, dqr, dkr, dvr,
    g1s, g1r, g1own, qsib_s, qsib_r, qown, qz_s, qz_r, qfin,
    rows_s, rows_r, obuf,
    lsem, ssem, rsem,
):
    CN, ZN, TB, D, HW, FS, R = sizes
    QR = R // CN
    HR = R // 2
    s_i, c_i, t_i = lax.axis_index("shard"), lax.axis_index("ctx"), lax.axis_index("tp")
    o_i = 1 - t_i
    half_chips = CN // 2
    tstar = c_i // half_chips
    place = c_i % half_chips
    TK = CN * TB
    inv_d = 1.0 / D

    def at_ctx(j):
        return (s_i, flip(c_i, j, CN), t_i)

    def at_z(j):
        return (flip(s_i, j, ZN), c_i, t_i)

    sib = (s_i, c_i, o_i)

    spots = {}

    def spot(name, count):
        if name not in spots:
            spots[name] = (sum(n for _, n in spots.values()), count)
        return spots[name][0]

    def put(name, count, j, src, dst, dev):
        base = spot(name, count)
        pltpu.make_async_remote_copy(
            src_ref=src, dst_ref=dst, send_sem=ssem.at[base + j], recv_sem=rsem.at[base + j],
            device_id=dev, device_id_type=MESH,
        ).start()

    def got(name, count, j, dst, dev):
        base = spot(name, count)
        pltpu.make_async_remote_copy(
            src_ref=dst, dst_ref=dst, send_sem=ssem.at[base + j], recv_sem=rsem.at[base + j],
            device_id=dev, device_id_type=MESH,
        ).wait_recv()

    def sent(name, count, j, src, dev):
        base = spot(name, count)
        pltpu.make_async_remote_copy(
            src_ref=src, dst_ref=src, send_sem=ssem.at[base + j], recv_sem=rsem.at[base + j],
            device_id=dev, device_id_type=MESH,
        ).wait_send()

    x_src = img_h.at[0, pl.ds(t_i * TB, TB)]
    c_src = cot_h.at[0, pl.ds(t_i * TB, TB)]
    locals_ = [
        pltpu.make_async_copy(wk_h, wl.at[1], lsem.at[0]),
        pltpu.make_async_copy(wv_h, wl.at[2], lsem.at[1]),
        pltpu.make_async_copy(wq_h, wl.at[0], lsem.at[2]),
        pltpu.make_async_copy(x_src, xg.at[0], lsem.at[3]),
        pltpu.make_async_copy(wo_h, wol, lsem.at[4]),
        pltpu.make_async_copy(wdn_h.at[pl.ds(c_i * FS, FS)], wdl, lsem.at[5]),
        pltpu.make_async_copy(wup_h.at[:, pl.ds(c_i * FS, FS)], wup.at[t_i, s_i], lsem.at[6]),
        pltpu.make_async_copy(c_src, ctg.at[0], lsem.at[7]),
    ]
    for copy in locals_:
        copy.start()

    barrier = pltpu.get_barrier_semaphore()
    greet = [at_ctx(j) for j in range(1, CN)] + [at_z(j) for j in range(1, ZN)] + [sib]
    for dev in greet:
        pl.semaphore_signal(barrier, inc=1, device_id=dev, device_id_type=MESH)
    pl.semaphore_wait(barrier, len(greet))

    for j in range(1, CN):
        put("x", CN, j, x_src, xg.at[j], at_ctx(j))
    smalls[t_i, s_i] = small_h[...]
    for j in range(1, ZN):
        put("small", ZN, j, small_h, smalls.at[t_i, s_i], at_z(j))

    order_w = (1, 2, 0)

    @pl.when(t_i == tstar)
    def _():
        pick = (
            lax.broadcasted_iota(jnp.int32, (half_chips * HW, HW), 0)
            == lax.broadcasted_iota(jnp.int32, (half_chips * HW, HW), 1) + place * HW
        ).astype(full_type).astype(low_type)
        for n, g in enumerate(order_w):
            locals_[n].wait()
            wqkv[g, s_i] = dot(wl[g], pick).astype(low_type)
            for j in range(1, ZN):
                put("w%d" % g, ZN, j, wqkv.at[g, s_i], wqkv.at[g, s_i], at_z(j))
            put("w%d" % g, ZN, 0, wqkv.at[g, s_i], wqkv.at[g, s_i], sib)

    @pl.when(t_i != tstar)
    def _():
        for n in range(3):
            locals_[n].wait()
            spot("w%d" % order_w[n], ZN)

    locals_[4].wait()
    for kk in range(half_chips):
        wtmp[...] = wol[kk * HW:(kk + 1) * HW, :].astype(full_type).T.astype(low_type).reshape(CN, QR, HW)
        wot[half_chips * t_i + kk, s_i, c_i] = wtmp[c_i]
    for j in range(1, ZN):
        block = wot.at[pl.ds(half_chips * t_i, half_chips), s_i, c_i]
        put("woz", ZN, j, block, block, at_z(j))
    locals_[5].wait()
    wdt[t_i, s_i] = wdl[...].astype(full_type).T.astype(low_type)

    for j in range(1, ZN):
        got("small", ZN, j, smalls.at[t_i, flip(s_i, j, ZN)], at_z(j))
    put("smallt", 1, 0, smalls.at[t_i], smalls.at[t_i], sib)

    locals_[3].wait()

    def norm_rows(values):
        mean = jnp.sum(values, axis=-1, keepdims=True) * inv_d
        center = values - mean
        inverse = lax.rsqrt(jnp.sum(center * center, axis=-1, keepdims=True) * inv_d + norm_eps)
        return center * inverse, inverse

    ln_rows = jnp.concatenate([smalls[t_i, k][:, :R] for k in range(ZN)], axis=1)
    g1row, b1row, g2row, b2row = (ln_rows[k:k + 1] for k in range(4))

    def first_norm(j, _):
        @pl.when(j > 0)
        def _():
            got("x", CN, j, xg.at[j], at_ctx(j))

        normed, _unused = norm_rows(xg[j].astype(full_type))
        xh1[j] = normed
        h1[j] = (normed * g1row + b1row).astype(low_type)
        return 0

    lax.fori_loop(0, CN, first_norm, 0)

    got("smallt", 1, 0, smalls.at[o_i], sib)
    head_rows = smalls[0, 0][4:6, :HW]
    for a in range(2):
        for k in range(ZN):
            if a or k:
                head_rows = head_rows + smalls[a, k][4:6, :HW]
    qgrow, kgrow = head_rows[0:1], head_rows[1:2]

    lane = lax.broadcasted_iota(jnp.int32, (1, HW), 1) // 64
    heads = HW // 64
    mask_f = [(lane == h).astype(full_type) for h in range(heads)]
    mask_b = [m.astype(low_type) for m in mask_f]
    same_head = (
        lax.broadcasted_iota(jnp.int32, (HW, HW), 0) // 64
        == lax.broadcasted_iota(jnp.int32, (HW, HW), 1) // 64
    ).astype(full_type).astype(low_type)

    def head_mean(values):
        high = values.astype(low_type)
        rest = (values - high.astype(full_type)).astype(low_type)
        return (dot(high, same_head) + dot(rest, same_head)) * (1.0 / 64)

    def weight_ready(g):
        @pl.when(t_i != tstar)
        def _():
            got("w%d" % g, ZN, 0, wqkv.at[g, s_i], sib)

        for j in range(1, ZN):
            block = wqkv.at[g, flip(s_i, j, ZN)]
            got("w%d" % g, ZN, j, block, sib)

            @pl.when(t_i == tstar)
            def _():
                put("f%d" % g, ZN, j, block, block, sib) if False else pltpu.make_async_remote_copy(
                    src_ref=block, dst_ref=block,
                    send_sem=ssem.at[spot("f%d" % g, ZN) + j],
                    recv_sem=rsem.at[spot("w%d" % g, ZN) + j],
                    device_id=sib, device_id_type=MESH,
                ).start()

    def project(g):
        return dot(h1[...].reshape(TK, D), wqkv[g].reshape(D, HW))

    weight_ready(1)
    raw = project(1)
    inverse = lax.rsqrt(head_mean(raw * raw) + norm_eps)
    normed = raw * inverse
    nk[...] = normed
    sk[...] = inverse
    kall[0] = (normed * kgrow).astype(low_type)
    put("k", 1, 0, kall.at[0], kall.at[1], sib)
    weight_ready(2)
    vall[0] = project(2).astype(low_type)
    put("v", 1, 0, vall.at[0], vall.at[1], sib)
    weight_ready(0)
    for j in range(1, ZN):
        put("wdz", ZN, j, wdt.at[t_i, s_i], wdt.at[t_i, s_i], at_z(j))
    locals_[6].wait()
    for j in range(1, ZN):
        put("wuz", ZN, j, wup.at[t_i, s_i], wup.at[t_i, s_i], at_z(j))
    raw = project(0)
    inverse = lax.rsqrt(head_mean(raw * raw) + norm_eps)
    normed = raw * inverse
    nq[...] = normed
    sq[...] = inverse
    qs[...] = ((normed * qgrow).astype(low_type) * 0.125).astype(low_type).reshape(CN, TB, HW)

    mine = pl.ds(half_chips * t_i, half_chips)
    for j in range(1, ZN):
        got("woz", ZN, j, wot.at[mine, flip(s_i, j, ZN), c_i], at_z(j))
    for j in range(1, CN):
        put("woc", CN, j, wot.at[mine, :, c_i], wot.at[mine, :, c_i], at_ctx(j))
    for j in range(1, CN):
        put("ct", CN, j, c_src, ctg.at[j], at_ctx(j))
    got("k", 1, 0, kall.at[1], sib)
    got("v", 1, 0, vall.at[1], sib)

    step = 32
    ones_of = lax.broadcasted_iota(jnp.int32, (8, 128), 1)

    def stacked(block):
        return jnp.concatenate([block * m for m in mask_b], axis=0)

    def folded(block):
        total = block[0:TB] * mask_f[0]
        for h in range(1, heads):
            total = total + block[h * TB:(h + 1) * TB] * mask_f[h]
        return total

    pks[0] = jnp.full((8, 128), -3.0e38, full_type)

    def attend(i, _):
        j = CN - 1 - i

        @pl.when(i == 2)
        def _():
            for q in range(1, CN):
                got("woc", CN, q, wot.at[mine, :, flip(c_i, q, CN)], at_ctx(q))
            put("wot", 1, 0, wot.at[mine], wot.at[mine], sib)

        sbuf[...] = dot(stacked(qs[j]), kall[...].reshape(2 * TK, HW), NT)

        for h in range(heads):
            def soft(r, top_all):
                rows = pl.ds(pl.multiple_of(h * TB + r * step, step), step)
                scores = sbuf[rows]
                top = jnp.max(scores, axis=-1, keepdims=True)
                expo = jnp.exp(scores - top)
                total = jnp.sum(expo, axis=-1, keepdims=True)
                pst[j, rows] = expo * (1.0 / total)
                return jnp.maximum(top_all, jnp.max(top, axis=0, keepdims=True))

            peak = lax.fori_loop(0, TB // step, soft, jnp.full((1, 1), -3.0e38, full_type))
            pks[0] = jnp.where(ones_of == c_i * heads + h, jnp.maximum(pks[0], peak), pks[0])
        mixed = folded(dot(pst[j].astype(low_type), vall[...].reshape(2 * TK, HW)))
        attq[j] = mixed.astype(low_type)

        @pl.when(j > 0)
        def _():
            put("att", CN, j, attq.at[j], attr.at[j], at_ctx(j))

        return 0

    lax.fori_loop(0, CN, attend, 0)
    put("pkt", 1, 0, pks.at[0], pks.at[1], sib)

    got("wot", 1, 0, wot.at[pl.ds(half_chips * o_i, half_chips)], sib)
    branch = dot(attq[0], wot[c_i].reshape(D, HW), NT)
    for j in range(1, CN):
        got("att", CN, j, attr.at[j], at_ctx(j))
        branch = branch + dot(attr[j], wot[flip(c_i, j, CN)].reshape(D, HW), NT)
    resid = xg[0].astype(full_type) + branch
    boown[...] = resid
    xhat2, inv2 = norm_rows(resid)
    h2[0] = (xhat2 * g2row + b2row).astype(low_type)
    for j in range(1, CN):
        put("h2", CN, j, h2.at[0], h2.at[j], at_ctx(j))

    locals_[7].wait()
    for j in range(1, CN):
        got("ct", CN, j, ctg.at[j], at_ctx(j))
    for j in range(1, ZN):
        got("wdz", ZN, j, wdt.at[t_i, flip(s_i, j, ZN)], at_z(j))
    put("wdt", 1, 0, wdt.at[t_i], wdt.at[t_i], sib)
    ga[t_i] = dot(ctg[...].reshape(TK, D), wdt[t_i].reshape(D, FS)).reshape(CN, TB, FS)
    for j in range(1, ZN):
        got("wuz", ZN, j, wup.at[t_i, flip(s_i, j, ZN)], at_z(j))
    put("wut", 1, 0, wup.at[t_i], wup.at[t_i], sib)
    got("wdt", 1, 0, wdt.at[o_i], sib)
    ga[o_i] = dot(ctg[...].reshape(TK, D), wdt[o_i].reshape(D, FS)).reshape(CN, TB, FS)
    got("wut", 1, 0, wup.at[o_i], sib)

    def mlp(j, _):
        @pl.when(j > 0)
        def _():
            got("h2", CN, j, h2.at[j], at_ctx(j))

        block = h2[j]
        for a in range(2):
            up = dot(block, wup[a].reshape(D, FS))
            phi = 0.5 * (1.0 + lax.erf(up * 0.7071067811865476))
            dens = jnp.exp(up * up * -0.5) * 0.3989422804014327
            act[a, j] = (up * phi).astype(low_type)
            gu[a, j] = (ga[a, j] * (phi + up * dens)).astype(low_type)
        grad_two = dot(gu[0, j], wup[0].reshape(D, FS), NT) + dot(gu[1, j], wup[1].reshape(D, FS), NT)

        @pl.when(j == 0)
        def _():
            g2own[...] = grad_two

        @pl.when(j > 0)
        def _():
            g2s[j] = grad_two.astype(low_type)
            put("g2", CN, j, g2s.at[j], g2r.at[j], at_ctx(j))

        return 0

    lax.fori_loop(0, CN, mlp, 0)

    h2_all = h2[...].reshape(TK, D)
    ct_all = ctg[...].reshape(TK, D)
    gsib_s[0] = dot(h2_all, gu[o_i].reshape(TK, FS), TN).astype(low_type)
    put("gs", 2, 0, gsib_s.at[0], gsib_r.at[0], sib)
    gsib_s[1] = dot(ct_all, act[o_i].reshape(TK, FS), TN).astype(low_type)
    put("gs", 2, 1, gsib_s.at[1], gsib_r.at[1], sib)
    gown[0] = dot(h2_all, gu[t_i].reshape(TK, FS), TN)
    gown[1] = dot(ct_all, act[t_i].reshape(TK, FS), TN)

    def down(j, _):
        part = dot(act[0, j], wdt[0].reshape(D, FS), NT) + dot(act[1, j], wdt[1].reshape(D, FS), NT)

        @pl.when(j == 0)
        def _():
            boown[...] += part

        @pl.when(j > 0)
        def _():
            bos[j] = part.astype(low_type)

        return 0

    lax.fori_loop(0, CN, down, 0)

    for k in range(2):
        got("gs", 2, k, gsib_r.at[k], sib)
        gown[k] = gown[k] + gsib_r[k].astype(full_type)
        gz_s[k] = gown[k].astype(low_type).reshape(ZN, R, FS)
        for j in range(1, ZN):
            put("gz%d" % k, ZN, j, gz_s.at[k, flip(s_i, j, ZN)], gz_r.at[k, j], at_z(j))

    grad_two = g2own[...]
    for j in range(1, CN):
        got("g2", CN, j, g2r.at[j], at_ctx(j))
        grad_two = grad_two + g2r[j].astype(full_type)
    ln2g = jnp.sum(grad_two * xhat2, axis=0, keepdims=True)
    ln2b = jnp.sum(grad_two, axis=0, keepdims=True)
    hat = grad_two * g2row
    grad_resid = ctg[0].astype(full_type) + inv2 * (
        hat
        - jnp.sum(hat, axis=-1, keepdims=True) * inv_d
        - xhat2 * (jnp.sum(hat * xhat2, axis=-1, keepdims=True) * inv_d)
    )
    gres[...] = grad_resid
    gb = grad_resid.astype(low_type)
    gbg[0] = gb
    for j in range(CN - 1, 0, -1):
        gms[j] = dot(gb, wot[flip(c_i, j, CN)].reshape(D, HW)).astype(low_type)
        put("gm", CN, j, gms.at[j], gm.at[j], at_ctx(j))
    gm[0] = dot(gb, wot[c_i].reshape(D, HW)).astype(low_type)
    for j in range(1, CN):
        put("gb", CN, j, gbg.at[0], gbg.at[j], at_ctx(j))
    for j in range(1, CN):
        put("bo", CN, j, bos.at[j], bor.at[j], at_ctx(j))

    dkt[...] = jnp.zeros_like(dkt)
    dvt[...] = jnp.zeros_like(dvt)

    def attend_back(j, _):
        @pl.when(j > 0)
        def _():
            got("gm", CN, j, gm.at[j], at_ctx(j))

        grad_rows = stacked(gm[j])
        query_rows = stacked(qs[j])
        sbuf[...] = dot(grad_rows, vall[...].reshape(2 * TK, HW), NT)

        def soft(r, _):
            rows = pl.ds(pl.multiple_of(r * step, step), step)
            probs = pst[j, rows]
            grad_probs = sbuf[rows]
            inner = jnp.sum(probs * grad_probs, axis=-1, keepdims=True)
            sbuf[rows] = probs * (grad_probs - inner)
            return 0

        lax.fori_loop(0, heads * TB // step, soft, 0)
        grad_scores = sbuf[...].astype(low_type)
        dqb[j] = folded(dot(grad_scores, kall[...].reshape(2 * TK, HW))) * 0.125
        dvt[...] += dot(grad_rows, pst[j].astype(low_type), TN)
        dkt[...] += dot(query_rows, grad_scores, TN)
        return 0

    lax.fori_loop(0, CN, attend_back, 0)
    dks_s[0] = dvt[:, TK:].astype(low_type)
    dks_s[1] = dkt[:, TK:].astype(low_type)
    for k in range(2):
        put("dk", 2, k, dks_s.at[k], dks_r.at[k], sib)

    def unnorm(grad_n, gain_row, normed, inverse):
        gain_grad = jnp.sum(grad_n * normed, axis=0, keepdims=True)
        e = grad_n * gain_row
        return (inverse * (e - normed * head_mean(e * normed))).astype(low_type), gain_grad

    h1_all = h1[...].reshape(TK, D)

    def share_grad(n, left, right):
        full = dot(left, right, TN).reshape(ZN, 2, HR, HW)
        low_full = full.astype(low_type)
        for k in range(2):
            @pl.when(o_i == k)
            def _():
                qsib_s[n] = low_full[:, k]

            @pl.when(t_i == k)
            def _():
                qown[n] = full[:, k]

        put("qg", 4, n, qsib_s.at[n], qsib_r.at[n], sib)

    def reduce_grad(n):
        got("qg", 4, n, qsib_r.at[n], sib)
        total = qown[n] + qsib_r[n].astype(full_type)
        qown[n] = total
        qz_s[n] = total.astype(low_type)
        for j in range(1, ZN):
            put("qz%d" % n, ZN, j, qz_s.at[n, flip(s_i, j, ZN)], qz_r.at[n, j], at_z(j))

    grad_raw, q_gain_row = unnorm(dqb[...].reshape(TK, HW), qgrow, nq[...], sq[...])
    dqr[...] = grad_raw
    for j in range(1, CN):
        got("gb", CN, j, gbg.at[j], at_ctx(j))
    share_grad(3, gbg[...].reshape(TK, D), attq[...].reshape(TK, HW))
    share_grad(0, h1_all, dqr[...])
    got("dk", 2, 0, dks_r.at[0], sib)
    dvr[...] = (dvt[:, :TK] + dks_r[0].astype(full_type)).T.astype(low_type)
    share_grad(2, h1_all, dvr[...])
    got("dk", 2, 1, dks_r.at[1], sib)
    grad_k = (dkt[:, :TK] + dks_r[1].astype(full_type)).T
    grad_raw, k_gain_row = unnorm(grad_k, kgrow, nk[...], sk[...])
    dkr[...] = grad_raw

    ln1g = jnp.zeros((1, D), full_type)
    ln1b = jnp.zeros((1, D), full_type)
    for j in range(CN - 1, -1, -1):
        rows = slice(j * TB, (j + 1) * TB)
        part = (
            dot(dqr[rows], wqkv[0].reshape(D, HW), NT)
            + dot(dkr[rows], wqkv[1].reshape(D, HW), NT)
            + dot(dvr[rows], wqkv[2].reshape(D, HW), NT)
        )
        ln1g = ln1g + jnp.sum(part * xh1[j], axis=0, keepdims=True)
        ln1b = ln1b + jnp.sum(part, axis=0, keepdims=True)
        if j:
            g1s[j] = part.astype(low_type)
            put("g1", CN, j, g1s.at[j], g1r.at[j], at_ctx(j))
        else:
            g1own[...] = part
    share_grad(1, h1_all, dkr[...])
    rows_s[0] = jnp.zeros_like(rows_s[0])
    for k, row in enumerate((ln1g, ln1b, ln2g, ln2b)):
        rows_s[0, k:k + 1, :D] = row
    rows_s[0, 0:1, D:D + HW] = q_gain_row
    rows_s[0, 1:2, D:D + HW] = k_gain_row
    put("rt", 1, 0, rows_s.at[0], rows_r.at[0], sib)
    reduce_grad(3)
    reduce_grad(0)
    reduce_grad(2)
    reduce_grad(1)
    got("rt", 1, 0, rows_r.at[0], sib)
    rows_s[1] = rows_s[0] + rows_r[0]
    for j in range(1, ZN):
        put("rz", ZN, j, rows_s.at[1], rows_r.at[j], at_z(j))

    for k, out in ((0, upo), (1, dno)):
        total = gown[k, pl.ds(pl.multiple_of(s_i * R, R), R)]
        for j in range(1, ZN):
            got("gz%d" % k, ZN, j, gz_r.at[k, j], at_z(j))
            total = total + gz_r[k, j].astype(full_type)
        gfin[k] = total.astype(low_type)
        for j in range(1, CN):
            put("gc%d" % k, CN, j, gfin.at[k], out.at[c_i], at_ctx(j))
        pltpu.make_async_copy(gfin.at[k], out.at[c_i], lsem.at[8 + k]).start()

    total = boown[...]
    for j in range(1, CN):
        got("bo", CN, j, bor.at[j], at_ctx(j))
        total = total + bor[j].astype(full_type)
    own_rows = pl.ds(t_i * TB, TB)
    obuf[0] = total.astype(low_type)
    put("ob", 2, 0, obuf.at[0], bo_o.at[own_rows], sib)
    pltpu.make_async_copy(obuf.at[0], bo_o.at[own_rows], lsem.at[10]).start()

    got("pkt", 1, 0, pks.at[1], sib)
    pks[2] = jnp.maximum(pks[0], pks[1])
    for j in range(1, ZN):
        put("pkz", ZN, j, pks.at[2], pks.at[2 + j], at_z(j))

    xhat1, inv1 = norm_rows(xg[0].astype(full_type))
    grad_one = g1own[...]
    for j in range(1, CN):
        got("g1", CN, j, g1r.at[j], at_ctx(j))
        grad_one = grad_one + g1r[j].astype(full_type)
    hat = grad_one * g1row
    grad_in = gres[...] + inv1 * (
        hat
        - jnp.sum(hat, axis=-1, keepdims=True) * inv_d
        - xhat1 * (jnp.sum(hat * xhat1, axis=-1, keepdims=True) * inv_d)
    )
    obuf[1] = grad_in.astype(low_type)
    put("ob", 2, 1, obuf.at[1], ig_o.at[own_rows], sib)
    pltpu.make_async_copy(obuf.at[1], ig_o.at[own_rows], lsem.at[11]).start()

    peak = pks[2]
    for j in range(1, ZN):
        got("pkz", ZN, j, pks.at[2 + j], at_z(j))
        peak = jnp.maximum(peak, pks[2 + j])
    first = 2 + ZN
    pks[first] = peak
    for j in range(1, CN):
        put("pkc", CN, j, pks.at[first], pks.at[first + j], at_ctx(j))

    for n in (3, 0, 2, 1):
        total = qown[n, s_i]
        for j in range(1, ZN):
            got("qz%d" % n, ZN, j, qz_r.at[n, j], at_z(j))
            total = total + qz_r[n, j].astype(full_type)
        qfin[n] = total.astype(low_type)

    target = qkvo.at[place, t_i]
    for j in range(1, CN):
        pltpu.make_async_remote_copy(
            src_ref=qfin, dst_ref=target,
            send_sem=ssem.at[spot("qcs", CN) + j],
            recv_sem=rsem.at[spot("qcr", 2 * half_chips) + place * 2 + t_i],
            device_id=(s_i, flip(c_i, j, CN), tstar), device_id_type=MESH,
        ).start()

    @pl.when(t_i == tstar)
    def _():
        pltpu.make_async_copy(qfin, target, lsem.at[12]).start()

    @pl.when(t_i != tstar)
    def _():
        pltpu.make_async_remote_copy(
            src_ref=qfin, dst_ref=target,
            send_sem=ssem.at[spot("qcs", CN)],
            recv_sem=rsem.at[spot("qcr", 2 * half_chips) + place * 2 + t_i],
            device_id=sib, device_id_type=MESH,
        ).start()

    rows_sum = rows_s[1]
    for j in range(1, ZN):
        got("rz", ZN, j, rows_r.at[j], at_z(j))
        rows_sum = rows_sum + rows_r[j]
    rows_s[2] = rows_sum
    for j in range(1, CN):
        put("rc", CN, j, rows_s.at[2], rows_r.at[ZN + j], at_ctx(j))
    qkr_o[c_i] = rows_sum[:, D:]
    total = rows_sum[:, :D]
    for j in range(1, CN):
        got("rc", CN, j, rows_r.at[ZN + j], at_ctx(j))
        block = rows_r[ZN + j]
        total = total + block[:, :D]
        qkr_o[flip(c_i, j, CN)] = block[:, D:]
    lnr_o[...] = total
    for j in range(1, CN):
        got("pkc", CN, j, pks.at[first + j], at_ctx(j))
        peak = jnp.maximum(peak, pks[first + j])
    peak_o[...] = peak

    for k, out in ((0, upo), (1, dno)):
        for j in range(1, CN):
            got("gc%d" % k, CN, j, out.at[flip(c_i, j, CN)], at_ctx(j))
        pltpu.make_async_copy(gfin.at[k], out.at[c_i], lsem.at[8 + k]).wait()
    other_rows = pl.ds(o_i * TB, TB)
    for k, out in ((0, bo_o), (1, ig_o)):
        got("ob", 2, k, out.at[other_rows], sib)
        pltpu.make_async_copy(obuf.at[k], out.at[own_rows], lsem.at[10 + k]).wait()

    @pl.when(t_i == tstar)
    def _():
        pltpu.make_async_copy(qfin, target, lsem.at[12]).wait()

    for p in range(half_chips):
        for a in range(2):
            @pl.when((t_i != tstar) | (place != p) | (t_i != a))
            def _():
                pltpu.make_async_remote_copy(
                    src_ref=qfin, dst_ref=qkvo.at[p, a],
                    send_sem=ssem.at[spot("qcs", CN)],
                    recv_sem=rsem.at[spot("qcr", 2 * half_chips) + p * 2 + a],
                    device_id=sib, device_id_type=MESH,
                ).wait_recv()

    for j in range(1, CN):
        sent("x", CN, j, x_src, sib)
        sent("ct", CN, j, c_src, sib)
        sent("woc", CN, j, wot.at[mine, :, c_i], sib)
        sent("att", CN, j, attq.at[j], sib)
        sent("h2", CN, j, h2.at[0], sib)
        sent("g2", CN, j, g2s.at[j], sib)
        sent("gm", CN, j, gms.at[j], sib)
        sent("gb", CN, j, gbg.at[0], sib)
        sent("bo", CN, j, bos.at[j], sib)
        sent("g1", CN, j, g1s.at[j], sib)
        sent("pkc", CN, j, pks.at[first], sib)
        sent("rc", CN, j, rows_s.at[2], sib)
        sent("gc0", CN, j, gfin.at[0], sib)
        sent("gc1", CN, j, gfin.at[1], sib)
        sent("qcs", CN, j, qfin, sib)
    for j in range(1, ZN):
        sent("small", ZN, j, small_h, sib)
        sent("woz", ZN, j, wot.at[mine, s_i, c_i], sib)
        sent("wdz", ZN, j, wdt.at[t_i, s_i], sib)
        sent("wuz", ZN, j, wup.at[t_i, s_i], sib)
        sent("gz0", ZN, j, gz_s.at[0, 0], sib)
        sent("gz1", ZN, j, gz_s.at[1, 0], sib)
        sent("pkz", ZN, j, pks.at[2], sib)
        sent("rz", ZN, j, rows_s.at[1], sib)
        for n in range(4):
            sent("qz%d" % n, ZN, j, qz_s.at[n, 0], sib)
    sent("smallt", 1, 0, smalls.at[t_i], sib)
    sent("k", 1, 0, kall.at[0], sib)
    sent("v", 1, 0, vall.at[0], sib)
    sent("pkt", 1, 0, pks.at[0], sib)
    sent("wot", 1, 0, wot.at[mine], sib)
    sent("wdt", 1, 0, wdt.at[t_i], sib)
    sent("wut", 1, 0, wup.at[t_i], sib)
    sent("rt", 1, 0, rows_s.at[0], sib)
    for k in range(2):
        sent("gs", 2, k, gsib_s.at[k], sib)
        sent("dk", 2, k, dks_s.at[k], sib)
        sent("ob", 2, k, obuf.at[k], sib)
    for n in range(4):
        sent("qg", 4, n, qsib_s.at[n], sib)

    @pl.when(t_i == tstar)
    def _():
        for g in range(3):
            for j in range(ZN):
                sent("w%d" % g, ZN, j, wqkv.at[g, s_i], sib)
                if j:
                    sent("f%d" % g, ZN, j, wqkv.at[g, s_i], sib)

    @pl.when(t_i != tstar)
    def _():
        sent("qcs", CN, 0, qfin, sib)


SEMS = 320


def fused_call(sizes, *operands):
    CN, ZN, TB, D, HW, FS, R = sizes
    TK = CN * TB
    QR, HR = R // CN, R // 2
    half_chips = CN // 2
    heads = HW // 64
    lo, hi = low_type, full_type
    V = pltpu.VMEM
    any_spec = pl.BlockSpec(memory_space=pl.ANY)
    vm_spec = pl.BlockSpec(memory_space=pltpu.VMEM)
    out_shape = [
        jax.ShapeDtypeStruct((2 * TB, D), lo),
        jax.ShapeDtypeStruct((2 * TB, D), lo),
        jax.ShapeDtypeStruct((CN, R, FS), lo),
        jax.ShapeDtypeStruct((CN, R, FS), lo),
        jax.ShapeDtypeStruct((half_chips, 2, 4, HR, HW), lo),
        jax.ShapeDtypeStruct((8, D), hi),
        jax.ShapeDtypeStruct((CN, 8, 256), hi),
        jax.ShapeDtypeStruct((8, 128), hi),
    ]
    scratch = [
        V((CN, TB, D), lo), V((CN, TB, D), lo), V((2, ZN, 8, 256), hi),
        V((3, R, half_chips * HW), lo), V((half_chips * HW, R), lo), V((FS, R), lo),
        V((3, ZN, R, HW), lo), V((CN, ZN, CN, QR, HW), lo), V((2, ZN, R, FS), lo), V((2, ZN, R, FS), lo),
        V((CN, QR, HW), lo),
        V((CN, TB, D), hi), V((CN, TB, D), lo),
        V((TK, HW), hi), V((TK, HW), hi), V((TK, HW), hi), V((TK, HW), hi),
        V((CN, TB, HW), lo), V((2, TK, HW), lo), V((2, TK, HW), lo),
        V((CN, heads * TB, 2 * TK), hi), V((heads * TB, 2 * TK), hi),
        V((CN, TB, HW), lo), V((CN, TB, HW), lo), V((2 + ZN + CN, 8, 128), hi),
        V((CN, TB, D), lo), V((2, CN, TB, FS), hi), V((2, CN, TB, FS), lo), V((2, CN, TB, FS), lo),
        V((CN, TB, D), lo), V((CN, TB, D), lo), V((TB, D), hi),
        V((CN, TB, D), lo), V((CN, TB, D), lo), V((TB, D), hi),
        V((2, D, FS), lo), V((2, D, FS), lo), V((2, D, FS), hi),
        V((2, ZN, R, FS), lo), V((2, ZN, R, FS), lo), V((2, R, FS), lo),
        V((TB, D), hi), V((CN, TB, D), lo), V((CN, TB, HW), lo), V((CN, TB, HW), lo),
        V((CN, TB, HW), hi), V((HW, 2 * TK), hi), V((HW, 2 * TK), hi),
        V((2, HW, TK), lo), V((2, HW, TK), lo), V((TK, HW), lo), V((TK, HW), lo), V((TK, HW), lo),
        V((CN, TB, D), lo), V((CN, TB, D), lo), V((TB, D), hi),
        V((4, ZN, HR, HW), lo), V((4, ZN, HR, HW), lo), V((4, ZN, HR, HW), hi),
        V((4, ZN, HR, HW), lo), V((4, ZN, HR, HW), lo), V((4, HR, HW), lo),
        V((3, 8, D + 256), hi), V((ZN + CN, 8, D + 256), hi), V((2, TB, D), lo),
        pltpu.SemaphoreType.DMA((16,)), pltpu.SemaphoreType.DMA((SEMS,)), pltpu.SemaphoreType.DMA((SEMS,)),
    ]
    return pl.pallas_call(
        functools.partial(fused_kernel, sizes),
        out_shape=out_shape,
        in_specs=[any_spec, any_spec, vm_spec] + [any_spec] * 6,
        out_specs=[any_spec] * 5 + [vm_spec] * 3,
        scratch_shapes=scratch,
        compiler_params=pltpu.CompilerParams(
            collective_id=0, has_side_effects=True, vmem_limit_bytes=56 * 2**20
        ),
    )(*operands)


def fused_layer(
    images, cotangent, ln1_gain, ln1_bias, ln2_gain, ln2_bias, q_gain, k_gain,
    w_query, w_key, w_value, w_out, w_up, w_down,
):
    CN, ZN = lax.axis_size("ctx"), lax.axis_size("shard")
    s_i, c_i, t_i = lax.axis_index("shard"), lax.axis_index("ctx"), lax.axis_index("tp")
    TB = images.shape[1] // 2
    D = images.shape[2]
    R = w_query.shape[0]
    half_chips = CN // 2
    HW = w_query.shape[1] // half_chips
    FS = w_up.shape[1] // CN
    heads_here, piece = q_gain.shape
    sizes = (CN, ZN, TB, D, HW, FS, R)
    slot = jnp.arange(ZN) == s_i

    def head_row(gain):
        spread = jnp.where(slot[None, :, None], gain.astype(full_type)[:, None, :], 0.0)
        spread = spread.reshape(half_chips, HW)
        chosen = jnp.where((jnp.arange(half_chips) == c_i % half_chips)[:, None], spread, 0.0).sum(0)
        return jnp.where(t_i == c_i // half_chips, chosen, 0.0)

    def padded(row):
        return jnp.pad(row.astype(full_type), (0, 256 - row.shape[0]))

    small = jnp.stack(
        [padded(r) for r in (ln1_gain, ln1_bias, ln2_gain, ln2_bias, head_row(q_gain), head_row(k_gain))]
        + [jnp.zeros((256,), full_type)] * 2
    )
    bo, ig, up, dn, qkvo, lnr, qkr, peak = fused_call(
        sizes, images, cotangent, small, w_query, w_key, w_value, w_out, w_up, w_down
    )
    grads = qkvo.transpose(2, 1, 3, 0, 4).reshape(4, R, half_chips * HW).astype(full_type)
    g_up = up.transpose(1, 0, 2).reshape(R, CN * FS).astype(full_type)
    g_down = dn.transpose(0, 2, 1).reshape(CN * FS, R).astype(full_type)
    ln = lax.dynamic_slice(lnr, (0, s_i * R), (4, R))
    mine = lax.dynamic_slice(qkr, (t_i * half_chips, 0, 0), (half_chips, 2, HW))
    mine = mine.transpose(1, 0, 2).reshape(2, heads_here, ZN, piece)
    mine = lax.dynamic_slice(mine, (0, 0, s_i, 0), (2, heads_here, 1, piece))[:, :, 0]
    peaks = lax.dynamic_slice(peak[0], (t_i * heads_here,), (heads_here,))
    factor = jnp.sqrt(clip_level / jnp.maximum(peaks, clip_level))
    columns = jnp.repeat(factor, HW * half_chips // heads_here)
    query_clip = (w_query.astype(full_type) * columns).astype(low_type)
    key_clip = (w_key.astype(full_type) * columns).astype(low_type)
    return (
        bo.reshape(images.shape), ig.reshape(images.shape),
        ln[0], ln[1], ln[2], ln[3], mine[0], mine[1],
        grads[0], grads[1], grads[2], grads[3].T, g_up, g_down,
        query_clip, key_clip,
    )


def on_device(images, cotangent, ln1_gain, ln1_bias, ln2_gain, ln2_bias, q_gain, k_gain, *weights):
    fused = fits_fused(images, weights[0], weights[4], q_gain)
    layer = fused_layer if fused else general_layer
    return layer(images, cotangent, ln1_gain, ln1_bias, ln2_gain, ln2_bias, q_gain, k_gain, *weights)


def solution(mesh):
    return jax.shard_map(
        on_device,
        mesh=mesh,
        in_specs=(
            P("shard", "ctx", None),
            P("shard", "ctx", None),
            P("shard"),
            P("shard"),
            P("shard"),
            P("shard"),
            P("tp", "shard"),
            P("tp", "shard"),
            P("shard", "tp"),
            P("shard", "tp"),
            P("shard", "tp"),
            P("tp", "shard"),
            P("shard", "tp"),
            P("tp", "shard"),
        ),
        out_specs=(
            P("shard", "ctx", None),
            P("shard", "ctx", None),
            P("shard"),
            P("shard"),
            P("shard"),
            P("shard"),
            P("tp", "shard"),
            P("tp", "shard"),
            P("shard", "tp"),
            P("shard", "tp"),
            P("shard", "tp"),
            P("tp", "shard"),
            P("shard", "tp"),
            P("tp", "shard"),
            P("shard", "tp"),
            P("shard", "tp"),
        ),
        check_vma=False,
    )
```

```python
import functools
import jax
import jax.numpy as jnp
from jax import lax
from jax.experimental import pallas as pl
from jax.experimental.pallas import tpu as pltpu
from jax.sharding import PartitionSpec as P

norm_eps = 1e-06
clip_level = 0.5


def matmul(left, right):
    return jnp.dot(left, right, preferred_element_type=jnp.float32)


def norm_parts(values):
    center = values - jnp.mean(values, axis=-1, keepdims=True)
    inverse = lax.rsqrt(jnp.mean(center * center, axis=-1, keepdims=True) + norm_eps)
    return (center * inverse, inverse)


def norm_back(grad_hat, normed, inverse):
    return inverse * (
        grad_hat
        - jnp.mean(grad_hat, axis=-1, keepdims=True)
        - normed * jnp.mean(grad_hat * normed, axis=-1, keepdims=True)
    )


def head_scale(values, gain):
    inverse = lax.rsqrt(jnp.mean(values * values, axis=-1, keepdims=True) + norm_eps)
    return values * inverse * gain


def gelu_exact(values):
    return jax.nn.gelu(values, approximate=False)


def general_layer(
    images,
    cotangent,
    ln1_gain,
    ln1_bias,
    ln2_gain,
    ln2_bias,
    q_gain,
    k_gain,
    w_query,
    w_key,
    w_value,
    w_out,
    w_up,
    w_down,
):
    (
        full_query,
        full_key,
        full_value,
        full_up,
        full_out,
        full_down,
        gain_low_one,
        shift_low_one,
        gain_low_two,
        shift_low_two,
        query_gain_low,
        key_gain_low,
    ) = (
        lax.all_gather(w_query, "shard", axis=0, tiled=True),
        lax.all_gather(w_key, "shard", axis=0, tiled=True),
        lax.all_gather(w_value, "shard", axis=0, tiled=True),
        lax.all_gather(w_up, "shard", axis=0, tiled=True),
        lax.all_gather(w_out, "shard", axis=1, tiled=True),
        lax.all_gather(w_down, "shard", axis=1, tiled=True),
        lax.all_gather(ln1_gain, "shard", axis=0, tiled=True),
        lax.all_gather(ln1_bias, "shard", axis=0, tiled=True),
        lax.all_gather(ln2_gain, "shard", axis=0, tiled=True),
        lax.all_gather(ln2_bias, "shard", axis=0, tiled=True),
        lax.all_gather(q_gain, "shard", axis=1, tiled=True),
        lax.all_gather(k_gain, "shard", axis=1, tiled=True),
    )
    gain_one = gain_low_one.astype(jnp.float32)
    shift_one = shift_low_one.astype(jnp.float32)
    gain_two = gain_low_two.astype(jnp.float32)
    shift_two = shift_low_two.astype(jnp.float32)
    query_gain = query_gain_low.astype(jnp.float32)
    key_gain = key_gain_low.astype(jnp.float32)
    count_img, local_len, width = images.shape
    tokens = count_img * local_len
    heads_here, head_size = query_gain.shape
    local_width = heads_here * head_size
    full_len = local_len * lax.axis_size("ctx")
    group = 1
    groups = count_img // group
    scale = head_size ** (-0.5)
    flat = images.reshape(tokens, width).astype(jnp.float32)
    normed_one, inverse_one = norm_parts(flat)
    hidden_one = (normed_one * gain_one + shift_one).astype(jnp.bfloat16)
    query_raw = matmul(hidden_one, full_query).reshape(tokens, heads_here, head_size)
    key_raw = matmul(hidden_one, full_key).reshape(tokens, heads_here, head_size)
    query_norm = head_scale(query_raw, query_gain).astype(jnp.bfloat16)
    key_norm = head_scale(key_raw, key_gain).astype(jnp.bfloat16)
    value_low = matmul(hidden_one, full_value).astype(jnp.bfloat16)
    key_all, value_all = (
        lax.all_gather(
            key_norm.reshape(count_img, local_len, local_width), "ctx", axis=1, tiled=True
        ),
        lax.all_gather(
            value_low.reshape(count_img, local_len, local_width), "ctx", axis=1, tiled=True
        ),
    )
    query_grp = query_norm.reshape(groups, group, local_len, heads_here, head_size)
    key_grp = key_all.reshape(groups, group, full_len, heads_here, head_size)
    value_grp = value_all.reshape(groups, group, full_len, heads_here, head_size)

    def attend(pieces):
        query_blk, key_blk, value_blk = pieces
        scores = (
            jnp.einsum("gqhd,gkhd->ghqk", query_blk, key_blk, preferred_element_type=jnp.float32)
            * scale
        )
        top = jnp.max(scores, axis=-1, keepdims=True)
        expo = jnp.exp(scores - top)
        total = jnp.sum(expo, axis=-1, keepdims=True)
        probs = (expo / total).astype(jnp.bfloat16)
        mixed_blk = jnp.einsum(
            "ghqk,gkhd->gqhd", probs, value_blk, preferred_element_type=jnp.float32
        )
        return (mixed_blk, top + jnp.log(total), jnp.max(top, axis=(0, 2, 3)))

    mixed, log_total, group_peaks = lax.map(attend, (query_grp, key_grp, value_grp))
    local_peak = jnp.max(group_peaks, axis=0)
    peak_all = lax.pmax(local_peak, ("shard", "ctx"))
    attended = mixed.reshape(tokens, local_width).astype(jnp.bfloat16)
    branch_attn = lax.psum(matmul(attended, full_out), "tp")
    resid = flat + branch_attn
    normed_two, inverse_two = norm_parts(resid)
    hidden_two = (normed_two * gain_two + shift_two).astype(jnp.bfloat16)
    up_raw = matmul(hidden_two, full_up)
    active = gelu_exact(up_raw).astype(jnp.bfloat16)
    branch_mlp = lax.psum(matmul(active, full_down).astype(jnp.bfloat16), "tp").astype(jnp.float32)
    block_out = (resid + branch_mlp).astype(jnp.bfloat16).reshape(images.shape)
    grad_out = cotangent.reshape(tokens, width).astype(jnp.float32)
    grad_down = cotangent.reshape(tokens, width)
    grad_w_down = jnp.dot(active.T, grad_down, preferred_element_type=jnp.float32)
    grad_active = matmul(grad_down, full_down.T)
    unused_up, gelu_pull = jax.vjp(gelu_exact, up_raw)
    grad_up = gelu_pull(grad_active)[0].astype(jnp.bfloat16)
    grad_w_up = jnp.dot(hidden_two.T, grad_up, preferred_element_type=jnp.float32)
    grad_two = lax.psum(matmul(grad_up, full_up.T), "tp")
    grad_gain_two = jnp.sum(grad_two * normed_two, axis=0)
    grad_shift_two = jnp.sum(grad_two, axis=0)
    grad_resid = grad_out + norm_back(grad_two * gain_two, normed_two, inverse_two)
    grad_branch = grad_resid.astype(jnp.bfloat16)
    grad_w_out = jnp.dot(attended.T, grad_branch, preferred_element_type=jnp.float32)
    grad_mixed = matmul(grad_branch, full_out.T).astype(jnp.bfloat16)
    grad_grp = grad_mixed.reshape(groups, group, local_len, heads_here, head_size)

    def attend_back(pieces):
        query_blk, key_blk, value_blk, log_blk, grad_blk = pieces
        scores = (
            jnp.einsum("gqhd,gkhd->ghqk", query_blk, key_blk, preferred_element_type=jnp.float32)
            * scale
        )
        probs = jnp.exp(scores - log_blk)
        grad_probs = jnp.einsum(
            "gqhd,gkhd->ghqk", grad_blk, value_blk, preferred_element_type=jnp.float32
        )
        grad_scores = (
            probs * (grad_probs - jnp.sum(probs * grad_probs, axis=-1, keepdims=True))
        ).astype(jnp.bfloat16)
        grad_val = jnp.einsum(
            "ghqk,gqhd->gkhd",
            probs.astype(jnp.bfloat16),
            grad_blk,
            preferred_element_type=jnp.float32,
        )
        grad_qry = (
            jnp.einsum("ghqk,gkhd->gqhd", grad_scores, key_blk, preferred_element_type=jnp.float32)
            * scale
        )
        grad_kys = (
            jnp.einsum(
                "ghqk,gqhd->gkhd", grad_scores, query_blk, preferred_element_type=jnp.float32
            )
            * scale
        )
        return (grad_qry, grad_kys, grad_val)

    grad_query_n, grad_key_full, grad_value_full = lax.map(
        attend_back, (query_grp, key_grp, value_grp, log_total, grad_grp)
    )
    grad_key_n, grad_value_n = (
        lax.psum_scatter(
            grad_key_full.reshape(count_img, full_len, local_width),
            "ctx",
            scatter_dimension=1,
            tiled=True,
        ),
        lax.psum_scatter(
            grad_value_full.reshape(count_img, full_len, local_width),
            "ctx",
            scatter_dimension=1,
            tiled=True,
        ),
    )
    unused_query, query_pull = jax.vjp(head_scale, query_raw, query_gain)
    grad_query_raw, grad_query_gain = query_pull(
        grad_query_n.reshape(tokens, heads_here, head_size)
    )
    unused_key, key_pull = jax.vjp(head_scale, key_raw, key_gain)
    grad_key_raw, grad_key_gain = key_pull(grad_key_n.reshape(tokens, heads_here, head_size))
    grad_query_low = grad_query_raw.reshape(tokens, local_width).astype(jnp.bfloat16)
    grad_key_low = grad_key_raw.reshape(tokens, local_width).astype(jnp.bfloat16)
    grad_value_low = grad_value_n.reshape(tokens, local_width).astype(jnp.bfloat16)
    grad_w_query = jnp.dot(hidden_one.T, grad_query_low, preferred_element_type=jnp.float32)
    grad_w_key = jnp.dot(hidden_one.T, grad_key_low, preferred_element_type=jnp.float32)
    grad_w_value = jnp.dot(hidden_one.T, grad_value_low, preferred_element_type=jnp.float32)
    grad_one_part = (
        matmul(grad_query_low, full_query.T)
        + matmul(grad_key_low, full_key.T)
        + matmul(grad_value_low, full_value.T)
    )
    grad_one = lax.psum(grad_one_part, "tp")
    grad_gain_one = jnp.sum(grad_one * normed_one, axis=0)
    grad_shift_one = jnp.sum(grad_one, axis=0)
    input_grad = (
        (grad_resid + norm_back(grad_one * gain_one, normed_one, inverse_one))
        .astype(jnp.bfloat16)
        .reshape(images.shape)
    )
    (
        sum_query,
        sum_key,
        sum_value,
        sum_up,
        sum_out,
        sum_down,
        sum_gain_one,
        sum_shift_one,
        sum_gain_two,
        sum_shift_two,
        sum_qgain,
        sum_kgain,
    ) = lax.psum(
        (
            grad_w_query,
            grad_w_key,
            grad_w_value,
            grad_w_up,
            grad_w_out,
            grad_w_down,
            grad_gain_one,
            grad_shift_one,
            grad_gain_two,
            grad_shift_two,
            grad_query_gain,
            grad_key_gain,
        ),
        "ctx",
    )
    (
        part_query,
        part_key,
        part_value,
        part_up,
        part_out,
        part_down,
        part_gain_one,
        part_shift_one,
        part_gain_two,
        part_shift_two,
        part_qgain,
        part_kgain,
    ) = (
        lax.psum_scatter(sum_query, "shard", scatter_dimension=0, tiled=True),
        lax.psum_scatter(sum_key, "shard", scatter_dimension=0, tiled=True),
        lax.psum_scatter(sum_value, "shard", scatter_dimension=0, tiled=True),
        lax.psum_scatter(sum_up, "shard", scatter_dimension=0, tiled=True),
        lax.psum_scatter(sum_out, "shard", scatter_dimension=1, tiled=True),
        lax.psum_scatter(sum_down, "shard", scatter_dimension=1, tiled=True),
        lax.psum_scatter(sum_gain_one, "shard", scatter_dimension=0, tiled=True),
        lax.psum_scatter(sum_shift_one, "shard", scatter_dimension=0, tiled=True),
        lax.psum_scatter(sum_gain_two, "shard", scatter_dimension=0, tiled=True),
        lax.psum_scatter(sum_shift_two, "shard", scatter_dimension=0, tiled=True),
        lax.psum_scatter(sum_qgain, "shard", scatter_dimension=1, tiled=True),
        lax.psum_scatter(sum_kgain, "shard", scatter_dimension=1, tiled=True),
    )
    factor = jnp.sqrt(clip_level / jnp.maximum(peak_all, clip_level))
    columns = jnp.repeat(factor, head_size)
    query_clip = (w_query.astype(jnp.float32) * columns).astype(jnp.bfloat16)
    key_clip = (w_key.astype(jnp.float32) * columns).astype(jnp.bfloat16)
    return (
        block_out,
        input_grad,
        part_gain_one,
        part_shift_one,
        part_gain_two,
        part_shift_two,
        part_qgain,
        part_kgain,
        part_query,
        part_key,
        part_value,
        part_out,
        part_up,
        part_down,
        query_clip,
        key_clip,
    )


MESH = pl.DeviceIdType.MESH
NN = (((1,), (0,)), ((), ()))
NT = (((1,), (1,)), ((), ()))
TN = (((0,), (0,)), ((), ()))
low_type = jnp.bfloat16
full_type = jnp.float32


def dot(left, right, dims=NN):
    return lax.dot_general(left, right, dims, preferred_element_type=full_type)


def flip(place, bits, count):
    result = 0
    unit = 1
    while unit < count:
        result = result + ((place // unit + bits // unit) % 2) * unit
        unit *= 2
    return result


def fits_fused(images, w_query, w_up, q_gain):
    count_img, local_len, width = images.shape
    ctx, shard, tp = lax.axis_size("ctx"), lax.axis_size("shard"), lax.axis_size("tp")
    rows = w_query.shape[0]
    return (
        count_img == 1
        and tp == 2
        and ctx == 4
        and shard == 4
        and rows % (16 * ctx) == 0
        and local_len % 32 == 0
        and q_gain.shape[0] % 2 == 0
        and w_up.shape[1] % (128 * ctx) == 0
    )


def fused_kernel(
    sizes,
    img_h, cot_h, g1_h, b1_h, g2_h, b2_h, qg_h, kg_h, wq_h, wk_h, wv_h, wo_h, wup_h, wdn_h,
    bo_o, ig_o, upo, dno, qkvo, lnr_o, qkr_o, peak_o,
    xg, ctg, smalls, wl, wol, wqkv, wot, wup, wdt,
    xh1, h1, nq, nk, sq, sk, qs, kall, vall, pst, sbuf, attq, attr, pks,
    ptop, dsb,
    h2, ga, act, gu, g2s, g2r, g2own, bos, bor, boown,
    gsib_s, gsib_r, gown, gz_s, gz_r, gfin,
    gres, gbg, gms, gm, dqb, dkt, dvt, dks_s, dks_r, dqr, dkr, dvr,
    g1s, g1r, g1own, qsib_s, qsib_r, qown, qz_s, qz_r, qfin,
    rows_s, rows_r, obuf,
    lsem, ssem, rsem,
):
    CN, ZN, TB, D, HW, FS, R = sizes
    QR = R // CN
    HR = R // 2
    s_i, c_i, t_i = lax.axis_index("shard"), lax.axis_index("ctx"), lax.axis_index("tp")
    o_i = 1 - t_i
    half_chips = CN // 2
    tstar = c_i // half_chips
    place = c_i % half_chips
    TK = CN * TB
    inv_d = 1.0 / D

    def at_ctx(j):
        return (s_i, flip(c_i, j, CN), t_i)

    def at_z(j):
        return (flip(s_i, j, ZN), c_i, t_i)

    sib = (s_i, c_i, o_i)

    spots = {}

    def spot(name, count):
        if name not in spots:
            spots[name] = (sum(n for _, n in spots.values()), count)
        return spots[name][0]

    def put(name, count, j, src, dst, dev):
        base = spot(name, count)
        pltpu.make_async_remote_copy(
            src_ref=src, dst_ref=dst, send_sem=ssem.at[base + j], recv_sem=rsem.at[base + j],
            device_id=dev, device_id_type=MESH,
        ).start()

    def got(name, count, j, dst, dev):
        base = spot(name, count)
        pltpu.make_async_remote_copy(
            src_ref=dst, dst_ref=dst, send_sem=ssem.at[base + j], recv_sem=rsem.at[base + j],
            device_id=dev, device_id_type=MESH,
        ).wait_recv()

    def sent(name, count, j, src, dev):
        base = spot(name, count)
        pltpu.make_async_remote_copy(
            src_ref=src, dst_ref=src, send_sem=ssem.at[base + j], recv_sem=rsem.at[base + j],
            device_id=dev, device_id_type=MESH,
        ).wait_send()

    x_src = img_h.at[0, pl.ds(t_i * TB, TB)]
    c_src = cot_h.at[0, pl.ds(t_i * TB, TB)]
    locals_ = [
        pltpu.make_async_copy(wk_h, wl.at[1], lsem.at[0]),
        pltpu.make_async_copy(wv_h, wl.at[2], lsem.at[1]),
        pltpu.make_async_copy(wq_h, wl.at[0], lsem.at[2]),
        pltpu.make_async_copy(x_src, xg.at[0], lsem.at[3]),
        pltpu.make_async_copy(wo_h, wol, lsem.at[4]),
        pltpu.make_async_copy(wdn_h.at[:, pl.ds(c_i * FS, FS)], wdt.at[t_i, s_i], lsem.at[5]),
        pltpu.make_async_copy(wup_h.at[:, pl.ds(c_i * FS, FS)], wup.at[t_i, s_i], lsem.at[6]),
        pltpu.make_async_copy(c_src, ctg.at[0], lsem.at[7]),
    ]
    for copy in locals_:
        copy.start()

    barrier = pltpu.get_barrier_semaphore()
    greet = [at_ctx(j) for j in range(1, CN)] + [at_z(j) for j in range(1, ZN)] + [sib]
    for dev in greet:
        pl.semaphore_signal(barrier, inc=1, device_id=dev, device_id_type=MESH)

    smalls[t_i, s_i] = jnp.zeros((8, 256), full_type)
    for k, ref in enumerate((g1_h, b1_h, g2_h, b2_h)):
        smalls[t_i, s_i, k:k + 1, :R] = ref[...].astype(full_type).reshape(1, R)
    heads = HW // 64
    piece = qg_h.shape[1]
    lane_of = lax.broadcasted_iota(jnp.int32, (piece, HW), 1)
    spread = (
        (lane_of % piece == lax.broadcasted_iota(jnp.int32, (piece, HW), 0)) & ((lane_of % 64) // piece == s_i)
    ).astype(full_type).astype(low_type)
    head_of = lax.broadcasted_iota(jnp.int32, (qg_h.shape[0], HW), 0)
    wanted = head_of == place * heads + lax.broadcasted_iota(jnp.int32, (qg_h.shape[0], HW), 1) // 64
    wanted = wanted & (t_i == tstar)
    for k, ref in ((4, qg_h), (5, kg_h)):
        row = jnp.sum(jnp.where(wanted, dot(ref[...], spread), 0.0), axis=0, keepdims=True)
        smalls[t_i, s_i, k:k + 1, :HW] = row

    pl.semaphore_wait(barrier, len(greet))

    for j in range(1, CN):
        put("x", CN, j, x_src, xg.at[j], at_ctx(j))
    for j in range(1, ZN):
        put("small", ZN, j, smalls.at[t_i, s_i], smalls.at[t_i, s_i], at_z(j))

    order_w = (1, 2, 0)

    def picker(at):
        return (
            lax.broadcasted_iota(jnp.int32, (half_chips * HW, HW), 0)
            == lax.broadcasted_iota(jnp.int32, (half_chips * HW, HW), 1) + at * HW
        ).astype(full_type).astype(low_type)

    @pl.when(t_i == tstar)
    def _():
        pick = picker(place)
        for n, g in enumerate(order_w):
            locals_[n].wait()
            wqkv[g, s_i] = dot(wl[g], pick).astype(low_type)
            for j in range(1, ZN):
                put("w%d" % g, ZN, j, wqkv.at[g, s_i], wqkv.at[g, s_i], at_z(j))
            put("w%d" % g, ZN, 0, wqkv.at[g, s_i], wqkv.at[g, s_i], sib)

    @pl.when(t_i != tstar)
    def _():
        for n in range(3):
            locals_[n].wait()
            spot("w%d" % order_w[n], ZN)

    locals_[4].wait()
    wo_rows = wol[pl.ds(c_i * QR, QR)]
    for kk in range(half_chips):
        wot[half_chips * t_i + kk, s_i, c_i] = dot(wo_rows, picker(kk)).astype(low_type)
    for j in range(1, ZN):
        block = wot.at[pl.ds(half_chips * t_i, half_chips), s_i, c_i]
        put("woz", ZN, j, block, block, at_z(j))

    for j in range(1, ZN):
        got("small", ZN, j, smalls.at[t_i, flip(s_i, j, ZN)], at_z(j))
    put("smallt", 1, 0, smalls.at[t_i], smalls.at[t_i], sib)

    locals_[3].wait()

    def norm_rows(values):
        mean = jnp.sum(values, axis=-1, keepdims=True) * inv_d
        center = values - mean
        inverse = lax.rsqrt(jnp.sum(center * center, axis=-1, keepdims=True) * inv_d + norm_eps)
        return center * inverse, inverse

    ln_rows = jnp.concatenate([smalls[t_i, k][:, :R] for k in range(ZN)], axis=1)
    g1row, b1row, g2row, b2row = (ln_rows[k:k + 1] for k in range(4))

    def first_norm(j, _):
        @pl.when(j > 0)
        def _():
            got("x", CN, j, xg.at[j], at_ctx(j))

        normed, _unused = norm_rows(xg[j].astype(full_type))
        xh1[j] = normed
        h1[j] = (normed * g1row + b1row).astype(low_type)
        return 0

    lax.fori_loop(0, CN, first_norm, 0)

    got("smallt", 1, 0, smalls.at[o_i], sib)
    head_rows = smalls[0, 0][4:6, :HW]
    for a in range(2):
        for k in range(ZN):
            if a or k:
                head_rows = head_rows + smalls[a, k][4:6, :HW]
    qgrow, kgrow = head_rows[0:1], head_rows[1:2]

    lane = lax.broadcasted_iota(jnp.int32, (1, HW), 1) // 64
    mask_f = [(lane == h).astype(full_type) for h in range(heads)]
    mask_b = [m.astype(low_type) for m in mask_f]
    same_head = (
        lax.broadcasted_iota(jnp.int32, (HW, HW), 0) // 64
        == lax.broadcasted_iota(jnp.int32, (HW, HW), 1) // 64
    ).astype(full_type).astype(low_type)

    def head_mean(values):
        high = values.astype(low_type)
        rest = (values - high.astype(full_type)).astype(low_type)
        return (dot(high, same_head) + dot(rest, same_head)) * (1.0 / 64)

    def weight_ready(g):
        @pl.when(t_i != tstar)
        def _():
            got("w%d" % g, ZN, 0, wqkv.at[g, s_i], sib)

        for j in range(1, ZN):
            block = wqkv.at[g, flip(s_i, j, ZN)]
            got("w%d" % g, ZN, j, block, sib)

            @pl.when(t_i == tstar)
            def _():
                pltpu.make_async_remote_copy(
                    src_ref=block, dst_ref=block,
                    send_sem=ssem.at[spot("f%d" % g, ZN) + j],
                    recv_sem=rsem.at[spot("w%d" % g, ZN) + j],
                    device_id=sib, device_id_type=MESH,
                ).start()

    def project(g):
        return dot(h1[...].reshape(TK, D), wqkv[g].reshape(D, HW))

    weight_ready(1)
    raw = project(1)
    inverse = lax.rsqrt(head_mean(raw * raw) + norm_eps)
    normed = raw * inverse
    nk[...] = normed
    sk[...] = inverse
    kall[0] = (normed * kgrow).astype(low_type)
    put("k", 1, 0, kall.at[0], kall.at[1], sib)
    weight_ready(2)
    vall[0] = project(2).astype(low_type)
    put("v", 1, 0, vall.at[0], vall.at[1], sib)
    weight_ready(0)
    locals_[5].wait()
    for j in range(1, ZN):
        put("wdz", ZN, j, wdt.at[t_i, s_i], wdt.at[t_i, s_i], at_z(j))
    locals_[6].wait()
    for j in range(1, ZN):
        put("wuz", ZN, j, wup.at[t_i, s_i], wup.at[t_i, s_i], at_z(j))
    raw = project(0)
    inverse = lax.rsqrt(head_mean(raw * raw) + norm_eps)
    normed = raw * inverse
    nq[...] = normed
    sq[...] = inverse
    qs[...] = ((normed * qgrow).astype(low_type) * 0.125).astype(low_type).reshape(CN, TB, HW)

    mine = pl.ds(half_chips * t_i, half_chips)
    for j in range(1, ZN):
        got("woz", ZN, j, wot.at[mine, flip(s_i, j, ZN), c_i], at_z(j))
    for j in range(1, CN):
        put("woc", CN, j, wot.at[mine, :, c_i], wot.at[mine, :, c_i], at_ctx(j))
    for j in range(1, CN):
        put("ct", CN, j, c_src, ctg.at[j], at_ctx(j))
    got("k", 1, 0, kall.at[1], sib)
    got("v", 1, 0, vall.at[1], sib)

    def stacked(block):
        return jnp.concatenate([block * m for m in mask_b], axis=0)

    def folded(block):
        total = block[0:TB] * mask_f[0]
        for h in range(1, heads):
            total = total + block[h * TB:(h + 1) * TB] * mask_f[h]
        return total

    ptop[...] = jnp.full(ptop.shape, -3.0e38, full_type)

    def attend(i, _):
        j = CN - 1 - i

        @pl.when(i == 2)
        def _():
            for q in range(1, CN):
                got("woc", CN, q, wot.at[mine, :, flip(c_i, q, CN)], at_ctx(q))
            put("wot", 1, 0, wot.at[mine], wot.at[mine], sib)

        sbuf[...] = dot(stacked(qs[j]), kall[...].reshape(2 * TK, HW), NT)
        for h in range(heads):
            rows = slice(h * TB, (h + 1) * TB)
            scores = sbuf[rows]
            ptop[h:h + 1] = jnp.maximum(ptop[h:h + 1], jnp.max(scores, axis=0, keepdims=True))
            expo = jnp.exp(scores)
            pst[j, rows] = expo * (1.0 / jnp.sum(expo, axis=-1, keepdims=True))
        mixed = folded(dot(pst[j].astype(low_type), vall[...].reshape(2 * TK, HW)))
        attq[j] = mixed.astype(low_type)

        @pl.when(j > 0)
        def _():
            put("att", CN, j, attq.at[j], attr.at[j], at_ctx(j))

        return 0

    lax.fori_loop(0, CN, attend, 0)
    peak_rows = jnp.max(ptop[...], axis=-1, keepdims=True)
    lane_id = lax.broadcasted_iota(jnp.int32, (8, 128), 1)
    own_peak = jnp.full((8, 128), -3.0e38, full_type)
    for h in range(heads):
        own_peak = jnp.where(lane_id == c_i * heads + h, peak_rows[h:h + 1], own_peak)
    pks[0] = own_peak
    put("pkt", 1, 0, pks.at[0], pks.at[1], sib)

    got("wot", 1, 0, wot.at[pl.ds(half_chips * o_i, half_chips)], sib)
    branch = dot(attq[0], wot[c_i].reshape(D, HW), NT)
    for j in range(1, CN):
        got("att", CN, j, attr.at[j], at_ctx(j))
        branch = branch + dot(attr[j], wot[flip(c_i, j, CN)].reshape(D, HW), NT)
    resid = xg[0].astype(full_type) + branch
    boown[...] = resid
    xhat2, inv2 = norm_rows(resid)
    h2[0] = (xhat2 * g2row + b2row).astype(low_type)
    for j in range(1, CN):
        put("h2", CN, j, h2.at[0], h2.at[j], at_ctx(j))

    locals_[7].wait()
    for j in range(1, CN):
        got("ct", CN, j, ctg.at[j], at_ctx(j))
    for j in range(1, ZN):
        got("wdz", ZN, j, wdt.at[t_i, flip(s_i, j, ZN)], at_z(j))
    put("wdt", 1, 0, wdt.at[t_i], wdt.at[t_i], sib)
    ga[t_i] = dot(ctg[...].reshape(TK, D), wdt[t_i].reshape(D, FS)).reshape(CN, TB, FS)
    for j in range(1, ZN):
        got("wuz", ZN, j, wup.at[t_i, flip(s_i, j, ZN)], at_z(j))
    put("wut", 1, 0, wup.at[t_i], wup.at[t_i], sib)
    got("wdt", 1, 0, wdt.at[o_i], sib)
    ga[o_i] = dot(ctg[...].reshape(TK, D), wdt[o_i].reshape(D, FS)).reshape(CN, TB, FS)
    got("wut", 1, 0, wup.at[o_i], sib)

    def mlp(j, _):
        @pl.when(j > 0)
        def _():
            got("h2", CN, j, h2.at[j], at_ctx(j))

        block = h2[j]
        for a in range(2):
            up = dot(block, wup[a].reshape(D, FS))
            phi = 0.5 * (1.0 + lax.erf(up * 0.7071067811865476))
            dens = jnp.exp(up * up * -0.5) * 0.3989422804014327
            act[a, j] = (up * phi).astype(low_type)
            gu[a, j] = (ga[a, j] * (phi + up * dens)).astype(low_type)
        grad_two = dot(gu[0, j], wup[0].reshape(D, FS), NT) + dot(gu[1, j], wup[1].reshape(D, FS), NT)

        @pl.when(j == 0)
        def _():
            g2own[...] = grad_two

        @pl.when(j > 0)
        def _():
            g2s[j] = grad_two.astype(low_type)
            put("g2", CN, j, g2s.at[j], g2r.at[j], at_ctx(j))

        return 0

    lax.fori_loop(0, CN, mlp, 0)

    h2_all = h2[...].reshape(TK, D)
    ct_all = ctg[...].reshape(TK, D)
    gsib_s[0] = dot(h2_all, gu[o_i].reshape(TK, FS), TN).astype(low_type)
    put("gs", 2, 0, gsib_s.at[0], gsib_r.at[0], sib)
    gsib_s[1] = dot(ct_all, act[o_i].reshape(TK, FS), TN).astype(low_type)
    put("gs", 2, 1, gsib_s.at[1], gsib_r.at[1], sib)
    gown[0] = dot(h2_all, gu[t_i].reshape(TK, FS), TN)
    gown[1] = dot(ct_all, act[t_i].reshape(TK, FS), TN)

    def down(j, _):
        part = dot(act[0, j], wdt[0].reshape(D, FS), NT) + dot(act[1, j], wdt[1].reshape(D, FS), NT)

        @pl.when(j == 0)
        def _():
            boown[...] += part

        @pl.when(j > 0)
        def _():
            bos[j] = part.astype(low_type)

        return 0

    lax.fori_loop(0, CN, down, 0)

    for k in range(2):
        got("gs", 2, k, gsib_r.at[k], sib)
        gown[k] = gown[k] + gsib_r[k].astype(full_type)
        gz_s[k] = gown[k].astype(low_type).reshape(ZN, R, FS)

    def send_mlp(k):
        for j in range(1, ZN):
            put("gz%d" % k, ZN, j, gz_s.at[k, flip(s_i, j, ZN)], gz_r.at[k, j], at_z(j))

    def share_mlp(k, out):
        total = gown[k, pl.ds(pl.multiple_of(s_i * R, R), R)]
        for j in range(1, ZN):
            got("gz%d" % k, ZN, j, gz_r.at[k, j], at_z(j))
            total = total + gz_r[k, j].astype(full_type)
        gfin[k] = total.astype(low_type)
        for j in range(1, CN):
            put("gc%d" % k, CN, j, gfin.at[k], out.at[c_i], at_ctx(j))
        pltpu.make_async_copy(gfin.at[k], out.at[c_i], lsem.at[8 + k]).start()

    send_mlp(0)

    grad_two = g2own[...]
    for j in range(1, CN):
        got("g2", CN, j, g2r.at[j], at_ctx(j))
        grad_two = grad_two + g2r[j].astype(full_type)
    ln2g = jnp.sum(grad_two * xhat2, axis=0, keepdims=True)
    ln2b = jnp.sum(grad_two, axis=0, keepdims=True)
    hat = grad_two * g2row
    grad_resid = ctg[0].astype(full_type) + inv2 * (
        hat
        - jnp.sum(hat, axis=-1, keepdims=True) * inv_d
        - xhat2 * (jnp.sum(hat * xhat2, axis=-1, keepdims=True) * inv_d)
    )
    gres[...] = grad_resid
    gb = grad_resid.astype(low_type)
    gbg[0] = gb
    for j in range(CN - 1, 0, -1):
        gms[j] = dot(gb, wot[flip(c_i, j, CN)].reshape(D, HW)).astype(low_type)
        put("gm", CN, j, gms.at[j], gm.at[j], at_ctx(j))
    gm[0] = dot(gb, wot[c_i].reshape(D, HW)).astype(low_type)
    for j in range(1, CN):
        put("gb", CN, j, gbg.at[0], gbg.at[j], at_ctx(j))
    for j in range(1, CN):
        put("bo", CN, j, bos.at[j], bor.at[j], at_ctx(j))

    dkt[...] = jnp.zeros_like(dkt)
    dvt[...] = jnp.zeros_like(dvt)

    def attend_back(j, _):
        @pl.when(j > 0)
        def _():
            got("gm", CN, j, gm.at[j], at_ctx(j))

        @pl.when(j == 1)
        def _():
            send_mlp(1)

        @pl.when(j == CN - 1)
        def _():
            share_mlp(0, upo)

        grad_rows = stacked(gm[j])
        query_rows = stacked(qs[j])
        sbuf[...] = dot(grad_rows, vall[...].reshape(2 * TK, HW), NT)

        for h in range(heads):
            rows = slice(h * TB, (h + 1) * TB)
            probs, grad_probs = pst[j, rows], sbuf[rows]
            inner = jnp.sum(probs * grad_probs, axis=-1, keepdims=True)
            dsb[rows] = (probs * (grad_probs - inner)).astype(low_type)
        grad_scores = dsb[...]
        dqb[j] = folded(dot(grad_scores, kall[...].reshape(2 * TK, HW))) * 0.125
        dvt[...] += dot(grad_rows, pst[j].astype(low_type), TN)
        dkt[...] += dot(query_rows, grad_scores, TN)
        return 0

    lax.fori_loop(0, CN, attend_back, 0)
    dks_s[0] = dvt[:, TK:].astype(low_type)
    dks_s[1] = dkt[:, TK:].astype(low_type)
    for k in range(2):
        put("dk", 2, k, dks_s.at[k], dks_r.at[k], sib)

    def unnorm(grad_n, gain_row, normed, inverse):
        gain_grad = jnp.sum(grad_n * normed, axis=0, keepdims=True)
        e = grad_n * gain_row
        return (inverse * (e - normed * head_mean(e * normed))).astype(low_type), gain_grad

    h1_all = h1[...].reshape(TK, D)

    def share_grad(n, left, right):
        full = dot(left, right, TN).reshape(ZN, 2, HR, HW)
        low_full = full.astype(low_type)
        for k in range(2):
            @pl.when(o_i == k)
            def _():
                qsib_s[n] = low_full[:, k]

            @pl.when(t_i == k)
            def _():
                qown[n] = full[:, k]

        put("qg", 4, n, qsib_s.at[n], qsib_r.at[n], sib)

    def reduce_grad(n):
        got("qg", 4, n, qsib_r.at[n], sib)
        total = qown[n] + qsib_r[n].astype(full_type)
        qown[n] = total
        qz_s[n] = total.astype(low_type)
        for j in range(1, ZN):
            put("qz%d" % n, ZN, j, qz_s.at[n, flip(s_i, j, ZN)], qz_r.at[n, j], at_z(j))

    grad_raw, q_gain_row = unnorm(dqb[...].reshape(TK, HW), qgrow, nq[...], sq[...])
    dqr[...] = grad_raw
    share_grad(0, h1_all, dqr[...])
    got("dk", 2, 0, dks_r.at[0], sib)
    dvr[...] = (dvt[:, :TK] + dks_r[0].astype(full_type)).T.astype(low_type)
    share_grad(2, h1_all, dvr[...])
    got("dk", 2, 1, dks_r.at[1], sib)
    grad_k = (dkt[:, :TK] + dks_r[1].astype(full_type)).T
    grad_raw, k_gain_row = unnorm(grad_k, kgrow, nk[...], sk[...])
    dkr[...] = grad_raw
    share_grad(1, h1_all, dkr[...])
    reduce_grad(0)

    ln1g = jnp.zeros((1, D), full_type)
    ln1b = jnp.zeros((1, D), full_type)
    for j in range(CN - 1, -1, -1):
        rows = slice(j * TB, (j + 1) * TB)
        part = (
            dot(dqr[rows], wqkv[0].reshape(D, HW), NT)
            + dot(dkr[rows], wqkv[1].reshape(D, HW), NT)
            + dot(dvr[rows], wqkv[2].reshape(D, HW), NT)
        )
        if j:
            g1s[j] = part.astype(low_type)
            put("g1", CN, j, g1s.at[j], g1r.at[j], at_ctx(j))
        else:
            g1own[...] = part
        ln1g = ln1g + jnp.sum(part * xh1[j], axis=0, keepdims=True)
        ln1b = ln1b + jnp.sum(part, axis=0, keepdims=True)
        if j == CN - 1:
            reduce_grad(2)
        elif j == CN - 2:
            reduce_grad(1)
    rows_s[0] = jnp.zeros_like(rows_s[0])
    for k, row in enumerate((ln1g, ln1b, ln2g, ln2b)):
        rows_s[0, k:k + 1, :D] = row
    rows_s[0, 0:1, D:D + HW] = q_gain_row
    rows_s[0, 1:2, D:D + HW] = k_gain_row
    put("rt", 1, 0, rows_s.at[0], rows_r.at[0], sib)
    for j in range(1, CN):
        got("gb", CN, j, gbg.at[j], at_ctx(j))
    share_grad(3, gbg[...].reshape(TK, D), attq[...].reshape(TK, HW))

    total = boown[...]
    for j in range(1, CN):
        got("bo", CN, j, bor.at[j], at_ctx(j))
        total = total + bor[j].astype(full_type)
    own_rows = pl.ds(t_i * TB, TB)
    obuf[0] = total.astype(low_type)
    put("ob", 2, 0, obuf.at[0], bo_o.at[own_rows], sib)
    pltpu.make_async_copy(obuf.at[0], bo_o.at[own_rows], lsem.at[10]).start()
    reduce_grad(3)

    got("rt", 1, 0, rows_r.at[0], sib)
    rows_s[1] = rows_s[0] + rows_r[0]
    for j in range(1, ZN):
        put("rz", ZN, j, rows_s.at[1], rows_r.at[j], at_z(j))
    got("pkt", 1, 0, pks.at[1], sib)
    pks[2] = jnp.maximum(pks[0], pks[1])
    for j in range(1, ZN):
        put("pkz", ZN, j, pks.at[2], pks.at[2 + j], at_z(j))

    share_mlp(1, dno)

    def share_fin(n):
        total = qown[n, s_i]
        for j in range(1, ZN):
            got("qz%d" % n, ZN, j, qz_r.at[n, j], at_z(j))
            total = total + qz_r[n, j].astype(full_type)
        qfin[n] = total.astype(low_type)
        slot = spot("qcr%d" % n, 2 * half_chips) + place * 2 + t_i
        for j in range(1, CN):
            pltpu.make_async_remote_copy(
                src_ref=qfin.at[n], dst_ref=qkvo.at[place, t_i, n],
                send_sem=ssem.at[spot("qcs%d" % n, CN) + j], recv_sem=rsem.at[slot],
                device_id=(s_i, flip(c_i, j, CN), tstar), device_id_type=MESH,
            ).start()

        @pl.when(t_i == tstar)
        def _():
            pltpu.make_async_copy(qfin.at[n], qkvo.at[place, t_i, n], lsem.at[12 + n]).start()

        @pl.when(t_i != tstar)
        def _():
            pltpu.make_async_remote_copy(
                src_ref=qfin.at[n], dst_ref=qkvo.at[place, t_i, n],
                send_sem=ssem.at[spot("qcs%d" % n, CN)], recv_sem=rsem.at[slot],
                device_id=sib, device_id_type=MESH,
            ).start()

    share_fin(0)
    share_fin(2)

    xhat1, inv1 = norm_rows(xg[0].astype(full_type))
    grad_one = g1own[...]
    for j in range(1, CN):
        got("g1", CN, j, g1r.at[j], at_ctx(j))
        grad_one = grad_one + g1r[j].astype(full_type)
    hat = grad_one * g1row
    grad_in = gres[...] + inv1 * (
        hat
        - jnp.sum(hat, axis=-1, keepdims=True) * inv_d
        - xhat1 * (jnp.sum(hat * xhat1, axis=-1, keepdims=True) * inv_d)
    )
    obuf[1] = grad_in.astype(low_type)
    put("ob", 2, 1, obuf.at[1], ig_o.at[own_rows], sib)
    pltpu.make_async_copy(obuf.at[1], ig_o.at[own_rows], lsem.at[11]).start()

    share_fin(1)
    share_fin(3)

    rows_sum = rows_s[1]
    for j in range(1, ZN):
        got("rz", ZN, j, rows_r.at[j], at_z(j))
        rows_sum = rows_sum + rows_r[j]
    rows_s[2] = rows_sum
    for j in range(1, CN):
        put("rc", CN, j, rows_s.at[2], rows_r.at[ZN + j], at_ctx(j))
    peak = pks[2]
    for j in range(1, ZN):
        got("pkz", ZN, j, pks.at[2 + j], at_z(j))
        peak = jnp.maximum(peak, pks[2 + j])
    first = 2 + ZN
    pks[first] = peak
    for j in range(1, CN):
        put("pkc", CN, j, pks.at[first], pks.at[first + j], at_ctx(j))
    qkr_o[c_i] = rows_sum[:, D:]
    total = rows_sum[:, :D]
    for j in range(1, CN):
        got("rc", CN, j, rows_r.at[ZN + j], at_ctx(j))
        block = rows_r[ZN + j]
        total = total + block[:, :D]
        qkr_o[flip(c_i, j, CN)] = block[:, D:]
    lnr_o[...] = total
    for j in range(1, CN):
        got("pkc", CN, j, pks.at[first + j], at_ctx(j))
        peak = jnp.maximum(peak, pks[first + j])
    peak_o[...] = peak

    for k, out in ((0, upo), (1, dno)):
        for j in range(1, CN):
            got("gc%d" % k, CN, j, out.at[flip(c_i, j, CN)], at_ctx(j))
        pltpu.make_async_copy(gfin.at[k], out.at[c_i], lsem.at[8 + k]).wait()
    other_rows = pl.ds(o_i * TB, TB)
    for k, out in ((0, bo_o), (1, ig_o)):
        got("ob", 2, k, out.at[other_rows], sib)
        pltpu.make_async_copy(obuf.at[k], out.at[own_rows], lsem.at[10 + k]).wait()

    @pl.when(t_i == tstar)
    def _():
        for n in range(4):
            pltpu.make_async_copy(qfin.at[n], qkvo.at[place, t_i, n], lsem.at[12 + n]).wait()

    for p in range(half_chips):
        for a in range(2):
            @pl.when((t_i != tstar) | (place != p) | (t_i != a))
            def _():
                for n in range(4):
                    pltpu.make_async_remote_copy(
                        src_ref=qfin.at[n], dst_ref=qkvo.at[p, a, n],
                        send_sem=ssem.at[spot("qcs%d" % n, CN)],
                        recv_sem=rsem.at[spot("qcr%d" % n, 2 * half_chips) + p * 2 + a],
                        device_id=sib, device_id_type=MESH,
                    ).wait_recv()

    for j in range(1, CN):
        sent("x", CN, j, x_src, sib)
        sent("ct", CN, j, c_src, sib)
        sent("woc", CN, j, wot.at[mine, :, c_i], sib)
        sent("att", CN, j, attq.at[j], sib)
        sent("h2", CN, j, h2.at[0], sib)
        sent("g2", CN, j, g2s.at[j], sib)
        sent("gm", CN, j, gms.at[j], sib)
        sent("gb", CN, j, gbg.at[0], sib)
        sent("bo", CN, j, bos.at[j], sib)
        sent("g1", CN, j, g1s.at[j], sib)
        sent("pkc", CN, j, pks.at[first], sib)
        sent("rc", CN, j, rows_s.at[2], sib)
        sent("gc0", CN, j, gfin.at[0], sib)
        sent("gc1", CN, j, gfin.at[1], sib)
        for n in range(4):
            sent("qcs%d" % n, CN, j, qfin.at[n], sib)
    for j in range(1, ZN):
        sent("small", ZN, j, smalls.at[t_i, s_i], sib)
        sent("woz", ZN, j, wot.at[mine, s_i, c_i], sib)
        sent("wdz", ZN, j, wdt.at[t_i, s_i], sib)
        sent("wuz", ZN, j, wup.at[t_i, s_i], sib)
        sent("gz0", ZN, j, gz_s.at[0, 0], sib)
        sent("gz1", ZN, j, gz_s.at[1, 0], sib)
        sent("pkz", ZN, j, pks.at[2], sib)
        sent("rz", ZN, j, rows_s.at[1], sib)
        for n in range(4):
            sent("qz%d" % n, ZN, j, qz_s.at[n, 0], sib)
    sent("smallt", 1, 0, smalls.at[t_i], sib)
    sent("k", 1, 0, kall.at[0], sib)
    sent("v", 1, 0, vall.at[0], sib)
    sent("pkt", 1, 0, pks.at[0], sib)
    sent("wot", 1, 0, wot.at[mine], sib)
    sent("wdt", 1, 0, wdt.at[t_i], sib)
    sent("wut", 1, 0, wup.at[t_i], sib)
    sent("rt", 1, 0, rows_s.at[0], sib)
    for k in range(2):
        sent("gs", 2, k, gsib_s.at[k], sib)
        sent("dk", 2, k, dks_s.at[k], sib)
        sent("ob", 2, k, obuf.at[k], sib)
    for n in range(4):
        sent("qg", 4, n, qsib_s.at[n], sib)

    @pl.when(t_i == tstar)
    def _():
        for g in range(3):
            for j in range(ZN):
                sent("w%d" % g, ZN, j, wqkv.at[g, s_i], sib)
                if j:
                    sent("f%d" % g, ZN, j, wqkv.at[g, s_i], sib)

    @pl.when(t_i != tstar)
    def _():
        for n in range(4):
            sent("qcs%d" % n, CN, 0, qfin.at[n], sib)


SEMS = 320


def fused_call(sizes, *operands):
    CN, ZN, TB, D, HW, FS, R = sizes
    TK = CN * TB
    QR, HR = R // CN, R // 2
    half_chips = CN // 2
    heads = HW // 64
    lo, hi = low_type, full_type
    V = pltpu.VMEM
    any_spec = pl.BlockSpec(memory_space=pl.ANY)
    vm_spec = pl.BlockSpec(memory_space=pltpu.VMEM)
    out_shape = [
        jax.ShapeDtypeStruct((2 * TB, D), lo),
        jax.ShapeDtypeStruct((2 * TB, D), lo),
        jax.ShapeDtypeStruct((CN, R, FS), lo),
        jax.ShapeDtypeStruct((CN, R, FS), lo),
        jax.ShapeDtypeStruct((half_chips, 2, 4, HR, HW), lo),
        jax.ShapeDtypeStruct((8, D), hi),
        jax.ShapeDtypeStruct((CN, 8, 256), hi),
        jax.ShapeDtypeStruct((8, 128), hi),
    ]
    scratch = [
        V((CN, TB, D), lo), V((CN, TB, D), lo), V((2, ZN, 8, 256), hi),
        V((3, R, half_chips * HW), lo), V((R, half_chips * HW), lo),
        V((3, ZN, R, HW), lo), V((CN, ZN, CN, QR, HW), lo), V((2, ZN, R, FS), lo), V((2, ZN, R, FS), lo),
        V((CN, TB, D), hi), V((CN, TB, D), lo),
        V((TK, HW), hi), V((TK, HW), hi), V((TK, HW), hi), V((TK, HW), hi),
        V((CN, TB, HW), lo), V((2, TK, HW), lo), V((2, TK, HW), lo),
        V((CN, heads * TB, 2 * TK), hi), V((heads * TB, 2 * TK), hi),
        V((CN, TB, HW), lo), V((CN, TB, HW), lo), V((2 + ZN + CN, 8, 128), hi),
        V((heads, 2 * TK), hi), V((heads * TB, 2 * TK), lo),
        V((CN, TB, D), lo), V((2, CN, TB, FS), hi), V((2, CN, TB, FS), lo), V((2, CN, TB, FS), lo),
        V((CN, TB, D), lo), V((CN, TB, D), lo), V((TB, D), hi),
        V((CN, TB, D), lo), V((CN, TB, D), lo), V((TB, D), hi),
        V((2, D, FS), lo), V((2, D, FS), lo), V((2, D, FS), hi),
        V((2, ZN, R, FS), lo), V((2, ZN, R, FS), lo), V((2, R, FS), lo),
        V((TB, D), hi), V((CN, TB, D), lo), V((CN, TB, HW), lo), V((CN, TB, HW), lo),
        V((CN, TB, HW), hi), V((HW, 2 * TK), hi), V((HW, 2 * TK), hi),
        V((2, HW, TK), lo), V((2, HW, TK), lo), V((TK, HW), lo), V((TK, HW), lo), V((TK, HW), lo),
        V((CN, TB, D), lo), V((CN, TB, D), lo), V((TB, D), hi),
        V((4, ZN, HR, HW), lo), V((4, ZN, HR, HW), lo), V((4, ZN, HR, HW), hi),
        V((4, ZN, HR, HW), lo), V((4, ZN, HR, HW), lo), V((4, HR, HW), lo),
        V((3, 8, D + 256), hi), V((ZN + CN, 8, D + 256), hi), V((2, TB, D), lo),
        pltpu.SemaphoreType.DMA((16,)), pltpu.SemaphoreType.DMA((SEMS,)), pltpu.SemaphoreType.DMA((SEMS,)),
    ]
    return pl.pallas_call(
        functools.partial(fused_kernel, sizes),
        out_shape=out_shape,
        in_specs=[any_spec] * 2 + [vm_spec] * 6 + [any_spec] * 6,
        out_specs=[any_spec] * 5 + [vm_spec] * 3,
        scratch_shapes=scratch,
        compiler_params=pltpu.CompilerParams(
            collective_id=0, has_side_effects=True, vmem_limit_bytes=56 * 2**20
        ),
    )(*operands)


def finish_kernel(
    sizes,
    bo, ig, upo, dno, qkvo, lnr, qkr, peak, wq, wk,
    bo_o, ig_o, l1g, l1b, l2g, l2b, qg_o, kg_o, gq, gk, gv, go, gu, gd, cq, ck,
):
    CN, ZN, TB, D, HW, FS, R = sizes
    half_chips = CN // 2
    s_i, t_i = lax.axis_index("shard"), lax.axis_index("tp")
    bo_o[...] = bo[...]
    ig_o[...] = ig[...]
    for n, out in enumerate((gq, gk, gv, go)):
        for a in range(2):
            parts = [qkvo[p, a, n] for p in range(half_chips)]
            out[a * (R // 2):(a + 1) * (R // 2)] = jnp.concatenate(parts, axis=1).astype(full_type)
    for c in range(CN):
        gu[:, c * FS:(c + 1) * FS] = upo[c].astype(full_type)
        gd[:, c * FS:(c + 1) * FS] = dno[c].astype(full_type)
    rows = jnp.zeros((8, R), full_type)
    for z in range(ZN):
        rows = jnp.where(s_i == z, lnr[:, z * R:(z + 1) * R], rows)
    for k, out in enumerate((l1g, l1b, l2g, l2b)):
        out[...] = rows[k:k + 1].reshape(R)
    heads = HW // 64
    piece = qg_o.shape[1]
    for p in range(half_chips):
        chip = qkr[t_i * half_chips + p]
        for h in range(heads):
            for z in range(ZN):
                at = h * 64 + z * piece

                @pl.when(s_i == z)
                def _():
                    qg_o[p * heads + h:p * heads + h + 1] = chip[0:1, at:at + piece]
                    kg_o[p * heads + h:p * heads + h + 1] = chip[1:2, at:at + piece]
    factor = jnp.sqrt(clip_level / jnp.maximum(peak[0:1], clip_level))
    here = half_chips * heads
    lanes = lax.broadcasted_iota(jnp.int32, (1, here * 64), 1) // 64
    ids = lax.broadcasted_iota(jnp.int32, (1, 128), 1)
    columns = jnp.ones((1, here * 64), full_type)
    for h in range(here):
        one = jnp.sum(jnp.where(ids == t_i * here + h, factor, 0.0), axis=-1, keepdims=True)
        columns = jnp.where(lanes == h, one, columns)
    cq[...] = (wq[...].astype(full_type) * columns).astype(low_type)
    ck[...] = (wk[...].astype(full_type) * columns).astype(low_type)


def fused_layer(
    images, cotangent, ln1_gain, ln1_bias, ln2_gain, ln2_bias, q_gain, k_gain,
    w_query, w_key, w_value, w_out, w_up, w_down,
):
    CN, ZN = lax.axis_size("ctx"), lax.axis_size("shard")
    TB = images.shape[1] // 2
    D = images.shape[2]
    R = w_query.shape[0]
    HW = w_query.shape[1] // (CN // 2)
    FS = w_up.shape[1] // CN
    sizes = (CN, ZN, TB, D, HW, FS, R)
    results = fused_call(
        sizes, images, cotangent, ln1_gain, ln1_bias, ln2_gain, ln2_bias, q_gain, k_gain,
        w_query, w_key, w_value, w_out.T, w_up, w_down.T,
    )
    row = jax.ShapeDtypeStruct((R,), full_type)
    gain = jax.ShapeDtypeStruct(q_gain.shape, full_type)
    square = jax.ShapeDtypeStruct(w_query.shape, full_type)
    wide = jax.ShapeDtypeStruct(w_up.shape, full_type)
    tokens = jax.ShapeDtypeStruct(images.shape[1:], low_type)
    clipped = jax.ShapeDtypeStruct(w_query.shape, low_type)
    out = pl.pallas_call(
        functools.partial(finish_kernel, sizes),
        out_shape=[tokens] * 2 + [row] * 4 + [gain] * 2 + [square] * 4 + [wide] * 2 + [clipped] * 2,
        in_specs=[pl.BlockSpec(memory_space=pltpu.VMEM)] * 10,
        out_specs=[pl.BlockSpec(memory_space=pltpu.VMEM)] * 16,
        compiler_params=pltpu.CompilerParams(vmem_limit_bytes=40 * 2**20),
    )(*results, w_query, w_key)
    out = list(out)
    out[0], out[1] = out[0].reshape(images.shape), out[1].reshape(images.shape)
    out[11], out[13] = out[11].T, out[13].T
    return tuple(out)


def on_device(images, cotangent, ln1_gain, ln1_bias, ln2_gain, ln2_bias, q_gain, k_gain, *weights):
    fused = fits_fused(images, weights[0], weights[4], q_gain)
    layer = fused_layer if fused else general_layer
    return layer(images, cotangent, ln1_gain, ln1_bias, ln2_gain, ln2_bias, q_gain, k_gain, *weights)


def solution(mesh):
    return jax.shard_map(
        on_device,
        mesh=mesh,
        in_specs=(
            P("shard", "ctx", None),
            P("shard", "ctx", None),
            P("shard"),
            P("shard"),
            P("shard"),
            P("shard"),
            P("tp", "shard"),
            P("tp", "shard"),
            P("shard", "tp"),
            P("shard", "tp"),
            P("shard", "tp"),
            P("tp", "shard"),
            P("shard", "tp"),
            P("tp", "shard"),
        ),
        out_specs=(
            P("shard", "ctx", None),
            P("shard", "ctx", None),
            P("shard"),
            P("shard"),
            P("shard"),
            P("shard"),
            P("tp", "shard"),
            P("tp", "shard"),
            P("shard", "tp"),
            P("shard", "tp"),
            P("shard", "tp"),
            P("tp", "shard"),
            P("shard", "tp"),
            P("tp", "shard"),
            P("shard", "tp"),
            P("shard", "tp"),
        ),
        check_vma=False,
    )
```

```python
import functools
import jax
import jax.numpy as jnp
from jax import lax
from jax.experimental import pallas as pl
from jax.experimental.pallas import tpu as pltpu
from jax.sharding import PartitionSpec as P

norm_eps = 1e-06
clip_level = 0.5


def matmul(left, right):
    return jnp.dot(left, right, preferred_element_type=jnp.float32)


def norm_parts(values):
    center = values - jnp.mean(values, axis=-1, keepdims=True)
    inverse = lax.rsqrt(jnp.mean(center * center, axis=-1, keepdims=True) + norm_eps)
    return (center * inverse, inverse)


def norm_back(grad_hat, normed, inverse):
    return inverse * (
        grad_hat
        - jnp.mean(grad_hat, axis=-1, keepdims=True)
        - normed * jnp.mean(grad_hat * normed, axis=-1, keepdims=True)
    )


def head_scale(values, gain):
    inverse = lax.rsqrt(jnp.mean(values * values, axis=-1, keepdims=True) + norm_eps)
    return values * inverse * gain


def gelu_exact(values):
    return jax.nn.gelu(values, approximate=False)


def general_layer(
    images,
    cotangent,
    ln1_gain,
    ln1_bias,
    ln2_gain,
    ln2_bias,
    q_gain,
    k_gain,
    w_query,
    w_key,
    w_value,
    w_out,
    w_up,
    w_down,
):
    (
        full_query,
        full_key,
        full_value,
        full_up,
        full_out,
        full_down,
        gain_low_one,
        shift_low_one,
        gain_low_two,
        shift_low_two,
        query_gain_low,
        key_gain_low,
    ) = (
        lax.all_gather(w_query, "shard", axis=0, tiled=True),
        lax.all_gather(w_key, "shard", axis=0, tiled=True),
        lax.all_gather(w_value, "shard", axis=0, tiled=True),
        lax.all_gather(w_up, "shard", axis=0, tiled=True),
        lax.all_gather(w_out, "shard", axis=1, tiled=True),
        lax.all_gather(w_down, "shard", axis=1, tiled=True),
        lax.all_gather(ln1_gain, "shard", axis=0, tiled=True),
        lax.all_gather(ln1_bias, "shard", axis=0, tiled=True),
        lax.all_gather(ln2_gain, "shard", axis=0, tiled=True),
        lax.all_gather(ln2_bias, "shard", axis=0, tiled=True),
        lax.all_gather(q_gain, "shard", axis=1, tiled=True),
        lax.all_gather(k_gain, "shard", axis=1, tiled=True),
    )
    gain_one = gain_low_one.astype(jnp.float32)
    shift_one = shift_low_one.astype(jnp.float32)
    gain_two = gain_low_two.astype(jnp.float32)
    shift_two = shift_low_two.astype(jnp.float32)
    query_gain = query_gain_low.astype(jnp.float32)
    key_gain = key_gain_low.astype(jnp.float32)
    count_img, local_len, width = images.shape
    tokens = count_img * local_len
    heads_here, head_size = query_gain.shape
    local_width = heads_here * head_size
    full_len = local_len * lax.axis_size("ctx")
    group = 1
    groups = count_img // group
    scale = head_size ** (-0.5)
    flat = images.reshape(tokens, width).astype(jnp.float32)
    normed_one, inverse_one = norm_parts(flat)
    hidden_one = (normed_one * gain_one + shift_one).astype(jnp.bfloat16)
    query_raw = matmul(hidden_one, full_query).reshape(tokens, heads_here, head_size)
    key_raw = matmul(hidden_one, full_key).reshape(tokens, heads_here, head_size)
    query_norm = head_scale(query_raw, query_gain).astype(jnp.bfloat16)
    key_norm = head_scale(key_raw, key_gain).astype(jnp.bfloat16)
    value_low = matmul(hidden_one, full_value).astype(jnp.bfloat16)
    key_all, value_all = (
        lax.all_gather(
            key_norm.reshape(count_img, local_len, local_width), "ctx", axis=1, tiled=True
        ),
        lax.all_gather(
            value_low.reshape(count_img, local_len, local_width), "ctx", axis=1, tiled=True
        ),
    )
    query_grp = query_norm.reshape(groups, group, local_len, heads_here, head_size)
    key_grp = key_all.reshape(groups, group, full_len, heads_here, head_size)
    value_grp = value_all.reshape(groups, group, full_len, heads_here, head_size)

    def attend(pieces):
        query_blk, key_blk, value_blk = pieces
        scores = (
            jnp.einsum("gqhd,gkhd->ghqk", query_blk, key_blk, preferred_element_type=jnp.float32)
            * scale
        )
        top = jnp.max(scores, axis=-1, keepdims=True)
        expo = jnp.exp(scores - top)
        total = jnp.sum(expo, axis=-1, keepdims=True)
        probs = (expo / total).astype(jnp.bfloat16)
        mixed_blk = jnp.einsum(
            "ghqk,gkhd->gqhd", probs, value_blk, preferred_element_type=jnp.float32
        )
        return (mixed_blk, top + jnp.log(total), jnp.max(top, axis=(0, 2, 3)))

    mixed, log_total, group_peaks = lax.map(attend, (query_grp, key_grp, value_grp))
    local_peak = jnp.max(group_peaks, axis=0)
    peak_all = lax.pmax(local_peak, ("shard", "ctx"))
    attended = mixed.reshape(tokens, local_width).astype(jnp.bfloat16)
    branch_attn = lax.psum(matmul(attended, full_out), "tp")
    resid = flat + branch_attn
    normed_two, inverse_two = norm_parts(resid)
    hidden_two = (normed_two * gain_two + shift_two).astype(jnp.bfloat16)
    up_raw = matmul(hidden_two, full_up)
    active = gelu_exact(up_raw).astype(jnp.bfloat16)
    branch_mlp = lax.psum(matmul(active, full_down).astype(jnp.bfloat16), "tp").astype(jnp.float32)
    block_out = (resid + branch_mlp).astype(jnp.bfloat16).reshape(images.shape)
    grad_out = cotangent.reshape(tokens, width).astype(jnp.float32)
    grad_down = cotangent.reshape(tokens, width)
    grad_w_down = jnp.dot(active.T, grad_down, preferred_element_type=jnp.float32)
    grad_active = matmul(grad_down, full_down.T)
    unused_up, gelu_pull = jax.vjp(gelu_exact, up_raw)
    grad_up = gelu_pull(grad_active)[0].astype(jnp.bfloat16)
    grad_w_up = jnp.dot(hidden_two.T, grad_up, preferred_element_type=jnp.float32)
    grad_two = lax.psum(matmul(grad_up, full_up.T), "tp")
    grad_gain_two = jnp.sum(grad_two * normed_two, axis=0)
    grad_shift_two = jnp.sum(grad_two, axis=0)
    grad_resid = grad_out + norm_back(grad_two * gain_two, normed_two, inverse_two)
    grad_branch = grad_resid.astype(jnp.bfloat16)
    grad_w_out = jnp.dot(attended.T, grad_branch, preferred_element_type=jnp.float32)
    grad_mixed = matmul(grad_branch, full_out.T).astype(jnp.bfloat16)
    grad_grp = grad_mixed.reshape(groups, group, local_len, heads_here, head_size)

    def attend_back(pieces):
        query_blk, key_blk, value_blk, log_blk, grad_blk = pieces
        scores = (
            jnp.einsum("gqhd,gkhd->ghqk", query_blk, key_blk, preferred_element_type=jnp.float32)
            * scale
        )
        probs = jnp.exp(scores - log_blk)
        grad_probs = jnp.einsum(
            "gqhd,gkhd->ghqk", grad_blk, value_blk, preferred_element_type=jnp.float32
        )
        grad_scores = (
            probs * (grad_probs - jnp.sum(probs * grad_probs, axis=-1, keepdims=True))
        ).astype(jnp.bfloat16)
        grad_val = jnp.einsum(
            "ghqk,gqhd->gkhd",
            probs.astype(jnp.bfloat16),
            grad_blk,
            preferred_element_type=jnp.float32,
        )
        grad_qry = (
            jnp.einsum("ghqk,gkhd->gqhd", grad_scores, key_blk, preferred_element_type=jnp.float32)
            * scale
        )
        grad_kys = (
            jnp.einsum(
                "ghqk,gqhd->gkhd", grad_scores, query_blk, preferred_element_type=jnp.float32
            )
            * scale
        )
        return (grad_qry, grad_kys, grad_val)

    grad_query_n, grad_key_full, grad_value_full = lax.map(
        attend_back, (query_grp, key_grp, value_grp, log_total, grad_grp)
    )
    grad_key_n, grad_value_n = (
        lax.psum_scatter(
            grad_key_full.reshape(count_img, full_len, local_width),
            "ctx",
            scatter_dimension=1,
            tiled=True,
        ),
        lax.psum_scatter(
            grad_value_full.reshape(count_img, full_len, local_width),
            "ctx",
            scatter_dimension=1,
            tiled=True,
        ),
    )
    unused_query, query_pull = jax.vjp(head_scale, query_raw, query_gain)
    grad_query_raw, grad_query_gain = query_pull(
        grad_query_n.reshape(tokens, heads_here, head_size)
    )
    unused_key, key_pull = jax.vjp(head_scale, key_raw, key_gain)
    grad_key_raw, grad_key_gain = key_pull(grad_key_n.reshape(tokens, heads_here, head_size))
    grad_query_low = grad_query_raw.reshape(tokens, local_width).astype(jnp.bfloat16)
    grad_key_low = grad_key_raw.reshape(tokens, local_width).astype(jnp.bfloat16)
    grad_value_low = grad_value_n.reshape(tokens, local_width).astype(jnp.bfloat16)
    grad_w_query = jnp.dot(hidden_one.T, grad_query_low, preferred_element_type=jnp.float32)
    grad_w_key = jnp.dot(hidden_one.T, grad_key_low, preferred_element_type=jnp.float32)
    grad_w_value = jnp.dot(hidden_one.T, grad_value_low, preferred_element_type=jnp.float32)
    grad_one_part = (
        matmul(grad_query_low, full_query.T)
        + matmul(grad_key_low, full_key.T)
        + matmul(grad_value_low, full_value.T)
    )
    grad_one = lax.psum(grad_one_part, "tp")
    grad_gain_one = jnp.sum(grad_one * normed_one, axis=0)
    grad_shift_one = jnp.sum(grad_one, axis=0)
    input_grad = (
        (grad_resid + norm_back(grad_one * gain_one, normed_one, inverse_one))
        .astype(jnp.bfloat16)
        .reshape(images.shape)
    )
    (
        sum_query,
        sum_key,
        sum_value,
        sum_up,
        sum_out,
        sum_down,
        sum_gain_one,
        sum_shift_one,
        sum_gain_two,
        sum_shift_two,
        sum_qgain,
        sum_kgain,
    ) = lax.psum(
        (
            grad_w_query,
            grad_w_key,
            grad_w_value,
            grad_w_up,
            grad_w_out,
            grad_w_down,
            grad_gain_one,
            grad_shift_one,
            grad_gain_two,
            grad_shift_two,
            grad_query_gain,
            grad_key_gain,
        ),
        "ctx",
    )
    (
        part_query,
        part_key,
        part_value,
        part_up,
        part_out,
        part_down,
        part_gain_one,
        part_shift_one,
        part_gain_two,
        part_shift_two,
        part_qgain,
        part_kgain,
    ) = (
        lax.psum_scatter(sum_query, "shard", scatter_dimension=0, tiled=True),
        lax.psum_scatter(sum_key, "shard", scatter_dimension=0, tiled=True),
        lax.psum_scatter(sum_value, "shard", scatter_dimension=0, tiled=True),
        lax.psum_scatter(sum_up, "shard", scatter_dimension=0, tiled=True),
        lax.psum_scatter(sum_out, "shard", scatter_dimension=1, tiled=True),
        lax.psum_scatter(sum_down, "shard", scatter_dimension=1, tiled=True),
        lax.psum_scatter(sum_gain_one, "shard", scatter_dimension=0, tiled=True),
        lax.psum_scatter(sum_shift_one, "shard", scatter_dimension=0, tiled=True),
        lax.psum_scatter(sum_gain_two, "shard", scatter_dimension=0, tiled=True),
        lax.psum_scatter(sum_shift_two, "shard", scatter_dimension=0, tiled=True),
        lax.psum_scatter(sum_qgain, "shard", scatter_dimension=1, tiled=True),
        lax.psum_scatter(sum_kgain, "shard", scatter_dimension=1, tiled=True),
    )
    factor = jnp.sqrt(clip_level / jnp.maximum(peak_all, clip_level))
    columns = jnp.repeat(factor, head_size)
    query_clip = (w_query.astype(jnp.float32) * columns).astype(jnp.bfloat16)
    key_clip = (w_key.astype(jnp.float32) * columns).astype(jnp.bfloat16)
    return (
        block_out,
        input_grad,
        part_gain_one,
        part_shift_one,
        part_gain_two,
        part_shift_two,
        part_qgain,
        part_kgain,
        part_query,
        part_key,
        part_value,
        part_out,
        part_up,
        part_down,
        query_clip,
        key_clip,
    )


MESH = pl.DeviceIdType.MESH
NN = (((1,), (0,)), ((), ()))
NT = (((1,), (1,)), ((), ()))
TN = (((0,), (0,)), ((), ()))
low_type = jnp.bfloat16
full_type = jnp.float32


def dot(left, right, dims=NN):
    return lax.dot_general(left, right, dims, preferred_element_type=full_type)


def flip(place, bits, count):
    result = 0
    unit = 1
    while unit < count:
        result = result + ((place // unit + bits // unit) % 2) * unit
        unit *= 2
    return result


def fits_fused(images, w_query, w_up, q_gain):
    count_img, local_len, width = images.shape
    ctx, shard, tp = lax.axis_size("ctx"), lax.axis_size("shard"), lax.axis_size("tp")
    rows = w_query.shape[0]
    return (
        count_img == 1
        and tp == 2
        and ctx == 4
        and shard == 4
        and rows % (16 * ctx) == 0
        and local_len % 32 == 0
        and q_gain.shape[0] % 2 == 0
        and w_up.shape[1] % (128 * ctx) == 0
    )


def fused_kernel(
    sizes,
    img_h, cot_h, g1_h, b1_h, g2_h, b2_h, qg_h, kg_h, wq_h, wk_h, wv_h, wo_h, wup_h, wdn_h,
    bo_o, ig_o, upo, dno, qkvo, lnr_o, qkr_o, peak_o,
    xg, ctg, smalls, wl, wol, wkv, wqb, wot, wup, wdt, h1_t, h2_t, ct_t,
    xh1, h1, nq, nk, sq, sk, qs, kall, vall, pst, sbuf, attq, attr, pks,
    ptop, dsb,
    h2, ga, act, gu, g2s, g2r, g2own, bos, bor, boown,
    gsib_s, gsib_r, gown, gkeep, gz_s, gz_r, gfin,
    gres, gbg, gms, gm, dqb, dkt, dvt, dks_s, dks_r, dqr, dkv,
    g1s, g1r, g1own, qsib_s, qsib_r, qown, qz_s, qz_r, qfin,
    rows_s, rows_r, obuf,
    lsem, ssem, rsem,
):
    CN, ZN, TB, D, HW, FS, R = sizes
    QR = R // CN
    HR = R // 2
    s_i, c_i, t_i = lax.axis_index("shard"), lax.axis_index("ctx"), lax.axis_index("tp")
    o_i = 1 - t_i
    half_chips = CN // 2
    tstar = c_i // half_chips
    place = c_i % half_chips
    TK = CN * TB
    inv_d = 1.0 / D

    def at_ctx(j):
        return (s_i, flip(c_i, j, CN), t_i)

    def at_z(j):
        return (flip(s_i, j, ZN), c_i, t_i)

    sib = (s_i, c_i, o_i)

    outer = (s_i == 0) | (s_i == ZN - 1)
    pair = flip(s_i, 1, ZN)
    far_in = flip(s_i, 3, ZN) * (1 - outer) + flip(s_i, 2, ZN) * outer
    far_out = flip(s_i, 2, ZN) * (1 - outer) + flip(s_i, 3, ZN) * outer

    def plane(z):
        return (z, c_i, t_i)

    spots = {}

    def spot(name, count):
        if name not in spots:
            spots[name] = (sum(n for _, n in spots.values()), count)
        return spots[name][0]

    def put(name, count, j, src, dst, dev):
        base = spot(name, count)
        pltpu.make_async_remote_copy(
            src_ref=src, dst_ref=dst, send_sem=ssem.at[base + j], recv_sem=rsem.at[base + j],
            device_id=dev, device_id_type=MESH,
        ).start()

    def put_as(name, count, send, recv, src, dst, dev):
        base = spot(name, count)
        pltpu.make_async_remote_copy(
            src_ref=src, dst_ref=dst, send_sem=ssem.at[base + send], recv_sem=rsem.at[base + recv],
            device_id=dev, device_id_type=MESH,
        ).start()

    def got(name, count, j, dst, dev):
        base = spot(name, count)
        pltpu.make_async_remote_copy(
            src_ref=dst, dst_ref=dst, send_sem=ssem.at[base + j], recv_sem=rsem.at[base + j],
            device_id=dev, device_id_type=MESH,
        ).wait_recv()

    def sent(name, count, j, src, dev):
        base = spot(name, count)
        pltpu.make_async_remote_copy(
            src_ref=src, dst_ref=src, send_sem=ssem.at[base + j], recv_sem=rsem.at[base + j],
            device_id=dev, device_id_type=MESH,
        ).wait_send()

    x_src = img_h.at[0, pl.ds(t_i * TB, TB)]
    c_src = cot_h.at[0, pl.ds(t_i * TB, TB)]
    locals_ = [
        pltpu.make_async_copy(wk_h, wl.at[1], lsem.at[0]),
        pltpu.make_async_copy(wv_h, wl.at[2], lsem.at[1]),
        pltpu.make_async_copy(wq_h, wl.at[0], lsem.at[2]),
        pltpu.make_async_copy(x_src, xg.at[0], lsem.at[3]),
        pltpu.make_async_copy(wo_h, wol, lsem.at[4]),
        pltpu.make_async_copy(wdn_h.at[:, pl.ds(c_i * FS, FS)], wdt.at[t_i, s_i], lsem.at[5]),
        pltpu.make_async_copy(wup_h.at[:, pl.ds(c_i * FS, FS)], wup.at[t_i, s_i], lsem.at[6]),
        pltpu.make_async_copy(c_src, ctg.at[0], lsem.at[7]),
    ]
    for copy in locals_:
        copy.start()

    barrier = pltpu.get_barrier_semaphore()
    greet = [at_ctx(j) for j in range(1, CN)] + [at_z(j) for j in range(1, ZN)] + [sib]
    for dev in greet:
        pl.semaphore_signal(barrier, inc=1, device_id=dev, device_id_type=MESH)

    smalls[t_i, s_i] = jnp.zeros((8, 256), full_type)
    for k, ref in enumerate((g1_h, b1_h, g2_h, b2_h)):
        smalls[t_i, s_i, k:k + 1, :R] = ref[...].astype(full_type).reshape(1, R)
    heads = HW // 64
    piece = qg_h.shape[1]
    lane_of = lax.broadcasted_iota(jnp.int32, (piece, HW), 1)
    spread = (
        (lane_of % piece == lax.broadcasted_iota(jnp.int32, (piece, HW), 0)) & ((lane_of % 64) // piece == s_i)
    ).astype(full_type).astype(low_type)
    head_of = lax.broadcasted_iota(jnp.int32, (qg_h.shape[0], HW), 0)
    wanted = head_of == place * heads + lax.broadcasted_iota(jnp.int32, (qg_h.shape[0], HW), 1) // 64
    wanted = wanted & (t_i == tstar)
    for k, ref in ((4, qg_h), (5, kg_h)):
        row = jnp.sum(jnp.where(wanted, dot(ref[...], spread), 0.0), axis=0, keepdims=True)
        smalls[t_i, s_i, k:k + 1, :HW] = row

    pl.semaphore_wait(barrier, len(greet))

    for j in range(1, CN):
        put("x", CN, j, x_src, xg.at[j], at_ctx(j))
    for j in range(1, ZN):
        put("small", ZN, j, smalls.at[t_i, s_i], smalls.at[t_i, s_i], at_z(j))

    def picker(at, lanes, offset):
        rows = lax.broadcasted_iota(jnp.int32, (half_chips * HW, lanes), 0)
        cols = lax.broadcasted_iota(jnp.int32, (half_chips * HW, lanes), 1) - offset
        return ((rows == cols + at * HW) & (cols >= 0) & (cols < HW)).astype(full_type).astype(low_type)

    projections = (("wkv", wkv), ("wq", wqb))

    @pl.when(t_i == tstar)
    def _():
        for n in range(3):
            locals_[n].wait()
        wkv[s_i] = (
            dot(wl[1], picker(place, 2 * HW, 0)) + dot(wl[2], picker(place, 2 * HW, HW))
        ).astype(low_type)
        wqb[s_i] = dot(wl[0], picker(place, HW, 0)).astype(low_type)
        for name, buf in projections:
            for j in range(1, ZN):
                put(name, ZN, j, buf.at[s_i], buf.at[s_i], at_z(j))
            put(name, ZN, 0, buf.at[s_i], buf.at[s_i], sib)

    @pl.when(t_i != tstar)
    def _():
        for n in range(3):
            locals_[n].wait()

    locals_[4].wait()
    wot[t_i, s_i, c_i] = wol[pl.ds(c_i * QR, QR)]
    for j in range(1, ZN):
        put("woz", ZN, j, wot.at[t_i, s_i, c_i], wot.at[t_i, s_i, c_i], at_z(j))

    for j in range(1, ZN):
        got("small", ZN, j, smalls.at[t_i, flip(s_i, j, ZN)], at_z(j))
    put("smallt", 1, 0, smalls.at[t_i], smalls.at[t_i], sib)

    locals_[3].wait()

    def norm_rows(values):
        mean = jnp.sum(values, axis=-1, keepdims=True) * inv_d
        center = values - mean
        inverse = lax.rsqrt(jnp.sum(center * center, axis=-1, keepdims=True) * inv_d + norm_eps)
        return center * inverse, inverse

    ln_rows = jnp.concatenate([smalls[t_i, k][:, :R] for k in range(ZN)], axis=1)
    g1row, b1row, g2row, b2row = (ln_rows[k:k + 1] for k in range(4))

    def first_norm(j, _):
        @pl.when(j > 0)
        def _():
            got("x", CN, j, xg.at[j], at_ctx(j))

        normed, _unused = norm_rows(xg[j].astype(full_type))
        xh1[j] = normed
        hidden = (normed * g1row + b1row).astype(low_type)
        h1[j] = hidden
        h1_t[:, pl.ds(pl.multiple_of(j * TB, TB), TB)] = hidden.T
        return 0

    HB = TB // 2

    def spread(name, src, dst_of):
        for j in (1, 2):
            put(name, 5, j, src, dst_of(j), at_ctx(j))

    def pass_on(name, buf):
        for j in (1, 2):
            got(name, 5, j, buf.at[j], at_ctx(j))
            half = pl.ds((j - 1) * HB, HB)
            put_as(name, 5, 2 + j, 2 + j, buf.at[j, half], buf.at[3, half], at_ctx(3 - j))

    def have_rest(name, buf):
        for j in (1, 2):
            half = pl.ds((j - 1) * HB, HB)
            got(name, 5, 2 + j, buf.at[3, half], at_ctx(3 - j))

    spread("ct", c_src, lambda j: ctg.at[j])
    lax.fori_loop(0, CN, first_norm, 0)

    got("smallt", 1, 0, smalls.at[o_i], sib)
    head_rows = smalls[0, 0][4:6, :HW]
    for a in range(2):
        for k in range(ZN):
            if a or k:
                head_rows = head_rows + smalls[a, k][4:6, :HW]
    qgrow, kgrow = head_rows[0:1], head_rows[1:2]

    lane = lax.broadcasted_iota(jnp.int32, (1, HW), 1) // 64
    mask_f = [(lane == h).astype(full_type) for h in range(heads)]
    mask_b = [m.astype(low_type) for m in mask_f]
    same_head = (
        lax.broadcasted_iota(jnp.int32, (HW, HW), 0) // 64
        == lax.broadcasted_iota(jnp.int32, (HW, HW), 1) // 64
    ).astype(full_type).astype(low_type)

    def head_mean(values):
        high = values.astype(low_type)
        rest = (values - high.astype(full_type)).astype(low_type)
        return (dot(high, same_head) + dot(rest, same_head)) * (1.0 / 64)

    def weight_ready(name, buf):
        @pl.when(t_i != tstar)
        def _():
            got(name, ZN, 0, buf.at[s_i], sib)

        for j in range(1, ZN):
            block = buf.at[flip(s_i, j, ZN)]
            got(name, ZN, j, block, sib)

            @pl.when(t_i == tstar)
            def _():
                pltpu.make_async_remote_copy(
                    src_ref=block, dst_ref=block,
                    send_sem=ssem.at[spot("f" + name, ZN) + j], recv_sem=rsem.at[spot(name, ZN) + j],
                    device_id=sib, device_id_type=MESH,
                ).start()

    h1_all = h1[...].reshape(TK, D)
    weight_ready(*projections[0])
    raw = dot(h1_all, wkv[...].reshape(D, 2 * HW))
    vall[0] = raw[:, HW:].astype(low_type)
    put("v", 1, 0, vall.at[0], vall.at[1], sib)
    raw = raw[:, :HW]
    inverse = lax.rsqrt(head_mean(raw * raw) + norm_eps)
    normed = raw * inverse
    nk[...] = normed
    sk[...] = inverse
    kall[0] = (normed * kgrow).astype(low_type)
    put("k", 1, 0, kall.at[0], kall.at[1], sib)
    weight_ready(*projections[1])
    mlp_weights = (("wd", wdt), ("wu", wup))

    def own_mlp(name, buf):
        block = buf.at[t_i, s_i]
        put_as(name, 5, 0, 0, block, block, plane(pair))

        @pl.when(jnp.logical_not(outer))
        def _():
            put_as(name, 5, 1, 1, block, block, plane(far_in))

    def pass_mlp(name, buf, stage):
        source, target = ((pair, far_in), (far_in, pair), (far_out, pair))[stage]
        recv = (2, 1, 2)[stage]

        @pl.when(jnp.logical_not(outer))
        def _():
            block = buf.at[t_i, source]
            got(name, 5, stage, block, plane(pair))
            put_as(name, 5, 2 + stage, recv, block, block, plane(target))

    def have_mlp(name, buf):
        @pl.when(outer)
        def _():
            for n, z in enumerate((pair, far_in, far_out)):
                got(name, 5, n, buf.at[t_i, z], plane(pair))

    locals_[5].wait()
    own_mlp(*mlp_weights[0])
    locals_[6].wait()
    own_mlp(*mlp_weights[1])
    for j in range(1, ZN):
        got("woz", ZN, j, wot.at[t_i, flip(s_i, j, ZN), c_i], at_z(j))
    for j in range(1, CN):
        put("woc", CN, j, wot.at[t_i, :, c_i], wot.at[t_i, :, c_i], at_ctx(j))
    raw = dot(h1_all, wqb[...].reshape(D, HW))
    inverse = lax.rsqrt(head_mean(raw * raw) + norm_eps)
    normed = raw * inverse
    nq[...] = normed
    sq[...] = inverse
    qs[...] = ((normed * qgrow).astype(low_type) * 0.125).astype(low_type).reshape(CN, TB, HW)

    pass_on("ct", ctg)
    got("k", 1, 0, kall.at[1], sib)
    got("v", 1, 0, vall.at[1], sib)

    def stacked(block):
        return jnp.concatenate([block * m for m in mask_b], axis=0)

    def folded(block):
        total = block[0:TB] * mask_f[0]
        for h in range(1, heads):
            total = total + block[h * TB:(h + 1) * TB] * mask_f[h]
        return total

    ptop[...] = jnp.full(ptop.shape, -3.0e38, full_type)

    def attend(i, _):
        j = CN - 1 - i

        for name, buf, when in (mlp_weights[0] + (1,), mlp_weights[1] + (2,)):
            @pl.when(i == when)
            def _():
                pass_mlp(name, buf, 0)
                pass_mlp(name, buf, 1)

        sbuf[...] = dot(stacked(qs[j]), kall[...].reshape(2 * TK, HW), NT)
        for h in range(heads):
            rows = slice(h * TB, (h + 1) * TB)
            scores = sbuf[rows]
            ptop[h:h + 1] = jnp.maximum(ptop[h:h + 1], jnp.max(scores, axis=0, keepdims=True))
            expo = jnp.exp(scores)
            pst[j, rows] = expo * (1.0 / jnp.sum(expo, axis=-1, keepdims=True))
        mixed = folded(dot(pst[j].astype(low_type), vall[...].reshape(2 * TK, HW)))
        attq[j] = mixed.astype(low_type)

        @pl.when(j > 0)
        def _():
            put("att", CN, j, attq.at[j], attr.at[j], at_ctx(j))

        return 0

    lax.fori_loop(0, CN, attend, 0)
    for j in range(1, CN):
        got("woc", CN, j, wot.at[t_i, :, flip(c_i, j, CN)], at_ctx(j))
    put("wot", 1, 0, wot.at[t_i], wot.at[t_i], sib)
    pass_mlp(*mlp_weights[0], 2)
    peak_rows = jnp.max(ptop[...], axis=-1, keepdims=True)
    lane_id = lax.broadcasted_iota(jnp.int32, (8, 128), 1)
    own_peak = jnp.full((8, 128), -3.0e38, full_type)
    for h in range(heads):
        own_peak = jnp.where(lane_id == c_i * heads + h, peak_rows[h:h + 1], own_peak)
    pks[0] = own_peak
    put("pkt", 1, 0, pks.at[0], pks.at[1], sib)

    def pair_up(own, other):
        even = place == 0
        return jnp.concatenate([jnp.where(even, own, other), jnp.where(even, other, own)], axis=1)

    got("wot", 1, 0, wot.at[o_i], sib)
    got("att", CN, 1, attr.at[1], at_ctx(1))
    branch = dot(pair_up(attq[0], attr[1]), wot[tstar].reshape(D, 2 * HW), NT)
    for j in (2, 3):
        got("att", CN, j, attr.at[j], at_ctx(j))
    branch = branch + dot(pair_up(attr[2], attr[3]), wot[1 - tstar].reshape(D, 2 * HW), NT)
    resid = xg[0].astype(full_type) + branch
    boown[...] = resid
    xhat2, inv2 = norm_rows(resid)
    h2[0] = (xhat2 * g2row + b2row).astype(low_type)
    for j in range(1, CN):
        put("h2", CN, j, h2.at[0], h2.at[j], at_ctx(j))

    pass_mlp(*mlp_weights[1], 2)
    locals_[7].wait()
    have_rest("ct", ctg)
    ct_t[...] = ctg[...].reshape(TK, D).T
    have_mlp(*mlp_weights[0])
    put("wdt", 1, 0, wdt.at[t_i], wdt.at[t_i], sib)
    ga[t_i] = dot(ctg[...].reshape(TK, D), wdt[t_i].reshape(D, FS)).reshape(CN, TB, FS)
    have_mlp(*mlp_weights[1])
    put("wut", 1, 0, wup.at[t_i], wup.at[t_i], sib)
    got("wdt", 1, 0, wdt.at[o_i], sib)
    ga[o_i] = dot(ctg[...].reshape(TK, D), wdt[o_i].reshape(D, FS)).reshape(CN, TB, FS)
    got("wut", 1, 0, wup.at[o_i], sib)

    def mlp(j, _):
        @pl.when(j > 0)
        def _():
            got("h2", CN, j, h2.at[j], at_ctx(j))

        block = h2[j]
        h2_t[:, pl.ds(pl.multiple_of(j * TB, TB), TB)] = block.T
        for a in range(2):
            up = dot(block, wup[a].reshape(D, FS))
            phi = 0.5 * (1.0 + lax.erf(up * 0.7071067811865476))
            dens = jnp.exp(up * up * -0.5) * 0.3989422804014327
            part = slice(a * FS, (a + 1) * FS)
            act[j, :, part] = (up * phi).astype(low_type)
            gu[j, :, part] = (ga[a, j] * (phi + up * dens)).astype(low_type)
        grad_two = (
            dot(gu[j, :, :FS], wup[0].reshape(D, FS), NT) + dot(gu[j, :, FS:], wup[1].reshape(D, FS), NT)
        )

        @pl.when(j == 0)
        def _():
            g2own[...] = grad_two

        @pl.when(j > 0)
        def _():
            g2s[j] = grad_two.astype(low_type)
            put("g2", CN, j, g2s.at[j], g2r.at[j], at_ctx(j))

        return 0

    lax.fori_loop(0, CN, mlp, 0)

    own_part = pl.ds(pl.multiple_of(t_i * FS, FS), FS)
    other_part = pl.ds(pl.multiple_of(o_i * FS, FS), FS)
    for k, (left, right) in enumerate(((h2_t, gu), (ct_t, act))):
        gown[k] = dot(left[...], right[...].reshape(TK, 2 * FS))
        gsib_s[k] = gown[k, :, other_part].astype(low_type)
        put("gs", 2, k, gsib_s.at[k], gsib_r.at[k], sib)

    def down(j, _):
        part = (
            dot(act[j, :, :FS], wdt[0].reshape(D, FS), NT) + dot(act[j, :, FS:], wdt[1].reshape(D, FS), NT)
        )

        @pl.when(j == 0)
        def _():
            boown[...] += part

        @pl.when(j > 0)
        def _():
            bos[j] = part.astype(low_type)

        return 0

    lax.fori_loop(0, CN, down, 0)

    for k in range(2):
        got("gs", 2, k, gsib_r.at[k], sib)
        total = gown[k, :, own_part] + gsib_r[k].astype(full_type)
        gkeep[k] = total
        gz_s[k] = total.astype(low_type).reshape(ZN, R, FS)

    @pl.when(outer)
    def _():
        for k in range(2):
            put("gz%d" % k, 4, 2, gz_s.at[k, far_out], gz_r.at[k, 2], plane(pair))
            put("gz%d" % k, 4, 3, gz_s.at[k, far_in], gz_r.at[k, 3], plane(pair))

    for k in range(2):
        put("gz%d" % k, 4, 0, gz_s.at[k, pair], gz_r.at[k, 0], plane(pair))

    def relay_mlp(k):
        @pl.when(jnp.logical_not(outer))
        def _():
            for n, z in ((2, far_out), (3, far_in)):
                got("gz%d" % k, 4, n, gz_r.at[k, n], plane(pair))
                mine_part = gkeep[k, pl.ds(pl.multiple_of(z * R, R), R)]
                gz_s[k, z] = (mine_part + gz_r[k, n].astype(full_type)).astype(low_type)
                base = spot("gz%d" % k, 4)
                pltpu.make_async_remote_copy(
                    src_ref=gz_s.at[k, z], dst_ref=gz_r.at[k, 1],
                    send_sem=ssem.at[base + n], recv_sem=rsem.at[base + 1],
                    device_id=plane(z), device_id_type=MESH,
                ).start()

    def share_mlp(k, out):
        total = gkeep[k, pl.ds(pl.multiple_of(s_i * R, R), R)]
        for n in range(2):
            got("gz%d" % k, 4, n, gz_r.at[k, n], plane(pair))
            total = total + gz_r[k, n].astype(full_type)
        gfin[k] = total.astype(low_type)
        spread("gc%d" % k, gfin.at[k], lambda j: out.at[c_i])
        pltpu.make_async_copy(gfin.at[k], out.at[c_i], lsem.at[8 + k]).start()

    grad_two = g2own[...]
    for j in range(1, CN):
        got("g2", CN, j, g2r.at[j], at_ctx(j))
        grad_two = grad_two + g2r[j].astype(full_type)
    ln2g = jnp.sum(grad_two * xhat2, axis=0, keepdims=True)
    ln2b = jnp.sum(grad_two, axis=0, keepdims=True)
    hat = grad_two * g2row
    grad_resid = ctg[0].astype(full_type) + inv2 * (
        hat
        - jnp.sum(hat, axis=-1, keepdims=True) * inv_d
        - xhat2 * (jnp.sum(hat * xhat2, axis=-1, keepdims=True) * inv_d)
    )
    gres[...] = grad_resid
    gb = grad_resid.astype(low_type)
    gbg[0] = gb
    for near in (0, 1):
        mixed = dot(gb, wot[(1 - tstar) * (1 - near) + tstar * near].reshape(D, 2 * HW)).astype(low_type)
        even, odd = mixed[:, :HW], mixed[:, HW:]
        first, second = (1, 0) if near else (3, 2)
        flag = place == 0
        gms[first] = jnp.where(flag, odd, even)
        gms[second] = jnp.where(flag, even, odd)
        for j in (first, second):
            if j:
                put("gm", CN, j, gms.at[j], gm.at[j], at_ctx(j))
    gm[0] = gms[0]
    spread("gb", gbg.at[0], lambda j: gbg.at[j])
    for j in (1, 2):
        half = pl.ds((j - 1) * HB, HB)
        put_as("bo", 5, 2 + j, 2 + j, bos.at[3, half], bor.at[3, half], at_ctx(j))

    dkt[...] = jnp.zeros_like(dkt)
    dvt[...] = jnp.zeros_like(dvt)

    def attend_back(j, _):
        @pl.when(j > 0)
        def _():
            got("gm", CN, j, gm.at[j], at_ctx(j))

        @pl.when(j == 1)
        def _():
            relay_mlp(0)

        @pl.when(j == 2)
        def _():
            relay_mlp(1)

        grad_rows = stacked(gm[j])
        query_rows = stacked(qs[j])
        sbuf[...] = dot(grad_rows, vall[...].reshape(2 * TK, HW), NT)

        for h in range(heads):
            rows = slice(h * TB, (h + 1) * TB)
            probs, grad_probs = pst[j, rows], sbuf[rows]
            inner = jnp.sum(probs * grad_probs, axis=-1, keepdims=True)
            dsb[rows] = (probs * (grad_probs - inner)).astype(low_type)
        grad_scores = dsb[...]
        dqb[j] = folded(dot(grad_scores, kall[...].reshape(2 * TK, HW))) * 0.125
        dvt[...] += dot(grad_rows, pst[j].astype(low_type), TN)
        dkt[...] += dot(query_rows, grad_scores, TN)
        return 0

    lax.fori_loop(0, CN, attend_back, 0)
    dks_s[0] = dvt[:, TK:].astype(low_type)
    dks_s[1] = dkt[:, TK:].astype(low_type)
    for k in range(2):
        put("dk", 2, k, dks_s.at[k], dks_r.at[k], sib)

    pass_on("gb", gbg)
    for j in (1, 2):
        half = pl.ds((j - 1) * HB, HB)
        got("bo", 5, 2 + j, bor.at[3, half], at_ctx(j))
        bos[3 - j, half] = (bos[3 - j, half].astype(full_type) + bor[3, half].astype(full_type)).astype(low_type)
    for j in (1, 2):
        put_as("bo", 5, j, j, bos.at[j], bor.at[j], at_ctx(j))

    def unnorm(grad_n, gain_row, normed, inverse):
        gain_grad = jnp.sum(grad_n * normed, axis=0, keepdims=True)
        e = grad_n * gain_row
        return (inverse * (e - normed * head_mean(e * normed))).astype(low_type), gain_grad

    def share_grad(n, full):
        full = full.reshape(ZN, 2, HR, 2 * HW)
        low_full = full.astype(low_type)
        for k in range(2):
            @pl.when(o_i == k)
            def _():
                qsib_s[n] = low_full[:, k]

            @pl.when(t_i == k)
            def _():
                qown[n] = full[:, k]

        put("qg", 2, n, qsib_s.at[n], qsib_r.at[n], sib)

    def reduce_grad(n):
        got("qg", 2, n, qsib_r.at[n], sib)
        total = qown[n] + qsib_r[n].astype(full_type)
        qown[n] = total
        qz_s[n] = total.astype(low_type)
        for j in range(1, ZN):
            put("qz%d" % n, ZN, j, qz_s.at[n, flip(s_i, j, ZN)], qz_r.at[n, j], at_z(j))

    grad_raw, q_gain_row = unnorm(dqb[...].reshape(TK, HW), qgrow, nq[...], sq[...])
    dqr[...] = grad_raw
    got("dk", 2, 0, dks_r.at[0], sib)
    grad_v = (dvt[:, :TK] + dks_r[0].astype(full_type)).T.astype(low_type)
    got("dk", 2, 1, dks_r.at[1], sib)
    grad_k = (dkt[:, :TK] + dks_r[1].astype(full_type)).T
    grad_raw, k_gain_row = unnorm(grad_k, kgrow, nk[...], sk[...])
    dkv[...] = jnp.concatenate([grad_raw, grad_v], axis=1)
    share_grad(0, dot(h1_t[...], dkv[...]))
    have_rest("gb", gbg)
    empty = jnp.zeros((TK, HW), low_type)
    share_grad(1, (
        dot(h1_t[...], jnp.concatenate([dqr[...], empty], axis=1))
        + dot(gbg[...].reshape(TK, D), jnp.concatenate([empty, attq[...].reshape(TK, HW)], axis=1), TN)
    ))
    reduce_grad(0)
    reduce_grad(1)

    ln1g = jnp.zeros((1, D), full_type)
    ln1b = jnp.zeros((1, D), full_type)
    for j in range(CN - 1, -1, -1):
        rows = slice(j * TB, (j + 1) * TB)
        part = dot(dqr[rows], wqb[...].reshape(D, HW), NT) + dot(dkv[rows], wkv[...].reshape(D, 2 * HW), NT)
        if j:
            g1s[j] = part.astype(low_type)
            put("g1", CN, j, g1s.at[j], g1r.at[j], at_ctx(j))
        else:
            g1own[...] = part
        ln1g = ln1g + jnp.sum(part * xh1[j], axis=0, keepdims=True)
        ln1b = ln1b + jnp.sum(part, axis=0, keepdims=True)
    rows_s[0] = jnp.zeros_like(rows_s[0])
    for k, row in enumerate((ln1g, ln1b, ln2g, ln2b)):
        rows_s[0, k:k + 1, :D] = row
    rows_s[0, 0:1, D:D + HW] = q_gain_row
    rows_s[0, 1:2, D:D + HW] = k_gain_row
    put("rt", 1, 0, rows_s.at[0], rows_r.at[0], sib)
    share_mlp(0, upo)
    share_mlp(1, dno)

    got("rt", 1, 0, rows_r.at[0], sib)
    rows_s[1] = rows_s[0] + rows_r[0]
    for j in range(1, ZN):
        put("rz", ZN, j, rows_s.at[1], rows_r.at[j], at_z(j))
    got("pkt", 1, 0, pks.at[1], sib)
    pks[2] = jnp.maximum(pks[0], pks[1])
    for j in range(1, ZN):
        put("pkz", ZN, j, pks.at[2], pks.at[2 + j], at_z(j))

    total = boown[...]
    for j in (1, 2):
        got("bo", 5, j, bor.at[j], at_ctx(j))
        total = total + bor[j].astype(full_type)
    own_rows = pl.ds(t_i * TB, TB)
    obuf[0] = total.astype(low_type)
    put("ob", 2, 0, obuf.at[0], bo_o.at[own_rows], sib)
    pltpu.make_async_copy(obuf.at[0], bo_o.at[own_rows], lsem.at[10]).start()

    def share_fin(n):
        total = qown[n, s_i]
        for j in range(1, ZN):
            got("qz%d" % n, ZN, j, qz_r.at[n, j], at_z(j))
            total = total + qz_r[n, j].astype(full_type)
        qfin[n] = total.astype(low_type)
        slot = spot("qcr%d" % n, 2 * half_chips) + place * 2 + t_i
        for j in range(1, CN):
            pltpu.make_async_remote_copy(
                src_ref=qfin.at[n], dst_ref=qkvo.at[place, t_i, n],
                send_sem=ssem.at[spot("qcs%d" % n, CN) + j], recv_sem=rsem.at[slot],
                device_id=(s_i, flip(c_i, j, CN), tstar), device_id_type=MESH,
            ).start()

        @pl.when(t_i == tstar)
        def _():
            pltpu.make_async_copy(qfin.at[n], qkvo.at[place, t_i, n], lsem.at[12 + n]).start()

        @pl.when(t_i != tstar)
        def _():
            pltpu.make_async_remote_copy(
                src_ref=qfin.at[n], dst_ref=qkvo.at[place, t_i, n],
                send_sem=ssem.at[spot("qcs%d" % n, CN)], recv_sem=rsem.at[slot],
                device_id=sib, device_id_type=MESH,
            ).start()

    share_fin(0)

    for k, out in ((0, upo), (1, dno)):
        for j in (1, 2):
            block = out.at[flip(c_i, j, CN)]
            got("gc%d" % k, 5, j, block, at_ctx(j))
            half = block.at[pl.ds((j - 1) * HR, HR)]
            put_as("gc%d" % k, 5, 2 + j, 2 + j, half, half, at_ctx(3 - j))

    share_fin(1)
    xhat1, inv1 = norm_rows(xg[0].astype(full_type))
    grad_one = g1own[...]
    for j in range(1, CN):
        got("g1", CN, j, g1r.at[j], at_ctx(j))
        grad_one = grad_one + g1r[j].astype(full_type)
    hat = grad_one * g1row
    grad_in = gres[...] + inv1 * (
        hat
        - jnp.sum(hat, axis=-1, keepdims=True) * inv_d
        - xhat1 * (jnp.sum(hat * xhat1, axis=-1, keepdims=True) * inv_d)
    )
    obuf[1] = grad_in.astype(low_type)
    put("ob", 2, 1, obuf.at[1], ig_o.at[own_rows], sib)
    pltpu.make_async_copy(obuf.at[1], ig_o.at[own_rows], lsem.at[11]).start()

    rows_sum = rows_s[1]
    for j in range(1, ZN):
        got("rz", ZN, j, rows_r.at[j], at_z(j))
        rows_sum = rows_sum + rows_r[j]
    rows_s[2] = rows_sum
    for j in range(1, CN):
        put("rc", CN, j, rows_s.at[2], rows_r.at[ZN + j], at_ctx(j))
    peak = pks[2]
    for j in range(1, ZN):
        got("pkz", ZN, j, pks.at[2 + j], at_z(j))
        peak = jnp.maximum(peak, pks[2 + j])
    first = 2 + ZN
    pks[first] = peak
    for j in range(1, CN):
        put("pkc", CN, j, pks.at[first], pks.at[first + j], at_ctx(j))
    qkr_o[c_i] = rows_sum[:, D:]
    total = rows_sum[:, :D]
    for j in range(1, CN):
        got("rc", CN, j, rows_r.at[ZN + j], at_ctx(j))
        block = rows_r[ZN + j]
        total = total + block[:, :D]
        qkr_o[flip(c_i, j, CN)] = block[:, D:]
    lnr_o[...] = total
    for j in range(1, CN):
        got("pkc", CN, j, pks.at[first + j], at_ctx(j))
        peak = jnp.maximum(peak, pks[first + j])
    peak_o[...] = peak

    for k, out in ((0, upo), (1, dno)):
        for j in (1, 2):
            half = out.at[flip(c_i, 3, CN), pl.ds((j - 1) * HR, HR)]
            got("gc%d" % k, 5, 2 + j, half, at_ctx(3 - j))
        pltpu.make_async_copy(gfin.at[k], out.at[c_i], lsem.at[8 + k]).wait()
    other_rows = pl.ds(o_i * TB, TB)
    for k, out in ((0, bo_o), (1, ig_o)):
        got("ob", 2, k, out.at[other_rows], sib)
        pltpu.make_async_copy(obuf.at[k], out.at[own_rows], lsem.at[10 + k]).wait()

    @pl.when(t_i == tstar)
    def _():
        for n in range(2):
            pltpu.make_async_copy(qfin.at[n], qkvo.at[place, t_i, n], lsem.at[12 + n]).wait()

    for p in range(half_chips):
        for a in range(2):
            @pl.when((t_i != tstar) | (place != p) | (t_i != a))
            def _():
                for n in range(2):
                    pltpu.make_async_remote_copy(
                        src_ref=qfin.at[n], dst_ref=qkvo.at[p, a, n],
                        send_sem=ssem.at[spot("qcs%d" % n, CN)],
                        recv_sem=rsem.at[spot("qcr%d" % n, 2 * half_chips) + p * 2 + a],
                        device_id=sib, device_id_type=MESH,
                    ).wait_recv()

    for j in range(1, CN):
        sent("x", CN, j, x_src, sib)
        sent("woc", CN, j, wot.at[t_i, :, c_i], sib)
        sent("att", CN, j, attq.at[j], sib)
        sent("h2", CN, j, h2.at[0], sib)
        sent("g2", CN, j, g2s.at[j], sib)
        sent("gm", CN, j, gms.at[j], sib)
        sent("g1", CN, j, g1s.at[j], sib)
        sent("pkc", CN, j, pks.at[first], sib)
        sent("rc", CN, j, rows_s.at[2], sib)
        for n in range(2):
            sent("qcs%d" % n, CN, j, qfin.at[n], sib)
    for j in range(1, ZN):
        sent("small", ZN, j, smalls.at[t_i, s_i], sib)
        sent("woz", ZN, j, wot.at[t_i, s_i, c_i], sib)
        sent("pkz", ZN, j, pks.at[2], sib)
        sent("rz", ZN, j, rows_s.at[1], sib)
        for n in range(2):
            sent("qz%d" % n, ZN, j, qz_s.at[n, 0], sib)
    for n in range(1, 5):
        for name, buf, half in (("ct", ctg, ctg), ("gb", gbg, gbg), ("bo", bos, bos)):
            sent(name, 5, n, buf.at[1] if n < 3 else half.at[1, pl.ds(0, HB)], sib)
        for k, out in ((0, upo), (1, dno)):
            sent("gc%d" % k, 5, n, gfin.at[k] if n < 3 else gfin.at[k, pl.ds(0, HR)], sib)
    for name, buf in mlp_weights:
        sent(name, 5, 0, buf.at[t_i, s_i], sib)

        @pl.when(jnp.logical_not(outer))
        def _():
            for n in range(1, 5):
                sent(name, 5, n, buf.at[t_i, s_i], sib)

    for k in range(2):
        for n in (0, 2, 3):
            sent("gz%d" % k, 4, n, gz_s.at[k, 0], sib)
    sent("smallt", 1, 0, smalls.at[t_i], sib)
    sent("k", 1, 0, kall.at[0], sib)
    sent("v", 1, 0, vall.at[0], sib)
    sent("pkt", 1, 0, pks.at[0], sib)
    sent("wot", 1, 0, wot.at[t_i], sib)
    sent("wdt", 1, 0, wdt.at[t_i], sib)
    sent("wut", 1, 0, wup.at[t_i], sib)
    sent("rt", 1, 0, rows_s.at[0], sib)
    for k in range(2):
        sent("gs", 2, k, gsib_s.at[k], sib)
        sent("dk", 2, k, dks_s.at[k], sib)
        sent("ob", 2, k, obuf.at[k], sib)
    for n in range(2):
        sent("qg", 2, n, qsib_s.at[n], sib)

    @pl.when(t_i == tstar)
    def _():
        for name, buf in projections:
            for j in range(ZN):
                sent(name, ZN, j, buf.at[s_i], sib)
                if j:
                    sent("f" + name, ZN, j, buf.at[s_i], sib)

    @pl.when(t_i != tstar)
    def _():
        for n in range(2):
            sent("qcs%d" % n, CN, 0, qfin.at[n], sib)


SEMS = 320


def fused_call(sizes, *operands):
    CN, ZN, TB, D, HW, FS, R = sizes
    TK = CN * TB
    QR, HR = R // CN, R // 2
    half_chips = CN // 2
    heads = HW // 64
    lo, hi = low_type, full_type
    V = pltpu.VMEM
    any_spec = pl.BlockSpec(memory_space=pl.ANY)
    vm_spec = pl.BlockSpec(memory_space=pltpu.VMEM)
    out_shape = [
        jax.ShapeDtypeStruct((2 * TB, D), lo),
        jax.ShapeDtypeStruct((2 * TB, D), lo),
        jax.ShapeDtypeStruct((CN, R, FS), lo),
        jax.ShapeDtypeStruct((CN, R, FS), lo),
        jax.ShapeDtypeStruct((half_chips, 2, 2, HR, 2 * HW), lo),
        jax.ShapeDtypeStruct((8, D), hi),
        jax.ShapeDtypeStruct((CN, 8, 256), hi),
        jax.ShapeDtypeStruct((8, 128), hi),
    ]
    scratch = [
        V((CN, TB, D), lo), V((CN, TB, D), lo), V((2, ZN, 8, 256), hi),
        V((3, R, half_chips * HW), lo), V((R, half_chips * HW), lo),
        V((ZN, R, 2 * HW), lo), V((ZN, R, HW), lo), V((2, ZN, CN, QR, 2 * HW), lo), V((2, ZN, R, FS), lo), V((2, ZN, R, FS), lo),
        V((D, TK), lo), V((D, TK), lo), V((D, TK), lo),
        V((CN, TB, D), hi), V((CN, TB, D), lo),
        V((TK, HW), hi), V((TK, HW), hi), V((TK, HW), hi), V((TK, HW), hi),
        V((CN, TB, HW), lo), V((2, TK, HW), lo), V((2, TK, HW), lo),
        V((CN, heads * TB, 2 * TK), hi), V((heads * TB, 2 * TK), hi),
        V((CN, TB, HW), lo), V((CN, TB, HW), lo), V((2 + ZN + CN, 8, 128), hi),
        V((heads, 2 * TK), hi), V((heads * TB, 2 * TK), lo),
        V((CN, TB, D), lo), V((2, CN, TB, FS), hi), V((CN, TB, 2 * FS), lo), V((CN, TB, 2 * FS), lo),
        V((CN, TB, D), lo), V((CN, TB, D), lo), V((TB, D), hi),
        V((CN, TB, D), lo), V((CN, TB, D), lo), V((TB, D), hi),
        V((2, D, FS), lo), V((2, D, FS), lo), V((2, D, 2 * FS), hi), V((2, D, FS), hi),
        V((2, ZN, R, FS), lo), V((2, ZN, R, FS), lo), V((2, R, FS), lo),
        V((TB, D), hi), V((CN, TB, D), lo), V((CN, TB, HW), lo), V((CN, TB, HW), lo),
        V((CN, TB, HW), hi), V((HW, 2 * TK), hi), V((HW, 2 * TK), hi),
        V((2, HW, TK), lo), V((2, HW, TK), lo), V((TK, HW), lo), V((TK, 2 * HW), lo),
        V((CN, TB, D), lo), V((CN, TB, D), lo), V((TB, D), hi),
        V((2, ZN, HR, 2 * HW), lo), V((2, ZN, HR, 2 * HW), lo), V((2, ZN, HR, 2 * HW), hi),
        V((2, ZN, HR, 2 * HW), lo), V((2, ZN, HR, 2 * HW), lo), V((2, HR, 2 * HW), lo),
        V((3, 8, D + 256), hi), V((ZN + CN, 8, D + 256), hi), V((2, TB, D), lo),
        pltpu.SemaphoreType.DMA((16,)), pltpu.SemaphoreType.DMA((SEMS,)), pltpu.SemaphoreType.DMA((SEMS,)),
    ]
    return pl.pallas_call(
        functools.partial(fused_kernel, sizes),
        out_shape=out_shape,
        in_specs=[any_spec] * 2 + [vm_spec] * 6 + [any_spec] * 6,
        out_specs=[any_spec] * 5 + [vm_spec] * 3,
        scratch_shapes=scratch,
        compiler_params=pltpu.CompilerParams(
            collective_id=0, has_side_effects=True, vmem_limit_bytes=56 * 2**20
        ),
    )(*operands)


def finish_kernel(
    sizes,
    bo, ig, up_h, dn_h, qkvo_h, lnr_h, qkr_h, peak_h, wq_h, wk_h,
    bo_o, ig_o, l1g, l1b, l2g, l2b, qg_o, kg_o, gq_o, gk_o, gv_o, go_o, gu_o, gd_o, cq_o, ck_o,
    upo, dno, qkvo, lnr, qkr, peak, wq, wk, bov, igv, gq, gk, gv, go, gu, gd, cq, ck, isem, osem,
):
    CN, ZN, TB, D, HW, FS, R = sizes
    half_chips = CN // 2
    s_i, t_i = lax.axis_index("shard"), lax.axis_index("tp")
    ins = [
        pltpu.make_async_copy(src, dst, isem.at[n])
        for n, (src, dst) in enumerate((
            (qkvo_h, qkvo), (up_h, upo), (dn_h, dno), (peak_h, peak), (wq_h, wq), (wk_h, wk),
            (lnr_h, lnr), (qkr_h, qkr), (bo, bov), (ig, igv),
        ))
    ]
    for n in (8, 9, 0, 1, 2, 3, 4, 5, 6, 7):
        ins[n].start()
    outs = []

    def leave(src, dst):
        copy = pltpu.make_async_copy(src, dst, osem.at[len(outs)])
        copy.start()
        outs.append(copy)

    for n, stage, out in ((8, bov, bo_o), (9, igv, ig_o)):
        ins[n].wait()
        leave(stage, out)
    ins[0].wait()
    for n, first, stage, out in ((1, 0, gq, gq_o), (0, 0, gk, gk_o), (0, HW, gv, gv_o), (1, HW, go, go_o)):
        for a in range(2):
            parts = [qkvo[p, a, n][:, first:first + HW] for p in range(half_chips)]
            stage[a * (R // 2):(a + 1) * (R // 2)] = jnp.concatenate(parts, axis=1).astype(full_type)
        leave(stage, out)
    for n, grads, stage, out in ((1, upo, gu, gu_o), (2, dno, gd, gd_o)):
        ins[n].wait()
        for c in range(CN):
            stage[:, c * FS:(c + 1) * FS] = grads[c].astype(full_type)
        leave(stage, out)
    heads = HW // 64
    for n in (3, 4, 5):
        ins[n].wait()
    factor = jnp.sqrt(clip_level / jnp.maximum(peak[0:1], clip_level))
    here = half_chips * heads
    lanes = lax.broadcasted_iota(jnp.int32, (1, here * 64), 1) // 64
    ids = lax.broadcasted_iota(jnp.int32, (1, 128), 1)
    columns = jnp.ones((1, here * 64), full_type)
    for h in range(here):
        one = jnp.sum(jnp.where(ids == t_i * here + h, factor, 0.0), axis=-1, keepdims=True)
        columns = jnp.where(lanes == h, one, columns)
    for weights, stage, out in ((wq, cq, cq_o), (wk, ck, ck_o)):
        stage[...] = (weights[...].astype(full_type) * columns).astype(low_type)
        leave(stage, out)
    ins[6].wait()
    ins[7].wait()
    rows = jnp.zeros((8, R), full_type)
    for z in range(ZN):
        rows = jnp.where(s_i == z, lnr[:, z * R:(z + 1) * R], rows)
    for k, out in enumerate((l1g, l1b, l2g, l2b)):
        out[...] = rows[k:k + 1].reshape(R)
    piece = qg_o.shape[1]
    for p in range(half_chips):
        chip = qkr[t_i * half_chips + p]
        for h in range(heads):
            for z in range(ZN):
                at = h * 64 + z * piece

                @pl.when(s_i == z)
                def _():
                    qg_o[p * heads + h:p * heads + h + 1] = chip[0:1, at:at + piece]
                    kg_o[p * heads + h:p * heads + h + 1] = chip[1:2, at:at + piece]
    for copy in outs:
        copy.wait()


def fused_layer(
    images, cotangent, ln1_gain, ln1_bias, ln2_gain, ln2_bias, q_gain, k_gain,
    w_query, w_key, w_value, w_out, w_up, w_down,
):
    CN, ZN = lax.axis_size("ctx"), lax.axis_size("shard")
    TB = images.shape[1] // 2
    D = images.shape[2]
    R = w_query.shape[0]
    HW = w_query.shape[1] // (CN // 2)
    FS = w_up.shape[1] // CN
    sizes = (CN, ZN, TB, D, HW, FS, R)
    results = fused_call(
        sizes, images, cotangent, ln1_gain, ln1_bias, ln2_gain, ln2_bias, q_gain, k_gain,
        w_query, w_key, w_value, w_out.T, w_up, w_down.T,
    )
    row = jax.ShapeDtypeStruct((R,), full_type)
    gain = jax.ShapeDtypeStruct(q_gain.shape, full_type)
    square = jax.ShapeDtypeStruct(w_query.shape, full_type)
    wide = jax.ShapeDtypeStruct(w_up.shape, full_type)
    tokens = jax.ShapeDtypeStruct(images.shape[1:], low_type)
    clipped = jax.ShapeDtypeStruct(w_query.shape, low_type)
    lo, hi = low_type, full_type
    V = pltpu.VMEM
    any_spec = pl.BlockSpec(memory_space=pl.ANY)
    vm_spec = pl.BlockSpec(memory_space=pltpu.VMEM)
    out = pl.pallas_call(
        functools.partial(finish_kernel, sizes),
        out_shape=[tokens] * 2 + [row] * 4 + [gain] * 2 + [square] * 4 + [wide] * 2 + [clipped] * 2,
        in_specs=[any_spec] * 10,
        out_specs=[any_spec] * 2 + [vm_spec] * 6 + [any_spec] * 8,
        scratch_shapes=[
            V((CN, R, FS), lo), V((CN, R, FS), lo), V((CN // 2, 2, 2, R // 2, 2 * HW), lo), V((8, D), hi),
            V((CN, 8, 256), hi), V((8, 128), hi), V(w_query.shape, lo), V(w_query.shape, lo),
            V(images.shape[1:], lo), V(images.shape[1:], lo),
        ]
        + [V(w_query.shape, hi)] * 4 + [V(w_up.shape, hi)] * 2 + [V(w_query.shape, lo)] * 2
        + [pltpu.SemaphoreType.DMA((10,)), pltpu.SemaphoreType.DMA((10,))],
        compiler_params=pltpu.CompilerParams(vmem_limit_bytes=60 * 2**20),
    )(*results, w_query, w_key)
    out = list(out)
    out[0], out[1] = out[0].reshape(images.shape), out[1].reshape(images.shape)
    out[11], out[13] = out[11].T, out[13].T
    return tuple(out)


def on_device(images, cotangent, ln1_gain, ln1_bias, ln2_gain, ln2_bias, q_gain, k_gain, *weights):
    fused = fits_fused(images, weights[0], weights[4], q_gain)
    layer = fused_layer if fused else general_layer
    return layer(images, cotangent, ln1_gain, ln1_bias, ln2_gain, ln2_bias, q_gain, k_gain, *weights)


def solution(mesh):
    return jax.shard_map(
        on_device,
        mesh=mesh,
        in_specs=(
            P("shard", "ctx", None),
            P("shard", "ctx", None),
            P("shard"),
            P("shard"),
            P("shard"),
            P("shard"),
            P("tp", "shard"),
            P("tp", "shard"),
            P("shard", "tp"),
            P("shard", "tp"),
            P("shard", "tp"),
            P("tp", "shard"),
            P("shard", "tp"),
            P("tp", "shard"),
        ),
        out_specs=(
            P("shard", "ctx", None),
            P("shard", "ctx", None),
            P("shard"),
            P("shard"),
            P("shard"),
            P("shard"),
            P("tp", "shard"),
            P("tp", "shard"),
            P("shard", "tp"),
            P("shard", "tp"),
            P("shard", "tp"),
            P("tp", "shard"),
            P("shard", "tp"),
            P("tp", "shard"),
            P("shard", "tp"),
            P("shard", "tp"),
        ),
        check_vma=False,
    )
```

```python
import functools
import jax
import jax.numpy as jnp
from jax import lax
from jax.experimental import pallas as pl
from jax.experimental.pallas import tpu as pltpu
from jax.sharding import PartitionSpec as P

norm_eps = 1e-06
clip_level = 0.5


def matmul(left, right):
    return jnp.dot(left, right, preferred_element_type=jnp.float32)


def norm_parts(values):
    center = values - jnp.mean(values, axis=-1, keepdims=True)
    inverse = lax.rsqrt(jnp.mean(center * center, axis=-1, keepdims=True) + norm_eps)
    return (center * inverse, inverse)


def norm_back(grad_hat, normed, inverse):
    return inverse * (
        grad_hat
        - jnp.mean(grad_hat, axis=-1, keepdims=True)
        - normed * jnp.mean(grad_hat * normed, axis=-1, keepdims=True)
    )


def head_scale(values, gain):
    inverse = lax.rsqrt(jnp.mean(values * values, axis=-1, keepdims=True) + norm_eps)
    return values * inverse * gain


def gelu_exact(values):
    return jax.nn.gelu(values, approximate=False)


def general_layer(
    images,
    cotangent,
    ln1_gain,
    ln1_bias,
    ln2_gain,
    ln2_bias,
    q_gain,
    k_gain,
    w_query,
    w_key,
    w_value,
    w_out,
    w_up,
    w_down,
):
    (
        full_query,
        full_key,
        full_value,
        full_up,
        full_out,
        full_down,
        gain_low_one,
        shift_low_one,
        gain_low_two,
        shift_low_two,
        query_gain_low,
        key_gain_low,
    ) = (
        lax.all_gather(w_query, "shard", axis=0, tiled=True),
        lax.all_gather(w_key, "shard", axis=0, tiled=True),
        lax.all_gather(w_value, "shard", axis=0, tiled=True),
        lax.all_gather(w_up, "shard", axis=0, tiled=True),
        lax.all_gather(w_out, "shard", axis=1, tiled=True),
        lax.all_gather(w_down, "shard", axis=1, tiled=True),
        lax.all_gather(ln1_gain, "shard", axis=0, tiled=True),
        lax.all_gather(ln1_bias, "shard", axis=0, tiled=True),
        lax.all_gather(ln2_gain, "shard", axis=0, tiled=True),
        lax.all_gather(ln2_bias, "shard", axis=0, tiled=True),
        lax.all_gather(q_gain, "shard", axis=1, tiled=True),
        lax.all_gather(k_gain, "shard", axis=1, tiled=True),
    )
    gain_one = gain_low_one.astype(jnp.float32)
    shift_one = shift_low_one.astype(jnp.float32)
    gain_two = gain_low_two.astype(jnp.float32)
    shift_two = shift_low_two.astype(jnp.float32)
    query_gain = query_gain_low.astype(jnp.float32)
    key_gain = key_gain_low.astype(jnp.float32)
    count_img, local_len, width = images.shape
    tokens = count_img * local_len
    heads_here, head_size = query_gain.shape
    local_width = heads_here * head_size
    full_len = local_len * lax.axis_size("ctx")
    group = 1
    groups = count_img // group
    scale = head_size ** (-0.5)
    flat = images.reshape(tokens, width).astype(jnp.float32)
    normed_one, inverse_one = norm_parts(flat)
    hidden_one = (normed_one * gain_one + shift_one).astype(jnp.bfloat16)
    query_raw = matmul(hidden_one, full_query).reshape(tokens, heads_here, head_size)
    key_raw = matmul(hidden_one, full_key).reshape(tokens, heads_here, head_size)
    query_norm = head_scale(query_raw, query_gain).astype(jnp.bfloat16)
    key_norm = head_scale(key_raw, key_gain).astype(jnp.bfloat16)
    value_low = matmul(hidden_one, full_value).astype(jnp.bfloat16)
    key_all, value_all = (
        lax.all_gather(
            key_norm.reshape(count_img, local_len, local_width), "ctx", axis=1, tiled=True
        ),
        lax.all_gather(
            value_low.reshape(count_img, local_len, local_width), "ctx", axis=1, tiled=True
        ),
    )
    query_grp = query_norm.reshape(groups, group, local_len, heads_here, head_size)
    key_grp = key_all.reshape(groups, group, full_len, heads_here, head_size)
    value_grp = value_all.reshape(groups, group, full_len, heads_here, head_size)

    def attend(pieces):
        query_blk, key_blk, value_blk = pieces
        scores = (
            jnp.einsum("gqhd,gkhd->ghqk", query_blk, key_blk, preferred_element_type=jnp.float32)
            * scale
        )
        top = jnp.max(scores, axis=-1, keepdims=True)
        expo = jnp.exp(scores - top)
        total = jnp.sum(expo, axis=-1, keepdims=True)
        probs = (expo / total).astype(jnp.bfloat16)
        mixed_blk = jnp.einsum(
            "ghqk,gkhd->gqhd", probs, value_blk, preferred_element_type=jnp.float32
        )
        return (mixed_blk, top + jnp.log(total), jnp.max(top, axis=(0, 2, 3)))

    mixed, log_total, group_peaks = lax.map(attend, (query_grp, key_grp, value_grp))
    local_peak = jnp.max(group_peaks, axis=0)
    peak_all = lax.pmax(local_peak, ("shard", "ctx"))
    attended = mixed.reshape(tokens, local_width).astype(jnp.bfloat16)
    branch_attn = lax.psum(matmul(attended, full_out), "tp")
    resid = flat + branch_attn
    normed_two, inverse_two = norm_parts(resid)
    hidden_two = (normed_two * gain_two + shift_two).astype(jnp.bfloat16)
    up_raw = matmul(hidden_two, full_up)
    active = gelu_exact(up_raw).astype(jnp.bfloat16)
    branch_mlp = lax.psum(matmul(active, full_down).astype(jnp.bfloat16), "tp").astype(jnp.float32)
    block_out = (resid + branch_mlp).astype(jnp.bfloat16).reshape(images.shape)
    grad_out = cotangent.reshape(tokens, width).astype(jnp.float32)
    grad_down = cotangent.reshape(tokens, width)
    grad_w_down = jnp.dot(active.T, grad_down, preferred_element_type=jnp.float32)
    grad_active = matmul(grad_down, full_down.T)
    unused_up, gelu_pull = jax.vjp(gelu_exact, up_raw)
    grad_up = gelu_pull(grad_active)[0].astype(jnp.bfloat16)
    grad_w_up = jnp.dot(hidden_two.T, grad_up, preferred_element_type=jnp.float32)
    grad_two = lax.psum(matmul(grad_up, full_up.T), "tp")
    grad_gain_two = jnp.sum(grad_two * normed_two, axis=0)
    grad_shift_two = jnp.sum(grad_two, axis=0)
    grad_resid = grad_out + norm_back(grad_two * gain_two, normed_two, inverse_two)
    grad_branch = grad_resid.astype(jnp.bfloat16)
    grad_w_out = jnp.dot(attended.T, grad_branch, preferred_element_type=jnp.float32)
    grad_mixed = matmul(grad_branch, full_out.T).astype(jnp.bfloat16)
    grad_grp = grad_mixed.reshape(groups, group, local_len, heads_here, head_size)

    def attend_back(pieces):
        query_blk, key_blk, value_blk, log_blk, grad_blk = pieces
        scores = (
            jnp.einsum("gqhd,gkhd->ghqk", query_blk, key_blk, preferred_element_type=jnp.float32)
            * scale
        )
        probs = jnp.exp(scores - log_blk)
        grad_probs = jnp.einsum(
            "gqhd,gkhd->ghqk", grad_blk, value_blk, preferred_element_type=jnp.float32
        )
        grad_scores = (
            probs * (grad_probs - jnp.sum(probs * grad_probs, axis=-1, keepdims=True))
        ).astype(jnp.bfloat16)
        grad_val = jnp.einsum(
            "ghqk,gqhd->gkhd",
            probs.astype(jnp.bfloat16),
            grad_blk,
            preferred_element_type=jnp.float32,
        )
        grad_qry = (
            jnp.einsum("ghqk,gkhd->gqhd", grad_scores, key_blk, preferred_element_type=jnp.float32)
            * scale
        )
        grad_kys = (
            jnp.einsum(
                "ghqk,gqhd->gkhd", grad_scores, query_blk, preferred_element_type=jnp.float32
            )
            * scale
        )
        return (grad_qry, grad_kys, grad_val)

    grad_query_n, grad_key_full, grad_value_full = lax.map(
        attend_back, (query_grp, key_grp, value_grp, log_total, grad_grp)
    )
    grad_key_n, grad_value_n = (
        lax.psum_scatter(
            grad_key_full.reshape(count_img, full_len, local_width),
            "ctx",
            scatter_dimension=1,
            tiled=True,
        ),
        lax.psum_scatter(
            grad_value_full.reshape(count_img, full_len, local_width),
            "ctx",
            scatter_dimension=1,
            tiled=True,
        ),
    )
    unused_query, query_pull = jax.vjp(head_scale, query_raw, query_gain)
    grad_query_raw, grad_query_gain = query_pull(
        grad_query_n.reshape(tokens, heads_here, head_size)
    )
    unused_key, key_pull = jax.vjp(head_scale, key_raw, key_gain)
    grad_key_raw, grad_key_gain = key_pull(grad_key_n.reshape(tokens, heads_here, head_size))
    grad_query_low = grad_query_raw.reshape(tokens, local_width).astype(jnp.bfloat16)
    grad_key_low = grad_key_raw.reshape(tokens, local_width).astype(jnp.bfloat16)
    grad_value_low = grad_value_n.reshape(tokens, local_width).astype(jnp.bfloat16)
    grad_w_query = jnp.dot(hidden_one.T, grad_query_low, preferred_element_type=jnp.float32)
    grad_w_key = jnp.dot(hidden_one.T, grad_key_low, preferred_element_type=jnp.float32)
    grad_w_value = jnp.dot(hidden_one.T, grad_value_low, preferred_element_type=jnp.float32)
    grad_one_part = (
        matmul(grad_query_low, full_query.T)
        + matmul(grad_key_low, full_key.T)
        + matmul(grad_value_low, full_value.T)
    )
    grad_one = lax.psum(grad_one_part, "tp")
    grad_gain_one = jnp.sum(grad_one * normed_one, axis=0)
    grad_shift_one = jnp.sum(grad_one, axis=0)
    input_grad = (
        (grad_resid + norm_back(grad_one * gain_one, normed_one, inverse_one))
        .astype(jnp.bfloat16)
        .reshape(images.shape)
    )
    (
        sum_query,
        sum_key,
        sum_value,
        sum_up,
        sum_out,
        sum_down,
        sum_gain_one,
        sum_shift_one,
        sum_gain_two,
        sum_shift_two,
        sum_qgain,
        sum_kgain,
    ) = lax.psum(
        (
            grad_w_query,
            grad_w_key,
            grad_w_value,
            grad_w_up,
            grad_w_out,
            grad_w_down,
            grad_gain_one,
            grad_shift_one,
            grad_gain_two,
            grad_shift_two,
            grad_query_gain,
            grad_key_gain,
        ),
        "ctx",
    )
    (
        part_query,
        part_key,
        part_value,
        part_up,
        part_out,
        part_down,
        part_gain_one,
        part_shift_one,
        part_gain_two,
        part_shift_two,
        part_qgain,
        part_kgain,
    ) = (
        lax.psum_scatter(sum_query, "shard", scatter_dimension=0, tiled=True),
        lax.psum_scatter(sum_key, "shard", scatter_dimension=0, tiled=True),
        lax.psum_scatter(sum_value, "shard", scatter_dimension=0, tiled=True),
        lax.psum_scatter(sum_up, "shard", scatter_dimension=0, tiled=True),
        lax.psum_scatter(sum_out, "shard", scatter_dimension=1, tiled=True),
        lax.psum_scatter(sum_down, "shard", scatter_dimension=1, tiled=True),
        lax.psum_scatter(sum_gain_one, "shard", scatter_dimension=0, tiled=True),
        lax.psum_scatter(sum_shift_one, "shard", scatter_dimension=0, tiled=True),
        lax.psum_scatter(sum_gain_two, "shard", scatter_dimension=0, tiled=True),
        lax.psum_scatter(sum_shift_two, "shard", scatter_dimension=0, tiled=True),
        lax.psum_scatter(sum_qgain, "shard", scatter_dimension=1, tiled=True),
        lax.psum_scatter(sum_kgain, "shard", scatter_dimension=1, tiled=True),
    )
    factor = jnp.sqrt(clip_level / jnp.maximum(peak_all, clip_level))
    columns = jnp.repeat(factor, head_size)
    query_clip = (w_query.astype(jnp.float32) * columns).astype(jnp.bfloat16)
    key_clip = (w_key.astype(jnp.float32) * columns).astype(jnp.bfloat16)
    return (
        block_out,
        input_grad,
        part_gain_one,
        part_shift_one,
        part_gain_two,
        part_shift_two,
        part_qgain,
        part_kgain,
        part_query,
        part_key,
        part_value,
        part_out,
        part_up,
        part_down,
        query_clip,
        key_clip,
    )


MESH = pl.DeviceIdType.MESH
NN = (((1,), (0,)), ((), ()))
NT = (((1,), (1,)), ((), ()))
TN = (((0,), (0,)), ((), ()))
low_type = jnp.bfloat16
full_type = jnp.float32


def dot(left, right, dims=NN):
    return lax.dot_general(left, right, dims, preferred_element_type=full_type)


def flip(place, bits, count):
    result = 0
    unit = 1
    while unit < count:
        result = result + ((place // unit + bits // unit) % 2) * unit
        unit *= 2
    return result


def fits_fused(images, w_query, w_up, q_gain):
    count_img, local_len, width = images.shape
    ctx, shard, tp = lax.axis_size("ctx"), lax.axis_size("shard"), lax.axis_size("tp")
    rows = w_query.shape[0]
    return (
        count_img == 1
        and tp == 2
        and ctx == 4
        and shard == 4
        and rows % (16 * ctx) == 0
        and local_len % 32 == 0
        and q_gain.shape[0] % 2 == 0
        and w_up.shape[1] % (128 * ctx) == 0
    )


def fused_kernel(
    sizes,
    img_h, cot_h, g1_h, b1_h, g2_h, b2_h, qg_h, kg_h, wq_h, wk_h, wv_h, wo_h, wup_h, wdn_h,
    bo_o, ig_o, upo, dno, qkvo, lnr_o, qkr_o, peak_o,
    xg, ctg, smalls, wl, wol, wkv, wqb, wob, wup, wdt, h1_t, h2_t, ct_t,
    xh1, h1, nq, nk, sq, sk, qs, kall, vall, pst, sbuf, attq, brs, brr, pks,
    ptop, dsb,
    h2, ga, act, gu, g2s, g2r, g2own, bos, bor, boown,
    gsib_s, gsib_r, gown, gkeep, gz_s, gz_r, gfin,
    gres, gbg, dqb, dkt, dvt, dks_s, dks_r, dqr, dkv,
    g1s, g1r, g1own, qsib_s, qsib_r, qown, qz_s, qz_r, qfin,
    rows_s, rows_r, obuf,
    lsem, ssem, rsem,
):
    CN, ZN, TB, D, HW, FS, R = sizes
    HR = R // 2
    s_i, c_i, t_i = lax.axis_index("shard"), lax.axis_index("ctx"), lax.axis_index("tp")
    o_i = 1 - t_i
    half_chips = CN // 2
    tstar = c_i // half_chips
    place = c_i % half_chips
    TK = CN * TB
    inv_d = 1.0 / D

    def at_ctx(j):
        return (s_i, flip(c_i, j, CN), t_i)

    def at_z(j):
        return (flip(s_i, j, ZN), c_i, t_i)

    sib = (s_i, c_i, o_i)

    outer = (s_i == 0) | (s_i == ZN - 1)
    pair = flip(s_i, 1, ZN)
    far_in = flip(s_i, 3, ZN) * (1 - outer) + flip(s_i, 2, ZN) * outer
    far_out = flip(s_i, 2, ZN) * (1 - outer) + flip(s_i, 3, ZN) * outer

    def plane(z):
        return (z, c_i, t_i)

    spots = {}
    from_one = ("x", "small", "fwkv", "fwq", "fwo", "br", "h2", "g2", "qz0", "qz1", "rz", "pkz", "rc", "pkc",
                "ct", "gb", "bo", "g1", "gc0", "gc1")

    def spot(name, count):
        if name not in spots:
            first = sum(n for _, n in spots.values())
            skip = 1 if name in from_one else 0
            spots[name] = (first - skip, count - skip)
        return spots[name][0]

    def put(name, count, j, src, dst, dev):
        base = spot(name, count)
        pltpu.make_async_remote_copy(
            src_ref=src, dst_ref=dst, send_sem=ssem.at[base + j], recv_sem=rsem.at[base + j],
            device_id=dev, device_id_type=MESH,
        ).start()

    def put_as(name, count, send, recv, src, dst, dev):
        base = spot(name, count)
        pltpu.make_async_remote_copy(
            src_ref=src, dst_ref=dst, send_sem=ssem.at[base + send], recv_sem=rsem.at[base + recv],
            device_id=dev, device_id_type=MESH,
        ).start()

    def got(name, count, j, dst, dev):
        base = spot(name, count)
        pltpu.make_async_remote_copy(
            src_ref=dst, dst_ref=dst, send_sem=ssem.at[base + j], recv_sem=rsem.at[base + j],
            device_id=dev, device_id_type=MESH,
        ).wait_recv()

    def sent(name, count, j, src, dev):
        base = spot(name, count)
        pltpu.make_async_remote_copy(
            src_ref=src, dst_ref=src, send_sem=ssem.at[base + j], recv_sem=rsem.at[base + j],
            device_id=dev, device_id_type=MESH,
        ).wait_send()

    x_src = img_h.at[0, pl.ds(t_i * TB, TB)]
    c_src = cot_h.at[0, pl.ds(t_i * TB, TB)]
    locals_ = [
        pltpu.make_async_copy(wk_h, wl.at[1], lsem.at[0]),
        pltpu.make_async_copy(wv_h, wl.at[2], lsem.at[1]),
        pltpu.make_async_copy(wq_h, wl.at[0], lsem.at[2]),
        pltpu.make_async_copy(x_src, xg.at[0], lsem.at[3]),
        pltpu.make_async_copy(wo_h, wol, lsem.at[4]),
        pltpu.make_async_copy(wdn_h.at[:, pl.ds(c_i * FS, FS)], wdt.at[t_i, s_i], lsem.at[5]),
        pltpu.make_async_copy(wup_h.at[:, pl.ds(c_i * FS, FS)], wup.at[t_i, s_i], lsem.at[6]),
        pltpu.make_async_copy(c_src, ctg.at[0], lsem.at[7]),
    ]
    for copy in locals_:
        copy.start()

    barrier = pltpu.get_barrier_semaphore()
    greet = [at_ctx(j) for j in range(1, CN)] + [at_z(j) for j in range(1, ZN)] + [sib]
    for dev in greet:
        pl.semaphore_signal(barrier, inc=1, device_id=dev, device_id_type=MESH)

    smalls[t_i, s_i] = jnp.zeros((8, 256), full_type)
    for k, ref in enumerate((g1_h, b1_h, g2_h, b2_h)):
        smalls[t_i, s_i, k:k + 1, :R] = ref[...].astype(full_type).reshape(1, R)
    heads = HW // 64
    piece = qg_h.shape[1]
    lane_of = lax.broadcasted_iota(jnp.int32, (piece, HW), 1)
    spread = (
        (lane_of % piece == lax.broadcasted_iota(jnp.int32, (piece, HW), 0)) & ((lane_of % 64) // piece == s_i)
    ).astype(full_type).astype(low_type)
    head_of = lax.broadcasted_iota(jnp.int32, (qg_h.shape[0], HW), 0)
    wanted = head_of == place * heads + lax.broadcasted_iota(jnp.int32, (qg_h.shape[0], HW), 1) // 64
    wanted = wanted & (t_i == tstar)
    for k, ref in ((4, qg_h), (5, kg_h)):
        row = jnp.sum(jnp.where(wanted, dot(ref[...], spread), 0.0), axis=0, keepdims=True)
        smalls[t_i, s_i, k:k + 1, :HW] = row

    pl.semaphore_wait(barrier, len(greet))

    for j in range(1, CN):
        put("x", CN, j, x_src, xg.at[j], at_ctx(j))
    for j in range(1, ZN):
        put("small", ZN, j, smalls.at[t_i, s_i], smalls.at[t_i, s_i], at_z(j))

    def picker(at, lanes, offset):
        rows = lax.broadcasted_iota(jnp.int32, (half_chips * HW, lanes), 0)
        cols = lax.broadcasted_iota(jnp.int32, (half_chips * HW, lanes), 1) - offset
        return ((rows == cols + at * HW) & (cols >= 0) & (cols < HW)).astype(full_type).astype(low_type)

    projections = (("wkv", wkv), ("wq", wqb), ("wo", wob))

    locals_[4].wait()

    @pl.when(t_i == tstar)
    def _():
        for n in range(3):
            locals_[n].wait()
        wkv[s_i] = (
            dot(wl[1], picker(place, 2 * HW, 0)) + dot(wl[2], picker(place, 2 * HW, HW))
        ).astype(low_type)
        wqb[s_i] = dot(wl[0], picker(place, HW, 0)).astype(low_type)
        wob[s_i] = dot(wol[...], picker(place, HW, 0)).astype(low_type)
        for name, buf in projections:
            for j in range(1, ZN):
                put(name, ZN, j, buf.at[s_i], buf.at[s_i], at_z(j))
            put(name, ZN, 0, buf.at[s_i], buf.at[s_i], sib)

    @pl.when(t_i != tstar)
    def _():
        for n in range(3):
            locals_[n].wait()

    for j in range(1, ZN):
        got("small", ZN, j, smalls.at[t_i, flip(s_i, j, ZN)], at_z(j))
    put("smallt", 1, 0, smalls.at[t_i], smalls.at[t_i], sib)

    locals_[3].wait()

    def norm_rows(values):
        mean = jnp.sum(values, axis=-1, keepdims=True) * inv_d
        center = values - mean
        inverse = lax.rsqrt(jnp.sum(center * center, axis=-1, keepdims=True) * inv_d + norm_eps)
        return center * inverse, inverse

    ln_rows = jnp.concatenate([smalls[t_i, k][:, :R] for k in range(ZN)], axis=1)
    g1row, b1row, g2row, b2row = (ln_rows[k:k + 1] for k in range(4))

    def first_norm(j, _):
        @pl.when(j > 0)
        def _():
            got("x", CN, j, xg.at[j], at_ctx(j))

        normed, _unused = norm_rows(xg[j].astype(full_type))
        xh1[j] = normed
        hidden = (normed * g1row + b1row).astype(low_type)
        h1[j] = hidden
        h1_t[:, pl.ds(pl.multiple_of(j * TB, TB), TB)] = hidden.T
        return 0

    HB = TB // 2

    def spread(name, src, dst_of):
        for j in (1, 2):
            put(name, 5, j, src, dst_of(j), at_ctx(j))

    def pass_on(name, buf):
        for j in (1, 2):
            got(name, 5, j, buf.at[j], at_ctx(j))
            half = pl.ds((j - 1) * HB, HB)
            put_as(name, 5, 2 + j, 2 + j, buf.at[j, half], buf.at[3, half], at_ctx(3 - j))

    def send_halves(name, src, land):
        for j in (1, 2):
            half = pl.ds((j - 1) * HB, HB)
            put_as(name, 5, 2 + j, 2 + j, src.at[3, half], land.at[3, half], at_ctx(j))

    def add_halves(name, src, land):
        for j in (1, 2):
            half = pl.ds((j - 1) * HB, HB)
            got(name, 5, 2 + j, land.at[3, half], at_ctx(j))
            src[3 - j, half] = (src[3 - j, half].astype(full_type) + land[3, half].astype(full_type)).astype(low_type)
        for j in (1, 2):
            put_as(name, 5, j, j, src.at[j], land.at[j], at_ctx(j))

    def have_rest(name, buf):
        for j in (1, 2):
            half = pl.ds((j - 1) * HB, HB)
            got(name, 5, 2 + j, buf.at[3, half], at_ctx(3 - j))

    spread("ct", c_src, lambda j: ctg.at[j])
    lax.fori_loop(0, CN, first_norm, 0)

    got("smallt", 1, 0, smalls.at[o_i], sib)
    head_rows = smalls[0, 0][4:6, :HW]
    for a in range(2):
        for k in range(ZN):
            if a or k:
                head_rows = head_rows + smalls[a, k][4:6, :HW]
    qgrow, kgrow = head_rows[0:1], head_rows[1:2]

    lane = lax.broadcasted_iota(jnp.int32, (1, HW), 1) // 64
    mask_f = [(lane == h).astype(full_type) for h in range(heads)]
    mask_b = [m.astype(low_type) for m in mask_f]
    same_head = (
        lax.broadcasted_iota(jnp.int32, (HW, HW), 0) // 64
        == lax.broadcasted_iota(jnp.int32, (HW, HW), 1) // 64
    ).astype(full_type).astype(low_type)

    def head_mean(values):
        high = values.astype(low_type)
        rest = (values - high.astype(full_type)).astype(low_type)
        return (dot(high, same_head) + dot(rest, same_head)) * (1.0 / 64)

    def weight_ready(name, buf):
        @pl.when(t_i != tstar)
        def _():
            got(name, ZN, 0, buf.at[s_i], sib)

        for j in range(1, ZN):
            block = buf.at[flip(s_i, j, ZN)]
            got(name, ZN, j, block, sib)

            @pl.when(t_i == tstar)
            def _():
                pltpu.make_async_remote_copy(
                    src_ref=block, dst_ref=block,
                    send_sem=ssem.at[spot("f" + name, ZN) + j], recv_sem=rsem.at[spot(name, ZN) + j],
                    device_id=sib, device_id_type=MESH,
                ).start()

    h1_all = h1[...].reshape(TK, D)
    weight_ready(*projections[0])
    raw = dot(h1_all, wkv[...].reshape(D, 2 * HW))
    vall[0] = raw[:, HW:].astype(low_type)
    put("v", 1, 0, vall.at[0], vall.at[1], sib)
    raw = raw[:, :HW]
    inverse = lax.rsqrt(head_mean(raw * raw) + norm_eps)
    normed = raw * inverse
    nk[...] = normed
    sk[...] = inverse
    kall[0] = (normed * kgrow).astype(low_type)
    put("k", 1, 0, kall.at[0], kall.at[1], sib)
    weight_ready(*projections[1])
    mlp_weights = (("wd", wdt), ("wu", wup))

    def own_mlp(name, buf):
        block = buf.at[t_i, s_i]
        put_as(name, 5, 0, 0, block, block, plane(pair))

        @pl.when(jnp.logical_not(outer))
        def _():
            put_as(name, 5, 1, 1, block, block, plane(far_in))

    def pass_mlp(name, buf, stage):
        source, target = ((pair, far_in), (far_in, pair), (far_out, pair))[stage]
        recv = (2, 1, 2)[stage]

        @pl.when(jnp.logical_not(outer))
        def _():
            block = buf.at[t_i, source]
            got(name, 5, stage, block, plane(pair))
            put_as(name, 5, 2 + stage, recv, block, block, plane(target))

    def have_mlp(name, buf):
        @pl.when(outer)
        def _():
            for n, z in enumerate((pair, far_in, far_out)):
                got(name, 5, n, buf.at[t_i, z], plane(pair))

    locals_[5].wait()
    own_mlp(*mlp_weights[0])
    locals_[6].wait()
    own_mlp(*mlp_weights[1])
    raw = dot(h1_all, wqb[...].reshape(D, HW))
    inverse = lax.rsqrt(head_mean(raw * raw) + norm_eps)
    normed = raw * inverse
    nq[...] = normed
    sq[...] = inverse
    qs[...] = ((normed * qgrow).astype(low_type) * 0.125).astype(low_type).reshape(CN, TB, HW)

    got("k", 1, 0, kall.at[1], sib)
    got("v", 1, 0, vall.at[1], sib)

    def stacked(block):
        return jnp.concatenate([block * m for m in mask_b], axis=0)

    def folded(block):
        total = block[0:TB] * mask_f[0]
        for h in range(1, heads):
            total = total + block[h * TB:(h + 1) * TB] * mask_f[h]
        return total

    ptop[...] = jnp.full(ptop.shape, -3.0e38, full_type)

    def attend(i, _):
        j = CN - 1 - i

        @pl.when(i == CN - 1)
        def _():
            pass_mlp(*mlp_weights[0], 0)
            pass_mlp(*mlp_weights[0], 1)

        sbuf[...] = dot(stacked(qs[j]), kall[...].reshape(2 * TK, HW), NT)
        for h in range(heads):
            rows = slice(h * TB, (h + 1) * TB)
            scores = sbuf[rows]
            ptop[h:h + 1] = jnp.maximum(ptop[h:h + 1], jnp.max(scores, axis=0, keepdims=True))
            expo = jnp.exp(scores)
            pst[j, rows] = expo * (1.0 / jnp.sum(expo, axis=-1, keepdims=True))
        mixed = folded(dot(pst[j].astype(low_type), vall[...].reshape(2 * TK, HW)))
        attq[j] = mixed.astype(low_type)

        @pl.when(i == 0)
        def _():
            weight_ready(*projections[2])

        branch = dot(attq[j], wob[...].reshape(D, HW), NT)

        @pl.when(j > 0)
        def _():
            brs[j] = branch.astype(low_type)
            put("br", CN, j, brs.at[j], brr.at[j], at_ctx(j))

        @pl.when(j == 0)
        def _():
            boown[...] = branch

        return 0

    lax.fori_loop(0, CN, attend, 0)
    pass_mlp(*mlp_weights[1], 0)
    pass_mlp(*mlp_weights[1], 1)
    pass_on("ct", ctg)
    pass_mlp(*mlp_weights[0], 2)
    peak_rows = jnp.max(ptop[...], axis=-1, keepdims=True)
    lane_id = lax.broadcasted_iota(jnp.int32, (8, 128), 1)
    own_peak = jnp.full((8, 128), -3.0e38, full_type)
    for h in range(heads):
        own_peak = jnp.where(lane_id == c_i * heads + h, peak_rows[h:h + 1], own_peak)
    pks[0] = own_peak
    put("pkt", 1, 0, pks.at[0], pks.at[1], sib)

    branch = boown[...]
    for j in (3, 2, 1):
        got("br", CN, j, brr.at[j], at_ctx(j))
        branch = branch + brr[j].astype(full_type)
    resid = xg[0].astype(full_type) + branch
    boown[...] = resid
    xhat2, inv2 = norm_rows(resid)
    h2[0] = (xhat2 * g2row + b2row).astype(low_type)
    for j in range(1, CN):
        put("h2", CN, j, h2.at[0], h2.at[j], at_ctx(j))

    pass_mlp(*mlp_weights[1], 2)
    locals_[7].wait()
    have_rest("ct", ctg)
    ct_t[...] = ctg[...].reshape(TK, D).T
    have_mlp(*mlp_weights[0])
    put("wdt", 1, 0, wdt.at[t_i], wdt.at[t_i], sib)
    ga[t_i] = dot(ctg[...].reshape(TK, D), wdt[t_i].reshape(D, FS)).reshape(CN, TB, FS)
    have_mlp(*mlp_weights[1])
    put("wut", 1, 0, wup.at[t_i], wup.at[t_i], sib)
    got("wdt", 1, 0, wdt.at[o_i], sib)
    ga[o_i] = dot(ctg[...].reshape(TK, D), wdt[o_i].reshape(D, FS)).reshape(CN, TB, FS)
    got("wut", 1, 0, wup.at[o_i], sib)

    def mlp(j, _):
        @pl.when(j > 0)
        def _():
            got("h2", CN, j, h2.at[j], at_ctx(j))

        block = h2[j]
        h2_t[:, pl.ds(pl.multiple_of(j * TB, TB), TB)] = block.T
        for a in range(2):
            up = dot(block, wup[a].reshape(D, FS))
            phi = 0.5 * (1.0 + lax.erf(up * 0.7071067811865476))
            dens = jnp.exp(up * up * -0.5) * 0.3989422804014327
            part = slice(a * FS, (a + 1) * FS)
            act[j, :, part] = (up * phi).astype(low_type)
            gu[j, :, part] = (ga[a, j] * (phi + up * dens)).astype(low_type)
        grad_two = (
            dot(gu[j, :, :FS], wup[0].reshape(D, FS), NT) + dot(gu[j, :, FS:], wup[1].reshape(D, FS), NT)
        )

        @pl.when(j == 0)
        def _():
            g2own[...] = grad_two

        @pl.when(j > 0)
        def _():
            g2s[j] = grad_two.astype(low_type)
            put("g2", CN, j, g2s.at[j], g2r.at[j], at_ctx(j))

        return 0

    lax.fori_loop(0, CN, mlp, 0)

    got("pkt", 1, 0, pks.at[1], sib)
    pks[2] = jnp.maximum(pks[0], pks[1])
    for j in range(1, ZN):
        put("pkz", ZN, j, pks.at[2], pks.at[2 + j], at_z(j))
    own_part = pl.ds(pl.multiple_of(t_i * FS, FS), FS)
    other_part = pl.ds(pl.multiple_of(o_i * FS, FS), FS)
    for k, (left, right) in enumerate(((h2_t, gu), (ct_t, act))):
        gown[k] = dot(left[...], right[...].reshape(TK, 2 * FS))
        gsib_s[k] = gown[k, :, other_part].astype(low_type)
        put("gs", 2, k, gsib_s.at[k], gsib_r.at[k], sib)

    def down(j, _):
        part = (
            dot(act[j, :, :FS], wdt[0].reshape(D, FS), NT) + dot(act[j, :, FS:], wdt[1].reshape(D, FS), NT)
        )

        @pl.when(j == 0)
        def _():
            boown[...] += part

        @pl.when(j > 0)
        def _():
            bos[j] = part.astype(low_type)

        return 0

    lax.fori_loop(0, CN, down, 0)

    for k in range(2):
        got("gs", 2, k, gsib_r.at[k], sib)
        total = gown[k, :, own_part] + gsib_r[k].astype(full_type)
        gkeep[k] = total
        gz_s[k] = total.astype(low_type).reshape(ZN, R, FS)

    @pl.when(outer)
    def _():
        for k in range(2):
            put("gz%d" % k, 4, 2, gz_s.at[k, far_out], gz_r.at[k, 2], plane(pair))
            put("gz%d" % k, 4, 3, gz_s.at[k, far_in], gz_r.at[k, 3], plane(pair))

    for k in range(2):
        put("gz%d" % k, 4, 0, gz_s.at[k, pair], gz_r.at[k, 0], plane(pair))

    def relay_mlp(k):
        @pl.when(jnp.logical_not(outer))
        def _():
            for n, z in ((2, far_out), (3, far_in)):
                got("gz%d" % k, 4, n, gz_r.at[k, n], plane(pair))
                mine_part = gkeep[k, pl.ds(pl.multiple_of(z * R, R), R)]
                gz_s[k, z] = (mine_part + gz_r[k, n].astype(full_type)).astype(low_type)
                base = spot("gz%d" % k, 4)
                pltpu.make_async_remote_copy(
                    src_ref=gz_s.at[k, z], dst_ref=gz_r.at[k, 1],
                    send_sem=ssem.at[base + n], recv_sem=rsem.at[base + 1],
                    device_id=plane(z), device_id_type=MESH,
                ).start()

    def share_mlp(k, out):
        total = gkeep[k, pl.ds(pl.multiple_of(s_i * R, R), R)]
        for n in range(2):
            got("gz%d" % k, 4, n, gz_r.at[k, n], plane(pair))
            total = total + gz_r[k, n].astype(full_type)
        gfin[k] = total.astype(low_type)
        spread("gc%d" % k, gfin.at[k], lambda j: out.at[c_i])
        pltpu.make_async_copy(gfin.at[k], out.at[c_i], lsem.at[8 + k]).start()

    grad_two = g2own[...]
    for j in range(1, CN):
        got("g2", CN, j, g2r.at[j], at_ctx(j))
        grad_two = grad_two + g2r[j].astype(full_type)
    ln2g = jnp.sum(grad_two * xhat2, axis=0, keepdims=True)
    ln2b = jnp.sum(grad_two, axis=0, keepdims=True)
    hat = grad_two * g2row
    grad_resid = ctg[0].astype(full_type) + inv2 * (
        hat
        - jnp.sum(hat, axis=-1, keepdims=True) * inv_d
        - xhat2 * (jnp.sum(hat * xhat2, axis=-1, keepdims=True) * inv_d)
    )
    gres[...] = grad_resid
    gb = grad_resid.astype(low_type)
    gbg[0] = gb
    spread("gb", gbg.at[0], lambda j: gbg.at[j])
    send_halves("bo", bos, bor)

    peak = pks[2]
    for j in range(1, ZN):
        got("pkz", ZN, j, pks.at[2 + j], at_z(j))
        peak = jnp.maximum(peak, pks[2 + j])
    first = 2 + ZN
    pks[first] = peak
    for j in range(1, CN):
        put("pkc", CN, j, pks.at[first], pks.at[first + j], at_ctx(j))

    dkt[...] = jnp.zeros_like(dkt)
    dvt[...] = jnp.zeros_like(dvt)

    def attend_back(j, _):
        @pl.when(j == 1)
        def _():
            pass_on("gb", gbg)
            relay_mlp(0)

        @pl.when(j == CN - 1)
        def _():
            add_halves("bo", bos, bor)
            have_rest("gb", gbg)
            relay_mlp(1)

        grad_rows = stacked(dot(gbg[j], wob[...].reshape(D, HW)).astype(low_type))
        query_rows = stacked(qs[j])
        sbuf[...] = dot(grad_rows, vall[...].reshape(2 * TK, HW), NT)

        for h in range(heads):
            rows = slice(h * TB, (h + 1) * TB)
            probs, grad_probs = pst[j, rows], sbuf[rows]
            inner = jnp.sum(probs * grad_probs, axis=-1, keepdims=True)
            dsb[rows] = (probs * (grad_probs - inner)).astype(low_type)
        grad_scores = dsb[...]
        dqb[j] = folded(dot(grad_scores, kall[...].reshape(2 * TK, HW))) * 0.125
        dvt[...] += dot(grad_rows, pst[j].astype(low_type), TN)
        dkt[...] += dot(query_rows, grad_scores, TN)
        return 0

    lax.fori_loop(0, CN, attend_back, 0)
    dks_s[0] = dvt[:, TK:].astype(low_type)
    dks_s[1] = dkt[:, TK:].astype(low_type)
    for k in range(2):
        put("dk", 2, k, dks_s.at[k], dks_r.at[k], sib)

    for j in range(1, CN):
        got("pkc", CN, j, pks.at[first + j], at_ctx(j))
        peak = jnp.maximum(peak, pks[first + j])
    peak_o[...] = peak

    def unnorm(grad_n, gain_row, normed, inverse):
        gain_grad = jnp.sum(grad_n * normed, axis=0, keepdims=True)
        e = grad_n * gain_row
        return (inverse * (e - normed * head_mean(e * normed))).astype(low_type), gain_grad

    def share_grad(n, full):
        full = full.reshape(ZN, 2, HR, 2 * HW)
        low_full = full.astype(low_type)
        for k in range(2):
            @pl.when(o_i == k)
            def _():
                qsib_s[n] = low_full[:, k]

            @pl.when(t_i == k)
            def _():
                qown[n] = full[:, k]

        put("qg", 2, n, qsib_s.at[n], qsib_r.at[n], sib)

    def reduce_grad(n):
        got("qg", 2, n, qsib_r.at[n], sib)
        total = qown[n] + qsib_r[n].astype(full_type)
        qown[n] = total
        qz_s[n] = total.astype(low_type)
        for j in range(1, ZN):
            put("qz%d" % n, ZN, j, qz_s.at[n, flip(s_i, j, ZN)], qz_r.at[n, j], at_z(j))

    grad_raw, q_gain_row = unnorm(dqb[...].reshape(TK, HW), qgrow, nq[...], sq[...])
    dqr[...] = grad_raw
    empty = jnp.zeros((TK, HW), low_type)
    share_grad(1, (
        dot(h1_t[...], jnp.concatenate([dqr[...], empty], axis=1))
        + dot(gbg[...].reshape(TK, D), jnp.concatenate([empty, attq[...].reshape(TK, HW)], axis=1), TN)
    ))
    got("dk", 2, 0, dks_r.at[0], sib)
    grad_v = (dvt[:, :TK] + dks_r[0].astype(full_type)).T.astype(low_type)
    got("dk", 2, 1, dks_r.at[1], sib)
    grad_k = (dkt[:, :TK] + dks_r[1].astype(full_type)).T
    grad_raw, k_gain_row = unnorm(grad_k, kgrow, nk[...], sk[...])
    dkv[...] = jnp.concatenate([grad_raw, grad_v], axis=1)
    share_grad(0, dot(h1_t[...], dkv[...]))
    reduce_grad(1)
    reduce_grad(0)

    ln1g = jnp.zeros((1, D), full_type)
    ln1b = jnp.zeros((1, D), full_type)
    for j in range(CN - 1, -1, -1):
        rows = slice(j * TB, (j + 1) * TB)
        part = dot(dqr[rows], wqb[...].reshape(D, HW), NT) + dot(dkv[rows], wkv[...].reshape(D, 2 * HW), NT)
        if j:
            g1s[j] = part.astype(low_type)
        else:
            g1own[...] = part
        if j == 3:
            send_halves("g1", g1s, g1r)
        ln1g = ln1g + jnp.sum(part * xh1[j], axis=0, keepdims=True)
        ln1b = ln1b + jnp.sum(part, axis=0, keepdims=True)
    rows_s[0] = jnp.zeros_like(rows_s[0])
    for k, row in enumerate((ln1g, ln1b, ln2g, ln2b)):
        rows_s[0, k:k + 1, :D] = row
    rows_s[0, 0:1, D:D + HW] = q_gain_row
    rows_s[0, 1:2, D:D + HW] = k_gain_row
    put("rt", 1, 0, rows_s.at[0], rows_r.at[0], sib)
    share_mlp(0, upo)
    add_halves("g1", g1s, g1r)
    share_mlp(1, dno)
    got("rt", 1, 0, rows_r.at[0], sib)
    rows_s[1] = rows_s[0] + rows_r[0]
    for j in range(1, ZN):
        put("rz", ZN, j, rows_s.at[1], rows_r.at[j], at_z(j))

    total = boown[...]
    for j in (1, 2):
        got("bo", 5, j, bor.at[j], at_ctx(j))
        total = total + bor[j].astype(full_type)
    own_rows = pl.ds(t_i * TB, TB)
    obuf[0] = total.astype(low_type)
    put("ob", 2, 0, obuf.at[0], bo_o.at[own_rows], sib)
    pltpu.make_async_copy(obuf.at[0], bo_o.at[own_rows], lsem.at[10]).start()

    def share_fin(n):
        total = qown[n, s_i]
        for j in range(1, ZN):
            got("qz%d" % n, ZN, j, qz_r.at[n, j], at_z(j))
            total = total + qz_r[n, j].astype(full_type)
        qfin[n] = total.astype(low_type)
        slot = spot("qcr%d" % n, 2 * half_chips) + place * 2 + t_i
        for j in range(1, CN):
            pltpu.make_async_remote_copy(
                src_ref=qfin.at[n], dst_ref=qkvo.at[place, t_i, n],
                send_sem=ssem.at[spot("qcs%d" % n, CN) + j], recv_sem=rsem.at[slot],
                device_id=(s_i, flip(c_i, j, CN), tstar), device_id_type=MESH,
            ).start()

        @pl.when(t_i == tstar)
        def _():
            pltpu.make_async_copy(qfin.at[n], qkvo.at[place, t_i, n], lsem.at[12 + n]).start()

        @pl.when(t_i != tstar)
        def _():
            pltpu.make_async_remote_copy(
                src_ref=qfin.at[n], dst_ref=qkvo.at[place, t_i, n],
                send_sem=ssem.at[spot("qcs%d" % n, CN)], recv_sem=rsem.at[slot],
                device_id=sib, device_id_type=MESH,
            ).start()

    def pass_grad(k, out):
        for j in (1, 2):
            block = out.at[flip(c_i, j, CN)]
            got("gc%d" % k, 5, j, block, at_ctx(j))
            half = block.at[pl.ds((j - 1) * HR, HR)]
            put_as("gc%d" % k, 5, 2 + j, 2 + j, half, half, at_ctx(3 - j))

    share_fin(1)
    pass_grad(0, upo)

    xhat1, inv1 = norm_rows(xg[0].astype(full_type))
    grad_one = g1own[...]
    for j in (1, 2):
        got("g1", 5, j, g1r.at[j], at_ctx(j))
        grad_one = grad_one + g1r[j].astype(full_type)
    hat = grad_one * g1row
    grad_in = gres[...] + inv1 * (
        hat
        - jnp.sum(hat, axis=-1, keepdims=True) * inv_d
        - xhat1 * (jnp.sum(hat * xhat1, axis=-1, keepdims=True) * inv_d)
    )
    obuf[1] = grad_in.astype(low_type)
    put("ob", 2, 1, obuf.at[1], ig_o.at[own_rows], sib)
    pltpu.make_async_copy(obuf.at[1], ig_o.at[own_rows], lsem.at[11]).start()

    pass_grad(1, dno)
    rows_sum = rows_s[1]
    for j in range(1, ZN):
        got("rz", ZN, j, rows_r.at[j], at_z(j))
        rows_sum = rows_sum + rows_r[j]
    rows_s[2] = rows_sum
    for j in range(1, CN):
        put("rc", CN, j, rows_s.at[2], rows_r.at[ZN + j], at_ctx(j))
    qkr_o[c_i] = rows_sum[:, D:]

    share_fin(0)

    total = rows_sum[:, :D]
    for j in range(1, CN):
        got("rc", CN, j, rows_r.at[ZN + j], at_ctx(j))
        block = rows_r[ZN + j]
        total = total + block[:, :D]
        qkr_o[flip(c_i, j, CN)] = block[:, D:]
    lnr_o[...] = total

    for k, out in ((0, upo), (1, dno)):
        for j in (1, 2):
            half = out.at[flip(c_i, 3, CN), pl.ds((j - 1) * HR, HR)]
            got("gc%d" % k, 5, 2 + j, half, at_ctx(3 - j))
        pltpu.make_async_copy(gfin.at[k], out.at[c_i], lsem.at[8 + k]).wait()
    other_rows = pl.ds(o_i * TB, TB)
    for k, out in ((0, bo_o), (1, ig_o)):
        got("ob", 2, k, out.at[other_rows], sib)
        pltpu.make_async_copy(obuf.at[k], out.at[own_rows], lsem.at[10 + k]).wait()

    @pl.when(t_i == tstar)
    def _():
        for n in range(2):
            pltpu.make_async_copy(qfin.at[n], qkvo.at[place, t_i, n], lsem.at[12 + n]).wait()

    for p in range(half_chips):
        for a in range(2):
            @pl.when((t_i != tstar) | (place != p) | (t_i != a))
            def _():
                for n in range(2):
                    pltpu.make_async_remote_copy(
                        src_ref=qfin.at[n], dst_ref=qkvo.at[p, a, n],
                        send_sem=ssem.at[spot("qcs%d" % n, CN)],
                        recv_sem=rsem.at[spot("qcr%d" % n, 2 * half_chips) + p * 2 + a],
                        device_id=sib, device_id_type=MESH,
                    ).wait_recv()

    for j in range(1, CN):
        sent("x", CN, j, x_src, sib)
        sent("br", CN, j, brs.at[j], sib)
        sent("h2", CN, j, h2.at[0], sib)
        sent("g2", CN, j, g2s.at[j], sib)
        sent("pkc", CN, j, pks.at[first], sib)
        sent("rc", CN, j, rows_s.at[2], sib)
        for n in range(2):
            sent("qcs%d" % n, CN, j, qfin.at[n], sib)
    for j in range(1, ZN):
        sent("small", ZN, j, smalls.at[t_i, s_i], sib)
        sent("pkz", ZN, j, pks.at[2], sib)
        sent("rz", ZN, j, rows_s.at[1], sib)
        for n in range(2):
            sent("qz%d" % n, ZN, j, qz_s.at[n, 0], sib)
    for n in range(1, 5):
        for name, buf, half in (("ct", ctg, ctg), ("gb", gbg, gbg), ("bo", bos, bos), ("g1", g1s, g1s)):
            sent(name, 5, n, buf.at[1] if n < 3 else half.at[1, pl.ds(0, HB)], sib)
        for k, out in ((0, upo), (1, dno)):
            sent("gc%d" % k, 5, n, gfin.at[k] if n < 3 else gfin.at[k, pl.ds(0, HR)], sib)
    for name, buf in mlp_weights:
        sent(name, 5, 0, buf.at[t_i, s_i], sib)

        @pl.when(jnp.logical_not(outer))
        def _():
            for n in range(1, 5):
                sent(name, 5, n, buf.at[t_i, s_i], sib)

    for k in range(2):
        for n in (0, 2, 3):
            sent("gz%d" % k, 4, n, gz_s.at[k, 0], sib)
    sent("smallt", 1, 0, smalls.at[t_i], sib)
    sent("k", 1, 0, kall.at[0], sib)
    sent("v", 1, 0, vall.at[0], sib)
    sent("pkt", 1, 0, pks.at[0], sib)
    sent("wdt", 1, 0, wdt.at[t_i], sib)
    sent("wut", 1, 0, wup.at[t_i], sib)
    sent("rt", 1, 0, rows_s.at[0], sib)
    for k in range(2):
        sent("gs", 2, k, gsib_s.at[k], sib)
        sent("dk", 2, k, dks_s.at[k], sib)
        sent("ob", 2, k, obuf.at[k], sib)
    for n in range(2):
        sent("qg", 2, n, qsib_s.at[n], sib)

    @pl.when(t_i == tstar)
    def _():
        for name, buf in projections:
            for j in range(ZN):
                sent(name, ZN, j, buf.at[s_i], sib)
                if j:
                    sent("f" + name, ZN, j, buf.at[s_i], sib)

    @pl.when(t_i != tstar)
    def _():
        for n in range(2):
            sent("qcs%d" % n, CN, 0, qfin.at[n], sib)


SEMS = 127


def fused_call(sizes, *operands):
    CN, ZN, TB, D, HW, FS, R = sizes
    TK = CN * TB
    HR = R // 2
    half_chips = CN // 2
    heads = HW // 64
    lo, hi = low_type, full_type
    V = pltpu.VMEM
    any_spec = pl.BlockSpec(memory_space=pl.ANY)
    vm_spec = pl.BlockSpec(memory_space=pltpu.VMEM)
    out_shape = [
        jax.ShapeDtypeStruct((2 * TB, D), lo),
        jax.ShapeDtypeStruct((2 * TB, D), lo),
        jax.ShapeDtypeStruct((CN, R, FS), lo),
        jax.ShapeDtypeStruct((CN, R, FS), lo),
        jax.ShapeDtypeStruct((half_chips, 2, 2, HR, 2 * HW), lo),
        jax.ShapeDtypeStruct((8, D), hi),
        jax.ShapeDtypeStruct((CN, 8, 256), hi),
        jax.ShapeDtypeStruct((8, 128), hi),
    ]
    scratch = [
        V((CN, TB, D), lo), V((CN, TB, D), lo), V((2, ZN, 8, 256), hi),
        V((3, R, half_chips * HW), lo), V((R, half_chips * HW), lo),
        V((ZN, R, 2 * HW), lo), V((ZN, R, HW), lo), V((ZN, R, HW), lo), V((2, ZN, R, FS), lo), V((2, ZN, R, FS), lo),
        V((D, TK), lo), V((D, TK), lo), V((D, TK), lo),
        V((CN, TB, D), hi), V((CN, TB, D), lo),
        V((TK, HW), hi), V((TK, HW), hi), V((TK, HW), hi), V((TK, HW), hi),
        V((CN, TB, HW), lo), V((2, TK, HW), lo), V((2, TK, HW), lo),
        V((CN, heads * TB, 2 * TK), hi), V((heads * TB, 2 * TK), hi),
        V((CN, TB, HW), lo), V((CN, TB, D), lo), V((CN, TB, D), lo), V((2 + ZN + CN, 8, 128), hi),
        V((heads, 2 * TK), hi), V((heads * TB, 2 * TK), lo),
        V((CN, TB, D), lo), V((2, CN, TB, FS), hi), V((CN, TB, 2 * FS), lo), V((CN, TB, 2 * FS), lo),
        V((CN, TB, D), lo), V((CN, TB, D), lo), V((TB, D), hi),
        V((CN, TB, D), lo), V((CN, TB, D), lo), V((TB, D), hi),
        V((2, D, FS), lo), V((2, D, FS), lo), V((2, D, 2 * FS), hi), V((2, D, FS), hi),
        V((2, ZN, R, FS), lo), V((2, ZN, R, FS), lo), V((2, R, FS), lo),
        V((TB, D), hi), V((CN, TB, D), lo),
        V((CN, TB, HW), hi), V((HW, 2 * TK), hi), V((HW, 2 * TK), hi),
        V((2, HW, TK), lo), V((2, HW, TK), lo), V((TK, HW), lo), V((TK, 2 * HW), lo),
        V((CN, TB, D), lo), V((CN, TB, D), lo), V((TB, D), hi),
        V((2, ZN, HR, 2 * HW), lo), V((2, ZN, HR, 2 * HW), lo), V((2, ZN, HR, 2 * HW), hi),
        V((2, ZN, HR, 2 * HW), lo), V((2, ZN, HR, 2 * HW), lo), V((2, HR, 2 * HW), lo),
        V((3, 8, D + 256), hi), V((ZN + CN, 8, D + 256), hi), V((2, TB, D), lo),
        pltpu.SemaphoreType.DMA((16,)), pltpu.SemaphoreType.DMA((SEMS,)), pltpu.SemaphoreType.DMA((SEMS,)),
    ]
    return pl.pallas_call(
        functools.partial(fused_kernel, sizes),
        out_shape=out_shape,
        in_specs=[any_spec] * 2 + [vm_spec] * 6 + [any_spec] * 6,
        out_specs=[any_spec] * 5 + [vm_spec] * 3,
        scratch_shapes=scratch,
        compiler_params=pltpu.CompilerParams(
            collective_id=0, has_side_effects=True, vmem_limit_bytes=56 * 2**20
        ),
    )(*operands)


def finish_kernel(
    sizes,
    bo, ig, up_h, dn_h, qkvo_h, lnr_h, qkr_h, peak_h, wq_h, wk_h,
    bo_o, ig_o, l1g, l1b, l2g, l2b, qg_o, kg_o, gq_o, gk_o, gv_o, go_o, gu_o, gd_o, cq_o, ck_o,
    upo, dno, qkvo, lnr, qkr, peak, wq, wk, bov, igv, gq, gk, gv, go, gu, gd, cq, ck, isem, osem,
):
    CN, ZN, TB, D, HW, FS, R = sizes
    half_chips = CN // 2
    s_i, t_i = lax.axis_index("shard"), lax.axis_index("tp")
    ins = [
        pltpu.make_async_copy(src, dst, isem.at[n])
        for n, (src, dst) in enumerate((
            (qkvo_h, qkvo), (up_h, upo), (dn_h, dno), (peak_h, peak), (wq_h, wq), (wk_h, wk),
            (lnr_h, lnr), (qkr_h, qkr), (bo, bov), (ig, igv),
        ))
    ]
    for n in (1, 2, 0, 8, 9, 3, 4, 5, 6, 7):
        ins[n].start()
    outs = []

    def leave(src, dst):
        copy = pltpu.make_async_copy(src, dst, osem.at[len(outs)])
        copy.start()
        outs.append(copy)

    for n, grads, stage, out in ((1, upo, gu, gu_o), (2, dno, gd, gd_o)):
        ins[n].wait()
        for c in range(CN):
            stage[:, c * FS:(c + 1) * FS] = grads[c].astype(full_type)
        leave(stage, out)
    for n, stage, out in ((8, bov, bo_o), (9, igv, ig_o)):
        ins[n].wait()
        leave(stage, out)
    ins[0].wait()
    for n, first, stage, out in ((1, 0, gq, gq_o), (0, 0, gk, gk_o), (0, HW, gv, gv_o), (1, HW, go, go_o)):
        for a in range(2):
            parts = [qkvo[p, a, n][:, first:first + HW] for p in range(half_chips)]
            stage[a * (R // 2):(a + 1) * (R // 2)] = jnp.concatenate(parts, axis=1).astype(full_type)
        leave(stage, out)
    heads = HW // 64
    for n in (3, 4, 5):
        ins[n].wait()
    factor = jnp.sqrt(clip_level / jnp.maximum(peak[0:1], clip_level))
    here = half_chips * heads
    lanes = lax.broadcasted_iota(jnp.int32, (1, here * 64), 1) // 64
    ids = lax.broadcasted_iota(jnp.int32, (1, 128), 1)
    columns = jnp.ones((1, here * 64), full_type)
    for h in range(here):
        one = jnp.sum(jnp.where(ids == t_i * here + h, factor, 0.0), axis=-1, keepdims=True)
        columns = jnp.where(lanes == h, one, columns)
    for weights, stage, out in ((wq, cq, cq_o), (wk, ck, ck_o)):
        stage[...] = (weights[...].astype(full_type) * columns).astype(low_type)
        leave(stage, out)
    ins[6].wait()
    ins[7].wait()
    rows = jnp.zeros((8, R), full_type)
    for z in range(ZN):
        rows = jnp.where(s_i == z, lnr[:, z * R:(z + 1) * R], rows)
    for k, out in enumerate((l1g, l1b, l2g, l2b)):
        out[...] = rows[k:k + 1].reshape(R)
    piece = qg_o.shape[1]
    for p in range(half_chips):
        chip = qkr[t_i * half_chips + p]
        for h in range(heads):
            for z in range(ZN):
                at = h * 64 + z * piece

                @pl.when(s_i == z)
                def _():
                    qg_o[p * heads + h:p * heads + h + 1] = chip[0:1, at:at + piece]
                    kg_o[p * heads + h:p * heads + h + 1] = chip[1:2, at:at + piece]
    for copy in outs:
        copy.wait()


def fused_layer(
    images, cotangent, ln1_gain, ln1_bias, ln2_gain, ln2_bias, q_gain, k_gain,
    w_query, w_key, w_value, w_out, w_up, w_down,
):
    CN, ZN = lax.axis_size("ctx"), lax.axis_size("shard")
    TB = images.shape[1] // 2
    D = images.shape[2]
    R = w_query.shape[0]
    HW = w_query.shape[1] // (CN // 2)
    FS = w_up.shape[1] // CN
    sizes = (CN, ZN, TB, D, HW, FS, R)
    results = fused_call(
        sizes, images, cotangent, ln1_gain, ln1_bias, ln2_gain, ln2_bias, q_gain, k_gain,
        w_query, w_key, w_value, w_out.T, w_up, w_down.T,
    )
    row = jax.ShapeDtypeStruct((R,), full_type)
    gain = jax.ShapeDtypeStruct(q_gain.shape, full_type)
    square = jax.ShapeDtypeStruct(w_query.shape, full_type)
    wide = jax.ShapeDtypeStruct(w_up.shape, full_type)
    tokens = jax.ShapeDtypeStruct(images.shape[1:], low_type)
    clipped = jax.ShapeDtypeStruct(w_query.shape, low_type)
    lo, hi = low_type, full_type
    V = pltpu.VMEM
    any_spec = pl.BlockSpec(memory_space=pl.ANY)
    vm_spec = pl.BlockSpec(memory_space=pltpu.VMEM)
    out = pl.pallas_call(
        functools.partial(finish_kernel, sizes),
        out_shape=[tokens] * 2 + [row] * 4 + [gain] * 2 + [square] * 4 + [wide] * 2 + [clipped] * 2,
        in_specs=[any_spec] * 10,
        out_specs=[any_spec] * 2 + [vm_spec] * 6 + [any_spec] * 8,
        scratch_shapes=[
            V((CN, R, FS), lo), V((CN, R, FS), lo), V((CN // 2, 2, 2, R // 2, 2 * HW), lo), V((8, D), hi),
            V((CN, 8, 256), hi), V((8, 128), hi), V(w_query.shape, lo), V(w_query.shape, lo),
            V(images.shape[1:], lo), V(images.shape[1:], lo),
        ]
        + [V(w_query.shape, hi)] * 4 + [V(w_up.shape, hi)] * 2 + [V(w_query.shape, lo)] * 2
        + [pltpu.SemaphoreType.DMA((10,)), pltpu.SemaphoreType.DMA((10,))],
        compiler_params=pltpu.CompilerParams(vmem_limit_bytes=60 * 2**20),
    )(*results, w_query, w_key)
    out = list(out)
    out[0], out[1] = out[0].reshape(images.shape), out[1].reshape(images.shape)
    out[11], out[13] = out[11].T, out[13].T
    return tuple(out)


def on_device(images, cotangent, ln1_gain, ln1_bias, ln2_gain, ln2_bias, q_gain, k_gain, *weights):
    fused = fits_fused(images, weights[0], weights[4], q_gain)
    layer = fused_layer if fused else general_layer
    return layer(images, cotangent, ln1_gain, ln1_bias, ln2_gain, ln2_bias, q_gain, k_gain, *weights)


def solution(mesh):
    return jax.shard_map(
        on_device,
        mesh=mesh,
        in_specs=(
            P("shard", "ctx", None),
            P("shard", "ctx", None),
            P("shard"),
            P("shard"),
            P("shard"),
            P("shard"),
            P("tp", "shard"),
            P("tp", "shard"),
            P("shard", "tp"),
            P("shard", "tp"),
            P("shard", "tp"),
            P("tp", "shard"),
            P("shard", "tp"),
            P("tp", "shard"),
        ),
        out_specs=(
            P("shard", "ctx", None),
            P("shard", "ctx", None),
            P("shard"),
            P("shard"),
            P("shard"),
            P("shard"),
            P("tp", "shard"),
            P("tp", "shard"),
            P("shard", "tp"),
            P("shard", "tp"),
            P("shard", "tp"),
            P("tp", "shard"),
            P("shard", "tp"),
            P("tp", "shard"),
            P("shard", "tp"),
            P("shard", "tp"),
        ),
        check_vma=False,
    )
```

```python
import functools
import jax
import jax.numpy as jnp
from jax import lax
from jax.experimental import pallas as pl
from jax.experimental.pallas import tpu as pltpu
from jax.sharding import PartitionSpec as P

norm_eps = 1e-06
clip_level = 0.5


def matmul(left, right):
    return jnp.dot(left, right, preferred_element_type=jnp.float32)


def norm_parts(values):
    center = values - jnp.mean(values, axis=-1, keepdims=True)
    inverse = lax.rsqrt(jnp.mean(center * center, axis=-1, keepdims=True) + norm_eps)
    return (center * inverse, inverse)


def norm_back(grad_hat, normed, inverse):
    return inverse * (
        grad_hat
        - jnp.mean(grad_hat, axis=-1, keepdims=True)
        - normed * jnp.mean(grad_hat * normed, axis=-1, keepdims=True)
    )


def head_scale(values, gain):
    inverse = lax.rsqrt(jnp.mean(values * values, axis=-1, keepdims=True) + norm_eps)
    return values * inverse * gain


def gelu_exact(values):
    return jax.nn.gelu(values, approximate=False)


def general_layer(
    images,
    cotangent,
    ln1_gain,
    ln1_bias,
    ln2_gain,
    ln2_bias,
    q_gain,
    k_gain,
    w_query,
    w_key,
    w_value,
    w_out,
    w_up,
    w_down,
):
    (
        full_query,
        full_key,
        full_value,
        full_up,
        full_out,
        full_down,
        gain_low_one,
        shift_low_one,
        gain_low_two,
        shift_low_two,
        query_gain_low,
        key_gain_low,
    ) = (
        lax.all_gather(w_query, "shard", axis=0, tiled=True),
        lax.all_gather(w_key, "shard", axis=0, tiled=True),
        lax.all_gather(w_value, "shard", axis=0, tiled=True),
        lax.all_gather(w_up, "shard", axis=0, tiled=True),
        lax.all_gather(w_out, "shard", axis=1, tiled=True),
        lax.all_gather(w_down, "shard", axis=1, tiled=True),
        lax.all_gather(ln1_gain, "shard", axis=0, tiled=True),
        lax.all_gather(ln1_bias, "shard", axis=0, tiled=True),
        lax.all_gather(ln2_gain, "shard", axis=0, tiled=True),
        lax.all_gather(ln2_bias, "shard", axis=0, tiled=True),
        lax.all_gather(q_gain, "shard", axis=1, tiled=True),
        lax.all_gather(k_gain, "shard", axis=1, tiled=True),
    )
    gain_one = gain_low_one.astype(jnp.float32)
    shift_one = shift_low_one.astype(jnp.float32)
    gain_two = gain_low_two.astype(jnp.float32)
    shift_two = shift_low_two.astype(jnp.float32)
    query_gain = query_gain_low.astype(jnp.float32)
    key_gain = key_gain_low.astype(jnp.float32)
    count_img, local_len, width = images.shape
    tokens = count_img * local_len
    heads_here, head_size = query_gain.shape
    local_width = heads_here * head_size
    full_len = local_len * lax.axis_size("ctx")
    group = 1
    groups = count_img // group
    scale = head_size ** (-0.5)
    flat = images.reshape(tokens, width).astype(jnp.float32)
    normed_one, inverse_one = norm_parts(flat)
    hidden_one = (normed_one * gain_one + shift_one).astype(jnp.bfloat16)
    query_raw = matmul(hidden_one, full_query).reshape(tokens, heads_here, head_size)
    key_raw = matmul(hidden_one, full_key).reshape(tokens, heads_here, head_size)
    query_norm = head_scale(query_raw, query_gain).astype(jnp.bfloat16)
    key_norm = head_scale(key_raw, key_gain).astype(jnp.bfloat16)
    value_low = matmul(hidden_one, full_value).astype(jnp.bfloat16)
    key_all, value_all = (
        lax.all_gather(
            key_norm.reshape(count_img, local_len, local_width), "ctx", axis=1, tiled=True
        ),
        lax.all_gather(
            value_low.reshape(count_img, local_len, local_width), "ctx", axis=1, tiled=True
        ),
    )
    query_grp = query_norm.reshape(groups, group, local_len, heads_here, head_size)
    key_grp = key_all.reshape(groups, group, full_len, heads_here, head_size)
    value_grp = value_all.reshape(groups, group, full_len, heads_here, head_size)

    def attend(pieces):
        query_blk, key_blk, value_blk = pieces
        scores = (
            jnp.einsum("gqhd,gkhd->ghqk", query_blk, key_blk, preferred_element_type=jnp.float32)
            * scale
        )
        top = jnp.max(scores, axis=-1, keepdims=True)
        expo = jnp.exp(scores - top)
        total = jnp.sum(expo, axis=-1, keepdims=True)
        probs = (expo / total).astype(jnp.bfloat16)
        mixed_blk = jnp.einsum(
            "ghqk,gkhd->gqhd", probs, value_blk, preferred_element_type=jnp.float32
        )
        return (mixed_blk, top + jnp.log(total), jnp.max(top, axis=(0, 2, 3)))

    mixed, log_total, group_peaks = lax.map(attend, (query_grp, key_grp, value_grp))
    local_peak = jnp.max(group_peaks, axis=0)
    peak_all = lax.pmax(local_peak, ("shard", "ctx"))
    attended = mixed.reshape(tokens, local_width).astype(jnp.bfloat16)
    branch_attn = lax.psum(matmul(attended, full_out), "tp")
    resid = flat + branch_attn
    normed_two, inverse_two = norm_parts(resid)
    hidden_two = (normed_two * gain_two + shift_two).astype(jnp.bfloat16)
    up_raw = matmul(hidden_two, full_up)
    active = gelu_exact(up_raw).astype(jnp.bfloat16)
    branch_mlp = lax.psum(matmul(active, full_down).astype(jnp.bfloat16), "tp").astype(jnp.float32)
    block_out = (resid + branch_mlp).astype(jnp.bfloat16).reshape(images.shape)
    grad_out = cotangent.reshape(tokens, width).astype(jnp.float32)
    grad_down = cotangent.reshape(tokens, width)
    grad_w_down = jnp.dot(active.T, grad_down, preferred_element_type=jnp.float32)
    grad_active = matmul(grad_down, full_down.T)
    unused_up, gelu_pull = jax.vjp(gelu_exact, up_raw)
    grad_up = gelu_pull(grad_active)[0].astype(jnp.bfloat16)
    grad_w_up = jnp.dot(hidden_two.T, grad_up, preferred_element_type=jnp.float32)
    grad_two = lax.psum(matmul(grad_up, full_up.T), "tp")
    grad_gain_two = jnp.sum(grad_two * normed_two, axis=0)
    grad_shift_two = jnp.sum(grad_two, axis=0)
    grad_resid = grad_out + norm_back(grad_two * gain_two, normed_two, inverse_two)
    grad_branch = grad_resid.astype(jnp.bfloat16)
    grad_w_out = jnp.dot(attended.T, grad_branch, preferred_element_type=jnp.float32)
    grad_mixed = matmul(grad_branch, full_out.T).astype(jnp.bfloat16)
    grad_grp = grad_mixed.reshape(groups, group, local_len, heads_here, head_size)

    def attend_back(pieces):
        query_blk, key_blk, value_blk, log_blk, grad_blk = pieces
        scores = (
            jnp.einsum("gqhd,gkhd->ghqk", query_blk, key_blk, preferred_element_type=jnp.float32)
            * scale
        )
        probs = jnp.exp(scores - log_blk)
        grad_probs = jnp.einsum(
            "gqhd,gkhd->ghqk", grad_blk, value_blk, preferred_element_type=jnp.float32
        )
        grad_scores = (
            probs * (grad_probs - jnp.sum(probs * grad_probs, axis=-1, keepdims=True))
        ).astype(jnp.bfloat16)
        grad_val = jnp.einsum(
            "ghqk,gqhd->gkhd",
            probs.astype(jnp.bfloat16),
            grad_blk,
            preferred_element_type=jnp.float32,
        )
        grad_qry = (
            jnp.einsum("ghqk,gkhd->gqhd", grad_scores, key_blk, preferred_element_type=jnp.float32)
            * scale
        )
        grad_kys = (
            jnp.einsum(
                "ghqk,gqhd->gkhd", grad_scores, query_blk, preferred_element_type=jnp.float32
            )
            * scale
        )
        return (grad_qry, grad_kys, grad_val)

    grad_query_n, grad_key_full, grad_value_full = lax.map(
        attend_back, (query_grp, key_grp, value_grp, log_total, grad_grp)
    )
    grad_key_n, grad_value_n = (
        lax.psum_scatter(
            grad_key_full.reshape(count_img, full_len, local_width),
            "ctx",
            scatter_dimension=1,
            tiled=True,
        ),
        lax.psum_scatter(
            grad_value_full.reshape(count_img, full_len, local_width),
            "ctx",
            scatter_dimension=1,
            tiled=True,
        ),
    )
    unused_query, query_pull = jax.vjp(head_scale, query_raw, query_gain)
    grad_query_raw, grad_query_gain = query_pull(
        grad_query_n.reshape(tokens, heads_here, head_size)
    )
    unused_key, key_pull = jax.vjp(head_scale, key_raw, key_gain)
    grad_key_raw, grad_key_gain = key_pull(grad_key_n.reshape(tokens, heads_here, head_size))
    grad_query_low = grad_query_raw.reshape(tokens, local_width).astype(jnp.bfloat16)
    grad_key_low = grad_key_raw.reshape(tokens, local_width).astype(jnp.bfloat16)
    grad_value_low = grad_value_n.reshape(tokens, local_width).astype(jnp.bfloat16)
    grad_w_query = jnp.dot(hidden_one.T, grad_query_low, preferred_element_type=jnp.float32)
    grad_w_key = jnp.dot(hidden_one.T, grad_key_low, preferred_element_type=jnp.float32)
    grad_w_value = jnp.dot(hidden_one.T, grad_value_low, preferred_element_type=jnp.float32)
    grad_one_part = (
        matmul(grad_query_low, full_query.T)
        + matmul(grad_key_low, full_key.T)
        + matmul(grad_value_low, full_value.T)
    )
    grad_one = lax.psum(grad_one_part, "tp")
    grad_gain_one = jnp.sum(grad_one * normed_one, axis=0)
    grad_shift_one = jnp.sum(grad_one, axis=0)
    input_grad = (
        (grad_resid + norm_back(grad_one * gain_one, normed_one, inverse_one))
        .astype(jnp.bfloat16)
        .reshape(images.shape)
    )
    (
        sum_query,
        sum_key,
        sum_value,
        sum_up,
        sum_out,
        sum_down,
        sum_gain_one,
        sum_shift_one,
        sum_gain_two,
        sum_shift_two,
        sum_qgain,
        sum_kgain,
    ) = lax.psum(
        (
            grad_w_query,
            grad_w_key,
            grad_w_value,
            grad_w_up,
            grad_w_out,
            grad_w_down,
            grad_gain_one,
            grad_shift_one,
            grad_gain_two,
            grad_shift_two,
            grad_query_gain,
            grad_key_gain,
        ),
        "ctx",
    )
    (
        part_query,
        part_key,
        part_value,
        part_up,
        part_out,
        part_down,
        part_gain_one,
        part_shift_one,
        part_gain_two,
        part_shift_two,
        part_qgain,
        part_kgain,
    ) = (
        lax.psum_scatter(sum_query, "shard", scatter_dimension=0, tiled=True),
        lax.psum_scatter(sum_key, "shard", scatter_dimension=0, tiled=True),
        lax.psum_scatter(sum_value, "shard", scatter_dimension=0, tiled=True),
        lax.psum_scatter(sum_up, "shard", scatter_dimension=0, tiled=True),
        lax.psum_scatter(sum_out, "shard", scatter_dimension=1, tiled=True),
        lax.psum_scatter(sum_down, "shard", scatter_dimension=1, tiled=True),
        lax.psum_scatter(sum_gain_one, "shard", scatter_dimension=0, tiled=True),
        lax.psum_scatter(sum_shift_one, "shard", scatter_dimension=0, tiled=True),
        lax.psum_scatter(sum_gain_two, "shard", scatter_dimension=0, tiled=True),
        lax.psum_scatter(sum_shift_two, "shard", scatter_dimension=0, tiled=True),
        lax.psum_scatter(sum_qgain, "shard", scatter_dimension=1, tiled=True),
        lax.psum_scatter(sum_kgain, "shard", scatter_dimension=1, tiled=True),
    )
    factor = jnp.sqrt(clip_level / jnp.maximum(peak_all, clip_level))
    columns = jnp.repeat(factor, head_size)
    query_clip = (w_query.astype(jnp.float32) * columns).astype(jnp.bfloat16)
    key_clip = (w_key.astype(jnp.float32) * columns).astype(jnp.bfloat16)
    return (
        block_out,
        input_grad,
        part_gain_one,
        part_shift_one,
        part_gain_two,
        part_shift_two,
        part_qgain,
        part_kgain,
        part_query,
        part_key,
        part_value,
        part_out,
        part_up,
        part_down,
        query_clip,
        key_clip,
    )


MESH = pl.DeviceIdType.MESH
NN = (((1,), (0,)), ((), ()))
NT = (((1,), (1,)), ((), ()))
TN = (((0,), (0,)), ((), ()))
low_type = jnp.bfloat16
full_type = jnp.float32


def dot(left, right, dims=NN):
    return lax.dot_general(left, right, dims, preferred_element_type=full_type)


def flip(place, bits, count):
    result = 0
    unit = 1
    while unit < count:
        result = result + ((place // unit + bits // unit) % 2) * unit
        unit *= 2
    return result


def fits_fused(images, w_query, w_up, q_gain):
    count_img, local_len, width = images.shape
    ctx, shard, tp = lax.axis_size("ctx"), lax.axis_size("shard"), lax.axis_size("tp")
    rows = w_query.shape[0]
    return (
        count_img == 1
        and tp == 2
        and ctx == 4
        and shard == 4
        and rows % (16 * ctx) == 0
        and local_len % 32 == 0
        and q_gain.shape[0] % 2 == 0
        and w_up.shape[1] % (128 * ctx) == 0
    )


def fused_kernel(
    sizes,
    img_h, cot_h, g1_a, b1_a, g2_a, b2_a, qg_a, kg_a, wq_h, wk_h, wv_h, wo_h, wup_h, wdn_h,
    bo_o, ig_o, upo, dno, qkvo, lnr_o, qkr_o, peak_o,
    xg, ctg, smalls, wl, wol, wkv, wqp, wop, wqb, wob, wup, wdt, h1_t, h2_t, ct_t,
    xh1, h1, nq, nk, sq, sk, qs, kall, vall, pst, sbuf, attq, brs, brr, pks,
    ptop, dsb,
    h2, ga, act, gu, g2s, g2r, g2own, bos, bor, boown,
    gsib_s, gsib_r, gown, gkeep, gz_s, gz_r, gfin,
    gres, gbg, dqb, dkt, dvt, dks_s, dks_r, dqr, dkv,
    g1s, g1r, g1own, qsib_s, qsib_r, qown, qz_s, qz_r, qfin,
    rows_s, rows_r, obuf, g1_h, b1_h, g2_h, b2_h, qg_h, kg_h, lnr_v, qkr_v, peak_v,
    lsem, ssem, rsem,
):
    CN, ZN, TB, D, HW, FS, R = sizes
    HR = R // 2
    s_i, c_i, t_i = lax.axis_index("shard"), lax.axis_index("ctx"), lax.axis_index("tp")
    o_i = 1 - t_i
    half_chips = CN // 2
    tstar = c_i // half_chips
    place = c_i % half_chips
    TK = CN * TB
    inv_d = 1.0 / D

    def at_ctx(j):
        return (s_i, flip(c_i, j, CN), t_i)

    def at_z(j):
        return (flip(s_i, j, ZN), c_i, t_i)

    sib = (s_i, c_i, o_i)

    outer = (s_i == 0) | (s_i == ZN - 1)
    pair = flip(s_i, 1, ZN)
    far_in = flip(s_i, 3, ZN) * (1 - outer) + flip(s_i, 2, ZN) * outer
    far_out = flip(s_i, 2, ZN) * (1 - outer) + flip(s_i, 3, ZN) * outer

    def plane(z):
        return (z, c_i, t_i)

    spots = {}
    from_one = ("x", "small", "fwkv", "fwq", "fwo", "br", "h2", "g2", "qz0", "qz1", "rz", "pkz", "rc", "pkc",
                "ct", "gb", "bo", "g1", "gc0", "gc1")

    def spot(name, count):
        if name not in spots:
            first = sum(n for _, n in spots.values())
            skip = 1 if name in from_one else 0
            spots[name] = (first - skip, count - skip)
        return spots[name][0]

    def put(name, count, j, src, dst, dev):
        base = spot(name, count)
        pltpu.make_async_remote_copy(
            src_ref=src, dst_ref=dst, send_sem=ssem.at[base + j], recv_sem=rsem.at[base + j],
            device_id=dev, device_id_type=MESH,
        ).start()

    def put_as(name, count, send, recv, src, dst, dev):
        base = spot(name, count)
        pltpu.make_async_remote_copy(
            src_ref=src, dst_ref=dst, send_sem=ssem.at[base + send], recv_sem=rsem.at[base + recv],
            device_id=dev, device_id_type=MESH,
        ).start()

    def got(name, count, j, dst, dev):
        base = spot(name, count)
        pltpu.make_async_remote_copy(
            src_ref=dst, dst_ref=dst, send_sem=ssem.at[base + j], recv_sem=rsem.at[base + j],
            device_id=dev, device_id_type=MESH,
        ).wait_recv()

    def sent(name, count, j, src, dev):
        base = spot(name, count)
        pltpu.make_async_remote_copy(
            src_ref=src, dst_ref=src, send_sem=ssem.at[base + j], recv_sem=rsem.at[base + j],
            device_id=dev, device_id_type=MESH,
        ).wait_send()

    x_src = img_h.at[0, pl.ds(t_i * TB, TB)]
    c_src = cot_h.at[0, pl.ds(t_i * TB, TB)]
    locals_ = [
        pltpu.make_async_copy(wk_h, wl.at[1], lsem.at[0]),
        pltpu.make_async_copy(wv_h, wl.at[2], lsem.at[1]),
        pltpu.make_async_copy(wq_h, wl.at[0], lsem.at[2]),
        pltpu.make_async_copy(x_src, xg.at[0], lsem.at[3]),
        pltpu.make_async_copy(wo_h, wol, lsem.at[4]),
        pltpu.make_async_copy(wdn_h.at[:, pl.ds(c_i * FS, FS)], wdt.at[t_i, s_i], lsem.at[5]),
        pltpu.make_async_copy(wup_h.at[:, pl.ds(c_i * FS, FS)], wup.at[t_i, s_i], lsem.at[6]),
        pltpu.make_async_copy(c_src, ctg.at[0], lsem.at[7]),
    ]
    gains = [
        pltpu.make_async_copy(src, dst, lsem.at[16 + n])
        for n, (src, dst) in enumerate((
            (g1_a, g1_h), (b1_a, b1_h), (g2_a, g2_h), (b2_a, b2_h), (qg_a, qg_h), (kg_a, kg_h),
        ))
    ]
    for copy in gains + locals_:
        copy.start()

    barrier = pltpu.get_barrier_semaphore()
    greet = [at_ctx(j) for j in range(1, CN)] + [at_z(j) for j in range(1, ZN)] + [sib]
    for dev in greet:
        pl.semaphore_signal(barrier, inc=1, device_id=dev, device_id_type=MESH)

    for copy in gains:
        copy.wait()
    smalls[t_i, s_i] = jnp.zeros((8, 256), full_type)
    for k, ref in enumerate((g1_h, b1_h, g2_h, b2_h)):
        smalls[t_i, s_i, k:k + 1, :R] = ref[...].astype(full_type).reshape(1, R)
    heads = HW // 64
    piece = qg_h.shape[1]
    lane_of = lax.broadcasted_iota(jnp.int32, (piece, HW), 1)
    spread = (
        (lane_of % piece == lax.broadcasted_iota(jnp.int32, (piece, HW), 0)) & ((lane_of % 64) // piece == s_i)
    ).astype(full_type).astype(low_type)
    head_of = lax.broadcasted_iota(jnp.int32, (qg_h.shape[0], HW), 0)
    wanted = head_of == place * heads + lax.broadcasted_iota(jnp.int32, (qg_h.shape[0], HW), 1) // 64
    wanted = wanted & (t_i == tstar)
    for k, ref in ((4, qg_h), (5, kg_h)):
        row = jnp.sum(jnp.where(wanted, dot(ref[...], spread), 0.0), axis=0, keepdims=True)
        smalls[t_i, s_i, k:k + 1, :HW] = row

    pl.semaphore_wait(barrier, len(greet))

    for j in range(1, CN):
        put("x", CN, j, x_src, xg.at[j], at_ctx(j))
    for j in range(1, ZN):
        put("small", ZN, j, smalls.at[t_i, s_i], smalls.at[t_i, s_i], at_z(j))

    def picker(at, lanes, offset):
        rows = lax.broadcasted_iota(jnp.int32, (half_chips * HW, lanes), 0)
        cols = lax.broadcasted_iota(jnp.int32, (half_chips * HW, lanes), 1) - offset
        return ((rows == cols + at * HW) & (cols >= 0) & (cols < HW)).astype(full_type).astype(low_type)

    projections = (("wkv", wkv), ("wq", wqp), ("wo", wop))

    def send_projection(name, buf):
        for j in range(1, ZN):
            put(name, ZN, j, buf.at[s_i], buf.at[s_i], at_z(j))
        put(name, ZN, 0, buf.at[s_i], buf.at[s_i], sib)

    locals_[4].wait()

    @pl.when(t_i == tstar)
    def _():
        for n in range(3):
            locals_[n].wait()
        wkv[s_i] = (
            dot(wl[1], picker(place, 2 * HW, 0)) + dot(wl[2], picker(place, 2 * HW, HW))
        ).astype(low_type)
        for source, packed in ((wl.at[0], wqp), (wol, wop)):
            packed[s_i] = (
                dot(source[:HR], picker(place, 2 * HW, 0)) + dot(source[HR:], picker(place, 2 * HW, HW))
            ).astype(low_type)
        send_projection(*projections[0])

    @pl.when(t_i != tstar)
    def _():
        for n in range(3):
            locals_[n].wait()

    for j in range(1, ZN):
        got("small", ZN, j, smalls.at[t_i, flip(s_i, j, ZN)], at_z(j))
    put("smallt", 1, 0, smalls.at[t_i], smalls.at[t_i], sib)

    locals_[3].wait()

    def norm_rows(values):
        mean = jnp.sum(values, axis=-1, keepdims=True) * inv_d
        center = values - mean
        inverse = lax.rsqrt(jnp.sum(center * center, axis=-1, keepdims=True) * inv_d + norm_eps)
        return center * inverse, inverse

    ln_rows = jnp.concatenate([smalls[t_i, k][:, :R] for k in range(ZN)], axis=1)
    g1row, b1row, g2row, b2row = (ln_rows[k:k + 1] for k in range(4))

    def first_norm(j, _):
        @pl.when(j > 0)
        def _():
            got("x", CN, j, xg.at[j], at_ctx(j))

        for n in (1, 2):
            @pl.when((j == n) & (t_i == tstar))
            def _():
                send_projection(*projections[n])

        normed, _unused = norm_rows(xg[j].astype(full_type))
        xh1[j] = normed
        hidden = (normed * g1row + b1row).astype(low_type)
        h1[j] = hidden
        h1_t[:, pl.ds(pl.multiple_of(j * TB, TB), TB)] = hidden.T
        return 0

    HB = TB // 2

    def spread(name, src, dst_of):
        for j in (1, 2):
            put(name, 5, j, src, dst_of(j), at_ctx(j))

    def pass_on(name, buf):
        for j in (1, 2):
            got(name, 5, j, buf.at[j], at_ctx(j))
            half = pl.ds((j - 1) * HB, HB)
            put_as(name, 5, 2 + j, 2 + j, buf.at[j, half], buf.at[3, half], at_ctx(3 - j))

    def send_halves(name, src, land):
        for j in (1, 2):
            half = pl.ds((j - 1) * HB, HB)
            put_as(name, 5, 2 + j, 2 + j, src.at[3, half], land.at[3, half], at_ctx(j))

    def add_halves(name, src, land):
        for j in (1, 2):
            half = pl.ds((j - 1) * HB, HB)
            got(name, 5, 2 + j, land.at[3, half], at_ctx(j))
            src[3 - j, half] = (src[3 - j, half].astype(full_type) + land[3, half].astype(full_type)).astype(low_type)
        for j in (1, 2):
            put_as(name, 5, j, j, src.at[j], land.at[j], at_ctx(j))

    def have_rest(name, buf):
        for j in (1, 2):
            half = pl.ds((j - 1) * HB, HB)
            got(name, 5, 2 + j, buf.at[3, half], at_ctx(3 - j))

    spread("ct", c_src, lambda j: ctg.at[j])
    lax.fori_loop(0, CN, first_norm, 0)

    got("smallt", 1, 0, smalls.at[o_i], sib)
    head_rows = smalls[0, 0][4:6, :HW]
    for a in range(2):
        for k in range(ZN):
            if a or k:
                head_rows = head_rows + smalls[a, k][4:6, :HW]
    qgrow, kgrow = head_rows[0:1], head_rows[1:2]

    lane = lax.broadcasted_iota(jnp.int32, (1, HW), 1) // 64
    mask_f = [(lane == h).astype(full_type) for h in range(heads)]
    mask_b = [m.astype(low_type) for m in mask_f]
    same_head = (
        lax.broadcasted_iota(jnp.int32, (HW, HW), 0) // 64
        == lax.broadcasted_iota(jnp.int32, (HW, HW), 1) // 64
    ).astype(full_type).astype(low_type)

    def head_mean(values):
        high = values.astype(low_type)
        rest = (values - high.astype(full_type)).astype(low_type)
        return (dot(high, same_head) + dot(rest, same_head)) * (1.0 / 64)

    def weight_ready(name, buf):
        @pl.when(t_i != tstar)
        def _():
            got(name, ZN, 0, buf.at[s_i], sib)

        for j in range(1, ZN):
            block = buf.at[flip(s_i, j, ZN)]
            got(name, ZN, j, block, sib)

            @pl.when(t_i == tstar)
            def _():
                pltpu.make_async_remote_copy(
                    src_ref=block, dst_ref=block,
                    send_sem=ssem.at[spot("f" + name, ZN) + j], recv_sem=rsem.at[spot(name, ZN) + j],
                    device_id=sib, device_id_type=MESH,
                ).start()

    def unpack(packed, buf):
        for z in range(ZN):
            block = packed[z]
            buf[z, :HR] = block[:, :HW]
            buf[z, HR:] = block[:, HW:]

    h1_all = h1[...].reshape(TK, D)
    weight_ready(*projections[0])
    raw = dot(h1_all, wkv[...].reshape(D, 2 * HW))
    vall[0] = raw[:, HW:].astype(low_type)
    put("v", 1, 0, vall.at[0], vall.at[1], sib)
    raw = raw[:, :HW]
    inverse = lax.rsqrt(head_mean(raw * raw) + norm_eps)
    normed = raw * inverse
    nk[...] = normed
    sk[...] = inverse
    kall[0] = (normed * kgrow).astype(low_type)
    put("k", 1, 0, kall.at[0], kall.at[1], sib)
    weight_ready(*projections[1])
    unpack(wqp, wqb)
    mlp_weights = (("wd", wdt), ("wu", wup))

    def own_mlp(name, buf):
        block = buf.at[t_i, s_i]
        put_as(name, 5, 0, 0, block, block, plane(pair))

        @pl.when(jnp.logical_not(outer))
        def _():
            put_as(name, 5, 1, 1, block, block, plane(far_in))

    def pass_mlp(name, buf, stage):
        source, target = ((pair, far_in), (far_in, pair), (far_out, pair))[stage]
        recv = (2, 1, 2)[stage]

        @pl.when(jnp.logical_not(outer))
        def _():
            block = buf.at[t_i, source]
            got(name, 5, stage, block, plane(pair))
            put_as(name, 5, 2 + stage, recv, block, block, plane(target))

    def have_mlp(name, buf):
        @pl.when(outer)
        def _():
            for n, z in enumerate((pair, far_in, far_out)):
                got(name, 5, n, buf.at[t_i, z], plane(pair))

    locals_[5].wait()
    own_mlp(*mlp_weights[0])
    locals_[6].wait()
    own_mlp(*mlp_weights[1])
    raw = dot(h1_all, wqb[...].reshape(D, HW))
    inverse = lax.rsqrt(head_mean(raw * raw) + norm_eps)
    normed = raw * inverse
    nq[...] = normed
    sq[...] = inverse
    qs[...] = ((normed * qgrow).astype(low_type) * 0.125).astype(low_type).reshape(CN, TB, HW)

    got("k", 1, 0, kall.at[1], sib)
    got("v", 1, 0, vall.at[1], sib)

    def stacked(block):
        return jnp.concatenate([block * m for m in mask_b], axis=0)

    def folded(block):
        total = block[0:TB] * mask_f[0]
        for h in range(1, heads):
            total = total + block[h * TB:(h + 1) * TB] * mask_f[h]
        return total

    ptop[...] = jnp.full(ptop.shape, -3.0e38, full_type)

    def attend(i, _):
        j = CN - 1 - i

        @pl.when(i == CN - 1)
        def _():
            pass_mlp(*mlp_weights[0], 0)
            pass_mlp(*mlp_weights[0], 1)

        sbuf[...] = dot(stacked(qs[j]), kall[...].reshape(2 * TK, HW), NT)
        for h in range(heads):
            rows = slice(h * TB, (h + 1) * TB)
            scores = sbuf[rows]
            ptop[h:h + 1] = jnp.maximum(ptop[h:h + 1], jnp.max(scores, axis=0, keepdims=True))
            expo = jnp.exp(scores)
            pst[j, rows] = expo * (1.0 / jnp.sum(expo, axis=-1, keepdims=True))
        mixed = folded(dot(pst[j].astype(low_type), vall[...].reshape(2 * TK, HW)))
        attq[j] = mixed.astype(low_type)

        @pl.when(i == 0)
        def _():
            weight_ready(*projections[2])
            unpack(wop, wob)

        branch = dot(attq[j], wob[...].reshape(D, HW), NT)

        @pl.when(j > 0)
        def _():
            brs[j] = branch.astype(low_type)
            put("br", CN, j, brs.at[j], brr.at[j], at_ctx(j))

        @pl.when(j == 0)
        def _():
            boown[...] = branch

        return 0

    lax.fori_loop(0, CN, attend, 0)
    pass_mlp(*mlp_weights[1], 0)
    pass_mlp(*mlp_weights[1], 1)
    pass_on("ct", ctg)
    pass_mlp(*mlp_weights[0], 2)
    peak_rows = jnp.max(ptop[...], axis=-1, keepdims=True)
    lane_id = lax.broadcasted_iota(jnp.int32, (8, 128), 1)
    own_peak = jnp.full((8, 128), -3.0e38, full_type)
    for h in range(heads):
        own_peak = jnp.where(lane_id == c_i * heads + h, peak_rows[h:h + 1], own_peak)
    pks[0] = own_peak
    put("pkt", 1, 0, pks.at[0], pks.at[1], sib)

    branch = boown[...]
    for j in (3, 2, 1):
        if j == 1:
            pass_mlp(*mlp_weights[1], 2)
        got("br", CN, j, brr.at[j], at_ctx(j))
        branch = branch + brr[j].astype(full_type)
    resid = xg[0].astype(full_type) + branch
    boown[...] = resid
    xhat2, inv2 = norm_rows(resid)
    h2[0] = (xhat2 * g2row + b2row).astype(low_type)
    for j in range(1, CN):
        put("h2", CN, j, h2.at[0], h2.at[j], at_ctx(j))

    locals_[7].wait()
    have_rest("ct", ctg)
    ct_t[...] = ctg[...].reshape(TK, D).T
    have_mlp(*mlp_weights[0])
    put("wdt", 1, 0, wdt.at[t_i], wdt.at[t_i], sib)
    ga[t_i] = dot(ctg[...].reshape(TK, D), wdt[t_i].reshape(D, FS)).reshape(CN, TB, FS)
    have_mlp(*mlp_weights[1])
    put("wut", 1, 0, wup.at[t_i], wup.at[t_i], sib)
    got("wdt", 1, 0, wdt.at[o_i], sib)
    ga[o_i] = dot(ctg[...].reshape(TK, D), wdt[o_i].reshape(D, FS)).reshape(CN, TB, FS)
    got("wut", 1, 0, wup.at[o_i], sib)

    def mlp(j, _):
        @pl.when(j > 0)
        def _():
            got("h2", CN, j, h2.at[j], at_ctx(j))

        block = h2[j]
        h2_t[:, pl.ds(pl.multiple_of(j * TB, TB), TB)] = block.T
        for a in range(2):
            up = dot(block, wup[a].reshape(D, FS))
            phi = 0.5 * (1.0 + lax.erf(up * 0.7071067811865476))
            dens = jnp.exp(up * up * -0.5) * 0.3989422804014327
            part = slice(a * FS, (a + 1) * FS)
            act[j, :, part] = (up * phi).astype(low_type)
            gu[j, :, part] = (ga[a, j] * (phi + up * dens)).astype(low_type)
        grad_two = (
            dot(gu[j, :, :FS], wup[0].reshape(D, FS), NT) + dot(gu[j, :, FS:], wup[1].reshape(D, FS), NT)
        )

        @pl.when(j == 0)
        def _():
            g2own[...] = grad_two

        @pl.when(j > 0)
        def _():
            g2s[j] = grad_two.astype(low_type)
            put("g2", CN, j, g2s.at[j], g2r.at[j], at_ctx(j))

        return 0

    lax.fori_loop(0, CN, mlp, 0)

    got("pkt", 1, 0, pks.at[1], sib)
    pks[2] = jnp.maximum(pks[0], pks[1])
    for j in range(1, ZN):
        put("pkz", ZN, j, pks.at[2], pks.at[2 + j], at_z(j))
    own_part = pl.ds(pl.multiple_of(t_i * FS, FS), FS)
    other_part = pl.ds(pl.multiple_of(o_i * FS, FS), FS)
    for k, (left, right) in enumerate(((h2_t, gu), (ct_t, act))):
        gown[k] = dot(left[...], right[...].reshape(TK, 2 * FS))
        gsib_s[k] = gown[k, :, other_part].astype(low_type)
        put("gs", 2, k, gsib_s.at[k], gsib_r.at[k], sib)

    def send_far(k):
        @pl.when(outer)
        def _():
            put("gz%d" % k, 4, 2, gz_s.at[k, far_out], gz_r.at[k, 2], plane(pair))
            put("gz%d" % k, 4, 3, gz_s.at[k, far_in], gz_r.at[k, 3], plane(pair))

    def send_near(k):
        put("gz%d" % k, 4, 0, gz_s.at[k, pair], gz_r.at[k, 0], plane(pair))

    for k in range(2):
        got("gs", 2, k, gsib_r.at[k], sib)
        total = gown[k, :, own_part] + gsib_r[k].astype(full_type)
        gkeep[k] = total
        gz_s[k] = total.astype(low_type).reshape(ZN, R, FS)
        if k == 0:
            send_far(0)
            send_near(0)

    def down(j, _):
        part = (
            dot(act[j, :, :FS], wdt[0].reshape(D, FS), NT) + dot(act[j, :, FS:], wdt[1].reshape(D, FS), NT)
        )

        @pl.when(j == 0)
        def _():
            boown[...] += part

        @pl.when(j > 0)
        def _():
            bos[j] = part.astype(low_type)

        return 0

    lax.fori_loop(0, CN, down, 0)

    def relay_mlp(k):
        @pl.when(jnp.logical_not(outer))
        def _():
            for n, z in ((2, far_out), (3, far_in)):
                got("gz%d" % k, 4, n, gz_r.at[k, n], plane(pair))
                mine_part = gkeep[k, pl.ds(pl.multiple_of(z * R, R), R)]
                gz_s[k, z] = (mine_part + gz_r[k, n].astype(full_type)).astype(low_type)
                base = spot("gz%d" % k, 4)
                pltpu.make_async_remote_copy(
                    src_ref=gz_s.at[k, z], dst_ref=gz_r.at[k, 1],
                    send_sem=ssem.at[base + n], recv_sem=rsem.at[base + 1],
                    device_id=plane(z), device_id_type=MESH,
                ).start()

    def share_mlp(k, out):
        total = gkeep[k, pl.ds(pl.multiple_of(s_i * R, R), R)]
        for n in range(2):
            got("gz%d" % k, 4, n, gz_r.at[k, n], plane(pair))
            total = total + gz_r[k, n].astype(full_type)
        gfin[k] = total.astype(low_type)
        spread("gc%d" % k, gfin.at[k], lambda j: out.at[c_i])
        pltpu.make_async_copy(gfin.at[k], out.at[c_i], lsem.at[8 + k]).start()

    grad_two = g2own[...]
    for j in range(1, CN):
        got("g2", CN, j, g2r.at[j], at_ctx(j))
        grad_two = grad_two + g2r[j].astype(full_type)
    ln2g = jnp.sum(grad_two * xhat2, axis=0, keepdims=True)
    ln2b = jnp.sum(grad_two, axis=0, keepdims=True)
    hat = grad_two * g2row
    grad_resid = ctg[0].astype(full_type) + inv2 * (
        hat
        - jnp.sum(hat, axis=-1, keepdims=True) * inv_d
        - xhat2 * (jnp.sum(hat * xhat2, axis=-1, keepdims=True) * inv_d)
    )
    gres[...] = grad_resid
    gb = grad_resid.astype(low_type)
    gbg[0] = gb
    spread("gb", gbg.at[0], lambda j: gbg.at[j])
    send_halves("bo", bos, bor)
    send_far(1)
    send_near(1)

    peak = pks[2]
    for j in range(1, ZN):
        got("pkz", ZN, j, pks.at[2 + j], at_z(j))
        peak = jnp.maximum(peak, pks[2 + j])
    first = 2 + ZN
    pks[first] = peak
    for j in range(1, CN):
        put("pkc", CN, j, pks.at[first], pks.at[first + j], at_ctx(j))

    dkt[...] = jnp.zeros_like(dkt)
    dvt[...] = jnp.zeros_like(dvt)

    def attend_back(j, _):
        @pl.when(j == 1)
        def _():
            relay_mlp(0)
            pass_on("gb", gbg)

        @pl.when(j == CN - 1)
        def _():
            add_halves("bo", bos, bor)
            have_rest("gb", gbg)

        grad_rows = stacked(dot(gbg[j], wob[...].reshape(D, HW)).astype(low_type))
        query_rows = stacked(qs[j])
        sbuf[...] = dot(grad_rows, vall[...].reshape(2 * TK, HW), NT)

        for h in range(heads):
            rows = slice(h * TB, (h + 1) * TB)
            probs, grad_probs = pst[j, rows], sbuf[rows]
            inner = jnp.sum(probs * grad_probs, axis=-1, keepdims=True)
            dsb[rows] = (probs * (grad_probs - inner)).astype(low_type)
        grad_scores = dsb[...]
        dqb[j] = folded(dot(grad_scores, kall[...].reshape(2 * TK, HW))) * 0.125
        dvt[...] += dot(grad_rows, pst[j].astype(low_type), TN)
        dkt[...] += dot(query_rows, grad_scores, TN)
        return 0

    lax.fori_loop(0, CN, attend_back, 0)
    dks_s[0] = dvt[:, TK:].astype(low_type)
    dks_s[1] = dkt[:, TK:].astype(low_type)
    for k in range(2):
        put("dk", 2, k, dks_s.at[k], dks_r.at[k], sib)

    for j in range(1, CN):
        got("pkc", CN, j, pks.at[first + j], at_ctx(j))
        peak = jnp.maximum(peak, pks[first + j])
    peak_v[...] = peak
    pltpu.make_async_copy(peak_v, peak_o, lsem.at[22]).start()

    relay_mlp(1)
    share_mlp(0, upo)
    def unnorm(grad_n, gain_row, normed, inverse):
        gain_grad = jnp.sum(grad_n * normed, axis=0, keepdims=True)
        e = grad_n * gain_row
        return (inverse * (e - normed * head_mean(e * normed))).astype(low_type), gain_grad

    def share_grad(n, full):
        full = full.reshape(ZN, 2, HR, 2 * HW)
        low_full = full.astype(low_type)
        for k in range(2):
            @pl.when(o_i == k)
            def _():
                qsib_s[n] = low_full[:, k]

            @pl.when(t_i == k)
            def _():
                qown[n] = full[:, k]

        put("qg", 2, n, qsib_s.at[n], qsib_r.at[n], sib)

    def reduce_grad(n):
        got("qg", 2, n, qsib_r.at[n], sib)
        total = qown[n] + qsib_r[n].astype(full_type)
        qown[n] = total
        qz_s[n] = total.astype(low_type)
        for j in range(1, ZN):
            put("qz%d" % n, ZN, j, qz_s.at[n, flip(s_i, j, ZN)], qz_r.at[n, j], at_z(j))

    grad_raw, q_gain_row = unnorm(dqb[...].reshape(TK, HW), qgrow, nq[...], sq[...])
    dqr[...] = grad_raw
    empty = jnp.zeros((TK, HW), low_type)
    share_grad(1, (
        dot(h1_t[...], jnp.concatenate([dqr[...], empty], axis=1))
        + dot(gbg[...].reshape(TK, D), jnp.concatenate([empty, attq[...].reshape(TK, HW)], axis=1), TN)
    ))
    got("dk", 2, 0, dks_r.at[0], sib)
    grad_v = (dvt[:, :TK] + dks_r[0].astype(full_type)).T.astype(low_type)
    got("dk", 2, 1, dks_r.at[1], sib)
    grad_k = (dkt[:, :TK] + dks_r[1].astype(full_type)).T
    grad_raw, k_gain_row = unnorm(grad_k, kgrow, nk[...], sk[...])
    dkv[...] = jnp.concatenate([grad_raw, grad_v], axis=1)
    ln1g = jnp.zeros((1, D), full_type)
    ln1b = jnp.zeros((1, D), full_type)
    for j in range(CN - 1, -1, -1):
        rows = slice(j * TB, (j + 1) * TB)
        part = dot(dqr[rows], wqb[...].reshape(D, HW), NT) + dot(dkv[rows], wkv[...].reshape(D, 2 * HW), NT)
        if j:
            g1s[j] = part.astype(low_type)
        else:
            g1own[...] = part
        if j == 3:
            send_halves("g1", g1s, g1r)
            share_grad(0, dot(h1_t[...], dkv[...]))
            reduce_grad(1)
        ln1g = ln1g + jnp.sum(part * xh1[j], axis=0, keepdims=True)
        ln1b = ln1b + jnp.sum(part, axis=0, keepdims=True)
        if j == 1:
            reduce_grad(0)
    rows_s[0] = jnp.zeros_like(rows_s[0])
    HD2 = D // 2
    for k, row in enumerate((ln1g, ln1b, ln2g, ln2b)):
        rows_s[0, 2 * k:2 * k + 1, :HD2] = row[:, :HD2]
        rows_s[0, 2 * k + 1:2 * k + 2, :HD2] = row[:, HD2:]
    rows_s[0, 0:1, HD2:HD2 + HW] = q_gain_row
    rows_s[0, 1:2, HD2:HD2 + HW] = k_gain_row
    put("rt", 1, 0, rows_s.at[0], rows_r.at[0], sib)
    add_halves("g1", g1s, g1r)
    share_mlp(1, dno)
    got("rt", 1, 0, rows_r.at[0], sib)
    rows_s[1] = rows_s[0] + rows_r[0]
    for j in range(1, ZN):
        put("rz", ZN, j, rows_s.at[1], rows_r.at[j], at_z(j))

    total = boown[...]
    for j in (1, 2):
        got("bo", 5, j, bor.at[j], at_ctx(j))
        total = total + bor[j].astype(full_type)
    own_rows = pl.ds(t_i * TB, TB)
    obuf[0] = total.astype(low_type)
    put("ob", 2, 0, obuf.at[0], bo_o.at[own_rows], sib)
    pltpu.make_async_copy(obuf.at[0], bo_o.at[own_rows], lsem.at[10]).start()

    def share_fin(n):
        total = qown[n, s_i]
        for j in range(1, ZN):
            got("qz%d" % n, ZN, j, qz_r.at[n, j], at_z(j))
            total = total + qz_r[n, j].astype(full_type)
        qfin[n] = total.astype(low_type)
        slot = spot("qcr%d" % n, 2 * half_chips) + place * 2 + t_i
        for j in range(1, CN):
            pltpu.make_async_remote_copy(
                src_ref=qfin.at[n], dst_ref=qkvo.at[place, t_i, n],
                send_sem=ssem.at[spot("qcs%d" % n, CN) + j], recv_sem=rsem.at[slot],
                device_id=(s_i, flip(c_i, j, CN), tstar), device_id_type=MESH,
            ).start()

        @pl.when(t_i == tstar)
        def _():
            pltpu.make_async_copy(qfin.at[n], qkvo.at[place, t_i, n], lsem.at[12 + n]).start()

        @pl.when(t_i != tstar)
        def _():
            pltpu.make_async_remote_copy(
                src_ref=qfin.at[n], dst_ref=qkvo.at[place, t_i, n],
                send_sem=ssem.at[spot("qcs%d" % n, CN)], recv_sem=rsem.at[slot],
                device_id=sib, device_id_type=MESH,
            ).start()

    def pass_grad(k, out):
        for j in (1, 2):
            block = out.at[flip(c_i, j, CN)]
            got("gc%d" % k, 5, j, block, at_ctx(j))
            half = block.at[pl.ds((j - 1) * HR, HR)]
            put_as("gc%d" % k, 5, 2 + j, 2 + j, half, half, at_ctx(3 - j))

    share_fin(1)
    pass_grad(0, upo)

    xhat1, inv1 = norm_rows(xg[0].astype(full_type))
    grad_one = g1own[...]
    for j in (1, 2):
        got("g1", 5, j, g1r.at[j], at_ctx(j))
        grad_one = grad_one + g1r[j].astype(full_type)
    hat = grad_one * g1row
    grad_in = gres[...] + inv1 * (
        hat
        - jnp.sum(hat, axis=-1, keepdims=True) * inv_d
        - xhat1 * (jnp.sum(hat * xhat1, axis=-1, keepdims=True) * inv_d)
    )
    obuf[1] = grad_in.astype(low_type)
    put("ob", 2, 1, obuf.at[1], ig_o.at[own_rows], sib)
    pltpu.make_async_copy(obuf.at[1], ig_o.at[own_rows], lsem.at[11]).start()

    pass_grad(1, dno)
    rows_sum = rows_s[1]
    for j in range(1, ZN):
        got("rz", ZN, j, rows_r.at[j], at_z(j))
        rows_sum = rows_sum + rows_r[j]
    rows_s[2] = rows_sum
    for j in range(1, CN):
        put("rc", CN, j, rows_s.at[2], rows_r.at[ZN + j], at_ctx(j))
    qkr_v[c_i] = rows_sum[:, HD2:]

    share_fin(0)

    total = rows_sum[:, :HD2]
    for j in range(1, CN):
        got("rc", CN, j, rows_r.at[ZN + j], at_ctx(j))
        block = rows_r[ZN + j]
        total = total + block[:, :HD2]
        qkr_v[flip(c_i, j, CN)] = block[:, HD2:]
    lnr_v[...] = total
    pltpu.make_async_copy(lnr_v, lnr_o, lsem.at[23]).start()
    pltpu.make_async_copy(qkr_v, qkr_o, lsem.at[24]).start()

    for n, (src, dst) in enumerate(((peak_v, peak_o), (lnr_v, lnr_o), (qkr_v, qkr_o))):
        pltpu.make_async_copy(src, dst, lsem.at[22 + n]).wait()
    for k, out in ((0, upo), (1, dno)):
        for j in (1, 2):
            half = out.at[flip(c_i, 3, CN), pl.ds((j - 1) * HR, HR)]
            got("gc%d" % k, 5, 2 + j, half, at_ctx(3 - j))
        pltpu.make_async_copy(gfin.at[k], out.at[c_i], lsem.at[8 + k]).wait()
    other_rows = pl.ds(o_i * TB, TB)
    for k, out in ((0, bo_o), (1, ig_o)):
        got("ob", 2, k, out.at[other_rows], sib)
        pltpu.make_async_copy(obuf.at[k], out.at[own_rows], lsem.at[10 + k]).wait()

    @pl.when(t_i == tstar)
    def _():
        for n in range(2):
            pltpu.make_async_copy(qfin.at[n], qkvo.at[place, t_i, n], lsem.at[12 + n]).wait()

    for p in range(half_chips):
        for a in range(2):
            @pl.when((t_i != tstar) | (place != p) | (t_i != a))
            def _():
                for n in range(2):
                    pltpu.make_async_remote_copy(
                        src_ref=qfin.at[n], dst_ref=qkvo.at[p, a, n],
                        send_sem=ssem.at[spot("qcs%d" % n, CN)],
                        recv_sem=rsem.at[spot("qcr%d" % n, 2 * half_chips) + p * 2 + a],
                        device_id=sib, device_id_type=MESH,
                    ).wait_recv()

    for j in range(1, CN):
        sent("x", CN, j, x_src, sib)
        sent("br", CN, j, brs.at[j], sib)
        sent("h2", CN, j, h2.at[0], sib)
        sent("g2", CN, j, g2s.at[j], sib)
        sent("pkc", CN, j, pks.at[first], sib)
        sent("rc", CN, j, rows_s.at[2], sib)
        for n in range(2):
            sent("qcs%d" % n, CN, j, qfin.at[n], sib)
    for j in range(1, ZN):
        sent("small", ZN, j, smalls.at[t_i, s_i], sib)
        sent("pkz", ZN, j, pks.at[2], sib)
        sent("rz", ZN, j, rows_s.at[1], sib)
        for n in range(2):
            sent("qz%d" % n, ZN, j, qz_s.at[n, 0], sib)
    for n in range(1, 5):
        for name, buf, half in (("ct", ctg, ctg), ("gb", gbg, gbg), ("bo", bos, bos), ("g1", g1s, g1s)):
            sent(name, 5, n, buf.at[1] if n < 3 else half.at[1, pl.ds(0, HB)], sib)
        for k, out in ((0, upo), (1, dno)):
            sent("gc%d" % k, 5, n, gfin.at[k] if n < 3 else gfin.at[k, pl.ds(0, HR)], sib)
    for name, buf in mlp_weights:
        sent(name, 5, 0, buf.at[t_i, s_i], sib)

        @pl.when(jnp.logical_not(outer))
        def _():
            for n in range(1, 5):
                sent(name, 5, n, buf.at[t_i, s_i], sib)

    for k in range(2):
        for n in (0, 2, 3):
            sent("gz%d" % k, 4, n, gz_s.at[k, 0], sib)
    sent("smallt", 1, 0, smalls.at[t_i], sib)
    sent("k", 1, 0, kall.at[0], sib)
    sent("v", 1, 0, vall.at[0], sib)
    sent("pkt", 1, 0, pks.at[0], sib)
    sent("wdt", 1, 0, wdt.at[t_i], sib)
    sent("wut", 1, 0, wup.at[t_i], sib)
    sent("rt", 1, 0, rows_s.at[0], sib)
    for k in range(2):
        sent("gs", 2, k, gsib_s.at[k], sib)
        sent("dk", 2, k, dks_s.at[k], sib)
        sent("ob", 2, k, obuf.at[k], sib)
    for n in range(2):
        sent("qg", 2, n, qsib_s.at[n], sib)

    @pl.when(t_i == tstar)
    def _():
        for name, buf in projections:
            for j in range(ZN):
                sent(name, ZN, j, buf.at[s_i], sib)
                if j:
                    sent("f" + name, ZN, j, buf.at[s_i], sib)

    @pl.when(t_i != tstar)
    def _():
        for n in range(2):
            sent("qcs%d" % n, CN, 0, qfin.at[n], sib)


SEMS = 127


def fused_call(sizes, *operands):
    CN, ZN, TB, D, HW, FS, R = sizes
    TK = CN * TB
    HR = R // 2
    half_chips = CN // 2
    heads = HW // 64
    lo, hi = low_type, full_type
    V = pltpu.VMEM
    any_spec = pl.BlockSpec(memory_space=pl.ANY)
    gain_shape = operands[6].shape
    out_shape = [
        jax.ShapeDtypeStruct((2 * TB, D), lo),
        jax.ShapeDtypeStruct((2 * TB, D), lo),
        jax.ShapeDtypeStruct((CN, R, FS), lo),
        jax.ShapeDtypeStruct((CN, R, FS), lo),
        jax.ShapeDtypeStruct((half_chips, 2, 2, HR, 2 * HW), lo),
        jax.ShapeDtypeStruct((8, D // 2), hi),
        jax.ShapeDtypeStruct((CN, 8, 256), hi),
        jax.ShapeDtypeStruct((8, 128), hi),
    ]
    scratch = [
        V((CN, TB, D), lo), V((CN, TB, D), lo), V((2, ZN, 8, 256), hi),
        V((3, R, half_chips * HW), lo), V((R, half_chips * HW), lo),
        V((ZN, R, 2 * HW), lo), V((ZN, HR, 2 * HW), lo), V((ZN, HR, 2 * HW), lo),
        V((ZN, R, HW), lo), V((ZN, R, HW), lo), V((2, ZN, R, FS), lo), V((2, ZN, R, FS), lo),
        V((D, TK), lo), V((D, TK), lo), V((D, TK), lo),
        V((CN, TB, D), hi), V((CN, TB, D), lo),
        V((TK, HW), hi), V((TK, HW), hi), V((TK, HW), hi), V((TK, HW), hi),
        V((CN, TB, HW), lo), V((2, TK, HW), lo), V((2, TK, HW), lo),
        V((CN, heads * TB, 2 * TK), hi), V((heads * TB, 2 * TK), hi),
        V((CN, TB, HW), lo), V((CN, TB, D), lo), V((CN, TB, D), lo), V((2 + ZN + CN, 8, 128), hi),
        V((heads, 2 * TK), hi), V((heads * TB, 2 * TK), lo),
        V((CN, TB, D), lo), V((2, CN, TB, FS), hi), V((CN, TB, 2 * FS), lo), V((CN, TB, 2 * FS), lo),
        V((CN, TB, D), lo), V((CN, TB, D), lo), V((TB, D), hi),
        V((CN, TB, D), lo), V((CN, TB, D), lo), V((TB, D), hi),
        V((2, D, FS), lo), V((2, D, FS), lo), V((2, D, 2 * FS), hi), V((2, D, FS), hi),
        V((2, ZN, R, FS), lo), V((2, ZN, R, FS), lo), V((2, R, FS), lo),
        V((TB, D), hi), V((CN, TB, D), lo),
        V((CN, TB, HW), hi), V((HW, 2 * TK), hi), V((HW, 2 * TK), hi),
        V((2, HW, TK), lo), V((2, HW, TK), lo), V((TK, HW), lo), V((TK, 2 * HW), lo),
        V((CN, TB, D), lo), V((CN, TB, D), lo), V((TB, D), hi),
        V((2, ZN, HR, 2 * HW), lo), V((2, ZN, HR, 2 * HW), lo), V((2, ZN, HR, 2 * HW), hi),
        V((2, ZN, HR, 2 * HW), lo), V((2, ZN, HR, 2 * HW), lo), V((2, HR, 2 * HW), lo),
        V((3, 8, D // 2 + 256), hi), V((ZN + CN, 8, D // 2 + 256), hi), V((2, TB, D), lo),
        V((R,), lo), V((R,), lo), V((R,), lo), V((R,), lo), V(gain_shape, lo), V(gain_shape, lo),
        V((8, D // 2), hi), V((CN, 8, 256), hi), V((8, 128), hi),
        pltpu.SemaphoreType.DMA((25,)), pltpu.SemaphoreType.DMA((SEMS,)), pltpu.SemaphoreType.DMA((SEMS,)),
    ]
    return pl.pallas_call(
        functools.partial(fused_kernel, sizes),
        out_shape=out_shape,
        in_specs=[any_spec] * 14,
        out_specs=[any_spec] * 8,
        scratch_shapes=scratch,
        compiler_params=pltpu.CompilerParams(
            collective_id=0, has_side_effects=True, vmem_limit_bytes=56 * 2**20
        ),
    )(*operands)


def finish_kernel(
    sizes,
    bo, ig, up_h, dn_h, qkvo_h, lnr_h, qkr_h, peak_h, wq_h, wk_h,
    bo_o, ig_o, l1g, l1b, l2g, l2b, qg_o, kg_o, gq_o, gk_o, gv_o, go_o, gu_o, gd_o, cq_o, ck_o,
    upo, dno, qkvo, lnr, qkr, peak, wq, wk, bov, igv, gq, gk, gv, go, gu, gd, cq, ck, isem, osem,
):
    CN, ZN, TB, D, HW, FS, R = sizes
    half_chips = CN // 2
    s_i, t_i = lax.axis_index("shard"), lax.axis_index("tp")
    ins = [
        pltpu.make_async_copy(src, dst, isem.at[n])
        for n, (src, dst) in enumerate((
            (qkvo_h, qkvo), (up_h, upo), (dn_h, dno), (peak_h, peak), (wq_h, wq), (wk_h, wk),
            (lnr_h, lnr), (qkr_h, qkr), (bo, bov), (ig, igv),
        ))
    ]
    for n in (1, 2, 0, 8, 9, 3, 4, 5, 6, 7):
        ins[n].start()
    outs = []

    def leave(src, dst):
        copy = pltpu.make_async_copy(src, dst, osem.at[len(outs)])
        copy.start()
        outs.append(copy)

    for n, grads, stage, out in ((1, upo, gu, gu_o), (2, dno, gd, gd_o)):
        ins[n].wait()
        for c in range(CN):
            stage[:, c * FS:(c + 1) * FS] = grads[c].astype(full_type)
        leave(stage, out)
    for n, stage, out in ((8, bov, bo_o), (9, igv, ig_o)):
        ins[n].wait()
        leave(stage, out)
    ins[0].wait()
    for n, first, stage, out in ((1, 0, gq, gq_o), (0, 0, gk, gk_o), (0, HW, gv, gv_o), (1, HW, go, go_o)):
        for a in range(2):
            parts = [qkvo[p, a, n][:, first:first + HW] for p in range(half_chips)]
            stage[a * (R // 2):(a + 1) * (R // 2)] = jnp.concatenate(parts, axis=1).astype(full_type)
        leave(stage, out)
    heads = HW // 64
    for n in (3, 4, 5):
        ins[n].wait()
    factor = jnp.sqrt(clip_level / jnp.maximum(peak[0:1], clip_level))
    here = half_chips * heads
    lanes = lax.broadcasted_iota(jnp.int32, (1, here * 64), 1) // 64
    ids = lax.broadcasted_iota(jnp.int32, (1, 128), 1)
    columns = jnp.ones((1, here * 64), full_type)
    for h in range(here):
        one = jnp.sum(jnp.where(ids == t_i * here + h, factor, 0.0), axis=-1, keepdims=True)
        columns = jnp.where(lanes == h, one, columns)
    for weights, stage, out in ((wq, cq, cq_o), (wk, ck, ck_o)):
        stage[...] = (weights[...].astype(full_type) * columns).astype(low_type)
        leave(stage, out)
    ins[6].wait()
    ins[7].wait()
    for k, out in enumerate((l1g, l1b, l2g, l2b)):
        row = jnp.zeros((1, R), full_type)
        for z in range(ZN):
            at = z * R % (D // 2)
            source = 2 * k + z * R // (D // 2)
            row = jnp.where(s_i == z, lnr[source:source + 1, at:at + R], row)
        out[...] = row.reshape(R)
    piece = qg_o.shape[1]
    for p in range(half_chips):
        chip = qkr[t_i * half_chips + p]
        for h in range(heads):
            for z in range(ZN):
                at = h * 64 + z * piece

                @pl.when(s_i == z)
                def _():
                    qg_o[p * heads + h:p * heads + h + 1] = chip[0:1, at:at + piece]
                    kg_o[p * heads + h:p * heads + h + 1] = chip[1:2, at:at + piece]
    for copy in outs:
        copy.wait()


def fused_layer(
    images, cotangent, ln1_gain, ln1_bias, ln2_gain, ln2_bias, q_gain, k_gain,
    w_query, w_key, w_value, w_out, w_up, w_down,
):
    CN, ZN = lax.axis_size("ctx"), lax.axis_size("shard")
    TB = images.shape[1] // 2
    D = images.shape[2]
    R = w_query.shape[0]
    HW = w_query.shape[1] // (CN // 2)
    FS = w_up.shape[1] // CN
    sizes = (CN, ZN, TB, D, HW, FS, R)
    results = fused_call(
        sizes, images, cotangent, ln1_gain, ln1_bias, ln2_gain, ln2_bias, q_gain, k_gain,
        w_query, w_key, w_value, w_out.T, w_up, w_down.T,
    )
    row = jax.ShapeDtypeStruct((R,), full_type)
    gain = jax.ShapeDtypeStruct(q_gain.shape, full_type)
    square = jax.ShapeDtypeStruct(w_query.shape, full_type)
    wide = jax.ShapeDtypeStruct(w_up.shape, full_type)
    tokens = jax.ShapeDtypeStruct(images.shape[1:], low_type)
    clipped = jax.ShapeDtypeStruct(w_query.shape, low_type)
    lo, hi = low_type, full_type
    V = pltpu.VMEM
    any_spec = pl.BlockSpec(memory_space=pl.ANY)
    vm_spec = pl.BlockSpec(memory_space=pltpu.VMEM)
    out = pl.pallas_call(
        functools.partial(finish_kernel, sizes),
        out_shape=[tokens] * 2 + [row] * 4 + [gain] * 2 + [square] * 4 + [wide] * 2 + [clipped] * 2,
        in_specs=[any_spec] * 10,
        out_specs=[any_spec] * 2 + [vm_spec] * 6 + [any_spec] * 8,
        scratch_shapes=[
            V((CN, R, FS), lo), V((CN, R, FS), lo), V((CN // 2, 2, 2, R // 2, 2 * HW), lo), V((8, D // 2), hi),
            V((CN, 8, 256), hi), V((8, 128), hi), V(w_query.shape, lo), V(w_query.shape, lo),
            V(images.shape[1:], lo), V(images.shape[1:], lo),
        ]
        + [V(w_query.shape, hi)] * 4 + [V(w_up.shape, hi)] * 2 + [V(w_query.shape, lo)] * 2
        + [pltpu.SemaphoreType.DMA((10,)), pltpu.SemaphoreType.DMA((10,))],
        compiler_params=pltpu.CompilerParams(vmem_limit_bytes=60 * 2**20),
    )(*results, w_query, w_key)
    out = list(out)
    out[0], out[1] = out[0].reshape(images.shape), out[1].reshape(images.shape)
    out[11], out[13] = out[11].T, out[13].T
    return tuple(out)


def on_device(images, cotangent, ln1_gain, ln1_bias, ln2_gain, ln2_bias, q_gain, k_gain, *weights):
    fused = fits_fused(images, weights[0], weights[4], q_gain)
    layer = fused_layer if fused else general_layer
    return layer(images, cotangent, ln1_gain, ln1_bias, ln2_gain, ln2_bias, q_gain, k_gain, *weights)


def solution(mesh):
    return jax.shard_map(
        on_device,
        mesh=mesh,
        in_specs=(
            P("shard", "ctx", None),
            P("shard", "ctx", None),
            P("shard"),
            P("shard"),
            P("shard"),
            P("shard"),
            P("tp", "shard"),
            P("tp", "shard"),
            P("shard", "tp"),
            P("shard", "tp"),
            P("shard", "tp"),
            P("tp", "shard"),
            P("shard", "tp"),
            P("tp", "shard"),
        ),
        out_specs=(
            P("shard", "ctx", None),
            P("shard", "ctx", None),
            P("shard"),
            P("shard"),
            P("shard"),
            P("shard"),
            P("tp", "shard"),
            P("tp", "shard"),
            P("shard", "tp"),
            P("shard", "tp"),
            P("shard", "tp"),
            P("tp", "shard"),
            P("shard", "tp"),
            P("tp", "shard"),
            P("shard", "tp"),
            P("shard", "tp"),
        ),
        check_vma=False,
    )
```

```python
import functools
import jax
import jax.numpy as jnp
from jax import lax
from jax.experimental import pallas as pl
from jax.experimental.pallas import tpu as pltpu
from jax.sharding import PartitionSpec as P

norm_eps = 1e-06
clip_level = 0.5


def matmul(left, right):
    return jnp.dot(left, right, preferred_element_type=jnp.float32)


def norm_parts(values):
    center = values - jnp.mean(values, axis=-1, keepdims=True)
    inverse = lax.rsqrt(jnp.mean(center * center, axis=-1, keepdims=True) + norm_eps)
    return (center * inverse, inverse)


def norm_back(grad_hat, normed, inverse):
    return inverse * (
        grad_hat
        - jnp.mean(grad_hat, axis=-1, keepdims=True)
        - normed * jnp.mean(grad_hat * normed, axis=-1, keepdims=True)
    )


def head_scale(values, gain):
    inverse = lax.rsqrt(jnp.mean(values * values, axis=-1, keepdims=True) + norm_eps)
    return values * inverse * gain


def gelu_exact(values):
    return jax.nn.gelu(values, approximate=False)


def general_layer(
    images,
    cotangent,
    ln1_gain,
    ln1_bias,
    ln2_gain,
    ln2_bias,
    q_gain,
    k_gain,
    w_query,
    w_key,
    w_value,
    w_out,
    w_up,
    w_down,
):
    (
        full_query,
        full_key,
        full_value,
        full_up,
        full_out,
        full_down,
        gain_low_one,
        shift_low_one,
        gain_low_two,
        shift_low_two,
        query_gain_low,
        key_gain_low,
    ) = (
        lax.all_gather(w_query, "shard", axis=0, tiled=True),
        lax.all_gather(w_key, "shard", axis=0, tiled=True),
        lax.all_gather(w_value, "shard", axis=0, tiled=True),
        lax.all_gather(w_up, "shard", axis=0, tiled=True),
        lax.all_gather(w_out, "shard", axis=1, tiled=True),
        lax.all_gather(w_down, "shard", axis=1, tiled=True),
        lax.all_gather(ln1_gain, "shard", axis=0, tiled=True),
        lax.all_gather(ln1_bias, "shard", axis=0, tiled=True),
        lax.all_gather(ln2_gain, "shard", axis=0, tiled=True),
        lax.all_gather(ln2_bias, "shard", axis=0, tiled=True),
        lax.all_gather(q_gain, "shard", axis=1, tiled=True),
        lax.all_gather(k_gain, "shard", axis=1, tiled=True),
    )
    gain_one = gain_low_one.astype(jnp.float32)
    shift_one = shift_low_one.astype(jnp.float32)
    gain_two = gain_low_two.astype(jnp.float32)
    shift_two = shift_low_two.astype(jnp.float32)
    query_gain = query_gain_low.astype(jnp.float32)
    key_gain = key_gain_low.astype(jnp.float32)
    count_img, local_len, width = images.shape
    tokens = count_img * local_len
    heads_here, head_size = query_gain.shape
    local_width = heads_here * head_size
    full_len = local_len * lax.axis_size("ctx")
    group = 1
    groups = count_img // group
    scale = head_size ** (-0.5)
    flat = images.reshape(tokens, width).astype(jnp.float32)
    normed_one, inverse_one = norm_parts(flat)
    hidden_one = (normed_one * gain_one + shift_one).astype(jnp.bfloat16)
    query_raw = matmul(hidden_one, full_query).reshape(tokens, heads_here, head_size)
    key_raw = matmul(hidden_one, full_key).reshape(tokens, heads_here, head_size)
    query_norm = head_scale(query_raw, query_gain).astype(jnp.bfloat16)
    key_norm = head_scale(key_raw, key_gain).astype(jnp.bfloat16)
    value_low = matmul(hidden_one, full_value).astype(jnp.bfloat16)
    key_all, value_all = (
        lax.all_gather(
            key_norm.reshape(count_img, local_len, local_width), "ctx", axis=1, tiled=True
        ),
        lax.all_gather(
            value_low.reshape(count_img, local_len, local_width), "ctx", axis=1, tiled=True
        ),
    )
    query_grp = query_norm.reshape(groups, group, local_len, heads_here, head_size)
    key_grp = key_all.reshape(groups, group, full_len, heads_here, head_size)
    value_grp = value_all.reshape(groups, group, full_len, heads_here, head_size)

    def attend(pieces):
        query_blk, key_blk, value_blk = pieces
        scores = (
            jnp.einsum("gqhd,gkhd->ghqk", query_blk, key_blk, preferred_element_type=jnp.float32)
            * scale
        )
        top = jnp.max(scores, axis=-1, keepdims=True)
        expo = jnp.exp(scores - top)
        total = jnp.sum(expo, axis=-1, keepdims=True)
        probs = (expo / total).astype(jnp.bfloat16)
        mixed_blk = jnp.einsum(
            "ghqk,gkhd->gqhd", probs, value_blk, preferred_element_type=jnp.float32
        )
        return (mixed_blk, top + jnp.log(total), jnp.max(top, axis=(0, 2, 3)))

    mixed, log_total, group_peaks = lax.map(attend, (query_grp, key_grp, value_grp))
    local_peak = jnp.max(group_peaks, axis=0)
    peak_all = lax.pmax(local_peak, ("shard", "ctx"))
    attended = mixed.reshape(tokens, local_width).astype(jnp.bfloat16)
    branch_attn = lax.psum(matmul(attended, full_out), "tp")
    resid = flat + branch_attn
    normed_two, inverse_two = norm_parts(resid)
    hidden_two = (normed_two * gain_two + shift_two).astype(jnp.bfloat16)
    up_raw = matmul(hidden_two, full_up)
    active = gelu_exact(up_raw).astype(jnp.bfloat16)
    branch_mlp = lax.psum(matmul(active, full_down).astype(jnp.bfloat16), "tp").astype(jnp.float32)
    block_out = (resid + branch_mlp).astype(jnp.bfloat16).reshape(images.shape)
    grad_out = cotangent.reshape(tokens, width).astype(jnp.float32)
    grad_down = cotangent.reshape(tokens, width)
    grad_w_down = jnp.dot(active.T, grad_down, preferred_element_type=jnp.float32)
    grad_active = matmul(grad_down, full_down.T)
    unused_up, gelu_pull = jax.vjp(gelu_exact, up_raw)
    grad_up = gelu_pull(grad_active)[0].astype(jnp.bfloat16)
    grad_w_up = jnp.dot(hidden_two.T, grad_up, preferred_element_type=jnp.float32)
    grad_two = lax.psum(matmul(grad_up, full_up.T), "tp")
    grad_gain_two = jnp.sum(grad_two * normed_two, axis=0)
    grad_shift_two = jnp.sum(grad_two, axis=0)
    grad_resid = grad_out + norm_back(grad_two * gain_two, normed_two, inverse_two)
    grad_branch = grad_resid.astype(jnp.bfloat16)
    grad_w_out = jnp.dot(attended.T, grad_branch, preferred_element_type=jnp.float32)
    grad_mixed = matmul(grad_branch, full_out.T).astype(jnp.bfloat16)
    grad_grp = grad_mixed.reshape(groups, group, local_len, heads_here, head_size)

    def attend_back(pieces):
        query_blk, key_blk, value_blk, log_blk, grad_blk = pieces
        scores = (
            jnp.einsum("gqhd,gkhd->ghqk", query_blk, key_blk, preferred_element_type=jnp.float32)
            * scale
        )
        probs = jnp.exp(scores - log_blk)
        grad_probs = jnp.einsum(
            "gqhd,gkhd->ghqk", grad_blk, value_blk, preferred_element_type=jnp.float32
        )
        grad_scores = (
            probs * (grad_probs - jnp.sum(probs * grad_probs, axis=-1, keepdims=True))
        ).astype(jnp.bfloat16)
        grad_val = jnp.einsum(
            "ghqk,gqhd->gkhd",
            probs.astype(jnp.bfloat16),
            grad_blk,
            preferred_element_type=jnp.float32,
        )
        grad_qry = (
            jnp.einsum("ghqk,gkhd->gqhd", grad_scores, key_blk, preferred_element_type=jnp.float32)
            * scale
        )
        grad_kys = (
            jnp.einsum(
                "ghqk,gqhd->gkhd", grad_scores, query_blk, preferred_element_type=jnp.float32
            )
            * scale
        )
        return (grad_qry, grad_kys, grad_val)

    grad_query_n, grad_key_full, grad_value_full = lax.map(
        attend_back, (query_grp, key_grp, value_grp, log_total, grad_grp)
    )
    grad_key_n, grad_value_n = (
        lax.psum_scatter(
            grad_key_full.reshape(count_img, full_len, local_width),
            "ctx",
            scatter_dimension=1,
            tiled=True,
        ),
        lax.psum_scatter(
            grad_value_full.reshape(count_img, full_len, local_width),
            "ctx",
            scatter_dimension=1,
            tiled=True,
        ),
    )
    unused_query, query_pull = jax.vjp(head_scale, query_raw, query_gain)
    grad_query_raw, grad_query_gain = query_pull(
        grad_query_n.reshape(tokens, heads_here, head_size)
    )
    unused_key, key_pull = jax.vjp(head_scale, key_raw, key_gain)
    grad_key_raw, grad_key_gain = key_pull(grad_key_n.reshape(tokens, heads_here, head_size))
    grad_query_low = grad_query_raw.reshape(tokens, local_width).astype(jnp.bfloat16)
    grad_key_low = grad_key_raw.reshape(tokens, local_width).astype(jnp.bfloat16)
    grad_value_low = grad_value_n.reshape(tokens, local_width).astype(jnp.bfloat16)
    grad_w_query = jnp.dot(hidden_one.T, grad_query_low, preferred_element_type=jnp.float32)
    grad_w_key = jnp.dot(hidden_one.T, grad_key_low, preferred_element_type=jnp.float32)
    grad_w_value = jnp.dot(hidden_one.T, grad_value_low, preferred_element_type=jnp.float32)
    grad_one_part = (
        matmul(grad_query_low, full_query.T)
        + matmul(grad_key_low, full_key.T)
        + matmul(grad_value_low, full_value.T)
    )
    grad_one = lax.psum(grad_one_part, "tp")
    grad_gain_one = jnp.sum(grad_one * normed_one, axis=0)
    grad_shift_one = jnp.sum(grad_one, axis=0)
    input_grad = (
        (grad_resid + norm_back(grad_one * gain_one, normed_one, inverse_one))
        .astype(jnp.bfloat16)
        .reshape(images.shape)
    )
    (
        sum_query,
        sum_key,
        sum_value,
        sum_up,
        sum_out,
        sum_down,
        sum_gain_one,
        sum_shift_one,
        sum_gain_two,
        sum_shift_two,
        sum_qgain,
        sum_kgain,
    ) = lax.psum(
        (
            grad_w_query,
            grad_w_key,
            grad_w_value,
            grad_w_up,
            grad_w_out,
            grad_w_down,
            grad_gain_one,
            grad_shift_one,
            grad_gain_two,
            grad_shift_two,
            grad_query_gain,
            grad_key_gain,
        ),
        "ctx",
    )
    (
        part_query,
        part_key,
        part_value,
        part_up,
        part_out,
        part_down,
        part_gain_one,
        part_shift_one,
        part_gain_two,
        part_shift_two,
        part_qgain,
        part_kgain,
    ) = (
        lax.psum_scatter(sum_query, "shard", scatter_dimension=0, tiled=True),
        lax.psum_scatter(sum_key, "shard", scatter_dimension=0, tiled=True),
        lax.psum_scatter(sum_value, "shard", scatter_dimension=0, tiled=True),
        lax.psum_scatter(sum_up, "shard", scatter_dimension=0, tiled=True),
        lax.psum_scatter(sum_out, "shard", scatter_dimension=1, tiled=True),
        lax.psum_scatter(sum_down, "shard", scatter_dimension=1, tiled=True),
        lax.psum_scatter(sum_gain_one, "shard", scatter_dimension=0, tiled=True),
        lax.psum_scatter(sum_shift_one, "shard", scatter_dimension=0, tiled=True),
        lax.psum_scatter(sum_gain_two, "shard", scatter_dimension=0, tiled=True),
        lax.psum_scatter(sum_shift_two, "shard", scatter_dimension=0, tiled=True),
        lax.psum_scatter(sum_qgain, "shard", scatter_dimension=1, tiled=True),
        lax.psum_scatter(sum_kgain, "shard", scatter_dimension=1, tiled=True),
    )
    factor = jnp.sqrt(clip_level / jnp.maximum(peak_all, clip_level))
    columns = jnp.repeat(factor, head_size)
    query_clip = (w_query.astype(jnp.float32) * columns).astype(jnp.bfloat16)
    key_clip = (w_key.astype(jnp.float32) * columns).astype(jnp.bfloat16)
    return (
        block_out,
        input_grad,
        part_gain_one,
        part_shift_one,
        part_gain_two,
        part_shift_two,
        part_qgain,
        part_kgain,
        part_query,
        part_key,
        part_value,
        part_out,
        part_up,
        part_down,
        query_clip,
        key_clip,
    )


MESH = pl.DeviceIdType.MESH
NN = (((1,), (0,)), ((), ()))
NT = (((1,), (1,)), ((), ()))
TN = (((0,), (0,)), ((), ()))
low_type = jnp.bfloat16
full_type = jnp.float32


def dot(left, right, dims=NN):
    return lax.dot_general(left, right, dims, preferred_element_type=full_type)


def flip(place, bits, count):
    result = 0
    unit = 1
    while unit < count:
        result = result + ((place // unit + bits // unit) % 2) * unit
        unit *= 2
    return result


def fits_fused(images, w_query, w_up, q_gain):
    count_img, local_len, width = images.shape
    ctx, shard, tp = lax.axis_size("ctx"), lax.axis_size("shard"), lax.axis_size("tp")
    rows = w_query.shape[0]
    return (
        count_img == 1
        and tp == 2
        and ctx == 4
        and shard == 4
        and rows % (16 * ctx) == 0
        and local_len % 32 == 0
        and q_gain.shape[0] % 2 == 0
        and w_up.shape[1] % (128 * ctx) == 0
    )


def fused_kernel(
    sizes,
    img_h, cot_h, g1_a, b1_a, g2_a, b2_a, qg_a, kg_a, wq_h, wk_h, wv_h, wo_h, wup_h, wdn_h,
    bo_o, ig_o, upo, dno, qkvo, lnr_o, qkr_o, peak_o,
    xg, ctg, smalls, wl, wol, wkv, wqp, wop, wqb, wob, wup, wdt, h1_t, h2_t, ct_t,
    xh1, h1, nq, nk, sq, sk, qs, kall, vall, pst, sbuf, attq, brs, brr, pks,
    ptop, dsb,
    h2, ga, act, gu, g2s, g2r, g2own, bos, bor, boown,
    gsib_s, gsib_r, gkeep, gz_s, gz_r, gfin,
    gres, gbg, dqb, dkt, dvt, dks_s, dks_r, dqr, dkv,
    g1s, g1r, g1own, qsib_s, qsib_r, qown, qz_s, qz_r, qfin,
    rows_s, rows_r, obuf, g1_h, b1_h, g2_h, b2_h, qg_h, kg_h, lnr_v, qkr_v, peak_v,
    lsem, ssem, rsem,
):
    CN, ZN, TB, D, HW, FS, R = sizes
    HR = R // 2
    s_i, c_i, t_i = lax.axis_index("shard"), lax.axis_index("ctx"), lax.axis_index("tp")
    o_i = 1 - t_i
    half_chips = CN // 2
    tstar = c_i // half_chips
    place = c_i % half_chips
    TK = CN * TB
    inv_d = 1.0 / D

    def at_ctx(j):
        return (s_i, flip(c_i, j, CN), t_i)

    def at_z(j):
        return (flip(s_i, j, ZN), c_i, t_i)

    sib = (s_i, c_i, o_i)

    outer = (s_i == 0) | (s_i == ZN - 1)
    pair = flip(s_i, 1, ZN)
    far_in = flip(s_i, 3, ZN) * (1 - outer) + flip(s_i, 2, ZN) * outer
    far_out = flip(s_i, 2, ZN) * (1 - outer) + flip(s_i, 3, ZN) * outer

    def plane(z):
        return (z, c_i, t_i)

    arrivals, leavings = {}, {}
    from_one = ("x", "small", "br", "h2", "g2", "qz0", "qz1", "qz2", "rz", "pkz", "rc", "pkc",
                "ct", "gb", "bo", "g1", "gc0", "gc1")
    apart = ("wd", "wu", "gs", "dk", "qg", "ob")

    def spot(name, count):
        if name not in arrivals:
            first = sum(n for _, n in arrivals.values())
            skip = 1 if name in from_one else 0
            arrivals[name] = (first - skip, count - skip)
        return arrivals[name][0]

    def arrival(name, count, j):
        return rsem.at[spot(name, count) + j]

    def leaving(name, count, j):
        if name not in leavings:
            leavings[name] = (sum(n for _, n in leavings.values()), count if name in apart else 1)
        return ssem.at[leavings[name][0] + (j if name in apart else 0)]

    def put_as(name, count, send, recv, src, dst, dev):
        pltpu.make_async_remote_copy(
            src_ref=src, dst_ref=dst, send_sem=leaving(name, count, send), recv_sem=arrival(name, count, recv),
            device_id=dev, device_id_type=MESH,
        ).start()

    def put(name, count, j, src, dst, dev):
        put_as(name, count, j, j, src, dst, dev)

    def got(name, count, j, dst, dev):
        pltpu.make_async_remote_copy(
            src_ref=dst, dst_ref=dst, send_sem=ssem.at[0], recv_sem=arrival(name, count, j),
            device_id=dev, device_id_type=MESH,
        ).wait_recv()

    def sent(name, count, j, src):
        pltpu.make_async_remote_copy(
            src_ref=src, dst_ref=src, send_sem=leaving(name, count, j), recv_sem=rsem.at[0],
            device_id=sib, device_id_type=MESH,
        ).wait_send()

    x_src = img_h.at[0, pl.ds(t_i * TB, TB)]
    c_src = cot_h.at[0, pl.ds(t_i * TB, TB)]
    locals_ = [
        pltpu.make_async_copy(wk_h, wl.at[1], lsem.at[0]),
        pltpu.make_async_copy(wv_h, wl.at[2], lsem.at[1]),
        pltpu.make_async_copy(wq_h, wl.at[0], lsem.at[2]),
        pltpu.make_async_copy(x_src, xg.at[0], lsem.at[3]),
        pltpu.make_async_copy(wo_h, wol, lsem.at[4]),
        pltpu.make_async_copy(wdn_h.at[:, pl.ds(c_i * FS, FS)], wdt.at[t_i, s_i], lsem.at[5]),
        pltpu.make_async_copy(wup_h.at[:, pl.ds(c_i * FS, FS)], wup.at[t_i, s_i], lsem.at[6]),
        pltpu.make_async_copy(c_src, ctg.at[0], lsem.at[7]),
    ]
    gains = [
        pltpu.make_async_copy(src, dst, lsem.at[16 + n])
        for n, (src, dst) in enumerate((
            (g1_a, g1_h), (b1_a, b1_h), (g2_a, g2_h), (b2_a, b2_h), (qg_a, qg_h), (kg_a, kg_h),
        ))
    ]
    for copy in gains + locals_:
        copy.start()

    barrier = pltpu.get_barrier_semaphore()
    greet = [at_ctx(j) for j in range(1, CN)] + [at_z(j) for j in range(1, ZN)] + [sib]
    for dev in greet:
        pl.semaphore_signal(barrier, inc=1, device_id=dev, device_id_type=MESH)

    for copy in gains:
        copy.wait()
    smalls[t_i, s_i] = jnp.zeros((8, 256), full_type)
    for k, ref in enumerate((g1_h, b1_h, g2_h, b2_h)):
        smalls[t_i, s_i, k:k + 1, :R] = ref[...].astype(full_type).reshape(1, R)
    heads = HW // 64
    piece = qg_h.shape[1]
    lane_of = lax.broadcasted_iota(jnp.int32, (piece, HW), 1)
    spread = (
        (lane_of % piece == lax.broadcasted_iota(jnp.int32, (piece, HW), 0)) & ((lane_of % 64) // piece == s_i)
    ).astype(full_type).astype(low_type)
    head_of = lax.broadcasted_iota(jnp.int32, (qg_h.shape[0], HW), 0)
    wanted = head_of == place * heads + lax.broadcasted_iota(jnp.int32, (qg_h.shape[0], HW), 1) // 64
    wanted = wanted & (t_i == tstar)
    for k, ref in ((4, qg_h), (5, kg_h)):
        row = jnp.sum(jnp.where(wanted, dot(ref[...], spread), 0.0), axis=0, keepdims=True)
        smalls[t_i, s_i, k:k + 1, :HW] = row

    pl.semaphore_wait(barrier, len(greet))

    for j in range(1, CN):
        put("x", CN, j, x_src, xg.at[j], at_ctx(j))
    for j in range(1, ZN):
        put("small", ZN, j, smalls.at[t_i, s_i], smalls.at[t_i, s_i], at_z(j))

    def picker(at, lanes, offset):
        rows = lax.broadcasted_iota(jnp.int32, (half_chips * HW, lanes), 0)
        cols = lax.broadcasted_iota(jnp.int32, (half_chips * HW, lanes), 1) - offset
        return ((rows == cols + at * HW) & (cols >= 0) & (cols < HW)).astype(full_type).astype(low_type)

    projections = (("wkv", wkv), ("wq", wqp), ("wo", wop))

    def send_projection(name, buf):
        for j in range(1, ZN):
            put(name, ZN, j, buf.at[s_i], buf.at[s_i], at_z(j))
        put(name, ZN, 0, buf.at[s_i], buf.at[s_i], sib)

    locals_[4].wait()

    @pl.when(t_i == tstar)
    def _():
        for n in range(3):
            locals_[n].wait()
        wkv[s_i] = (
            dot(wl[1], picker(place, 2 * HW, 0)) + dot(wl[2], picker(place, 2 * HW, HW))
        ).astype(low_type)
        send_projection(*projections[0])
        for source, packed in ((wl.at[0], wqp), (wol, wop)):
            packed[s_i] = (
                dot(source[:HR], picker(place, 2 * HW, 0)) + dot(source[HR:], picker(place, 2 * HW, HW))
            ).astype(low_type)

    @pl.when(t_i != tstar)
    def _():
        for n in range(3):
            locals_[n].wait()

    for j in range(1, ZN):
        got("small", ZN, j, smalls.at[t_i, flip(s_i, j, ZN)], at_z(j))
    put("smallt", 1, 0, smalls.at[t_i], smalls.at[t_i], sib)

    locals_[3].wait()

    def norm_rows(values):
        mean = jnp.sum(values, axis=-1, keepdims=True) * inv_d
        center = values - mean
        inverse = lax.rsqrt(jnp.sum(center * center, axis=-1, keepdims=True) * inv_d + norm_eps)
        return center * inverse, inverse

    ln_rows = jnp.concatenate([smalls[t_i, k][:, :R] for k in range(ZN)], axis=1)
    g1row, b1row, g2row, b2row = (ln_rows[k:k + 1] for k in range(4))

    def first_norm(j, _):
        @pl.when(j > 0)
        def _():
            got("x", CN, j, xg.at[j], at_ctx(j))

        for n in (1, 2):
            @pl.when((j == n) & (t_i == tstar))
            def _():
                send_projection(*projections[n])

        normed, _unused = norm_rows(xg[j].astype(full_type))
        xh1[j] = normed
        hidden = (normed * g1row + b1row).astype(low_type)
        h1[j] = hidden
        h1_t[:, pl.ds(pl.multiple_of(j * TB, TB), TB)] = hidden.T
        return 0

    HB = TB // 2

    def spread(name, src, dst_of):
        for j in (1, 2):
            put(name, 5, j, src, dst_of(j), at_ctx(j))

    def pass_on(name, buf):
        for j in (1, 2):
            got(name, 5, j, buf.at[j], at_ctx(j))
            half = pl.ds((j - 1) * HB, HB)
            put_as(name, 5, 2 + j, 2 + j, buf.at[j, half], buf.at[3, half], at_ctx(3 - j))

    def send_halves(name, src, land):
        for j in (1, 2):
            half = pl.ds((j - 1) * HB, HB)
            put_as(name, 5, 2 + j, 2 + j, src.at[3, half], land.at[3, half], at_ctx(j))

    def add_halves(name, src, land):
        for j in (1, 2):
            half = pl.ds((j - 1) * HB, HB)
            got(name, 5, 2 + j, land.at[3, half], at_ctx(j))
            src[3 - j, half] = (src[3 - j, half].astype(full_type) + land[3, half].astype(full_type)).astype(low_type)
        for j in (1, 2):
            put_as(name, 5, j, j, src.at[j], land.at[j], at_ctx(j))

    def have_rest(name, buf):
        for j in (1, 2):
            half = pl.ds((j - 1) * HB, HB)
            got(name, 5, 2 + j, buf.at[3, half], at_ctx(3 - j))

    spread("ct", c_src, lambda j: ctg.at[j])
    lax.fori_loop(0, CN, first_norm, 0)

    got("smallt", 1, 0, smalls.at[o_i], sib)
    head_rows = smalls[0, 0][4:6, :HW]
    for a in range(2):
        for k in range(ZN):
            if a or k:
                head_rows = head_rows + smalls[a, k][4:6, :HW]
    qgrow, kgrow = head_rows[0:1], head_rows[1:2]

    lane = lax.broadcasted_iota(jnp.int32, (1, HW), 1) // 64
    mask_f = [(lane == h).astype(full_type) for h in range(heads)]
    mask_b = [m.astype(low_type) for m in mask_f]
    same_head = (
        lax.broadcasted_iota(jnp.int32, (HW, HW), 0) // 64
        == lax.broadcasted_iota(jnp.int32, (HW, HW), 1) // 64
    ).astype(full_type).astype(low_type)

    def head_mean(values):
        high = values.astype(low_type)
        rest = (values - high.astype(full_type)).astype(low_type)
        return (dot(high, same_head) + dot(rest, same_head)) * (1.0 / 64)

    def weight_ready(name, buf):
        @pl.when(t_i != tstar)
        def _():
            got(name, ZN, 0, buf.at[s_i], sib)

        for j in range(1, ZN):
            block = buf.at[flip(s_i, j, ZN)]
            got(name, ZN, j, block, sib)

            @pl.when(t_i == tstar)
            def _():
                pltpu.make_async_remote_copy(
                    src_ref=block, dst_ref=block,
                    send_sem=leaving("f" + name, ZN, j), recv_sem=arrival(name, ZN, j),
                    device_id=sib, device_id_type=MESH,
                ).start()

    def unpack(packed, buf):
        for z in range(ZN):
            block = packed[z]
            buf[z, :HR] = block[:, :HW]
            buf[z, HR:] = block[:, HW:]

    h1_all = h1[...].reshape(TK, D)
    weight_ready(*projections[0])
    raw = dot(h1_all, wkv[...].reshape(D, 2 * HW))
    vall[0] = raw[:, HW:].astype(low_type)
    put("v", 1, 0, vall.at[0], vall.at[1], sib)
    raw = raw[:, :HW]
    inverse = lax.rsqrt(head_mean(raw * raw) + norm_eps)
    normed = raw * inverse
    nk[...] = normed
    sk[...] = inverse
    kall[0] = (normed * kgrow).astype(low_type)
    put("k", 1, 0, kall.at[0], kall.at[1], sib)
    weight_ready(*projections[1])
    unpack(wqp, wqb)
    mlp_weights = (("wd", wdt), ("wu", wup))

    def own_mlp(name, buf):
        block = buf.at[t_i, s_i]
        put_as(name, 5, 0, 0, block, block, plane(pair))

        @pl.when(jnp.logical_not(outer))
        def _():
            put_as(name, 5, 1, 1, block, block, plane(far_in))

    def pass_mlp(name, buf, stage):
        source, target = ((pair, far_in), (far_in, pair), (far_out, pair))[stage]
        recv = (2, 1, 2)[stage]

        @pl.when(jnp.logical_not(outer))
        def _():
            block = buf.at[t_i, source]
            got(name, 5, stage, block, plane(pair))
            put_as(name, 5, 2 + stage, recv, block, block, plane(target))

    def have_mlp(name, buf):
        @pl.when(outer)
        def _():
            for n, z in enumerate((pair, far_in, far_out)):
                got(name, 5, n, buf.at[t_i, z], plane(pair))

    locals_[5].wait()
    own_mlp(*mlp_weights[0])
    locals_[6].wait()
    own_mlp(*mlp_weights[1])
    raw = dot(h1_all, wqb[...].reshape(D, HW))
    inverse = lax.rsqrt(head_mean(raw * raw) + norm_eps)
    normed = raw * inverse
    nq[...] = normed
    sq[...] = inverse
    qs[...] = ((normed * qgrow).astype(low_type) * 0.125).astype(low_type).reshape(CN, TB, HW)

    got("k", 1, 0, kall.at[1], sib)
    got("v", 1, 0, vall.at[1], sib)

    def stacked(block):
        return jnp.concatenate([block * m for m in mask_b], axis=0)

    def folded(block):
        total = block[0:TB] * mask_f[0]
        for h in range(1, heads):
            total = total + block[h * TB:(h + 1) * TB] * mask_f[h]
        return total

    ptop[...] = jnp.full(ptop.shape, -3.0e38, full_type)

    def attend(i, _):
        j = CN - 1 - i

        @pl.when(i == CN - 1)
        def _():
            pass_mlp(*mlp_weights[0], 0)
            pass_mlp(*mlp_weights[0], 1)

        sbuf[...] = dot(stacked(qs[j]), kall[...].reshape(2 * TK, HW), NT)
        for h in range(heads):
            rows = slice(h * TB, (h + 1) * TB)
            scores = sbuf[rows]
            ptop[h:h + 1] = jnp.maximum(ptop[h:h + 1], jnp.max(scores, axis=0, keepdims=True))
            expo = jnp.exp(scores)
            pst[j, rows] = expo * (1.0 / jnp.sum(expo, axis=-1, keepdims=True))
        mixed = folded(dot(pst[j].astype(low_type), vall[...].reshape(2 * TK, HW)))
        attq[j] = mixed.astype(low_type)

        @pl.when(i == 0)
        def _():
            weight_ready(*projections[2])
            unpack(wop, wob)

        branch = dot(attq[j], wob[...].reshape(D, HW), NT)

        @pl.when(j > 0)
        def _():
            brs[j] = branch.astype(low_type)
            put("br", CN, j, brs.at[j], brr.at[j], at_ctx(j))

        @pl.when(j == 0)
        def _():
            boown[...] = branch

        return 0

    lax.fori_loop(0, CN, attend, 0)
    pass_mlp(*mlp_weights[1], 0)
    pass_mlp(*mlp_weights[1], 1)
    pass_on("ct", ctg)
    pass_mlp(*mlp_weights[0], 2)
    peak_rows = jnp.max(ptop[...], axis=-1, keepdims=True)
    lane_id = lax.broadcasted_iota(jnp.int32, (8, 128), 1)
    own_peak = jnp.full((8, 128), -3.0e38, full_type)
    for h in range(heads):
        own_peak = jnp.where(lane_id == c_i * heads + h, peak_rows[h:h + 1], own_peak)
    pks[0] = own_peak
    put("pkt", 1, 0, pks.at[0], pks.at[1], sib)

    branch = boown[...]
    for j in (3, 2, 1):
        if j == 1:
            pass_mlp(*mlp_weights[1], 2)
        got("br", CN, j, brr.at[j], at_ctx(j))
        branch = branch + brr[j].astype(full_type)
    resid = xg[0].astype(full_type) + branch
    boown[...] = resid
    xhat2, inv2 = norm_rows(resid)
    h2[0] = (xhat2 * g2row + b2row).astype(low_type)
    for j in range(1, CN):
        put("h2", CN, j, h2.at[0], h2.at[j], at_ctx(j))

    locals_[7].wait()
    have_rest("ct", ctg)
    ct_t[...] = ctg[...].reshape(TK, D).T
    have_mlp(*mlp_weights[0])
    put("wdt", 1, 0, wdt.at[t_i], wdt.at[t_i], sib)
    ga[t_i] = dot(ctg[...].reshape(TK, D), wdt[t_i].reshape(D, FS)).reshape(CN, TB, FS)
    have_mlp(*mlp_weights[1])
    put("wut", 1, 0, wup.at[t_i], wup.at[t_i], sib)
    got("wdt", 1, 0, wdt.at[o_i], sib)
    ga[o_i] = dot(ctg[...].reshape(TK, D), wdt[o_i].reshape(D, FS)).reshape(CN, TB, FS)
    got("wut", 1, 0, wup.at[o_i], sib)

    def mlp(j, _):
        @pl.when(j > 0)
        def _():
            got("h2", CN, j, h2.at[j], at_ctx(j))

        block = h2[j]
        h2_t[:, pl.ds(pl.multiple_of(j * TB, TB), TB)] = block.T
        for a in range(2):
            up = dot(block, wup[a].reshape(D, FS))
            phi = 0.5 * (1.0 + lax.erf(up * 0.7071067811865476))
            dens = jnp.exp(up * up * -0.5) * 0.3989422804014327
            part = slice(a * FS, (a + 1) * FS)
            act[j, :, part] = (up * phi).astype(low_type)
            gu[j, :, part] = (ga[a, j] * (phi + up * dens)).astype(low_type)
        grad_two = (
            dot(gu[j, :, :FS], wup[0].reshape(D, FS), NT) + dot(gu[j, :, FS:], wup[1].reshape(D, FS), NT)
        )

        @pl.when(j == 0)
        def _():
            g2own[...] = grad_two

        @pl.when(j > 0)
        def _():
            g2s[j] = grad_two.astype(low_type)
            put("g2", CN, j, g2s.at[j], g2r.at[j], at_ctx(j))

        return 0

    lax.fori_loop(0, CN, mlp, 0)

    got("pkt", 1, 0, pks.at[1], sib)
    pks[2] = jnp.maximum(pks[0], pks[1])
    for j in range(1, ZN):
        put("pkz", ZN, j, pks.at[2], pks.at[2 + j], at_z(j))
    own_part = pl.ds(pl.multiple_of(t_i * FS, FS), FS)
    other_part = pl.ds(pl.multiple_of(o_i * FS, FS), FS)
    pairs = ((h2_t, gu), (ct_t, act))
    for k, (left, right) in enumerate(pairs):
        gsib_s[k] = dot(left[...], right[:, :, other_part].reshape(TK, FS)).astype(low_type)
        put("gs", 2, k, gsib_s.at[k], gsib_r.at[k], sib)

    def send_far(k):
        @pl.when(outer)
        def _():
            put("gz%d" % k, 4, 2, gz_s.at[k, far_out], gz_r.at[k, 2], plane(pair))
            put("gz%d" % k, 4, 3, gz_s.at[k, far_in], gz_r.at[k, 3], plane(pair))

    def send_near(k):
        put("gz%d" % k, 4, 0, gz_s.at[k, pair], gz_r.at[k, 0], plane(pair))

    own_grads = [dot(left[...], right[:, :, own_part].reshape(TK, FS)) for left, right in pairs]
    for k in range(2):
        got("gs", 2, k, gsib_r.at[k], sib)
        total = own_grads[k] + gsib_r[k].astype(full_type)
        gkeep[k] = total
        gz_s[k] = total.astype(low_type).reshape(ZN, R, FS)
        send_far(k)
    send_near(0)
    send_near(1)

    def down(j, _):
        part = (
            dot(act[j, :, :FS], wdt[0].reshape(D, FS), NT) + dot(act[j, :, FS:], wdt[1].reshape(D, FS), NT)
        )

        @pl.when(j == 0)
        def _():
            boown[...] += part

        @pl.when(j > 0)
        def _():
            bos[j] = part.astype(low_type)

        return 0

    lax.fori_loop(0, CN, down, 0)

    def relay_mlp(k):
        @pl.when(jnp.logical_not(outer))
        def _():
            for n, z in ((2, far_out), (3, far_in)):
                got("gz%d" % k, 4, n, gz_r.at[k, n], plane(pair))
                mine_part = gkeep[k, pl.ds(pl.multiple_of(z * R, R), R)]
                gz_s[k, z] = (mine_part + gz_r[k, n].astype(full_type)).astype(low_type)
                put_as("gz%d" % k, 4, n, 1, gz_s.at[k, z], gz_r.at[k, 1], plane(z))

    def share_mlp(k, out):
        total = gkeep[k, pl.ds(pl.multiple_of(s_i * R, R), R)]
        for n in range(2):
            got("gz%d" % k, 4, n, gz_r.at[k, n], plane(pair))
            total = total + gz_r[k, n].astype(full_type)
        gfin[k] = total.astype(low_type)
        spread("gc%d" % k, gfin.at[k], lambda j: out.at[c_i])
        pltpu.make_async_copy(gfin.at[k], out.at[c_i], lsem.at[8 + k]).start()

    grad_two = g2own[...]
    for j in range(1, CN):
        got("g2", CN, j, g2r.at[j], at_ctx(j))
        grad_two = grad_two + g2r[j].astype(full_type)
    ln2g = jnp.sum(grad_two * xhat2, axis=0, keepdims=True)
    ln2b = jnp.sum(grad_two, axis=0, keepdims=True)
    hat = grad_two * g2row
    grad_resid = ctg[0].astype(full_type) + inv2 * (
        hat
        - jnp.sum(hat, axis=-1, keepdims=True) * inv_d
        - xhat2 * (jnp.sum(hat * xhat2, axis=-1, keepdims=True) * inv_d)
    )
    gres[...] = grad_resid
    gb = grad_resid.astype(low_type)
    gbg[0] = gb
    spread("gb", gbg.at[0], lambda j: gbg.at[j])
    send_halves("bo", bos, bor)

    peak = pks[2]
    for j in range(1, ZN):
        got("pkz", ZN, j, pks.at[2 + j], at_z(j))
        peak = jnp.maximum(peak, pks[2 + j])
    first = 2 + ZN
    pks[first] = peak
    for j in range(1, CN):
        put("pkc", CN, j, pks.at[first], pks.at[first + j], at_ctx(j))

    dkt[...] = jnp.zeros_like(dkt)
    dvt[...] = jnp.zeros_like(dvt)

    def attend_back(j, _):
        @pl.when(j == 1)
        def _():
            relay_mlp(0)
            pass_on("gb", gbg)

        @pl.when(j == CN - 1)
        def _():
            add_halves("bo", bos, bor)
            have_rest("gb", gbg)

        grad_rows = stacked(dot(gbg[j], wob[...].reshape(D, HW)).astype(low_type))
        query_rows = stacked(qs[j])
        sbuf[...] = dot(grad_rows, vall[...].reshape(2 * TK, HW), NT)

        for h in range(heads):
            rows = slice(h * TB, (h + 1) * TB)
            probs, grad_probs = pst[j, rows], sbuf[rows]
            inner = jnp.sum(probs * grad_probs, axis=-1, keepdims=True)
            dsb[rows] = (probs * (grad_probs - inner)).astype(low_type)
        grad_scores = dsb[...]
        dqb[j] = folded(dot(grad_scores, kall[...].reshape(2 * TK, HW))) * 0.125
        dvt[...] += dot(grad_rows, pst[j].astype(low_type), TN)
        dkt[...] += dot(query_rows, grad_scores, TN)
        return 0

    lax.fori_loop(0, CN, attend_back, 0)
    dks_s[0] = dvt[:, TK:].astype(low_type)
    dks_s[1] = dkt[:, TK:].astype(low_type)
    for k in range(2):
        put("dk", 2, k, dks_s.at[k], dks_r.at[k], sib)

    for j in range(1, CN):
        got("pkc", CN, j, pks.at[first + j], at_ctx(j))
        peak = jnp.maximum(peak, pks[first + j])
    peak_v[...] = peak
    pltpu.make_async_copy(peak_v, peak_o, lsem.at[22]).start()

    relay_mlp(1)
    share_mlp(0, upo)
    def unnorm(grad_n, gain_row, normed, inverse):
        gain_grad = jnp.sum(grad_n * normed, axis=0, keepdims=True)
        e = grad_n * gain_row
        return (inverse * (e - normed * head_mean(e * normed))).astype(low_type), gain_grad

    def share_grad(n, full):
        full = full.reshape(ZN, 2, HR, 2 * HW)
        low_full = full.astype(low_type)
        for k in range(2):
            @pl.when(o_i == k)
            def _():
                qsib_s[n] = low_full[:, k]

            @pl.when(t_i == k)
            def _():
                qown[n] = full[:, k]

        put("qg", 2, n, qsib_s.at[n], qsib_r.at[n], sib)

    pieces = {1: (("qz1", 0, HR),), 0: (("qz0", 0, HR // 2), ("qz2", HR // 2, HR // 2))}

    def reduce_grad(n):
        got("qg", 2, n, qsib_r.at[n], sib)
        total = qown[n] + qsib_r[n].astype(full_type)
        qown[n] = total
        qz_s[n] = total.astype(low_type)
        for name, first, count in pieces[n]:
            rows = pl.ds(first, count)
            for j in range(1, ZN):
                put(name, ZN, j, qz_s.at[n, flip(s_i, j, ZN), rows], qz_r.at[n, j, rows], at_z(j))

    grad_raw, q_gain_row = unnorm(dqb[...].reshape(TK, HW), qgrow, nq[...], sq[...])
    dqr[...] = grad_raw
    empty = jnp.zeros((TK, HW), low_type)
    share_grad(1, (
        dot(h1_t[...], jnp.concatenate([dqr[...], empty], axis=1))
        + dot(gbg[...].reshape(TK, D), jnp.concatenate([empty, attq[...].reshape(TK, HW)], axis=1), TN)
    ))
    got("dk", 2, 0, dks_r.at[0], sib)
    grad_v = (dvt[:, :TK] + dks_r[0].astype(full_type)).T.astype(low_type)
    got("dk", 2, 1, dks_r.at[1], sib)
    grad_k = (dkt[:, :TK] + dks_r[1].astype(full_type)).T
    grad_raw, k_gain_row = unnorm(grad_k, kgrow, nk[...], sk[...])
    dkv[...] = jnp.concatenate([grad_raw, grad_v], axis=1)
    ln1g = jnp.zeros((1, D), full_type)
    ln1b = jnp.zeros((1, D), full_type)
    for j in range(CN - 1, -1, -1):
        rows = slice(j * TB, (j + 1) * TB)
        part = dot(dqr[rows], wqb[...].reshape(D, HW), NT) + dot(dkv[rows], wkv[...].reshape(D, 2 * HW), NT)
        if j:
            g1s[j] = part.astype(low_type)
        else:
            g1own[...] = part
        if j == 3:
            send_halves("g1", g1s, g1r)
            share_grad(0, dot(h1_t[...], dkv[...]))
            reduce_grad(1)
        ln1g = ln1g + jnp.sum(part * xh1[j], axis=0, keepdims=True)
        ln1b = ln1b + jnp.sum(part, axis=0, keepdims=True)
        if j == 1:
            reduce_grad(0)
    rows_s[0] = jnp.zeros_like(rows_s[0])
    HD2 = D // 2
    for k, row in enumerate((ln1g, ln1b, ln2g, ln2b)):
        rows_s[0, 2 * k:2 * k + 1, :HD2] = row[:, :HD2]
        rows_s[0, 2 * k + 1:2 * k + 2, :HD2] = row[:, HD2:]
    rows_s[0, 0:1, HD2:HD2 + HW] = q_gain_row
    rows_s[0, 1:2, HD2:HD2 + HW] = k_gain_row
    put("rt", 1, 0, rows_s.at[0], rows_r.at[0], sib)
    add_halves("g1", g1s, g1r)
    share_mlp(1, dno)
    got("rt", 1, 0, rows_r.at[0], sib)
    rows_s[1] = rows_s[0] + rows_r[0]
    for j in range(1, ZN):
        put("rz", ZN, j, rows_s.at[1], rows_r.at[j], at_z(j))

    total = boown[...]
    for j in (1, 2):
        got("bo", 5, j, bor.at[j], at_ctx(j))
        total = total + bor[j].astype(full_type)
    own_rows = pl.ds(t_i * TB, TB)
    obuf[0] = total.astype(low_type)
    put("ob", 2, 0, obuf.at[0], bo_o.at[own_rows], sib)
    pltpu.make_async_copy(obuf.at[0], bo_o.at[own_rows], lsem.at[10]).start()

    def to_owner(name, first, count, n):
        rows = pl.ds(first, count)
        return qfin.at[n, rows], qkvo.at[place, t_i, n, rows]

    def share_fin(n, which=slice(None)):
        for name, first, count in pieces[n][which]:
            rows = slice(first, first + count)
            total = qown[n, s_i, rows]
            for j in range(1, ZN):
                got(name, ZN, j, qz_r.at[n, j, pl.ds(first, count)], at_z(j))
                total = total + qz_r[n, j, rows].astype(full_type)
            qfin[n, rows] = total.astype(low_type)
            src, dst = to_owner(name, first, count, n)
            slot = spot("r" + name, 2 * half_chips) + place * 2 + t_i
            for j in range(1, CN):
                pltpu.make_async_remote_copy(
                    src_ref=src, dst_ref=dst,
                    send_sem=leaving("s" + name, CN, j), recv_sem=rsem.at[slot],
                    device_id=(s_i, flip(c_i, j, CN), tstar), device_id_type=MESH,
                ).start()

            @pl.when(t_i == tstar)
            def _():
                pltpu.make_async_copy(src, dst, lsem.at[12 + (name == "qz2") * 2 + n]).start()

            @pl.when(t_i != tstar)
            def _():
                pltpu.make_async_remote_copy(
                    src_ref=src, dst_ref=dst,
                    send_sem=leaving("o" + name, 1, 0), recv_sem=rsem.at[slot],
                    device_id=sib, device_id_type=MESH,
                ).start()

    def pass_grad(k, out):
        for j in (1, 2):
            block = out.at[flip(c_i, j, CN)]
            got("gc%d" % k, 5, j, block, at_ctx(j))
            half = block.at[pl.ds((j - 1) * HR, HR)]
            put_as("gc%d" % k, 5, 2 + j, 2 + j, half, half, at_ctx(3 - j))

    share_fin(1)
    pass_grad(0, upo)

    xhat1, inv1 = norm_rows(xg[0].astype(full_type))
    grad_one = g1own[...]
    for j in (1, 2):
        got("g1", 5, j, g1r.at[j], at_ctx(j))
        grad_one = grad_one + g1r[j].astype(full_type)
    hat = grad_one * g1row
    grad_in = gres[...] + inv1 * (
        hat
        - jnp.sum(hat, axis=-1, keepdims=True) * inv_d
        - xhat1 * (jnp.sum(hat * xhat1, axis=-1, keepdims=True) * inv_d)
    )
    obuf[1] = grad_in.astype(low_type)
    put("ob", 2, 1, obuf.at[1], ig_o.at[own_rows], sib)
    pltpu.make_async_copy(obuf.at[1], ig_o.at[own_rows], lsem.at[11]).start()

    pass_grad(1, dno)
    share_fin(0, slice(0, 1))

    rows_sum = rows_s[1]
    for j in range(1, ZN):
        got("rz", ZN, j, rows_r.at[j], at_z(j))
        rows_sum = rows_sum + rows_r[j]
    rows_s[2] = rows_sum
    for j in range(1, CN):
        put("rc", CN, j, rows_s.at[2], rows_r.at[ZN + j], at_ctx(j))
    qkr_v[c_i] = rows_sum[:, HD2:]

    share_fin(0, slice(1, 2))
    total = rows_sum[:, :HD2]
    for j in range(1, CN):
        got("rc", CN, j, rows_r.at[ZN + j], at_ctx(j))
        block = rows_r[ZN + j]
        total = total + block[:, :HD2]
        qkr_v[flip(c_i, j, CN)] = block[:, HD2:]
    lnr_v[...] = total
    pltpu.make_async_copy(lnr_v, lnr_o, lsem.at[23]).start()
    pltpu.make_async_copy(qkr_v, qkr_o, lsem.at[24]).start()

    for n, (src, dst) in enumerate(((peak_v, peak_o), (lnr_v, lnr_o), (qkr_v, qkr_o))):
        pltpu.make_async_copy(src, dst, lsem.at[22 + n]).wait()
    for k, out in ((0, upo), (1, dno)):
        for j in (1, 2):
            half = out.at[flip(c_i, 3, CN), pl.ds((j - 1) * HR, HR)]
            got("gc%d" % k, 5, 2 + j, half, at_ctx(3 - j))
        pltpu.make_async_copy(gfin.at[k], out.at[c_i], lsem.at[8 + k]).wait()
    other_rows = pl.ds(o_i * TB, TB)
    for k, out in ((0, bo_o), (1, ig_o)):
        got("ob", 2, k, out.at[other_rows], sib)
        pltpu.make_async_copy(obuf.at[k], out.at[own_rows], lsem.at[10 + k]).wait()

    all_pieces = [(name, first, count, n) for n in pieces for name, first, count in pieces[n]]

    @pl.when(t_i == tstar)
    def _():
        for name, first, count, n in all_pieces:
            src, dst = to_owner(name, first, count, n)
            pltpu.make_async_copy(src, dst, lsem.at[12 + (name == "qz2") * 2 + n]).wait()

    for p in range(half_chips):
        for a in range(2):
            @pl.when((t_i != tstar) | (place != p) | (t_i != a))
            def _():
                for name, first, count, n in all_pieces:
                    rows = pl.ds(first, count)
                    pltpu.make_async_remote_copy(
                        src_ref=qfin.at[n, rows], dst_ref=qkvo.at[p, a, n, rows],
                        send_sem=ssem.at[0],
                        recv_sem=rsem.at[spot("r" + name, 2 * half_chips) + p * 2 + a],
                        device_id=sib, device_id_type=MESH,
                    ).wait_recv()

    three = pl.ds(1, 3)
    for name, ref in (
        ("x", xg), ("br", brs), ("h2", h2), ("g2", g2s), ("pkc", pks), ("rc", rows_r), ("small", smalls.at[t_i]),
        ("pkz", pks), ("rz", rows_r), ("ct", ctg), ("gb", gbg), ("bo", bos), ("g1", g1s),
        ("gc0", gz_s.at[0]), ("gc1", gz_s.at[1]), ("gz0", gz_s.at[0]), ("gz1", gz_s.at[1]),
    ):
        sent(name, 5, 0, ref.at[three])
    for name, first, count, n in all_pieces:
        for way in ("", "s"):
            sent(way + name, 4, 0, qz_s.at[n, three, pl.ds(first, count)])
    for name, buf in mlp_weights:
        sent(name, 5, 0, buf.at[t_i, s_i])

        @pl.when(jnp.logical_not(outer))
        def _():
            for n in range(1, 5):
                sent(name, 5, n, buf.at[t_i, s_i])

    for name, ref in (
        ("smallt", smalls.at[t_i]), ("k", kall.at[0]), ("v", vall.at[0]), ("pkt", pks.at[0]),
        ("wdt", wdt.at[t_i]), ("wut", wup.at[t_i]), ("rt", rows_s.at[0]),
    ):
        sent(name, 1, 0, ref)
    for k in range(2):
        sent("gs", 2, k, gsib_s.at[k])
        sent("dk", 2, k, dks_s.at[k])
        sent("ob", 2, k, obuf.at[k])
        sent("qg", 2, k, qsib_s.at[k])

    @pl.when(t_i == tstar)
    def _():
        for name, buf in projections:
            sent(name, ZN, 0, buf)
            sent("f" + name, ZN, 0, buf.at[three])

    @pl.when(t_i != tstar)
    def _():
        for name, first, count, n in all_pieces:
            sent("o" + name, 1, 0, qfin.at[n, pl.ds(first, count)])


ARRIVALS, LEAVINGS = 117, 57


def fused_call(sizes, *operands):
    CN, ZN, TB, D, HW, FS, R = sizes
    TK = CN * TB
    HR = R // 2
    half_chips = CN // 2
    heads = HW // 64
    lo, hi = low_type, full_type
    V = pltpu.VMEM
    any_spec = pl.BlockSpec(memory_space=pl.ANY)
    gain_shape = operands[6].shape
    out_shape = [
        jax.ShapeDtypeStruct((2 * TB, D), lo),
        jax.ShapeDtypeStruct((2 * TB, D), lo),
        jax.ShapeDtypeStruct((CN, R, FS), lo),
        jax.ShapeDtypeStruct((CN, R, FS), lo),
        jax.ShapeDtypeStruct((half_chips, 2, 2, HR, 2 * HW), lo),
        jax.ShapeDtypeStruct((8, D // 2), hi),
        jax.ShapeDtypeStruct((CN, 8, 256), hi),
        jax.ShapeDtypeStruct((8, 128), hi),
    ]
    scratch = [
        V((CN, TB, D), lo), V((CN, TB, D), lo), V((2, ZN, 8, 256), hi),
        V((3, R, half_chips * HW), lo), V((R, half_chips * HW), lo),
        V((ZN, R, 2 * HW), lo), V((ZN, HR, 2 * HW), lo), V((ZN, HR, 2 * HW), lo),
        V((ZN, R, HW), lo), V((ZN, R, HW), lo), V((2, ZN, R, FS), lo), V((2, ZN, R, FS), lo),
        V((D, TK), lo), V((D, TK), lo), V((D, TK), lo),
        V((CN, TB, D), hi), V((CN, TB, D), lo),
        V((TK, HW), hi), V((TK, HW), hi), V((TK, HW), hi), V((TK, HW), hi),
        V((CN, TB, HW), lo), V((2, TK, HW), lo), V((2, TK, HW), lo),
        V((CN, heads * TB, 2 * TK), hi), V((heads * TB, 2 * TK), hi),
        V((CN, TB, HW), lo), V((CN, TB, D), lo), V((CN, TB, D), lo), V((2 + ZN + CN, 8, 128), hi),
        V((heads, 2 * TK), hi), V((heads * TB, 2 * TK), lo),
        V((CN, TB, D), lo), V((2, CN, TB, FS), hi), V((CN, TB, 2 * FS), lo), V((CN, TB, 2 * FS), lo),
        V((CN, TB, D), lo), V((CN, TB, D), lo), V((TB, D), hi),
        V((CN, TB, D), lo), V((CN, TB, D), lo), V((TB, D), hi),
        V((2, D, FS), lo), V((2, D, FS), lo), V((2, D, FS), hi),
        V((2, ZN, R, FS), lo), V((2, ZN, R, FS), lo), V((2, R, FS), lo),
        V((TB, D), hi), V((CN, TB, D), lo),
        V((CN, TB, HW), hi), V((HW, 2 * TK), hi), V((HW, 2 * TK), hi),
        V((2, HW, TK), lo), V((2, HW, TK), lo), V((TK, HW), lo), V((TK, 2 * HW), lo),
        V((CN, TB, D), lo), V((CN, TB, D), lo), V((TB, D), hi),
        V((2, ZN, HR, 2 * HW), lo), V((2, ZN, HR, 2 * HW), lo), V((2, ZN, HR, 2 * HW), hi),
        V((2, ZN, HR, 2 * HW), lo), V((2, ZN, HR, 2 * HW), lo), V((2, HR, 2 * HW), lo),
        V((3, 8, D // 2 + 256), hi), V((ZN + CN, 8, D // 2 + 256), hi), V((2, TB, D), lo),
        V((R,), lo), V((R,), lo), V((R,), lo), V((R,), lo), V(gain_shape, lo), V(gain_shape, lo),
        V((8, D // 2), hi), V((CN, 8, 256), hi), V((8, 128), hi),
        pltpu.SemaphoreType.DMA((25,)), pltpu.SemaphoreType.DMA((LEAVINGS,)), pltpu.SemaphoreType.DMA((ARRIVALS,)),
    ]
    return pl.pallas_call(
        functools.partial(fused_kernel, sizes),
        out_shape=out_shape,
        in_specs=[any_spec] * 14,
        out_specs=[any_spec] * 8,
        scratch_shapes=scratch,
        compiler_params=pltpu.CompilerParams(
            collective_id=0, has_side_effects=True, vmem_limit_bytes=56 * 2**20
        ),
    )(*operands)


def finish_kernel(
    sizes,
    bo, ig, up_h, dn_h, qkvo_h, lnr_h, qkr_h, peak_h, wq_h, wk_h,
    bo_o, ig_o, l1g_o, l1b_o, l2g_o, l2b_o, qg_o, kg_o, gq_o, gk_o, gv_o, go_o, gu_o, gd_o, cq_o, ck_o,
    upo, dno, qkvo, lnr, qkr, peak, wq, wk, bov, igv, gq, gk, gv, go, gu, gd, cq, ck, l1g, l1b, l2g, l2b, qg, kg, isem, osem,
):
    CN, ZN, TB, D, HW, FS, R = sizes
    half_chips = CN // 2
    s_i, t_i = lax.axis_index("shard"), lax.axis_index("tp")
    ins = [
        pltpu.make_async_copy(src, dst, isem.at[n])
        for n, (src, dst) in enumerate((
            (qkvo_h, qkvo), (up_h, upo), (dn_h, dno), (peak_h, peak), (wq_h, wq), (wk_h, wk),
            (lnr_h, lnr), (qkr_h, qkr), (bo, bov), (ig, igv),
        ))
    ]
    for n in (1, 2, 0, 8, 9, 3, 4, 5, 6, 7):
        ins[n].start()
    outs = []

    def leave(src, dst):
        copy = pltpu.make_async_copy(src, dst, osem.at[len(outs)])
        copy.start()
        outs.append(copy)

    for n, grads, stage, out in ((1, upo, gu, gu_o), (2, dno, gd, gd_o)):
        ins[n].wait()
        for c in range(CN):
            stage[:, c * FS:(c + 1) * FS] = grads[c].astype(full_type)
        leave(stage, out)
    ins[0].wait()
    for n, first, stage, out in ((1, 0, gq, gq_o), (0, 0, gk, gk_o), (0, HW, gv, gv_o), (1, HW, go, go_o)):
        for a in range(2):
            parts = [qkvo[p, a, n][:, first:first + HW] for p in range(half_chips)]
            stage[a * (R // 2):(a + 1) * (R // 2)] = jnp.concatenate(parts, axis=1).astype(full_type)
        leave(stage, out)
    for n, stage, out in ((8, bov, bo_o), (9, igv, ig_o)):
        ins[n].wait()
        leave(stage, out)
    heads = HW // 64
    for n in (3, 4, 5):
        ins[n].wait()
    factor = jnp.sqrt(clip_level / jnp.maximum(peak[0:1], clip_level))
    here = half_chips * heads
    lanes = lax.broadcasted_iota(jnp.int32, (1, here * 64), 1) // 64
    ids = lax.broadcasted_iota(jnp.int32, (1, 128), 1)
    columns = jnp.ones((1, here * 64), full_type)
    for h in range(here):
        one = jnp.sum(jnp.where(ids == t_i * here + h, factor, 0.0), axis=-1, keepdims=True)
        columns = jnp.where(lanes == h, one, columns)
    for weights, stage, out in ((wq, cq, cq_o), (wk, ck, ck_o)):
        stage[...] = (weights[...].astype(full_type) * columns).astype(low_type)
        leave(stage, out)
    ins[6].wait()
    ins[7].wait()
    for k, (stage, out) in enumerate(((l1g, l1g_o), (l1b, l1b_o), (l2g, l2g_o), (l2b, l2b_o))):
        row = jnp.zeros((1, R), full_type)
        for z in range(ZN):
            at = z * R % (D // 2)
            source = 2 * k + z * R // (D // 2)
            row = jnp.where(s_i == z, lnr[source:source + 1, at:at + R], row)
        stage[...] = row.reshape(R)
        leave(stage, out)
    piece = qg.shape[1]
    for p in range(half_chips):
        chip = pltpu.roll(qkr[t_i * half_chips + p], (256 - s_i * piece) % 256, 1)
        for h in range(heads):
            for k, stage in ((0, qg), (1, kg)):
                stage[p * heads + h:p * heads + h + 1] = chip[k:k + 1, h * 64:h * 64 + piece]
    leave(qg, qg_o)
    leave(kg, kg_o)
    for copy in outs:
        copy.wait()


def fused_layer(
    images, cotangent, ln1_gain, ln1_bias, ln2_gain, ln2_bias, q_gain, k_gain,
    w_query, w_key, w_value, w_out, w_up, w_down,
):
    CN, ZN = lax.axis_size("ctx"), lax.axis_size("shard")
    TB = images.shape[1] // 2
    D = images.shape[2]
    R = w_query.shape[0]
    HW = w_query.shape[1] // (CN // 2)
    FS = w_up.shape[1] // CN
    sizes = (CN, ZN, TB, D, HW, FS, R)
    results = fused_call(
        sizes, images, cotangent, ln1_gain, ln1_bias, ln2_gain, ln2_bias, q_gain, k_gain,
        w_query, w_key, w_value, w_out.T, w_up, w_down.T,
    )
    row = jax.ShapeDtypeStruct((R,), full_type)
    gain = jax.ShapeDtypeStruct(q_gain.shape, full_type)
    square = jax.ShapeDtypeStruct(w_query.shape, full_type)
    wide = jax.ShapeDtypeStruct(w_up.shape, full_type)
    tokens = jax.ShapeDtypeStruct(images.shape[1:], low_type)
    clipped = jax.ShapeDtypeStruct(w_query.shape, low_type)
    lo, hi = low_type, full_type
    V = pltpu.VMEM
    any_spec = pl.BlockSpec(memory_space=pl.ANY)
    out = pl.pallas_call(
        functools.partial(finish_kernel, sizes),
        out_shape=[tokens] * 2 + [row] * 4 + [gain] * 2 + [square] * 4 + [wide] * 2 + [clipped] * 2,
        in_specs=[any_spec] * 10,
        out_specs=[any_spec] * 16,
        scratch_shapes=[
            V((CN, R, FS), lo), V((CN, R, FS), lo), V((CN // 2, 2, 2, R // 2, 2 * HW), lo), V((8, D // 2), hi),
            V((CN, 8, 256), hi), V((8, 128), hi), V(w_query.shape, lo), V(w_query.shape, lo),
            V(images.shape[1:], lo), V(images.shape[1:], lo),
        ]
        + [V(w_query.shape, hi)] * 4 + [V(w_up.shape, hi)] * 2 + [V(w_query.shape, lo)] * 2
        + [V((R,), hi)] * 4 + [V(q_gain.shape, hi)] * 2
        + [pltpu.SemaphoreType.DMA((10,)), pltpu.SemaphoreType.DMA((16,))],
        compiler_params=pltpu.CompilerParams(vmem_limit_bytes=60 * 2**20),
    )(*results, w_query, w_key)
    out = list(out)
    out[0], out[1] = out[0].reshape(images.shape), out[1].reshape(images.shape)
    out[11], out[13] = out[11].T, out[13].T
    return tuple(out)


def on_device(images, cotangent, ln1_gain, ln1_bias, ln2_gain, ln2_bias, q_gain, k_gain, *weights):
    fused = fits_fused(images, weights[0], weights[4], q_gain)
    layer = fused_layer if fused else general_layer
    return layer(images, cotangent, ln1_gain, ln1_bias, ln2_gain, ln2_bias, q_gain, k_gain, *weights)


def solution(mesh):
    return jax.shard_map(
        on_device,
        mesh=mesh,
        in_specs=(
            P("shard", "ctx", None),
            P("shard", "ctx", None),
            P("shard"),
            P("shard"),
            P("shard"),
            P("shard"),
            P("tp", "shard"),
            P("tp", "shard"),
            P("shard", "tp"),
            P("shard", "tp"),
            P("shard", "tp"),
            P("tp", "shard"),
            P("shard", "tp"),
            P("tp", "shard"),
        ),
        out_specs=(
            P("shard", "ctx", None),
            P("shard", "ctx", None),
            P("shard"),
            P("shard"),
            P("shard"),
            P("shard"),
            P("tp", "shard"),
            P("tp", "shard"),
            P("shard", "tp"),
            P("shard", "tp"),
            P("shard", "tp"),
            P("tp", "shard"),
            P("shard", "tp"),
            P("tp", "shard"),
            P("shard", "tp"),
            P("shard", "tp"),
        ),
        check_vma=False,
    )
```

```python
import functools
import jax
import jax.numpy as jnp
from jax import lax
from jax.experimental import pallas as pl
from jax.experimental.pallas import tpu as pltpu
from jax.sharding import PartitionSpec as P

norm_eps = 1e-06
clip_level = 0.5


def matmul(left, right):
    return jnp.dot(left, right, preferred_element_type=jnp.float32)


def norm_parts(values):
    center = values - jnp.mean(values, axis=-1, keepdims=True)
    inverse = lax.rsqrt(jnp.mean(center * center, axis=-1, keepdims=True) + norm_eps)
    return (center * inverse, inverse)


def norm_back(grad_hat, normed, inverse):
    return inverse * (
        grad_hat
        - jnp.mean(grad_hat, axis=-1, keepdims=True)
        - normed * jnp.mean(grad_hat * normed, axis=-1, keepdims=True)
    )


def head_scale(values, gain):
    inverse = lax.rsqrt(jnp.mean(values * values, axis=-1, keepdims=True) + norm_eps)
    return values * inverse * gain


def gelu_exact(values):
    return jax.nn.gelu(values, approximate=False)


def general_layer(
    images,
    cotangent,
    ln1_gain,
    ln1_bias,
    ln2_gain,
    ln2_bias,
    q_gain,
    k_gain,
    w_query,
    w_key,
    w_value,
    w_out,
    w_up,
    w_down,
):
    (
        full_query,
        full_key,
        full_value,
        full_up,
        full_out,
        full_down,
        gain_low_one,
        shift_low_one,
        gain_low_two,
        shift_low_two,
        query_gain_low,
        key_gain_low,
    ) = (
        lax.all_gather(w_query, "shard", axis=0, tiled=True),
        lax.all_gather(w_key, "shard", axis=0, tiled=True),
        lax.all_gather(w_value, "shard", axis=0, tiled=True),
        lax.all_gather(w_up, "shard", axis=0, tiled=True),
        lax.all_gather(w_out, "shard", axis=1, tiled=True),
        lax.all_gather(w_down, "shard", axis=1, tiled=True),
        lax.all_gather(ln1_gain, "shard", axis=0, tiled=True),
        lax.all_gather(ln1_bias, "shard", axis=0, tiled=True),
        lax.all_gather(ln2_gain, "shard", axis=0, tiled=True),
        lax.all_gather(ln2_bias, "shard", axis=0, tiled=True),
        lax.all_gather(q_gain, "shard", axis=1, tiled=True),
        lax.all_gather(k_gain, "shard", axis=1, tiled=True),
    )
    gain_one = gain_low_one.astype(jnp.float32)
    shift_one = shift_low_one.astype(jnp.float32)
    gain_two = gain_low_two.astype(jnp.float32)
    shift_two = shift_low_two.astype(jnp.float32)
    query_gain = query_gain_low.astype(jnp.float32)
    key_gain = key_gain_low.astype(jnp.float32)
    count_img, local_len, width = images.shape
    tokens = count_img * local_len
    heads_here, head_size = query_gain.shape
    local_width = heads_here * head_size
    full_len = local_len * lax.axis_size("ctx")
    group = 1
    groups = count_img // group
    scale = head_size ** (-0.5)
    flat = images.reshape(tokens, width).astype(jnp.float32)
    normed_one, inverse_one = norm_parts(flat)
    hidden_one = (normed_one * gain_one + shift_one).astype(jnp.bfloat16)
    query_raw = matmul(hidden_one, full_query).reshape(tokens, heads_here, head_size)
    key_raw = matmul(hidden_one, full_key).reshape(tokens, heads_here, head_size)
    query_norm = head_scale(query_raw, query_gain).astype(jnp.bfloat16)
    key_norm = head_scale(key_raw, key_gain).astype(jnp.bfloat16)
    value_low = matmul(hidden_one, full_value).astype(jnp.bfloat16)
    key_all, value_all = (
        lax.all_gather(
            key_norm.reshape(count_img, local_len, local_width), "ctx", axis=1, tiled=True
        ),
        lax.all_gather(
            value_low.reshape(count_img, local_len, local_width), "ctx", axis=1, tiled=True
        ),
    )
    query_grp = query_norm.reshape(groups, group, local_len, heads_here, head_size)
    key_grp = key_all.reshape(groups, group, full_len, heads_here, head_size)
    value_grp = value_all.reshape(groups, group, full_len, heads_here, head_size)

    def attend(pieces):
        query_blk, key_blk, value_blk = pieces
        scores = (
            jnp.einsum("gqhd,gkhd->ghqk", query_blk, key_blk, preferred_element_type=jnp.float32)
            * scale
        )
        top = jnp.max(scores, axis=-1, keepdims=True)
        expo = jnp.exp(scores - top)
        total = jnp.sum(expo, axis=-1, keepdims=True)
        probs = (expo / total).astype(jnp.bfloat16)
        mixed_blk = jnp.einsum(
            "ghqk,gkhd->gqhd", probs, value_blk, preferred_element_type=jnp.float32
        )
        return (mixed_blk, top + jnp.log(total), jnp.max(top, axis=(0, 2, 3)))

    mixed, log_total, group_peaks = lax.map(attend, (query_grp, key_grp, value_grp))
    local_peak = jnp.max(group_peaks, axis=0)
    peak_all = lax.pmax(local_peak, ("shard", "ctx"))
    attended = mixed.reshape(tokens, local_width).astype(jnp.bfloat16)
    branch_attn = lax.psum(matmul(attended, full_out), "tp")
    resid = flat + branch_attn
    normed_two, inverse_two = norm_parts(resid)
    hidden_two = (normed_two * gain_two + shift_two).astype(jnp.bfloat16)
    up_raw = matmul(hidden_two, full_up)
    active = gelu_exact(up_raw).astype(jnp.bfloat16)
    branch_mlp = lax.psum(matmul(active, full_down).astype(jnp.bfloat16), "tp").astype(jnp.float32)
    block_out = (resid + branch_mlp).astype(jnp.bfloat16).reshape(images.shape)
    grad_out = cotangent.reshape(tokens, width).astype(jnp.float32)
    grad_down = cotangent.reshape(tokens, width)
    grad_w_down = jnp.dot(active.T, grad_down, preferred_element_type=jnp.float32)
    grad_active = matmul(grad_down, full_down.T)
    unused_up, gelu_pull = jax.vjp(gelu_exact, up_raw)
    grad_up = gelu_pull(grad_active)[0].astype(jnp.bfloat16)
    grad_w_up = jnp.dot(hidden_two.T, grad_up, preferred_element_type=jnp.float32)
    grad_two = lax.psum(matmul(grad_up, full_up.T), "tp")
    grad_gain_two = jnp.sum(grad_two * normed_two, axis=0)
    grad_shift_two = jnp.sum(grad_two, axis=0)
    grad_resid = grad_out + norm_back(grad_two * gain_two, normed_two, inverse_two)
    grad_branch = grad_resid.astype(jnp.bfloat16)
    grad_w_out = jnp.dot(attended.T, grad_branch, preferred_element_type=jnp.float32)
    grad_mixed = matmul(grad_branch, full_out.T).astype(jnp.bfloat16)
    grad_grp = grad_mixed.reshape(groups, group, local_len, heads_here, head_size)

    def attend_back(pieces):
        query_blk, key_blk, value_blk, log_blk, grad_blk = pieces
        scores = (
            jnp.einsum("gqhd,gkhd->ghqk", query_blk, key_blk, preferred_element_type=jnp.float32)
            * scale
        )
        probs = jnp.exp(scores - log_blk)
        grad_probs = jnp.einsum(
            "gqhd,gkhd->ghqk", grad_blk, value_blk, preferred_element_type=jnp.float32
        )
        grad_scores = (
            probs * (grad_probs - jnp.sum(probs * grad_probs, axis=-1, keepdims=True))
        ).astype(jnp.bfloat16)
        grad_val = jnp.einsum(
            "ghqk,gqhd->gkhd",
            probs.astype(jnp.bfloat16),
            grad_blk,
            preferred_element_type=jnp.float32,
        )
        grad_qry = (
            jnp.einsum("ghqk,gkhd->gqhd", grad_scores, key_blk, preferred_element_type=jnp.float32)
            * scale
        )
        grad_kys = (
            jnp.einsum(
                "ghqk,gqhd->gkhd", grad_scores, query_blk, preferred_element_type=jnp.float32
            )
            * scale
        )
        return (grad_qry, grad_kys, grad_val)

    grad_query_n, grad_key_full, grad_value_full = lax.map(
        attend_back, (query_grp, key_grp, value_grp, log_total, grad_grp)
    )
    grad_key_n, grad_value_n = (
        lax.psum_scatter(
            grad_key_full.reshape(count_img, full_len, local_width),
            "ctx",
            scatter_dimension=1,
            tiled=True,
        ),
        lax.psum_scatter(
            grad_value_full.reshape(count_img, full_len, local_width),
            "ctx",
            scatter_dimension=1,
            tiled=True,
        ),
    )
    unused_query, query_pull = jax.vjp(head_scale, query_raw, query_gain)
    grad_query_raw, grad_query_gain = query_pull(
        grad_query_n.reshape(tokens, heads_here, head_size)
    )
    unused_key, key_pull = jax.vjp(head_scale, key_raw, key_gain)
    grad_key_raw, grad_key_gain = key_pull(grad_key_n.reshape(tokens, heads_here, head_size))
    grad_query_low = grad_query_raw.reshape(tokens, local_width).astype(jnp.bfloat16)
    grad_key_low = grad_key_raw.reshape(tokens, local_width).astype(jnp.bfloat16)
    grad_value_low = grad_value_n.reshape(tokens, local_width).astype(jnp.bfloat16)
    grad_w_query = jnp.dot(hidden_one.T, grad_query_low, preferred_element_type=jnp.float32)
    grad_w_key = jnp.dot(hidden_one.T, grad_key_low, preferred_element_type=jnp.float32)
    grad_w_value = jnp.dot(hidden_one.T, grad_value_low, preferred_element_type=jnp.float32)
    grad_one_part = (
        matmul(grad_query_low, full_query.T)
        + matmul(grad_key_low, full_key.T)
        + matmul(grad_value_low, full_value.T)
    )
    grad_one = lax.psum(grad_one_part, "tp")
    grad_gain_one = jnp.sum(grad_one * normed_one, axis=0)
    grad_shift_one = jnp.sum(grad_one, axis=0)
    input_grad = (
        (grad_resid + norm_back(grad_one * gain_one, normed_one, inverse_one))
        .astype(jnp.bfloat16)
        .reshape(images.shape)
    )
    (
        sum_query,
        sum_key,
        sum_value,
        sum_up,
        sum_out,
        sum_down,
        sum_gain_one,
        sum_shift_one,
        sum_gain_two,
        sum_shift_two,
        sum_qgain,
        sum_kgain,
    ) = lax.psum(
        (
            grad_w_query,
            grad_w_key,
            grad_w_value,
            grad_w_up,
            grad_w_out,
            grad_w_down,
            grad_gain_one,
            grad_shift_one,
            grad_gain_two,
            grad_shift_two,
            grad_query_gain,
            grad_key_gain,
        ),
        "ctx",
    )
    (
        part_query,
        part_key,
        part_value,
        part_up,
        part_out,
        part_down,
        part_gain_one,
        part_shift_one,
        part_gain_two,
        part_shift_two,
        part_qgain,
        part_kgain,
    ) = (
        lax.psum_scatter(sum_query, "shard", scatter_dimension=0, tiled=True),
        lax.psum_scatter(sum_key, "shard", scatter_dimension=0, tiled=True),
        lax.psum_scatter(sum_value, "shard", scatter_dimension=0, tiled=True),
        lax.psum_scatter(sum_up, "shard", scatter_dimension=0, tiled=True),
        lax.psum_scatter(sum_out, "shard", scatter_dimension=1, tiled=True),
        lax.psum_scatter(sum_down, "shard", scatter_dimension=1, tiled=True),
        lax.psum_scatter(sum_gain_one, "shard", scatter_dimension=0, tiled=True),
        lax.psum_scatter(sum_shift_one, "shard", scatter_dimension=0, tiled=True),
        lax.psum_scatter(sum_gain_two, "shard", scatter_dimension=0, tiled=True),
        lax.psum_scatter(sum_shift_two, "shard", scatter_dimension=0, tiled=True),
        lax.psum_scatter(sum_qgain, "shard", scatter_dimension=1, tiled=True),
        lax.psum_scatter(sum_kgain, "shard", scatter_dimension=1, tiled=True),
    )
    factor = jnp.sqrt(clip_level / jnp.maximum(peak_all, clip_level))
    columns = jnp.repeat(factor, head_size)
    query_clip = (w_query.astype(jnp.float32) * columns).astype(jnp.bfloat16)
    key_clip = (w_key.astype(jnp.float32) * columns).astype(jnp.bfloat16)
    return (
        block_out,
        input_grad,
        part_gain_one,
        part_shift_one,
        part_gain_two,
        part_shift_two,
        part_qgain,
        part_kgain,
        part_query,
        part_key,
        part_value,
        part_out,
        part_up,
        part_down,
        query_clip,
        key_clip,
    )


MESH = pl.DeviceIdType.MESH
NN = (((1,), (0,)), ((), ()))
NT = (((1,), (1,)), ((), ()))
TN = (((0,), (0,)), ((), ()))
low_type = jnp.bfloat16
full_type = jnp.float32


def dot(left, right, dims=NN):
    return lax.dot_general(left, right, dims, preferred_element_type=full_type)


def flip(place, bits, count):
    result = 0
    unit = 1
    while unit < count:
        result = result + ((place // unit + bits // unit) % 2) * unit
        unit *= 2
    return result


def fits_fused(images, w_query, w_up, q_gain):
    count_img, local_len, width = images.shape
    ctx, shard, tp = lax.axis_size("ctx"), lax.axis_size("shard"), lax.axis_size("tp")
    rows = w_query.shape[0]
    return (
        count_img == 1
        and tp == 2
        and ctx == 4
        and shard == 4
        and rows % (16 * ctx) == 0
        and local_len % 32 == 0
        and q_gain.shape[0] % 2 == 0
        and w_up.shape[1] % (128 * ctx) == 0
    )


def fused_kernel(
    sizes,
    img_h, cot_h, g1_a, b1_a, g2_a, b2_a, qg_a, kg_a, wq_h, wk_h, wv_h, wo_h, wup_h, wdn_h,
    bo_o, ig_o, upo, dno, qkvo, lnr_o, qkr_o, peak_o,
    xg, ctg, smalls, wl, wol, wkv, wqp, wop, wqb, wob, wup, wdt, h1_t, h2_t, ct_t,
    xh1, h1, nq, nk, sq, sk, qs, kall, vall, pst, sbuf, attq, brs, brr, pks,
    ptop, dsb,
    h2, ga, act, gu, g2s, g2r, g2own, bos, bor, boown,
    gsib_s, gsib_r, gkeep, gz_s, gz_r, gfin,
    gres, gbg, dqb, dkt, dvt, dks_s, dks_r, dqr, dkv,
    g1s, g1r, g1own, qsib_s, qsib_r, qown, qz_s, qz_r, qfin,
    rows_s, rows_r, obuf, g1_h, b1_h, g2_h, b2_h, qg_h, kg_h, lnr_v, qkr_v, peak_v,
    lsem, ssem, rsem,
):
    CN, ZN, TB, D, HW, FS, R = sizes
    HR = R // 2
    s_i, c_i, t_i = lax.axis_index("shard"), lax.axis_index("ctx"), lax.axis_index("tp")
    o_i = 1 - t_i
    half_chips = CN // 2
    tstar = c_i // half_chips
    place = c_i % half_chips
    TK = CN * TB
    inv_d = 1.0 / D

    def at_ctx(j):
        return (s_i, flip(c_i, j, CN), t_i)

    def at_z(j):
        return (flip(s_i, j, ZN), c_i, t_i)

    sib = (s_i, c_i, o_i)

    outer = (s_i == 0) | (s_i == ZN - 1)
    pair = flip(s_i, 1, ZN)
    far_in = flip(s_i, 3, ZN) * (1 - outer) + flip(s_i, 2, ZN) * outer
    far_out = flip(s_i, 2, ZN) * (1 - outer) + flip(s_i, 3, ZN) * outer

    def plane(z):
        return (z, c_i, t_i)

    arrivals, leavings = {}, {}
    from_one = ("x", "small", "br", "h2", "g2", "qz0", "qz2", "rz", "pkz", "rc", "pkc",
                "ct", "gb", "bo", "g1", "gc0", "gc1")
    apart = ("wd", "wu", "gs", "dk", "qg", "ob")

    def spot(name, count):
        if name not in arrivals:
            first = sum(n for _, n in arrivals.values())
            skip = 1 if name in from_one else 0
            arrivals[name] = (first - skip, count - skip)
        return arrivals[name][0]

    def arrival(name, count, j):
        return rsem.at[spot(name, count) + j]

    def leaving(name, count, j):
        if name not in leavings:
            leavings[name] = (sum(n for _, n in leavings.values()), count if name in apart else 1)
        return ssem.at[leavings[name][0] + (j if name in apart else 0)]

    def put_as(name, count, send, recv, src, dst, dev):
        pltpu.make_async_remote_copy(
            src_ref=src, dst_ref=dst, send_sem=leaving(name, count, send), recv_sem=arrival(name, count, recv),
            device_id=dev, device_id_type=MESH,
        ).start()

    def put(name, count, j, src, dst, dev):
        put_as(name, count, j, j, src, dst, dev)

    def got(name, count, j, dst, dev):
        pltpu.make_async_remote_copy(
            src_ref=dst, dst_ref=dst, send_sem=ssem.at[0], recv_sem=arrival(name, count, j),
            device_id=dev, device_id_type=MESH,
        ).wait_recv()

    def sent(name, count, j, src):
        pltpu.make_async_remote_copy(
            src_ref=src, dst_ref=src, send_sem=leaving(name, count, j), recv_sem=rsem.at[0],
            device_id=sib, device_id_type=MESH,
        ).wait_send()

    x_src = img_h.at[0, pl.ds(t_i * TB, TB)]
    c_src = cot_h.at[0, pl.ds(t_i * TB, TB)]
    locals_ = [
        pltpu.make_async_copy(wk_h, wl.at[1], lsem.at[0]),
        pltpu.make_async_copy(wv_h, wl.at[2], lsem.at[1]),
        pltpu.make_async_copy(wq_h, wl.at[0], lsem.at[2]),
        pltpu.make_async_copy(x_src, xg.at[0], lsem.at[3]),
        pltpu.make_async_copy(wo_h, wol, lsem.at[4]),
        pltpu.make_async_copy(wdn_h.at[:, pl.ds(c_i * FS, FS)], wdt.at[t_i, s_i], lsem.at[5]),
        pltpu.make_async_copy(wup_h.at[:, pl.ds(c_i * FS, FS)], wup.at[t_i, s_i], lsem.at[6]),
        pltpu.make_async_copy(c_src, ctg.at[0], lsem.at[7]),
    ]
    gains = [
        pltpu.make_async_copy(src, dst, lsem.at[16 + n])
        for n, (src, dst) in enumerate((
            (g1_a, g1_h), (b1_a, b1_h), (g2_a, g2_h), (b2_a, b2_h), (qg_a, qg_h), (kg_a, kg_h),
        ))
    ]
    for copy in gains + locals_:
        copy.start()

    barrier = pltpu.get_barrier_semaphore()
    greet = [at_ctx(j) for j in range(1, CN)] + [at_z(j) for j in range(1, ZN)] + [sib]
    for dev in greet:
        pl.semaphore_signal(barrier, inc=1, device_id=dev, device_id_type=MESH)

    for copy in gains:
        copy.wait()
    smalls[t_i, s_i] = jnp.zeros((8, 256), full_type)
    for k, ref in enumerate((g1_h, b1_h, g2_h, b2_h)):
        smalls[t_i, s_i, k:k + 1, :R] = ref[...].astype(full_type).reshape(1, R)
    heads = HW // 64
    piece = qg_h.shape[1]
    lane_of = lax.broadcasted_iota(jnp.int32, (piece, HW), 1)
    spread = (
        (lane_of % piece == lax.broadcasted_iota(jnp.int32, (piece, HW), 0)) & ((lane_of % 64) // piece == s_i)
    ).astype(full_type).astype(low_type)
    head_of = lax.broadcasted_iota(jnp.int32, (qg_h.shape[0], HW), 0)
    wanted = head_of == place * heads + lax.broadcasted_iota(jnp.int32, (qg_h.shape[0], HW), 1) // 64
    wanted = wanted & (t_i == tstar)
    for k, ref in ((4, qg_h), (5, kg_h)):
        row = jnp.sum(jnp.where(wanted, dot(ref[...], spread), 0.0), axis=0, keepdims=True)
        smalls[t_i, s_i, k:k + 1, :HW] = row

    pl.semaphore_wait(barrier, len(greet))

    for j in range(1, CN):
        put("x", CN, j, x_src, xg.at[j], at_ctx(j))
    for j in range(1, ZN):
        put("small", ZN, j, smalls.at[t_i, s_i], smalls.at[t_i, s_i], at_z(j))

    def picker(at, lanes, offset):
        rows = lax.broadcasted_iota(jnp.int32, (half_chips * HW, lanes), 0)
        cols = lax.broadcasted_iota(jnp.int32, (half_chips * HW, lanes), 1) - offset
        return ((rows == cols + at * HW) & (cols >= 0) & (cols < HW)).astype(full_type).astype(low_type)

    projections = (("wkv", wkv), ("wq", wqp), ("wo", wop))

    def send_projection(name, buf):
        for j in range(1, ZN):
            put(name, ZN, j, buf.at[s_i], buf.at[s_i], at_z(j))
        put(name, ZN, 0, buf.at[s_i], buf.at[s_i], sib)

    locals_[4].wait()

    @pl.when(t_i == tstar)
    def _():
        for n in range(3):
            locals_[n].wait()
        wkv[s_i] = (
            dot(wl[1], picker(place, 2 * HW, 0)) + dot(wl[2], picker(place, 2 * HW, HW))
        ).astype(low_type)
        send_projection(*projections[0])
        for source, packed in ((wl.at[0], wqp), (wol, wop)):
            packed[s_i] = (
                dot(source[:HR], picker(place, 2 * HW, 0)) + dot(source[HR:], picker(place, 2 * HW, HW))
            ).astype(low_type)

    @pl.when(t_i != tstar)
    def _():
        for n in range(3):
            locals_[n].wait()

    for j in range(1, ZN):
        got("small", ZN, j, smalls.at[t_i, flip(s_i, j, ZN)], at_z(j))
    put("smallt", 1, 0, smalls.at[t_i], smalls.at[t_i], sib)

    locals_[3].wait()

    def norm_rows(values):
        mean = jnp.sum(values, axis=-1, keepdims=True) * inv_d
        center = values - mean
        inverse = lax.rsqrt(jnp.sum(center * center, axis=-1, keepdims=True) * inv_d + norm_eps)
        return center * inverse, inverse

    ln_rows = jnp.concatenate([smalls[t_i, k][:, :R] for k in range(ZN)], axis=1)
    g1row, b1row, g2row, b2row = (ln_rows[k:k + 1] for k in range(4))

    def first_norm(j, _):
        @pl.when(j > 0)
        def _():
            got("x", CN, j, xg.at[j], at_ctx(j))

        for n in (1, 2):
            @pl.when((j == n) & (t_i == tstar))
            def _():
                send_projection(*projections[n])

        normed, _unused = norm_rows(xg[j].astype(full_type))
        xh1[j] = normed
        hidden = (normed * g1row + b1row).astype(low_type)
        h1[j] = hidden
        h1_t[:, pl.ds(pl.multiple_of(j * TB, TB), TB)] = hidden.T
        return 0

    HB = TB // 2

    def spread(name, src, dst_of):
        for j in (1, 2):
            put(name, 5, j, src, dst_of(j), at_ctx(j))

    def pass_on(name, buf):
        for j in (1, 2):
            got(name, 5, j, buf.at[j], at_ctx(j))
            half = pl.ds((j - 1) * HB, HB)
            put_as(name, 5, 2 + j, 2 + j, buf.at[j, half], buf.at[3, half], at_ctx(3 - j))

    def send_halves(name, src, land):
        for j in (1, 2):
            half = pl.ds((j - 1) * HB, HB)
            put_as(name, 5, 2 + j, 2 + j, src.at[3, half], land.at[3, half], at_ctx(j))

    def add_halves(name, src, land):
        for j in (1, 2):
            half = pl.ds((j - 1) * HB, HB)
            got(name, 5, 2 + j, land.at[3, half], at_ctx(j))
            src[3 - j, half] = (src[3 - j, half].astype(full_type) + land[3, half].astype(full_type)).astype(low_type)
        for j in (1, 2):
            put_as(name, 5, j, j, src.at[j], land.at[j], at_ctx(j))

    def have_rest(name, buf):
        for j in (1, 2):
            half = pl.ds((j - 1) * HB, HB)
            got(name, 5, 2 + j, buf.at[3, half], at_ctx(3 - j))

    spread("ct", c_src, lambda j: ctg.at[j])
    lax.fori_loop(0, CN, first_norm, 0)

    got("smallt", 1, 0, smalls.at[o_i], sib)
    head_rows = smalls[0, 0][4:6, :HW]
    for a in range(2):
        for k in range(ZN):
            if a or k:
                head_rows = head_rows + smalls[a, k][4:6, :HW]
    qgrow, kgrow = head_rows[0:1], head_rows[1:2]

    lane = lax.broadcasted_iota(jnp.int32, (1, HW), 1) // 64
    mask_f = [(lane == h).astype(full_type) for h in range(heads)]
    mask_b = [m.astype(low_type) for m in mask_f]
    same_head = (
        lax.broadcasted_iota(jnp.int32, (HW, HW), 0) // 64
        == lax.broadcasted_iota(jnp.int32, (HW, HW), 1) // 64
    ).astype(full_type).astype(low_type)

    def head_mean(values):
        high = values.astype(low_type)
        rest = (values - high.astype(full_type)).astype(low_type)
        return (dot(high, same_head) + dot(rest, same_head)) * (1.0 / 64)

    def weight_ready(name, buf):
        @pl.when(t_i != tstar)
        def _():
            got(name, ZN, 0, buf.at[s_i], sib)

        for j in range(1, ZN):
            block = buf.at[flip(s_i, j, ZN)]
            got(name, ZN, j, block, sib)

            @pl.when(t_i == tstar)
            def _():
                pltpu.make_async_remote_copy(
                    src_ref=block, dst_ref=block,
                    send_sem=leaving("f" + name, ZN, j), recv_sem=arrival(name, ZN, j),
                    device_id=sib, device_id_type=MESH,
                ).start()

    def unpack(packed, buf):
        for z in range(ZN):
            block = packed[z]
            buf[z, :HR] = block[:, :HW]
            buf[z, HR:] = block[:, HW:]

    h1_all = h1[...].reshape(TK, D)
    weight_ready(*projections[0])
    raw = dot(h1_all, wkv[...].reshape(D, 2 * HW))
    vall[0] = raw[:, HW:].astype(low_type)
    put("v", 1, 0, vall.at[0], vall.at[1], sib)
    raw = raw[:, :HW]
    inverse = lax.rsqrt(head_mean(raw * raw) + norm_eps)
    normed = raw * inverse
    nk[...] = normed
    sk[...] = inverse
    kall[0] = (normed * kgrow).astype(low_type)
    put("k", 1, 0, kall.at[0], kall.at[1], sib)
    weight_ready(*projections[1])
    unpack(wqp, wqb)
    mlp_weights = (("wd", wdt), ("wu", wup))

    def own_mlp(name, buf):
        block = buf.at[t_i, s_i]
        put_as(name, 5, 0, 0, block, block, plane(pair))

        @pl.when(jnp.logical_not(outer))
        def _():
            put_as(name, 5, 1, 1, block, block, plane(far_in))

    def pass_mlp(name, buf, stage):
        source, target = ((pair, far_in), (far_in, pair), (far_out, pair))[stage]
        recv = (2, 1, 2)[stage]

        @pl.when(jnp.logical_not(outer))
        def _():
            block = buf.at[t_i, source]
            got(name, 5, stage, block, plane(pair))
            put_as(name, 5, 2 + stage, recv, block, block, plane(target))

    def have_mlp(name, buf):
        @pl.when(outer)
        def _():
            for n, z in enumerate((pair, far_in, far_out)):
                got(name, 5, n, buf.at[t_i, z], plane(pair))

    locals_[5].wait()
    own_mlp(*mlp_weights[0])
    locals_[6].wait()
    own_mlp(*mlp_weights[1])
    raw = dot(h1_all, wqb[...].reshape(D, HW))
    inverse = lax.rsqrt(head_mean(raw * raw) + norm_eps)
    normed = raw * inverse
    nq[...] = normed
    sq[...] = inverse
    qs[...] = ((normed * qgrow).astype(low_type) * 0.125).astype(low_type).reshape(CN, TB, HW)

    got("k", 1, 0, kall.at[1], sib)
    got("v", 1, 0, vall.at[1], sib)

    def stacked(block):
        return jnp.concatenate([block * m for m in mask_b], axis=0)

    def folded(block):
        total = block[0:TB] * mask_f[0]
        for h in range(1, heads):
            total = total + block[h * TB:(h + 1) * TB] * mask_f[h]
        return total

    ptop[...] = jnp.full(ptop.shape, -3.0e38, full_type)

    def attend(i, _):
        j = CN - 1 - i

        @pl.when(i == CN - 1)
        def _():
            pass_mlp(*mlp_weights[0], 0)
            pass_mlp(*mlp_weights[0], 1)

        sbuf[...] = dot(stacked(qs[j]), kall[...].reshape(2 * TK, HW), NT)
        for h in range(heads):
            rows = slice(h * TB, (h + 1) * TB)
            scores = sbuf[rows]
            ptop[h:h + 1] = jnp.maximum(ptop[h:h + 1], jnp.max(scores, axis=0, keepdims=True))
            expo = jnp.exp(scores)
            pst[j, rows] = expo * (1.0 / jnp.sum(expo, axis=-1, keepdims=True))
        mixed = folded(dot(pst[j].astype(low_type), vall[...].reshape(2 * TK, HW)))
        attq[j] = mixed.astype(low_type)

        @pl.when(i == 0)
        def _():
            weight_ready(*projections[2])
            unpack(wop, wob)

        branch = dot(attq[j], wob[...].reshape(D, HW), NT)

        @pl.when(j > 0)
        def _():
            brs[j] = branch.astype(low_type)
            put("br", CN, j, brs.at[j], brr.at[j], at_ctx(j))

        @pl.when(j == 0)
        def _():
            boown[...] = branch

        return 0

    lax.fori_loop(0, CN, attend, 0)
    pass_mlp(*mlp_weights[1], 0)
    pass_mlp(*mlp_weights[1], 1)
    pass_on("ct", ctg)
    pass_mlp(*mlp_weights[0], 2)
    peak_rows = jnp.max(ptop[...], axis=-1, keepdims=True)
    lane_id = lax.broadcasted_iota(jnp.int32, (8, 128), 1)
    own_peak = jnp.full((8, 128), -3.0e38, full_type)
    for h in range(heads):
        own_peak = jnp.where(lane_id == c_i * heads + h, peak_rows[h:h + 1], own_peak)
    pks[0] = own_peak
    put("pkt", 1, 0, pks.at[0], pks.at[1], sib)

    branch = boown[...]
    for j in (3, 2, 1):
        if j == 1:
            pass_mlp(*mlp_weights[1], 2)
        got("br", CN, j, brr.at[j], at_ctx(j))
        branch = branch + brr[j].astype(full_type)
    resid = xg[0].astype(full_type) + branch
    boown[...] = resid
    xhat2, inv2 = norm_rows(resid)
    h2[0] = (xhat2 * g2row + b2row).astype(low_type)
    for j in range(1, CN):
        put("h2", CN, j, h2.at[0], h2.at[j], at_ctx(j))

    locals_[7].wait()
    have_rest("ct", ctg)
    ct_t[...] = ctg[...].reshape(TK, D).T
    have_mlp(*mlp_weights[0])
    put("wdt", 1, 0, wdt.at[t_i], wdt.at[t_i], sib)
    ga[t_i] = dot(ctg[...].reshape(TK, D), wdt[t_i].reshape(D, FS)).reshape(CN, TB, FS)
    have_mlp(*mlp_weights[1])
    put("wut", 1, 0, wup.at[t_i], wup.at[t_i], sib)
    got("wdt", 1, 0, wdt.at[o_i], sib)
    ga[o_i] = dot(ctg[...].reshape(TK, D), wdt[o_i].reshape(D, FS)).reshape(CN, TB, FS)
    got("wut", 1, 0, wup.at[o_i], sib)

    def mlp(j, _):
        @pl.when(j > 0)
        def _():
            got("h2", CN, j, h2.at[j], at_ctx(j))

        block = h2[j]
        h2_t[:, pl.ds(pl.multiple_of(j * TB, TB), TB)] = block.T
        for a in range(2):
            up = dot(block, wup[a].reshape(D, FS))
            phi = 0.5 * (1.0 + lax.erf(up * 0.7071067811865476))
            dens = jnp.exp(up * up * -0.5) * 0.3989422804014327
            part = slice(a * FS, (a + 1) * FS)
            act[j, :, part] = (up * phi).astype(low_type)
            gu[j, :, part] = (ga[a, j] * (phi + up * dens)).astype(low_type)
        grad_two = (
            dot(gu[j, :, :FS], wup[0].reshape(D, FS), NT) + dot(gu[j, :, FS:], wup[1].reshape(D, FS), NT)
        )

        @pl.when(j == 0)
        def _():
            g2own[...] = grad_two

        @pl.when(j > 0)
        def _():
            g2s[j] = grad_two.astype(low_type)
            put("g2", CN, j, g2s.at[j], g2r.at[j], at_ctx(j))

        return 0

    lax.fori_loop(0, CN, mlp, 0)

    got("pkt", 1, 0, pks.at[1], sib)
    pks[2] = jnp.maximum(pks[0], pks[1])
    for j in range(1, ZN):
        put("pkz", ZN, j, pks.at[2], pks.at[2 + j], at_z(j))
    own_part = pl.ds(pl.multiple_of(t_i * FS, FS), FS)
    other_part = pl.ds(pl.multiple_of(o_i * FS, FS), FS)
    pairs = ((h2_t, gu), (ct_t, act))
    for k, (left, right) in enumerate(pairs):
        gsib_s[k] = dot(left[...], right[:, :, other_part].reshape(TK, FS)).astype(low_type)
        put("gs", 2, k, gsib_s.at[k], gsib_r.at[k], sib)

    def send_far(k):
        @pl.when(outer)
        def _():
            put("gz%d" % k, 4, 2, gz_s.at[k, far_out], gz_r.at[k, 2], plane(pair))
            put("gz%d" % k, 4, 3, gz_s.at[k, far_in], gz_r.at[k, 3], plane(pair))

    def send_near(k):
        put("gz%d" % k, 4, 0, gz_s.at[k, pair], gz_r.at[k, 0], plane(pair))

    own_grads = [dot(left[...], right[:, :, own_part].reshape(TK, FS)) for left, right in pairs]
    for k in range(2):
        got("gs", 2, k, gsib_r.at[k], sib)
        total = own_grads[k] + gsib_r[k].astype(full_type)
        gkeep[k] = total
        gz_s[k] = total.astype(low_type).reshape(ZN, R, FS)
        send_far(k)
    send_near(0)
    send_near(1)

    def down(j, _):
        part = (
            dot(act[j, :, :FS], wdt[0].reshape(D, FS), NT) + dot(act[j, :, FS:], wdt[1].reshape(D, FS), NT)
        )

        @pl.when(j == 0)
        def _():
            boown[...] += part

        @pl.when(j > 0)
        def _():
            bos[j] = part.astype(low_type)

        return 0

    lax.fori_loop(0, CN, down, 0)

    def relay_mlp(k):
        @pl.when(jnp.logical_not(outer))
        def _():
            for n, z in ((2, far_out), (3, far_in)):
                got("gz%d" % k, 4, n, gz_r.at[k, n], plane(pair))
                mine_part = gkeep[k, pl.ds(pl.multiple_of(z * R, R), R)]
                gz_s[k, z] = (mine_part + gz_r[k, n].astype(full_type)).astype(low_type)
                put_as("gz%d" % k, 4, n, 1, gz_s.at[k, z], gz_r.at[k, 1], plane(z))

    def share_mlp(k, out):
        total = gkeep[k, pl.ds(pl.multiple_of(s_i * R, R), R)]
        for n in range(2):
            got("gz%d" % k, 4, n, gz_r.at[k, n], plane(pair))
            total = total + gz_r[k, n].astype(full_type)
        gfin[k] = total.astype(low_type)
        spread("gc%d" % k, gfin.at[k], lambda j: out.at[c_i])
        pltpu.make_async_copy(gfin.at[k], out.at[c_i], lsem.at[8 + k]).start()

    grad_two = g2own[...]
    for j in range(1, CN):
        got("g2", CN, j, g2r.at[j], at_ctx(j))
        grad_two = grad_two + g2r[j].astype(full_type)
    ln2g = jnp.sum(grad_two * xhat2, axis=0, keepdims=True)
    ln2b = jnp.sum(grad_two, axis=0, keepdims=True)
    hat = grad_two * g2row
    grad_resid = ctg[0].astype(full_type) + inv2 * (
        hat
        - jnp.sum(hat, axis=-1, keepdims=True) * inv_d
        - xhat2 * (jnp.sum(hat * xhat2, axis=-1, keepdims=True) * inv_d)
    )
    gres[...] = grad_resid
    gb = grad_resid.astype(low_type)
    gbg[0] = gb
    for j in (1, 2):
        half = pl.ds((j - 1) * HB, HB)
        put("gb", 7, j, gbg.at[0, half], gbg.at[j, half], at_ctx(j))
    for j in (1, 2):
        half = pl.ds((2 - j) * HB, HB)
        put("gb", 7, 4 + j, gbg.at[0, half], gbg.at[j, half], at_ctx(j))
    send_halves("bo", bos, bor)

    peak = pks[2]
    for j in range(1, ZN):
        got("pkz", ZN, j, pks.at[2 + j], at_z(j))
        peak = jnp.maximum(peak, pks[2 + j])
    first = 2 + ZN
    pks[first] = peak
    for j in range(1, CN):
        put("pkc", CN, j, pks.at[first], pks.at[first + j], at_ctx(j))

    dkt[...] = jnp.zeros_like(dkt)
    dvt[...] = jnp.zeros_like(dvt)

    def attend_back(j, _):
        @pl.when(j == 1)
        def _():
            for n in (1, 2):
                half = pl.ds((n - 1) * HB, HB)
                got("gb", 7, n, gbg.at[n, half], at_ctx(n))
                put_as("gb", 7, 2 + n, 2 + n, gbg.at[n, half], gbg.at[3, half], at_ctx(3 - n))
            relay_mlp(0)
            got("gb", 7, 5, gbg.at[1, pl.ds(HB, HB)], at_ctx(1))

        @pl.when(j == 2)
        def _():
            got("gb", 7, 6, gbg.at[2, pl.ds(0, HB)], at_ctx(2))

        @pl.when(j == CN - 1)
        def _():
            add_halves("bo", bos, bor)
            for n in (1, 2):
                got("gb", 7, 2 + n, gbg.at[3, pl.ds((n - 1) * HB, HB)], at_ctx(3 - n))

        grad_rows = stacked(dot(gbg[j], wob[...].reshape(D, HW)).astype(low_type))
        query_rows = stacked(qs[j])
        sbuf[...] = dot(grad_rows, vall[...].reshape(2 * TK, HW), NT)

        for h in range(heads):
            rows = slice(h * TB, (h + 1) * TB)
            probs, grad_probs = pst[j, rows], sbuf[rows]
            inner = jnp.sum(probs * grad_probs, axis=-1, keepdims=True)
            dsb[rows] = (probs * (grad_probs - inner)).astype(low_type)
        grad_scores = dsb[...]
        dqb[j] = folded(dot(grad_scores, kall[...].reshape(2 * TK, HW))) * 0.125
        dvt[...] += dot(grad_rows, pst[j].astype(low_type), TN)
        dkt[...] += dot(query_rows, grad_scores, TN)
        return 0

    lax.fori_loop(0, CN, attend_back, 0)
    dks_s[0] = dvt[:, TK:].astype(low_type)
    dks_s[1] = dkt[:, TK:].astype(low_type)
    for k in range(2):
        put("dk", 2, k, dks_s.at[k], dks_r.at[k], sib)

    for j in range(1, CN):
        got("pkc", CN, j, pks.at[first + j], at_ctx(j))
        peak = jnp.maximum(peak, pks[first + j])
    peak_v[...] = peak
    pltpu.make_async_copy(peak_v, peak_o, lsem.at[22]).start()

    relay_mlp(1)
    def unnorm(grad_n, gain_row, normed, inverse):
        gain_grad = jnp.sum(grad_n * normed, axis=0, keepdims=True)
        e = grad_n * gain_row
        return (inverse * (e - normed * head_mean(e * normed))).astype(low_type), gain_grad

    def share_grad(n, full):
        full = full.reshape(ZN, 2, HR, 2 * HW)
        low_full = full.astype(low_type)
        for k in range(2):
            @pl.when(o_i == k)
            def _():
                qsib_s[n] = low_full[:, k]

            @pl.when(t_i == k)
            def _():
                qown[n] = full[:, k]

        put("qg", 2, n, qsib_s.at[n], qsib_r.at[n], sib)

    pieces = {1: (("qz1", 0, HR),), 0: (("qz0", 0, HR // 2), ("qz2", HR // 2, HR // 2))}

    def reduce_grad(n):
        got("qg", 2, n, qsib_r.at[n], sib)
        total = qown[n] + qsib_r[n].astype(full_type)
        qown[n] = total
        qz_s[n] = total.astype(low_type)
        if n == 1:
            @pl.when(outer)
            def _():
                put("qz1", 4, 2, qz_s.at[1, far_out], qz_r.at[1, 2], plane(pair))
                put("qz1", 4, 3, qz_s.at[1, far_in], qz_r.at[1, 3], plane(pair))

            put("qz1", 4, 0, qz_s.at[1, pair], qz_r.at[1, 0], plane(pair))
            return
        for name, first, count in pieces[n]:
            rows = pl.ds(first, count)
            for j in range(1, ZN):
                put(name, ZN, j, qz_s.at[n, flip(s_i, j, ZN), rows], qz_r.at[n, j, rows], at_z(j))

    def relay_grad():
        @pl.when(jnp.logical_not(outer))
        def _():
            for n, z in ((2, far_out), (3, far_in)):
                got("qz1", 4, n, qz_r.at[1, n], plane(pair))
                qz_s[1, z] = (qown[1, z] + qz_r[1, n].astype(full_type)).astype(low_type)
                put_as("qz1", 4, n, 1, qz_s.at[1, z], qz_r.at[1, 1], plane(z))

    grad_raw, q_gain_row = unnorm(dqb[...].reshape(TK, HW), qgrow, nq[...], sq[...])
    dqr[...] = grad_raw
    empty = jnp.zeros((TK, HW), low_type)
    share_grad(1, (
        dot(h1_t[...], jnp.concatenate([dqr[...], empty], axis=1))
        + dot(gbg[...].reshape(TK, D), jnp.concatenate([empty, attq[...].reshape(TK, HW)], axis=1), TN)
    ))
    share_mlp(0, upo)
    got("dk", 2, 0, dks_r.at[0], sib)
    grad_v = (dvt[:, :TK] + dks_r[0].astype(full_type)).T.astype(low_type)
    got("dk", 2, 1, dks_r.at[1], sib)
    grad_k = (dkt[:, :TK] + dks_r[1].astype(full_type)).T
    grad_raw, k_gain_row = unnorm(grad_k, kgrow, nk[...], sk[...])
    dkv[...] = jnp.concatenate([grad_raw, grad_v], axis=1)
    ln1g = jnp.zeros((1, D), full_type)
    ln1b = jnp.zeros((1, D), full_type)
    for j in range(CN - 1, -1, -1):
        rows = slice(j * TB, (j + 1) * TB)
        part = dot(dqr[rows], wqb[...].reshape(D, HW), NT) + dot(dkv[rows], wkv[...].reshape(D, 2 * HW), NT)
        if j:
            g1s[j] = part.astype(low_type)
        else:
            g1own[...] = part
        if j == 3:
            send_halves("g1", g1s, g1r)
            share_grad(0, dot(h1_t[...], dkv[...]))
            reduce_grad(1)
        ln1g = ln1g + jnp.sum(part * xh1[j], axis=0, keepdims=True)
        ln1b = ln1b + jnp.sum(part, axis=0, keepdims=True)
        if j == 1:
            reduce_grad(0)
    rows_s[0] = jnp.zeros_like(rows_s[0])
    HD2 = D // 2
    for k, row in enumerate((ln1g, ln1b, ln2g, ln2b)):
        rows_s[0, 2 * k:2 * k + 1, :HD2] = row[:, :HD2]
        rows_s[0, 2 * k + 1:2 * k + 2, :HD2] = row[:, HD2:]
    rows_s[0, 0:1, HD2:HD2 + HW] = q_gain_row
    rows_s[0, 1:2, HD2:HD2 + HW] = k_gain_row
    put("rt", 1, 0, rows_s.at[0], rows_r.at[0], sib)
    add_halves("g1", g1s, g1r)
    relay_grad()
    share_mlp(1, dno)
    got("rt", 1, 0, rows_r.at[0], sib)
    rows_s[1] = rows_s[0] + rows_r[0]
    for j in range(1, ZN):
        put("rz", ZN, j, rows_s.at[1], rows_r.at[j], at_z(j))

    total = boown[...]
    for j in (1, 2):
        got("bo", 5, j, bor.at[j], at_ctx(j))
        total = total + bor[j].astype(full_type)
    own_rows = pl.ds(t_i * TB, TB)
    obuf[0] = total.astype(low_type)
    put("ob", 2, 0, obuf.at[0], bo_o.at[own_rows], sib)
    pltpu.make_async_copy(obuf.at[0], bo_o.at[own_rows], lsem.at[10]).start()

    def to_owner(name, first, count, n):
        rows = pl.ds(first, count)
        return qfin.at[n, rows], qkvo.at[place, t_i, n, rows]

    def share_fin(n, which=slice(None)):
        for name, first, count in pieces[n][which]:
            rows = slice(first, first + count)
            total = qown[n, s_i, rows]
            for j in (0, 1) if n == 1 else range(1, ZN):
                got(name, 4, j, qz_r.at[n, j, pl.ds(first, count)], at_z(1))
                total = total + qz_r[n, j, rows].astype(full_type)
            qfin[n, rows] = total.astype(low_type)
            src, dst = to_owner(name, first, count, n)
            slot = spot("r" + name, 2 * half_chips) + place * 2 + t_i
            for j in range(1, CN):
                pltpu.make_async_remote_copy(
                    src_ref=src, dst_ref=dst,
                    send_sem=leaving("s" + name, CN, j), recv_sem=rsem.at[slot],
                    device_id=(s_i, flip(c_i, j, CN), tstar), device_id_type=MESH,
                ).start()

            @pl.when(t_i == tstar)
            def _():
                pltpu.make_async_copy(src, dst, lsem.at[12 + (name == "qz2") * 2 + n]).start()

            @pl.when(t_i != tstar)
            def _():
                pltpu.make_async_remote_copy(
                    src_ref=src, dst_ref=dst,
                    send_sem=leaving("o" + name, 1, 0), recv_sem=rsem.at[slot],
                    device_id=sib, device_id_type=MESH,
                ).start()

    def pass_grad(k, out):
        for j in (1, 2):
            block = out.at[flip(c_i, j, CN)]
            got("gc%d" % k, 5, j, block, at_ctx(j))
            half = block.at[pl.ds((j - 1) * HR, HR)]
            put_as("gc%d" % k, 5, 2 + j, 2 + j, half, half, at_ctx(3 - j))

    pass_grad(0, upo)
    share_fin(0, slice(0, 1))

    xhat1, inv1 = norm_rows(xg[0].astype(full_type))
    grad_one = g1own[...]
    for j in (1, 2):
        got("g1", 5, j, g1r.at[j], at_ctx(j))
        grad_one = grad_one + g1r[j].astype(full_type)
    hat = grad_one * g1row
    grad_in = gres[...] + inv1 * (
        hat
        - jnp.sum(hat, axis=-1, keepdims=True) * inv_d
        - xhat1 * (jnp.sum(hat * xhat1, axis=-1, keepdims=True) * inv_d)
    )
    obuf[1] = grad_in.astype(low_type)
    put("ob", 2, 1, obuf.at[1], ig_o.at[own_rows], sib)
    pltpu.make_async_copy(obuf.at[1], ig_o.at[own_rows], lsem.at[11]).start()

    pass_grad(1, dno)
    share_fin(0, slice(1, 2))

    rows_sum = rows_s[1]
    for j in range(1, ZN):
        got("rz", ZN, j, rows_r.at[j], at_z(j))
        rows_sum = rows_sum + rows_r[j]
    rows_s[2] = rows_sum
    for j in range(1, CN):
        put("rc", CN, j, rows_s.at[2], rows_r.at[ZN + j], at_ctx(j))
    qkr_v[c_i] = rows_sum[:, HD2:]

    share_fin(1)
    total = rows_sum[:, :HD2]
    for j in range(1, CN):
        got("rc", CN, j, rows_r.at[ZN + j], at_ctx(j))
        block = rows_r[ZN + j]
        total = total + block[:, :HD2]
        qkr_v[flip(c_i, j, CN)] = block[:, HD2:]
    lnr_v[...] = total
    pltpu.make_async_copy(lnr_v, lnr_o, lsem.at[23]).start()
    pltpu.make_async_copy(qkr_v, qkr_o, lsem.at[24]).start()

    for n, (src, dst) in enumerate(((peak_v, peak_o), (lnr_v, lnr_o), (qkr_v, qkr_o))):
        pltpu.make_async_copy(src, dst, lsem.at[22 + n]).wait()
    for k, out in ((0, upo), (1, dno)):
        for j in (1, 2):
            half = out.at[flip(c_i, 3, CN), pl.ds((j - 1) * HR, HR)]
            got("gc%d" % k, 5, 2 + j, half, at_ctx(3 - j))
        pltpu.make_async_copy(gfin.at[k], out.at[c_i], lsem.at[8 + k]).wait()
    other_rows = pl.ds(o_i * TB, TB)
    for k, out in ((0, bo_o), (1, ig_o)):
        got("ob", 2, k, out.at[other_rows], sib)
        pltpu.make_async_copy(obuf.at[k], out.at[own_rows], lsem.at[10 + k]).wait()

    all_pieces = [(name, first, count, n) for n in pieces for name, first, count in pieces[n]]

    @pl.when(t_i == tstar)
    def _():
        for name, first, count, n in all_pieces:
            src, dst = to_owner(name, first, count, n)
            pltpu.make_async_copy(src, dst, lsem.at[12 + (name == "qz2") * 2 + n]).wait()

    for p in range(half_chips):
        for a in range(2):
            @pl.when((t_i != tstar) | (place != p) | (t_i != a))
            def _():
                for name, first, count, n in all_pieces:
                    rows = pl.ds(first, count)
                    pltpu.make_async_remote_copy(
                        src_ref=qfin.at[n, rows], dst_ref=qkvo.at[p, a, n, rows],
                        send_sem=ssem.at[0],
                        recv_sem=rsem.at[spot("r" + name, 2 * half_chips) + p * 2 + a],
                        device_id=sib, device_id_type=MESH,
                    ).wait_recv()

    three = pl.ds(1, 3)
    for name, ref in (
        ("x", xg), ("br", brs), ("h2", h2), ("g2", g2s), ("pkc", pks), ("rc", rows_r), ("small", smalls.at[t_i]),
        ("pkz", pks), ("rz", rows_r), ("ct", ctg), ("gb", gbg), ("bo", bos), ("g1", g1s),
        ("gc0", gz_s.at[0]), ("gc1", gz_s.at[1]), ("gz0", gz_s.at[0]), ("gz1", gz_s.at[1]),
    ):
        sent(name, 5, 0, ref.at[three])
    for name, first, count, n in all_pieces:
        for way in ("", "s"):
            sent(way + name, 4, 0, qz_s.at[n, three, pl.ds(first, count)])
    for name, buf in mlp_weights:
        sent(name, 5, 0, buf.at[t_i, s_i])

        @pl.when(jnp.logical_not(outer))
        def _():
            for n in range(1, 5):
                sent(name, 5, n, buf.at[t_i, s_i])

    for name, ref in (
        ("smallt", smalls.at[t_i]), ("k", kall.at[0]), ("v", vall.at[0]), ("pkt", pks.at[0]),
        ("wdt", wdt.at[t_i]), ("wut", wup.at[t_i]), ("rt", rows_s.at[0]),
    ):
        sent(name, 1, 0, ref)
    for k in range(2):
        sent("gs", 2, k, gsib_s.at[k])
        sent("dk", 2, k, dks_s.at[k])
        sent("ob", 2, k, obuf.at[k])
        sent("qg", 2, k, qsib_s.at[k])

    @pl.when(t_i == tstar)
    def _():
        for name, buf in projections:
            sent(name, ZN, 0, buf)
            sent("f" + name, ZN, 0, buf.at[three])

    @pl.when(t_i != tstar)
    def _():
        for name, first, count, n in all_pieces:
            sent("o" + name, 1, 0, qfin.at[n, pl.ds(first, count)])


ARRIVALS, LEAVINGS = 120, 57


def fused_call(sizes, *operands):
    CN, ZN, TB, D, HW, FS, R = sizes
    TK = CN * TB
    HR = R // 2
    half_chips = CN // 2
    heads = HW // 64
    lo, hi = low_type, full_type
    V = pltpu.VMEM
    any_spec = pl.BlockSpec(memory_space=pl.ANY)
    gain_shape = operands[6].shape
    out_shape = [
        jax.ShapeDtypeStruct((2 * TB, D), lo),
        jax.ShapeDtypeStruct((2 * TB, D), lo),
        jax.ShapeDtypeStruct((CN, R, FS), lo),
        jax.ShapeDtypeStruct((CN, R, FS), lo),
        jax.ShapeDtypeStruct((half_chips, 2, 2, HR, 2 * HW), lo),
        jax.ShapeDtypeStruct((8, D // 2), hi),
        jax.ShapeDtypeStruct((CN, 8, 256), hi),
        jax.ShapeDtypeStruct((8, 128), hi),
    ]
    scratch = [
        V((CN, TB, D), lo), V((CN, TB, D), lo), V((2, ZN, 8, 256), hi),
        V((3, R, half_chips * HW), lo), V((R, half_chips * HW), lo),
        V((ZN, R, 2 * HW), lo), V((ZN, HR, 2 * HW), lo), V((ZN, HR, 2 * HW), lo),
        V((ZN, R, HW), lo), V((ZN, R, HW), lo), V((2, ZN, R, FS), lo), V((2, ZN, R, FS), lo),
        V((D, TK), lo), V((D, TK), lo), V((D, TK), lo),
        V((CN, TB, D), hi), V((CN, TB, D), lo),
        V((TK, HW), hi), V((TK, HW), hi), V((TK, HW), hi), V((TK, HW), hi),
        V((CN, TB, HW), lo), V((2, TK, HW), lo), V((2, TK, HW), lo),
        V((CN, heads * TB, 2 * TK), hi), V((heads * TB, 2 * TK), hi),
        V((CN, TB, HW), lo), V((CN, TB, D), lo), V((CN, TB, D), lo), V((2 + ZN + CN, 8, 128), hi),
        V((heads, 2 * TK), hi), V((heads * TB, 2 * TK), lo),
        V((CN, TB, D), lo), V((2, CN, TB, FS), hi), V((CN, TB, 2 * FS), lo), V((CN, TB, 2 * FS), lo),
        V((CN, TB, D), lo), V((CN, TB, D), lo), V((TB, D), hi),
        V((CN, TB, D), lo), V((CN, TB, D), lo), V((TB, D), hi),
        V((2, D, FS), lo), V((2, D, FS), lo), V((2, D, FS), hi),
        V((2, ZN, R, FS), lo), V((2, ZN, R, FS), lo), V((2, R, FS), lo),
        V((TB, D), hi), V((CN, TB, D), lo),
        V((CN, TB, HW), hi), V((HW, 2 * TK), hi), V((HW, 2 * TK), hi),
        V((2, HW, TK), lo), V((2, HW, TK), lo), V((TK, HW), lo), V((TK, 2 * HW), lo),
        V((CN, TB, D), lo), V((CN, TB, D), lo), V((TB, D), hi),
        V((2, ZN, HR, 2 * HW), lo), V((2, ZN, HR, 2 * HW), lo), V((2, ZN, HR, 2 * HW), hi),
        V((2, ZN, HR, 2 * HW), lo), V((2, ZN, HR, 2 * HW), lo), V((2, HR, 2 * HW), lo),
        V((3, 8, D // 2 + 256), hi), V((ZN + CN, 8, D // 2 + 256), hi), V((2, TB, D), lo),
        V((R,), lo), V((R,), lo), V((R,), lo), V((R,), lo), V(gain_shape, lo), V(gain_shape, lo),
        V((8, D // 2), hi), V((CN, 8, 256), hi), V((8, 128), hi),
        pltpu.SemaphoreType.DMA((25,)), pltpu.SemaphoreType.DMA((LEAVINGS,)), pltpu.SemaphoreType.DMA((ARRIVALS,)),
    ]
    return pl.pallas_call(
        functools.partial(fused_kernel, sizes),
        out_shape=out_shape,
        in_specs=[any_spec] * 14,
        out_specs=[any_spec] * 8,
        scratch_shapes=scratch,
        compiler_params=pltpu.CompilerParams(
            collective_id=0, has_side_effects=True, vmem_limit_bytes=56 * 2**20
        ),
    )(*operands)


def finish_kernel(
    sizes,
    bo, ig, up_h, dn_h, qkvo_h, lnr_h, qkr_h, peak_h, wq_h, wk_h,
    bo_o, ig_o, l1g_o, l1b_o, l2g_o, l2b_o, qg_o, kg_o, gq_o, gk_o, gv_o, go_o, gu_o, gd_o, cq_o, ck_o,
    upo, dno, qkvo, lnr, qkr, peak, wq, wk, bov, igv, gq, gk, gv, go, gu, gd, cq, ck, l1g, l1b, l2g, l2b, qg, kg, isem, osem,
):
    CN, ZN, TB, D, HW, FS, R = sizes
    half_chips = CN // 2
    s_i, t_i = lax.axis_index("shard"), lax.axis_index("tp")
    ins = [
        pltpu.make_async_copy(src, dst, isem.at[n])
        for n, (src, dst) in enumerate((
            (qkvo_h, qkvo), (up_h, upo), (dn_h, dno), (peak_h, peak), (wq_h, wq), (wk_h, wk),
            (lnr_h, lnr), (qkr_h, qkr), (bo, bov), (ig, igv),
        ))
    ]
    for n in (1, 2, 0, 8, 9, 3, 4, 5, 6, 7):
        ins[n].start()
    outs = []

    def leave(src, dst):
        copy = pltpu.make_async_copy(src, dst, osem.at[len(outs)])
        copy.start()
        outs.append(copy)

    for n, grads, stage, out in ((1, upo, gu, gu_o), (2, dno, gd, gd_o)):
        ins[n].wait()
        for c in range(CN):
            stage[:, c * FS:(c + 1) * FS] = grads[c].astype(full_type)
        leave(stage, out)
    ins[0].wait()
    for n, first, stage, out in ((1, 0, gq, gq_o), (0, 0, gk, gk_o), (0, HW, gv, gv_o), (1, HW, go, go_o)):
        for a in range(2):
            parts = [qkvo[p, a, n][:, first:first + HW] for p in range(half_chips)]
            stage[a * (R // 2):(a + 1) * (R // 2)] = jnp.concatenate(parts, axis=1).astype(full_type)
        leave(stage, out)
    for n, stage, out in ((8, bov, bo_o), (9, igv, ig_o)):
        ins[n].wait()
        leave(stage, out)
    heads = HW // 64
    for n in (3, 4, 5):
        ins[n].wait()
    factor = jnp.sqrt(clip_level / jnp.maximum(peak[0:1], clip_level))
    here = half_chips * heads
    lanes = lax.broadcasted_iota(jnp.int32, (1, here * 64), 1) // 64
    ids = lax.broadcasted_iota(jnp.int32, (1, 128), 1)
    columns = jnp.ones((1, here * 64), full_type)
    for h in range(here):
        one = jnp.sum(jnp.where(ids == t_i * here + h, factor, 0.0), axis=-1, keepdims=True)
        columns = jnp.where(lanes == h, one, columns)
    for weights, stage, out in ((wq, cq, cq_o), (wk, ck, ck_o)):
        stage[...] = (weights[...].astype(full_type) * columns).astype(low_type)
        leave(stage, out)
    ins[6].wait()
    ins[7].wait()
    for k, (stage, out) in enumerate(((l1g, l1g_o), (l1b, l1b_o), (l2g, l2g_o), (l2b, l2b_o))):
        row = jnp.zeros((1, R), full_type)
        for z in range(ZN):
            at = z * R % (D // 2)
            source = 2 * k + z * R // (D // 2)
            row = jnp.where(s_i == z, lnr[source:source + 1, at:at + R], row)
        stage[...] = row.reshape(R)
        leave(stage, out)
    piece = qg.shape[1]
    for p in range(half_chips):
        chip = pltpu.roll(qkr[t_i * half_chips + p], (256 - s_i * piece) % 256, 1)
        for h in range(heads):
            for k, stage in ((0, qg), (1, kg)):
                stage[p * heads + h:p * heads + h + 1] = chip[k:k + 1, h * 64:h * 64 + piece]
    leave(qg, qg_o)
    leave(kg, kg_o)
    for copy in outs:
        copy.wait()


def fused_layer(
    images, cotangent, ln1_gain, ln1_bias, ln2_gain, ln2_bias, q_gain, k_gain,
    w_query, w_key, w_value, w_out, w_up, w_down,
):
    CN, ZN = lax.axis_size("ctx"), lax.axis_size("shard")
    TB = images.shape[1] // 2
    D = images.shape[2]
    R = w_query.shape[0]
    HW = w_query.shape[1] // (CN // 2)
    FS = w_up.shape[1] // CN
    sizes = (CN, ZN, TB, D, HW, FS, R)
    results = fused_call(
        sizes, images, cotangent, ln1_gain, ln1_bias, ln2_gain, ln2_bias, q_gain, k_gain,
        w_query, w_key, w_value, w_out.T, w_up, w_down.T,
    )
    row = jax.ShapeDtypeStruct((R,), full_type)
    gain = jax.ShapeDtypeStruct(q_gain.shape, full_type)
    square = jax.ShapeDtypeStruct(w_query.shape, full_type)
    wide = jax.ShapeDtypeStruct(w_up.shape, full_type)
    tokens = jax.ShapeDtypeStruct(images.shape[1:], low_type)
    clipped = jax.ShapeDtypeStruct(w_query.shape, low_type)
    lo, hi = low_type, full_type
    V = pltpu.VMEM
    any_spec = pl.BlockSpec(memory_space=pl.ANY)
    out = pl.pallas_call(
        functools.partial(finish_kernel, sizes),
        out_shape=[tokens] * 2 + [row] * 4 + [gain] * 2 + [square] * 4 + [wide] * 2 + [clipped] * 2,
        in_specs=[any_spec] * 10,
        out_specs=[any_spec] * 16,
        scratch_shapes=[
            V((CN, R, FS), lo), V((CN, R, FS), lo), V((CN // 2, 2, 2, R // 2, 2 * HW), lo), V((8, D // 2), hi),
            V((CN, 8, 256), hi), V((8, 128), hi), V(w_query.shape, lo), V(w_query.shape, lo),
            V(images.shape[1:], lo), V(images.shape[1:], lo),
        ]
        + [V(w_query.shape, hi)] * 4 + [V(w_up.shape, hi)] * 2 + [V(w_query.shape, lo)] * 2
        + [V((R,), hi)] * 4 + [V(q_gain.shape, hi)] * 2
        + [pltpu.SemaphoreType.DMA((10,)), pltpu.SemaphoreType.DMA((16,))],
        compiler_params=pltpu.CompilerParams(vmem_limit_bytes=60 * 2**20),
    )(*results, w_query, w_key)
    out = list(out)
    out[0], out[1] = out[0].reshape(images.shape), out[1].reshape(images.shape)
    out[11], out[13] = out[11].T, out[13].T
    return tuple(out)


def on_device(images, cotangent, ln1_gain, ln1_bias, ln2_gain, ln2_bias, q_gain, k_gain, *weights):
    fused = fits_fused(images, weights[0], weights[4], q_gain)
    layer = fused_layer if fused else general_layer
    return layer(images, cotangent, ln1_gain, ln1_bias, ln2_gain, ln2_bias, q_gain, k_gain, *weights)


def solution(mesh):
    return jax.shard_map(
        on_device,
        mesh=mesh,
        in_specs=(
            P("shard", "ctx", None),
            P("shard", "ctx", None),
            P("shard"),
            P("shard"),
            P("shard"),
            P("shard"),
            P("tp", "shard"),
            P("tp", "shard"),
            P("shard", "tp"),
            P("shard", "tp"),
            P("shard", "tp"),
            P("tp", "shard"),
            P("shard", "tp"),
            P("tp", "shard"),
        ),
        out_specs=(
            P("shard", "ctx", None),
            P("shard", "ctx", None),
            P("shard"),
            P("shard"),
            P("shard"),
            P("shard"),
            P("tp", "shard"),
            P("tp", "shard"),
            P("shard", "tp"),
            P("shard", "tp"),
            P("shard", "tp"),
            P("tp", "shard"),
            P("shard", "tp"),
            P("tp", "shard"),
            P("shard", "tp"),
            P("shard", "tp"),
        ),
        check_vma=False,
    )
```

```python
import functools
import jax
import jax.numpy as jnp
from jax import lax
from jax.experimental import pallas as pl
from jax.experimental.pallas import tpu as pltpu
from jax.sharding import PartitionSpec as P

norm_eps = 1e-06
clip_level = 0.5


def matmul(left, right):
    return jnp.dot(left, right, preferred_element_type=jnp.float32)


def norm_parts(values):
    center = values - jnp.mean(values, axis=-1, keepdims=True)
    inverse = lax.rsqrt(jnp.mean(center * center, axis=-1, keepdims=True) + norm_eps)
    return (center * inverse, inverse)


def norm_back(grad_hat, normed, inverse):
    return inverse * (
        grad_hat
        - jnp.mean(grad_hat, axis=-1, keepdims=True)
        - normed * jnp.mean(grad_hat * normed, axis=-1, keepdims=True)
    )


def head_scale(values, gain):
    inverse = lax.rsqrt(jnp.mean(values * values, axis=-1, keepdims=True) + norm_eps)
    return values * inverse * gain


def gelu_exact(values):
    return jax.nn.gelu(values, approximate=False)


def general_layer(
    images,
    cotangent,
    ln1_gain,
    ln1_bias,
    ln2_gain,
    ln2_bias,
    q_gain,
    k_gain,
    w_query,
    w_key,
    w_value,
    w_out,
    w_up,
    w_down,
):
    (
        full_query,
        full_key,
        full_value,
        full_up,
        full_out,
        full_down,
        gain_low_one,
        shift_low_one,
        gain_low_two,
        shift_low_two,
        query_gain_low,
        key_gain_low,
    ) = (
        lax.all_gather(w_query, "shard", axis=0, tiled=True),
        lax.all_gather(w_key, "shard", axis=0, tiled=True),
        lax.all_gather(w_value, "shard", axis=0, tiled=True),
        lax.all_gather(w_up, "shard", axis=0, tiled=True),
        lax.all_gather(w_out, "shard", axis=1, tiled=True),
        lax.all_gather(w_down, "shard", axis=1, tiled=True),
        lax.all_gather(ln1_gain, "shard", axis=0, tiled=True),
        lax.all_gather(ln1_bias, "shard", axis=0, tiled=True),
        lax.all_gather(ln2_gain, "shard", axis=0, tiled=True),
        lax.all_gather(ln2_bias, "shard", axis=0, tiled=True),
        lax.all_gather(q_gain, "shard", axis=1, tiled=True),
        lax.all_gather(k_gain, "shard", axis=1, tiled=True),
    )
    gain_one = gain_low_one.astype(jnp.float32)
    shift_one = shift_low_one.astype(jnp.float32)
    gain_two = gain_low_two.astype(jnp.float32)
    shift_two = shift_low_two.astype(jnp.float32)
    query_gain = query_gain_low.astype(jnp.float32)
    key_gain = key_gain_low.astype(jnp.float32)
    count_img, local_len, width = images.shape
    tokens = count_img * local_len
    heads_here, head_size = query_gain.shape
    local_width = heads_here * head_size
    full_len = local_len * lax.axis_size("ctx")
    group = 1
    groups = count_img // group
    scale = head_size ** (-0.5)
    flat = images.reshape(tokens, width).astype(jnp.float32)
    normed_one, inverse_one = norm_parts(flat)
    hidden_one = (normed_one * gain_one + shift_one).astype(jnp.bfloat16)
    query_raw = matmul(hidden_one, full_query).reshape(tokens, heads_here, head_size)
    key_raw = matmul(hidden_one, full_key).reshape(tokens, heads_here, head_size)
    query_norm = head_scale(query_raw, query_gain).astype(jnp.bfloat16)
    key_norm = head_scale(key_raw, key_gain).astype(jnp.bfloat16)
    value_low = matmul(hidden_one, full_value).astype(jnp.bfloat16)
    key_all, value_all = (
        lax.all_gather(
            key_norm.reshape(count_img, local_len, local_width), "ctx", axis=1, tiled=True
        ),
        lax.all_gather(
            value_low.reshape(count_img, local_len, local_width), "ctx", axis=1, tiled=True
        ),
    )
    query_grp = query_norm.reshape(groups, group, local_len, heads_here, head_size)
    key_grp = key_all.reshape(groups, group, full_len, heads_here, head_size)
    value_grp = value_all.reshape(groups, group, full_len, heads_here, head_size)

    def attend(pieces):
        query_blk, key_blk, value_blk = pieces
        scores = (
            jnp.einsum("gqhd,gkhd->ghqk", query_blk, key_blk, preferred_element_type=jnp.float32)
            * scale
        )
        top = jnp.max(scores, axis=-1, keepdims=True)
        expo = jnp.exp(scores - top)
        total = jnp.sum(expo, axis=-1, keepdims=True)
        probs = (expo / total).astype(jnp.bfloat16)
        mixed_blk = jnp.einsum(
            "ghqk,gkhd->gqhd", probs, value_blk, preferred_element_type=jnp.float32
        )
        return (mixed_blk, top + jnp.log(total), jnp.max(top, axis=(0, 2, 3)))

    mixed, log_total, group_peaks = lax.map(attend, (query_grp, key_grp, value_grp))
    local_peak = jnp.max(group_peaks, axis=0)
    peak_all = lax.pmax(local_peak, ("shard", "ctx"))
    attended = mixed.reshape(tokens, local_width).astype(jnp.bfloat16)
    branch_attn = lax.psum(matmul(attended, full_out), "tp")
    resid = flat + branch_attn
    normed_two, inverse_two = norm_parts(resid)
    hidden_two = (normed_two * gain_two + shift_two).astype(jnp.bfloat16)
    up_raw = matmul(hidden_two, full_up)
    active = gelu_exact(up_raw).astype(jnp.bfloat16)
    branch_mlp = lax.psum(matmul(active, full_down).astype(jnp.bfloat16), "tp").astype(jnp.float32)
    block_out = (resid + branch_mlp).astype(jnp.bfloat16).reshape(images.shape)
    grad_out = cotangent.reshape(tokens, width).astype(jnp.float32)
    grad_down = cotangent.reshape(tokens, width)
    grad_w_down = jnp.dot(active.T, grad_down, preferred_element_type=jnp.float32)
    grad_active = matmul(grad_down, full_down.T)
    unused_up, gelu_pull = jax.vjp(gelu_exact, up_raw)
    grad_up = gelu_pull(grad_active)[0].astype(jnp.bfloat16)
    grad_w_up = jnp.dot(hidden_two.T, grad_up, preferred_element_type=jnp.float32)
    grad_two = lax.psum(matmul(grad_up, full_up.T), "tp")
    grad_gain_two = jnp.sum(grad_two * normed_two, axis=0)
    grad_shift_two = jnp.sum(grad_two, axis=0)
    grad_resid = grad_out + norm_back(grad_two * gain_two, normed_two, inverse_two)
    grad_branch = grad_resid.astype(jnp.bfloat16)
    grad_w_out = jnp.dot(attended.T, grad_branch, preferred_element_type=jnp.float32)
    grad_mixed = matmul(grad_branch, full_out.T).astype(jnp.bfloat16)
    grad_grp = grad_mixed.reshape(groups, group, local_len, heads_here, head_size)

    def attend_back(pieces):
        query_blk, key_blk, value_blk, log_blk, grad_blk = pieces
        scores = (
            jnp.einsum("gqhd,gkhd->ghqk", query_blk, key_blk, preferred_element_type=jnp.float32)
            * scale
        )
        probs = jnp.exp(scores - log_blk)
        grad_probs = jnp.einsum(
            "gqhd,gkhd->ghqk", grad_blk, value_blk, preferred_element_type=jnp.float32
        )
        grad_scores = (
            probs * (grad_probs - jnp.sum(probs * grad_probs, axis=-1, keepdims=True))
        ).astype(jnp.bfloat16)
        grad_val = jnp.einsum(
            "ghqk,gqhd->gkhd",
            probs.astype(jnp.bfloat16),
            grad_blk,
            preferred_element_type=jnp.float32,
        )
        grad_qry = (
            jnp.einsum("ghqk,gkhd->gqhd", grad_scores, key_blk, preferred_element_type=jnp.float32)
            * scale
        )
        grad_kys = (
            jnp.einsum(
                "ghqk,gqhd->gkhd", grad_scores, query_blk, preferred_element_type=jnp.float32
            )
            * scale
        )
        return (grad_qry, grad_kys, grad_val)

    grad_query_n, grad_key_full, grad_value_full = lax.map(
        attend_back, (query_grp, key_grp, value_grp, log_total, grad_grp)
    )
    grad_key_n, grad_value_n = (
        lax.psum_scatter(
            grad_key_full.reshape(count_img, full_len, local_width),
            "ctx",
            scatter_dimension=1,
            tiled=True,
        ),
        lax.psum_scatter(
            grad_value_full.reshape(count_img, full_len, local_width),
            "ctx",
            scatter_dimension=1,
            tiled=True,
        ),
    )
    unused_query, query_pull = jax.vjp(head_scale, query_raw, query_gain)
    grad_query_raw, grad_query_gain = query_pull(
        grad_query_n.reshape(tokens, heads_here, head_size)
    )
    unused_key, key_pull = jax.vjp(head_scale, key_raw, key_gain)
    grad_key_raw, grad_key_gain = key_pull(grad_key_n.reshape(tokens, heads_here, head_size))
    grad_query_low = grad_query_raw.reshape(tokens, local_width).astype(jnp.bfloat16)
    grad_key_low = grad_key_raw.reshape(tokens, local_width).astype(jnp.bfloat16)
    grad_value_low = grad_value_n.reshape(tokens, local_width).astype(jnp.bfloat16)
    grad_w_query = jnp.dot(hidden_one.T, grad_query_low, preferred_element_type=jnp.float32)
    grad_w_key = jnp.dot(hidden_one.T, grad_key_low, preferred_element_type=jnp.float32)
    grad_w_value = jnp.dot(hidden_one.T, grad_value_low, preferred_element_type=jnp.float32)
    grad_one_part = (
        matmul(grad_query_low, full_query.T)
        + matmul(grad_key_low, full_key.T)
        + matmul(grad_value_low, full_value.T)
    )
    grad_one = lax.psum(grad_one_part, "tp")
    grad_gain_one = jnp.sum(grad_one * normed_one, axis=0)
    grad_shift_one = jnp.sum(grad_one, axis=0)
    input_grad = (
        (grad_resid + norm_back(grad_one * gain_one, normed_one, inverse_one))
        .astype(jnp.bfloat16)
        .reshape(images.shape)
    )
    (
        sum_query,
        sum_key,
        sum_value,
        sum_up,
        sum_out,
        sum_down,
        sum_gain_one,
        sum_shift_one,
        sum_gain_two,
        sum_shift_two,
        sum_qgain,
        sum_kgain,
    ) = lax.psum(
        (
            grad_w_query,
            grad_w_key,
            grad_w_value,
            grad_w_up,
            grad_w_out,
            grad_w_down,
            grad_gain_one,
            grad_shift_one,
            grad_gain_two,
            grad_shift_two,
            grad_query_gain,
            grad_key_gain,
        ),
        "ctx",
    )
    (
        part_query,
        part_key,
        part_value,
        part_up,
        part_out,
        part_down,
        part_gain_one,
        part_shift_one,
        part_gain_two,
        part_shift_two,
        part_qgain,
        part_kgain,
    ) = (
        lax.psum_scatter(sum_query, "shard", scatter_dimension=0, tiled=True),
        lax.psum_scatter(sum_key, "shard", scatter_dimension=0, tiled=True),
        lax.psum_scatter(sum_value, "shard", scatter_dimension=0, tiled=True),
        lax.psum_scatter(sum_up, "shard", scatter_dimension=0, tiled=True),
        lax.psum_scatter(sum_out, "shard", scatter_dimension=1, tiled=True),
        lax.psum_scatter(sum_down, "shard", scatter_dimension=1, tiled=True),
        lax.psum_scatter(sum_gain_one, "shard", scatter_dimension=0, tiled=True),
        lax.psum_scatter(sum_shift_one, "shard", scatter_dimension=0, tiled=True),
        lax.psum_scatter(sum_gain_two, "shard", scatter_dimension=0, tiled=True),
        lax.psum_scatter(sum_shift_two, "shard", scatter_dimension=0, tiled=True),
        lax.psum_scatter(sum_qgain, "shard", scatter_dimension=1, tiled=True),
        lax.psum_scatter(sum_kgain, "shard", scatter_dimension=1, tiled=True),
    )
    factor = jnp.sqrt(clip_level / jnp.maximum(peak_all, clip_level))
    columns = jnp.repeat(factor, head_size)
    query_clip = (w_query.astype(jnp.float32) * columns).astype(jnp.bfloat16)
    key_clip = (w_key.astype(jnp.float32) * columns).astype(jnp.bfloat16)
    return (
        block_out,
        input_grad,
        part_gain_one,
        part_shift_one,
        part_gain_two,
        part_shift_two,
        part_qgain,
        part_kgain,
        part_query,
        part_key,
        part_value,
        part_out,
        part_up,
        part_down,
        query_clip,
        key_clip,
    )


MESH = pl.DeviceIdType.MESH
NN = (((1,), (0,)), ((), ()))
NT = (((1,), (1,)), ((), ()))
TN = (((0,), (0,)), ((), ()))
low_type = jnp.bfloat16
full_type = jnp.float32


def dot(left, right, dims=NN):
    return lax.dot_general(left, right, dims, preferred_element_type=full_type)


def flip(place, bits, count):
    result = 0
    unit = 1
    while unit < count:
        result = result + ((place // unit + bits // unit) % 2) * unit
        unit *= 2
    return result


def fits_fused(images, w_query, w_up, q_gain):
    count_img, local_len, width = images.shape
    ctx, shard, tp = lax.axis_size("ctx"), lax.axis_size("shard"), lax.axis_size("tp")
    rows = w_query.shape[0]
    return (
        count_img == 1
        and tp == 2
        and ctx == 4
        and shard == 4
        and rows % (16 * ctx) == 0
        and local_len % 32 == 0
        and q_gain.shape[0] % 2 == 0
        and w_up.shape[1] % (128 * ctx) == 0
    )


def fused_kernel(
    sizes,
    img_h, cot_h, g1_a, b1_a, g2_a, b2_a, qg_a, kg_a, wq_h, wk_h, wv_h, wo_h, wup_h, wdn_h,
    bo_o, ig_o, upo, dno, qkvo, lnr_o, qkr_o, peak_o,
    xg, ctg, smalls, wl, wol, wkv, wqp, wop, wqb, wob, wup, wdt, h1_t, h2_t, ct_t,
    xh1, h1, nq, nk, sq, sk, qs, kall, vall, pst, sbuf, attq, brs, brr, pks,
    ptop, dsb,
    h2, ga, act, gu, g2s, g2r, g2own, bos, bor, boown,
    gsib_s, gsib_r, gkeep, gz_s, gz_r, gfin,
    gres, gbg, dqb, dkt, dvt, dks_s, dks_r, dqr, dkv,
    g1s, g1r, g1own, qsib_s, qsib_r, qown, qz_s, qz_r, qfin,
    rows_s, rows_r, obuf, g1_h, b1_h, g2_h, b2_h, qg_h, kg_h, lnr_v, qkr_v, peak_v,
    lsem, ssem, rsem,
):
    CN, ZN, TB, D, HW, FS, R = sizes
    HR = R // 2
    s_i, c_i, t_i = lax.axis_index("shard"), lax.axis_index("ctx"), lax.axis_index("tp")
    o_i = 1 - t_i
    half_chips = CN // 2
    tstar = c_i // half_chips
    place = c_i % half_chips
    TK = CN * TB
    inv_d = 1.0 / D

    def at_ctx(j):
        return (s_i, flip(c_i, j, CN), t_i)

    def at_z(j):
        return (flip(s_i, j, ZN), c_i, t_i)

    sib = (s_i, c_i, o_i)

    outer = (s_i == 0) | (s_i == ZN - 1)
    pair = flip(s_i, 1, ZN)
    far_in = flip(s_i, 3, ZN) * (1 - outer) + flip(s_i, 2, ZN) * outer
    far_out = flip(s_i, 2, ZN) * (1 - outer) + flip(s_i, 3, ZN) * outer

    def plane(z):
        return (z, c_i, t_i)

    arrivals, leavings = {}, {}
    from_one = ("x", "small", "br", "h2", "g2", "qz0", "qz2", "rz", "pkz", "rc", "pkc",
                "ct", "gb", "bo", "g1", "gc0", "gc1")
    apart = ("wd", "wu", "gs", "dk", "qg", "ob")

    def spot(name, count):
        if name not in arrivals:
            first = sum(n for _, n in arrivals.values())
            skip = 1 if name in from_one else 0
            arrivals[name] = (first - skip, count - skip)
        return arrivals[name][0]

    def arrival(name, count, j):
        return rsem.at[spot(name, count) + j]

    def leaving(name, count, j):
        if name not in leavings:
            leavings[name] = (sum(n for _, n in leavings.values()), count if name in apart else 1)
        return ssem.at[leavings[name][0] + (j if name in apart else 0)]

    def put_as(name, count, send, recv, src, dst, dev):
        pltpu.make_async_remote_copy(
            src_ref=src, dst_ref=dst, send_sem=leaving(name, count, send), recv_sem=arrival(name, count, recv),
            device_id=dev, device_id_type=MESH,
        ).start()

    def put(name, count, j, src, dst, dev):
        put_as(name, count, j, j, src, dst, dev)

    def got(name, count, j, dst, dev):
        pltpu.make_async_remote_copy(
            src_ref=dst, dst_ref=dst, send_sem=ssem.at[0], recv_sem=arrival(name, count, j),
            device_id=dev, device_id_type=MESH,
        ).wait_recv()

    def sent(name, count, j, src):
        pltpu.make_async_remote_copy(
            src_ref=src, dst_ref=src, send_sem=leaving(name, count, j), recv_sem=rsem.at[0],
            device_id=sib, device_id_type=MESH,
        ).wait_send()

    x_src = img_h.at[0, pl.ds(t_i * TB, TB)]
    c_src = cot_h.at[0, pl.ds(t_i * TB, TB)]
    locals_ = [
        pltpu.make_async_copy(wk_h, wl.at[1], lsem.at[0]),
        pltpu.make_async_copy(wv_h, wl.at[2], lsem.at[1]),
        pltpu.make_async_copy(wq_h, wl.at[0], lsem.at[2]),
        pltpu.make_async_copy(x_src, xg.at[0], lsem.at[3]),
        pltpu.make_async_copy(wo_h, wol, lsem.at[4]),
        pltpu.make_async_copy(wdn_h.at[:, pl.ds(c_i * FS, FS)], wdt.at[t_i, s_i], lsem.at[5]),
        pltpu.make_async_copy(wup_h.at[:, pl.ds(c_i * FS, FS)], wup.at[t_i, s_i], lsem.at[6]),
        pltpu.make_async_copy(c_src, ctg.at[0], lsem.at[7]),
    ]
    gains = [
        pltpu.make_async_copy(src, dst, lsem.at[16 + n])
        for n, (src, dst) in enumerate((
            (g1_a, g1_h), (b1_a, b1_h), (g2_a, g2_h), (b2_a, b2_h), (qg_a, qg_h), (kg_a, kg_h),
        ))
    ]
    for copy in gains + locals_:
        copy.start()

    barrier = pltpu.get_barrier_semaphore()
    greet = [at_ctx(j) for j in range(1, CN)] + [at_z(j) for j in range(1, ZN)] + [sib]
    for dev in greet:
        pl.semaphore_signal(barrier, inc=1, device_id=dev, device_id_type=MESH)

    for copy in gains:
        copy.wait()
    smalls[t_i, s_i] = jnp.zeros((8, 256), full_type)
    for k, ref in enumerate((g1_h, b1_h, g2_h, b2_h)):
        smalls[t_i, s_i, k:k + 1, :R] = ref[...].astype(full_type).reshape(1, R)
    heads = HW // 64
    piece = qg_h.shape[1]
    lane_of = lax.broadcasted_iota(jnp.int32, (piece, HW), 1)
    spread = (
        (lane_of % piece == lax.broadcasted_iota(jnp.int32, (piece, HW), 0)) & ((lane_of % 64) // piece == s_i)
    ).astype(full_type).astype(low_type)
    head_of = lax.broadcasted_iota(jnp.int32, (qg_h.shape[0], HW), 0)
    wanted = head_of == place * heads + lax.broadcasted_iota(jnp.int32, (qg_h.shape[0], HW), 1) // 64
    wanted = wanted & (t_i == tstar)
    for k, ref in ((4, qg_h), (5, kg_h)):
        row = jnp.sum(jnp.where(wanted, dot(ref[...], spread), 0.0), axis=0, keepdims=True)
        smalls[t_i, s_i, k:k + 1, :HW] = row

    pl.semaphore_wait(barrier, len(greet))

    for j in range(1, CN):
        put("x", CN, j, x_src, xg.at[j], at_ctx(j))
    for j in range(1, ZN):
        put("small", ZN, j, smalls.at[t_i, s_i], smalls.at[t_i, s_i], at_z(j))

    def picker(at, lanes, offset):
        rows = lax.broadcasted_iota(jnp.int32, (half_chips * HW, lanes), 0)
        cols = lax.broadcasted_iota(jnp.int32, (half_chips * HW, lanes), 1) - offset
        return ((rows == cols + at * HW) & (cols >= 0) & (cols < HW)).astype(full_type).astype(low_type)

    projections = (("wkv", wkv), ("wq", wqp), ("wo", wop))

    def send_projection(name, buf):
        for j in range(1, ZN):
            put(name, ZN, j, buf.at[s_i], buf.at[s_i], at_z(j))
        put(name, ZN, 0, buf.at[s_i], buf.at[s_i], sib)

    locals_[4].wait()

    @pl.when(t_i == tstar)
    def _():
        for n in range(3):
            locals_[n].wait()
        wkv[s_i] = (
            dot(wl[1], picker(place, 2 * HW, 0)) + dot(wl[2], picker(place, 2 * HW, HW))
        ).astype(low_type)
        send_projection(*projections[0])
        for source, packed in ((wl.at[0], wqp), (wol, wop)):
            packed[s_i] = (
                dot(source[:HR], picker(place, 2 * HW, 0)) + dot(source[HR:], picker(place, 2 * HW, HW))
            ).astype(low_type)

    @pl.when(t_i != tstar)
    def _():
        for n in range(3):
            locals_[n].wait()

    for j in range(1, ZN):
        got("small", ZN, j, smalls.at[t_i, flip(s_i, j, ZN)], at_z(j))
    put("smallt", 1, 0, smalls.at[t_i], smalls.at[t_i], sib)

    locals_[3].wait()

    def norm_rows(values):
        mean = jnp.sum(values, axis=-1, keepdims=True) * inv_d
        center = values - mean
        inverse = lax.rsqrt(jnp.sum(center * center, axis=-1, keepdims=True) * inv_d + norm_eps)
        return center * inverse, inverse

    ln_rows = jnp.concatenate([smalls[t_i, k][:, :R] for k in range(ZN)], axis=1)
    g1row, b1row, g2row, b2row = (ln_rows[k:k + 1] for k in range(4))

    def first_norm(j, _):
        @pl.when(j > 0)
        def _():
            got("x", CN, j, xg.at[j], at_ctx(j))

        for n in (1, 2):
            @pl.when((j == n) & (t_i == tstar))
            def _():
                send_projection(*projections[n])

        normed, _unused = norm_rows(xg[j].astype(full_type))
        xh1[j] = normed
        hidden = (normed * g1row + b1row).astype(low_type)
        h1[j] = hidden
        h1_t[:, pl.ds(pl.multiple_of(j * TB, TB), TB)] = hidden.T
        return 0

    HB = TB // 2

    def spread(name, src, dst_of):
        for j in (1, 2):
            put(name, 5, j, src, dst_of(j), at_ctx(j))

    def pass_on(name, buf):
        for j in (1, 2):
            got(name, 5, j, buf.at[j], at_ctx(j))
            half = pl.ds((j - 1) * HB, HB)
            put_as(name, 5, 2 + j, 2 + j, buf.at[j, half], buf.at[3, half], at_ctx(3 - j))

    def spread_halves(name, buf):
        for j in (1, 2):
            half = pl.ds((j - 1) * HB, HB)
            put(name, 7, j, buf.at[0, half], buf.at[j, half], at_ctx(j))
        for j in (1, 2):
            half = pl.ds((2 - j) * HB, HB)
            put(name, 7, 4 + j, buf.at[0, half], buf.at[j, half], at_ctx(j))

    def pass_halves(name, buf):
        for j in (1, 2):
            half = pl.ds((j - 1) * HB, HB)
            got(name, 7, j, buf.at[j, half], at_ctx(j))
            put_as(name, 7, 2 + j, 2 + j, buf.at[j, half], buf.at[3, half], at_ctx(3 - j))

    def second_half(name, buf, j):
        got(name, 7, 4 + j, buf.at[j, pl.ds((2 - j) * HB, HB)], at_ctx(j))

    def diagonal_halves(name, buf):
        for j in (1, 2):
            got(name, 7, 2 + j, buf.at[3, pl.ds((j - 1) * HB, HB)], at_ctx(3 - j))

    def send_halves(name, src, land):
        for j in (1, 2):
            half = pl.ds((j - 1) * HB, HB)
            put_as(name, 5, 2 + j, 2 + j, src.at[3, half], land.at[3, half], at_ctx(j))

    def add_halves(name, src, land):
        for j in (1, 2):
            half = pl.ds((j - 1) * HB, HB)
            got(name, 5, 2 + j, land.at[3, half], at_ctx(j))
            src[3 - j, half] = (src[3 - j, half].astype(full_type) + land[3, half].astype(full_type)).astype(low_type)
        for j in (1, 2):
            put_as(name, 5, j, j, src.at[j], land.at[j], at_ctx(j))

    def have_rest(name, buf):
        for j in (1, 2):
            half = pl.ds((j - 1) * HB, HB)
            got(name, 5, 2 + j, buf.at[3, half], at_ctx(3 - j))

    spread("ct", c_src, lambda j: ctg.at[j])
    lax.fori_loop(0, CN, first_norm, 0)

    got("smallt", 1, 0, smalls.at[o_i], sib)
    head_rows = smalls[0, 0][4:6, :HW]
    for a in range(2):
        for k in range(ZN):
            if a or k:
                head_rows = head_rows + smalls[a, k][4:6, :HW]
    qgrow, kgrow = head_rows[0:1], head_rows[1:2]

    lane = lax.broadcasted_iota(jnp.int32, (1, HW), 1) // 64
    mask_f = [(lane == h).astype(full_type) for h in range(heads)]
    mask_b = [m.astype(low_type) for m in mask_f]
    same_head = (
        lax.broadcasted_iota(jnp.int32, (HW, HW), 0) // 64
        == lax.broadcasted_iota(jnp.int32, (HW, HW), 1) // 64
    ).astype(full_type).astype(low_type)

    def head_mean(values):
        high = values.astype(low_type)
        rest = (values - high.astype(full_type)).astype(low_type)
        return (dot(high, same_head) + dot(rest, same_head)) * (1.0 / 64)

    def weight_ready(name, buf):
        @pl.when(t_i != tstar)
        def _():
            got(name, ZN, 0, buf.at[s_i], sib)

        for j in range(1, ZN):
            block = buf.at[flip(s_i, j, ZN)]
            got(name, ZN, j, block, sib)

            @pl.when(t_i == tstar)
            def _():
                pltpu.make_async_remote_copy(
                    src_ref=block, dst_ref=block,
                    send_sem=leaving("f" + name, ZN, j), recv_sem=arrival(name, ZN, j),
                    device_id=sib, device_id_type=MESH,
                ).start()

    def unpack(packed, buf):
        for z in range(ZN):
            block = packed[z]
            buf[z, :HR] = block[:, :HW]
            buf[z, HR:] = block[:, HW:]

    h1_all = h1[...].reshape(TK, D)
    weight_ready(*projections[0])
    raw = dot(h1_all, wkv[...].reshape(D, 2 * HW))
    vall[0] = raw[:, HW:].astype(low_type)
    put("v", 1, 0, vall.at[0], vall.at[1], sib)
    raw = raw[:, :HW]
    inverse = lax.rsqrt(head_mean(raw * raw) + norm_eps)
    normed = raw * inverse
    nk[...] = normed
    sk[...] = inverse
    kall[0] = (normed * kgrow).astype(low_type)
    put("k", 1, 0, kall.at[0], kall.at[1], sib)
    weight_ready(*projections[1])
    unpack(wqp, wqb)
    mlp_weights = (("wd", wdt), ("wu", wup))

    def own_mlp(name, buf):
        block = buf.at[t_i, s_i]
        put_as(name, 5, 0, 0, block, block, plane(pair))

        @pl.when(jnp.logical_not(outer))
        def _():
            put_as(name, 5, 1, 1, block, block, plane(far_in))

    def pass_mlp(name, buf, stage):
        source, target = ((pair, far_in), (far_in, pair), (far_out, pair))[stage]
        recv = (2, 1, 2)[stage]

        @pl.when(jnp.logical_not(outer))
        def _():
            block = buf.at[t_i, source]
            got(name, 5, stage, block, plane(pair))
            put_as(name, 5, 2 + stage, recv, block, block, plane(target))

    def have_mlp(name, buf):
        @pl.when(outer)
        def _():
            for n, z in enumerate((pair, far_in, far_out)):
                got(name, 5, n, buf.at[t_i, z], plane(pair))

    locals_[5].wait()
    own_mlp(*mlp_weights[0])
    locals_[6].wait()
    own_mlp(*mlp_weights[1])
    raw = dot(h1_all, wqb[...].reshape(D, HW))
    inverse = lax.rsqrt(head_mean(raw * raw) + norm_eps)
    normed = raw * inverse
    nq[...] = normed
    sq[...] = inverse
    qs[...] = ((normed * qgrow).astype(low_type) * 0.125).astype(low_type).reshape(CN, TB, HW)

    got("k", 1, 0, kall.at[1], sib)
    got("v", 1, 0, vall.at[1], sib)

    def stacked(block):
        return jnp.concatenate([block * m for m in mask_b], axis=0)

    def folded(block):
        total = block[0:TB] * mask_f[0]
        for h in range(1, heads):
            total = total + block[h * TB:(h + 1) * TB] * mask_f[h]
        return total

    ptop[...] = jnp.full(ptop.shape, -3.0e38, full_type)

    def attend(i, _):
        j = CN - 1 - i

        @pl.when(i == CN - 1)
        def _():
            pass_mlp(*mlp_weights[0], 0)
            pass_mlp(*mlp_weights[0], 1)

        sbuf[...] = dot(stacked(qs[j]), kall[...].reshape(2 * TK, HW), NT)
        for h in range(heads):
            rows = slice(h * TB, (h + 1) * TB)
            scores = sbuf[rows]
            ptop[h:h + 1] = jnp.maximum(ptop[h:h + 1], jnp.max(scores, axis=0, keepdims=True))
            expo = jnp.exp(scores)
            pst[j, rows] = expo * (1.0 / jnp.sum(expo, axis=-1, keepdims=True))
        mixed = folded(dot(pst[j].astype(low_type), vall[...].reshape(2 * TK, HW)))
        attq[j] = mixed.astype(low_type)

        @pl.when(i == 0)
        def _():
            weight_ready(*projections[2])
            unpack(wop, wob)

        branch = dot(attq[j], wob[...].reshape(D, HW), NT)

        @pl.when(j > 0)
        def _():
            brs[j] = branch.astype(low_type)
            put("br", CN, j, brs.at[j], brr.at[j], at_ctx(j))

        @pl.when(j == 0)
        def _():
            boown[...] = branch

        return 0

    lax.fori_loop(0, CN, attend, 0)
    pass_mlp(*mlp_weights[1], 0)
    pass_mlp(*mlp_weights[1], 1)
    pass_on("ct", ctg)
    pass_mlp(*mlp_weights[0], 2)
    peak_rows = jnp.max(ptop[...], axis=-1, keepdims=True)
    lane_id = lax.broadcasted_iota(jnp.int32, (8, 128), 1)
    own_peak = jnp.full((8, 128), -3.0e38, full_type)
    for h in range(heads):
        own_peak = jnp.where(lane_id == c_i * heads + h, peak_rows[h:h + 1], own_peak)
    pks[0] = own_peak
    put("pkt", 1, 0, pks.at[0], pks.at[1], sib)

    branch = boown[...]
    for j in (3, 2, 1):
        if j == 1:
            pass_mlp(*mlp_weights[1], 2)
        got("br", CN, j, brr.at[j], at_ctx(j))
        branch = branch + brr[j].astype(full_type)
    resid = xg[0].astype(full_type) + branch
    boown[...] = resid
    xhat2, inv2 = norm_rows(resid)
    h2[0] = (xhat2 * g2row + b2row).astype(low_type)
    spread_halves("h2", h2)

    locals_[7].wait()
    have_rest("ct", ctg)
    ct_t[...] = ctg[...].reshape(TK, D).T
    have_mlp(*mlp_weights[0])
    put("wdt", 1, 0, wdt.at[t_i], wdt.at[t_i], sib)
    ga[t_i] = dot(ctg[...].reshape(TK, D), wdt[t_i].reshape(D, FS)).reshape(CN, TB, FS)
    pass_halves("h2", h2)
    have_mlp(*mlp_weights[1])
    put("wut", 1, 0, wup.at[t_i], wup.at[t_i], sib)
    got("wdt", 1, 0, wdt.at[o_i], sib)
    ga[o_i] = dot(ctg[...].reshape(TK, D), wdt[o_i].reshape(D, FS)).reshape(CN, TB, FS)
    got("wut", 1, 0, wup.at[o_i], sib)

    def mlp(i, _):
        j = ((i + 1) % 3) * (1 - i // 3) + 3 * (i // 3)

        for n in (1, 2):
            @pl.when(j == n)
            def _():
                second_half("h2", h2, n)

        @pl.when(j == 3)
        def _():
            diagonal_halves("h2", h2)

        block = h2[j]
        h2_t[:, pl.ds(pl.multiple_of(j * TB, TB), TB)] = block.T
        for a in range(2):
            up = dot(block, wup[a].reshape(D, FS))
            phi = 0.5 * (1.0 + lax.erf(up * 0.7071067811865476))
            dens = jnp.exp(up * up * -0.5) * 0.3989422804014327
            part = slice(a * FS, (a + 1) * FS)
            act[j, :, part] = (up * phi).astype(low_type)
            gu[j, :, part] = (ga[a, j] * (phi + up * dens)).astype(low_type)
        grad_two = (
            dot(gu[j, :, :FS], wup[0].reshape(D, FS), NT) + dot(gu[j, :, FS:], wup[1].reshape(D, FS), NT)
        )

        @pl.when(j == 0)
        def _():
            g2own[...] = grad_two

        @pl.when(j > 0)
        def _():
            g2s[j] = grad_two.astype(low_type)
            put("g2", CN, j, g2s.at[j], g2r.at[j], at_ctx(j))

        return 0

    lax.fori_loop(0, CN, mlp, 0)

    got("pkt", 1, 0, pks.at[1], sib)
    pks[2] = jnp.maximum(pks[0], pks[1])
    for j in range(1, ZN):
        put("pkz", ZN, j, pks.at[2], pks.at[2 + j], at_z(j))
    own_part = pl.ds(pl.multiple_of(t_i * FS, FS), FS)
    other_part = pl.ds(pl.multiple_of(o_i * FS, FS), FS)
    pairs = ((h2_t, gu), (ct_t, act))
    for k, (left, right) in enumerate(pairs):
        gsib_s[k] = dot(left[...], right[:, :, other_part].reshape(TK, FS)).astype(low_type)
        put("gs", 2, k, gsib_s.at[k], gsib_r.at[k], sib)

    def send_far(k):
        @pl.when(outer)
        def _():
            put("gz%d" % k, 4, 2, gz_s.at[k, far_out], gz_r.at[k, 2], plane(pair))
            put("gz%d" % k, 4, 3, gz_s.at[k, far_in], gz_r.at[k, 3], plane(pair))

    def send_near(k):
        put("gz%d" % k, 4, 0, gz_s.at[k, pair], gz_r.at[k, 0], plane(pair))

    own_grads = [dot(left[...], right[:, :, own_part].reshape(TK, FS)) for left, right in pairs]
    for k in range(2):
        got("gs", 2, k, gsib_r.at[k], sib)
        total = own_grads[k] + gsib_r[k].astype(full_type)
        gkeep[k] = total
        gz_s[k] = total.astype(low_type).reshape(ZN, R, FS)
        send_far(k)
    send_near(0)
    send_near(1)

    def down(j, _):
        part = (
            dot(act[j, :, :FS], wdt[0].reshape(D, FS), NT) + dot(act[j, :, FS:], wdt[1].reshape(D, FS), NT)
        )

        @pl.when(j == 0)
        def _():
            boown[...] += part

        @pl.when(j > 0)
        def _():
            bos[j] = part.astype(low_type)

        return 0

    lax.fori_loop(0, CN, down, 0)

    def relay_mlp(k):
        @pl.when(jnp.logical_not(outer))
        def _():
            for n, z in ((2, far_out), (3, far_in)):
                got("gz%d" % k, 4, n, gz_r.at[k, n], plane(pair))
                mine_part = gkeep[k, pl.ds(pl.multiple_of(z * R, R), R)]
                gz_s[k, z] = (mine_part + gz_r[k, n].astype(full_type)).astype(low_type)
                put_as("gz%d" % k, 4, n, 1, gz_s.at[k, z], gz_r.at[k, 1], plane(z))

    def share_mlp(k, out):
        total = gkeep[k, pl.ds(pl.multiple_of(s_i * R, R), R)]
        for n in range(2):
            got("gz%d" % k, 4, n, gz_r.at[k, n], plane(pair))
            total = total + gz_r[k, n].astype(full_type)
        gfin[k] = total.astype(low_type)
        spread("gc%d" % k, gfin.at[k], lambda j: out.at[c_i])
        pltpu.make_async_copy(gfin.at[k], out.at[c_i], lsem.at[8 + k]).start()

    grad_two = g2own[...]
    for j in range(1, CN):
        got("g2", CN, j, g2r.at[j], at_ctx(j))
        grad_two = grad_two + g2r[j].astype(full_type)
    ln2g = jnp.sum(grad_two * xhat2, axis=0, keepdims=True)
    ln2b = jnp.sum(grad_two, axis=0, keepdims=True)
    hat = grad_two * g2row
    grad_resid = ctg[0].astype(full_type) + inv2 * (
        hat
        - jnp.sum(hat, axis=-1, keepdims=True) * inv_d
        - xhat2 * (jnp.sum(hat * xhat2, axis=-1, keepdims=True) * inv_d)
    )
    gres[...] = grad_resid
    gb = grad_resid.astype(low_type)
    gbg[0] = gb
    spread_halves("gb", gbg)
    send_halves("bo", bos, bor)

    peak = pks[2]
    for j in range(1, ZN):
        got("pkz", ZN, j, pks.at[2 + j], at_z(j))
        peak = jnp.maximum(peak, pks[2 + j])
    first = 2 + ZN
    pks[first] = peak
    for j in range(1, CN):
        put("pkc", CN, j, pks.at[first], pks.at[first + j], at_ctx(j))

    dkt[...] = jnp.zeros_like(dkt)
    dvt[...] = jnp.zeros_like(dvt)

    def attend_back(j, _):
        @pl.when(j == 1)
        def _():
            pass_halves("gb", gbg)
            relay_mlp(0)
            second_half("gb", gbg, 1)

        @pl.when(j == 2)
        def _():
            second_half("gb", gbg, 2)

        @pl.when(j == CN - 1)
        def _():
            add_halves("bo", bos, bor)
            diagonal_halves("gb", gbg)

        grad_rows = stacked(dot(gbg[j], wob[...].reshape(D, HW)).astype(low_type))
        query_rows = stacked(qs[j])
        sbuf[...] = dot(grad_rows, vall[...].reshape(2 * TK, HW), NT)

        for h in range(heads):
            rows = slice(h * TB, (h + 1) * TB)
            probs, grad_probs = pst[j, rows], sbuf[rows]
            inner = jnp.sum(probs * grad_probs, axis=-1, keepdims=True)
            dsb[rows] = (probs * (grad_probs - inner)).astype(low_type)
        grad_scores = dsb[...]
        dqb[j] = folded(dot(grad_scores, kall[...].reshape(2 * TK, HW))) * 0.125
        dvt[...] += dot(grad_rows, pst[j].astype(low_type), TN)
        dkt[...] += dot(query_rows, grad_scores, TN)
        return 0

    lax.fori_loop(0, CN, attend_back, 0)
    dks_s[0] = dvt[:, TK:].astype(low_type)
    dks_s[1] = dkt[:, TK:].astype(low_type)
    for k in range(2):
        put("dk", 2, k, dks_s.at[k], dks_r.at[k], sib)

    for j in range(1, CN):
        got("pkc", CN, j, pks.at[first + j], at_ctx(j))
        peak = jnp.maximum(peak, pks[first + j])
    peak_v[...] = peak
    pltpu.make_async_copy(peak_v, peak_o, lsem.at[22]).start()

    relay_mlp(1)
    def unnorm(grad_n, gain_row, normed, inverse):
        gain_grad = jnp.sum(grad_n * normed, axis=0, keepdims=True)
        e = grad_n * gain_row
        return (inverse * (e - normed * head_mean(e * normed))).astype(low_type), gain_grad

    def share_grad(n, full):
        full = full.reshape(ZN, 2, HR, 2 * HW)
        low_full = full.astype(low_type)
        for k in range(2):
            @pl.when(o_i == k)
            def _():
                qsib_s[n] = low_full[:, k]

            @pl.when(t_i == k)
            def _():
                qown[n] = full[:, k]

        put("qg", 2, n, qsib_s.at[n], qsib_r.at[n], sib)

    pieces = {1: (("qz1", 0, HR),), 0: (("qz0", 0, HR // 2), ("qz2", HR // 2, HR // 2))}

    def reduce_grad(n):
        got("qg", 2, n, qsib_r.at[n], sib)
        total = qown[n] + qsib_r[n].astype(full_type)
        qown[n] = total
        qz_s[n] = total.astype(low_type)
        if n == 1:
            @pl.when(outer)
            def _():
                put("qz1", 4, 2, qz_s.at[1, far_out], qz_r.at[1, 2], plane(pair))
                put("qz1", 4, 3, qz_s.at[1, far_in], qz_r.at[1, 3], plane(pair))

            put("qz1", 4, 0, qz_s.at[1, pair], qz_r.at[1, 0], plane(pair))
            return
        for name, first, count in pieces[n]:
            rows = pl.ds(first, count)
            for j in range(1, ZN):
                put(name, ZN, j, qz_s.at[n, flip(s_i, j, ZN), rows], qz_r.at[n, j, rows], at_z(j))

    def relay_grad():
        @pl.when(jnp.logical_not(outer))
        def _():
            for n, z in ((2, far_out), (3, far_in)):
                got("qz1", 4, n, qz_r.at[1, n], plane(pair))
                qz_s[1, z] = (qown[1, z] + qz_r[1, n].astype(full_type)).astype(low_type)
                put_as("qz1", 4, n, 1, qz_s.at[1, z], qz_r.at[1, 1], plane(z))

    grad_raw, q_gain_row = unnorm(dqb[...].reshape(TK, HW), qgrow, nq[...], sq[...])
    dqr[...] = grad_raw
    empty = jnp.zeros((TK, HW), low_type)
    share_grad(1, (
        dot(h1_t[...], jnp.concatenate([dqr[...], empty], axis=1))
        + dot(gbg[...].reshape(TK, D), jnp.concatenate([empty, attq[...].reshape(TK, HW)], axis=1), TN)
    ))
    share_mlp(0, upo)
    got("dk", 2, 0, dks_r.at[0], sib)
    grad_v = (dvt[:, :TK] + dks_r[0].astype(full_type)).T.astype(low_type)
    got("dk", 2, 1, dks_r.at[1], sib)
    grad_k = (dkt[:, :TK] + dks_r[1].astype(full_type)).T
    grad_raw, k_gain_row = unnorm(grad_k, kgrow, nk[...], sk[...])
    dkv[...] = jnp.concatenate([grad_raw, grad_v], axis=1)
    ln1g = jnp.zeros((1, D), full_type)
    ln1b = jnp.zeros((1, D), full_type)
    for j in range(CN - 1, -1, -1):
        rows = slice(j * TB, (j + 1) * TB)
        part = dot(dqr[rows], wqb[...].reshape(D, HW), NT) + dot(dkv[rows], wkv[...].reshape(D, 2 * HW), NT)
        if j:
            g1s[j] = part.astype(low_type)
        else:
            g1own[...] = part
        if j == 3:
            send_halves("g1", g1s, g1r)
            share_grad(0, dot(h1_t[...], dkv[...]))
            reduce_grad(1)
        ln1g = ln1g + jnp.sum(part * xh1[j], axis=0, keepdims=True)
        ln1b = ln1b + jnp.sum(part, axis=0, keepdims=True)
        if j == 1:
            reduce_grad(0)
    rows_s[0] = jnp.zeros_like(rows_s[0])
    HD2 = D // 2
    for k, row in enumerate((ln1g, ln1b, ln2g, ln2b)):
        rows_s[0, 2 * k:2 * k + 1, :HD2] = row[:, :HD2]
        rows_s[0, 2 * k + 1:2 * k + 2, :HD2] = row[:, HD2:]
    rows_s[0, 0:1, HD2:HD2 + HW] = q_gain_row
    rows_s[0, 1:2, HD2:HD2 + HW] = k_gain_row
    put("rt", 1, 0, rows_s.at[0], rows_r.at[0], sib)
    add_halves("g1", g1s, g1r)
    relay_grad()
    share_mlp(1, dno)
    got("rt", 1, 0, rows_r.at[0], sib)
    rows_s[1] = rows_s[0] + rows_r[0]
    for j in range(1, ZN):
        put("rz", ZN, j, rows_s.at[1], rows_r.at[j], at_z(j))

    total = boown[...]
    for j in (1, 2):
        got("bo", 5, j, bor.at[j], at_ctx(j))
        total = total + bor[j].astype(full_type)
    own_rows = pl.ds(t_i * TB, TB)
    obuf[0] = total.astype(low_type)
    put("ob", 2, 0, obuf.at[0], bo_o.at[own_rows], sib)
    pltpu.make_async_copy(obuf.at[0], bo_o.at[own_rows], lsem.at[10]).start()

    def to_owner(name, first, count, n):
        rows = pl.ds(first, count)
        return qfin.at[n, rows], qkvo.at[place, t_i, n, rows]

    def share_fin(n, which=slice(None)):
        for name, first, count in pieces[n][which]:
            rows = slice(first, first + count)
            total = qown[n, s_i, rows]
            for j in (0, 1) if n == 1 else range(1, ZN):
                got(name, 4, j, qz_r.at[n, j, pl.ds(first, count)], at_z(1))
                total = total + qz_r[n, j, rows].astype(full_type)
            qfin[n, rows] = total.astype(low_type)
            src, dst = to_owner(name, first, count, n)
            slot = spot("r" + name, 2 * half_chips) + place * 2 + t_i
            for j in range(1, CN):
                pltpu.make_async_remote_copy(
                    src_ref=src, dst_ref=dst,
                    send_sem=leaving("s" + name, CN, j), recv_sem=rsem.at[slot],
                    device_id=(s_i, flip(c_i, j, CN), tstar), device_id_type=MESH,
                ).start()

            @pl.when(t_i == tstar)
            def _():
                pltpu.make_async_copy(src, dst, lsem.at[12 + (name == "qz2") * 2 + n]).start()

            @pl.when(t_i != tstar)
            def _():
                pltpu.make_async_remote_copy(
                    src_ref=src, dst_ref=dst,
                    send_sem=leaving("o" + name, 1, 0), recv_sem=rsem.at[slot],
                    device_id=sib, device_id_type=MESH,
                ).start()

    def pass_grad(k, out):
        for j in (1, 2):
            block = out.at[flip(c_i, j, CN)]
            got("gc%d" % k, 5, j, block, at_ctx(j))
            half = block.at[pl.ds((j - 1) * HR, HR)]
            put_as("gc%d" % k, 5, 2 + j, 2 + j, half, half, at_ctx(3 - j))

    pass_grad(0, upo)
    share_fin(0, slice(0, 1))

    xhat1, inv1 = norm_rows(xg[0].astype(full_type))
    grad_one = g1own[...]
    for j in (1, 2):
        got("g1", 5, j, g1r.at[j], at_ctx(j))
        grad_one = grad_one + g1r[j].astype(full_type)
    hat = grad_one * g1row
    grad_in = gres[...] + inv1 * (
        hat
        - jnp.sum(hat, axis=-1, keepdims=True) * inv_d
        - xhat1 * (jnp.sum(hat * xhat1, axis=-1, keepdims=True) * inv_d)
    )
    obuf[1] = grad_in.astype(low_type)
    put("ob", 2, 1, obuf.at[1], ig_o.at[own_rows], sib)
    pltpu.make_async_copy(obuf.at[1], ig_o.at[own_rows], lsem.at[11]).start()

    pass_grad(1, dno)
    share_fin(0, slice(1, 2))

    rows_sum = rows_s[1]
    for j in range(1, ZN):
        got("rz", ZN, j, rows_r.at[j], at_z(j))
        rows_sum = rows_sum + rows_r[j]
    rows_s[2] = rows_sum
    for j in range(1, CN):
        put("rc", CN, j, rows_s.at[2], rows_r.at[ZN + j], at_ctx(j))
    qkr_v[c_i] = rows_sum[:, HD2:]

    share_fin(1)
    total = rows_sum[:, :HD2]
    for j in range(1, CN):
        got("rc", CN, j, rows_r.at[ZN + j], at_ctx(j))
        block = rows_r[ZN + j]
        total = total + block[:, :HD2]
        qkr_v[flip(c_i, j, CN)] = block[:, HD2:]
    lnr_v[...] = total
    pltpu.make_async_copy(lnr_v, lnr_o, lsem.at[23]).start()
    pltpu.make_async_copy(qkr_v, qkr_o, lsem.at[24]).start()

    for n, (src, dst) in enumerate(((peak_v, peak_o), (lnr_v, lnr_o), (qkr_v, qkr_o))):
        pltpu.make_async_copy(src, dst, lsem.at[22 + n]).wait()
    for k, out in ((0, upo), (1, dno)):
        for j in (1, 2):
            half = out.at[flip(c_i, 3, CN), pl.ds((j - 1) * HR, HR)]
            got("gc%d" % k, 5, 2 + j, half, at_ctx(3 - j))
        pltpu.make_async_copy(gfin.at[k], out.at[c_i], lsem.at[8 + k]).wait()
    other_rows = pl.ds(o_i * TB, TB)
    for k, out in ((0, bo_o), (1, ig_o)):
        got("ob", 2, k, out.at[other_rows], sib)
        pltpu.make_async_copy(obuf.at[k], out.at[own_rows], lsem.at[10 + k]).wait()

    all_pieces = [(name, first, count, n) for n in pieces for name, first, count in pieces[n]]

    @pl.when(t_i == tstar)
    def _():
        for name, first, count, n in all_pieces:
            src, dst = to_owner(name, first, count, n)
            pltpu.make_async_copy(src, dst, lsem.at[12 + (name == "qz2") * 2 + n]).wait()

    for p in range(half_chips):
        for a in range(2):
            @pl.when((t_i != tstar) | (place != p) | (t_i != a))
            def _():
                for name, first, count, n in all_pieces:
                    rows = pl.ds(first, count)
                    pltpu.make_async_remote_copy(
                        src_ref=qfin.at[n, rows], dst_ref=qkvo.at[p, a, n, rows],
                        send_sem=ssem.at[0],
                        recv_sem=rsem.at[spot("r" + name, 2 * half_chips) + p * 2 + a],
                        device_id=sib, device_id_type=MESH,
                    ).wait_recv()

    three = pl.ds(1, 3)
    for name, ref in (
        ("x", xg), ("br", brs), ("h2", h2), ("g2", g2s), ("pkc", pks), ("rc", rows_r), ("small", smalls.at[t_i]),
        ("pkz", pks), ("rz", rows_r), ("ct", ctg), ("gb", gbg), ("bo", bos), ("g1", g1s),
        ("gc0", gz_s.at[0]), ("gc1", gz_s.at[1]), ("gz0", gz_s.at[0]), ("gz1", gz_s.at[1]),
    ):
        sent(name, 5, 0, ref.at[three])
    for name, first, count, n in all_pieces:
        for way in ("", "s"):
            sent(way + name, 4, 0, qz_s.at[n, three, pl.ds(first, count)])
    for name, buf in mlp_weights:
        sent(name, 5, 0, buf.at[t_i, s_i])

        @pl.when(jnp.logical_not(outer))
        def _():
            for n in range(1, 5):
                sent(name, 5, n, buf.at[t_i, s_i])

    for name, ref in (
        ("smallt", smalls.at[t_i]), ("k", kall.at[0]), ("v", vall.at[0]), ("pkt", pks.at[0]),
        ("wdt", wdt.at[t_i]), ("wut", wup.at[t_i]), ("rt", rows_s.at[0]),
    ):
        sent(name, 1, 0, ref)
    for k in range(2):
        sent("gs", 2, k, gsib_s.at[k])
        sent("dk", 2, k, dks_s.at[k])
        sent("ob", 2, k, obuf.at[k])
        sent("qg", 2, k, qsib_s.at[k])

    @pl.when(t_i == tstar)
    def _():
        for name, buf in projections:
            sent(name, ZN, 0, buf)
            sent("f" + name, ZN, 0, buf.at[three])

    @pl.when(t_i != tstar)
    def _():
        for name, first, count, n in all_pieces:
            sent("o" + name, 1, 0, qfin.at[n, pl.ds(first, count)])


ARRIVALS, LEAVINGS = 123, 57


def fused_call(sizes, *operands):
    CN, ZN, TB, D, HW, FS, R = sizes
    TK = CN * TB
    HR = R // 2
    half_chips = CN // 2
    heads = HW // 64
    lo, hi = low_type, full_type
    V = pltpu.VMEM
    any_spec = pl.BlockSpec(memory_space=pl.ANY)
    gain_shape = operands[6].shape
    out_shape = [
        jax.ShapeDtypeStruct((2 * TB, D), lo),
        jax.ShapeDtypeStruct((2 * TB, D), lo),
        jax.ShapeDtypeStruct((CN, R, FS), lo),
        jax.ShapeDtypeStruct((CN, R, FS), lo),
        jax.ShapeDtypeStruct((half_chips, 2, 2, HR, 2 * HW), lo),
        jax.ShapeDtypeStruct((8, D // 2), hi),
        jax.ShapeDtypeStruct((CN, 8, 256), hi),
        jax.ShapeDtypeStruct((8, 128), hi),
    ]
    scratch = [
        V((CN, TB, D), lo), V((CN, TB, D), lo), V((2, ZN, 8, 256), hi),
        V((3, R, half_chips * HW), lo), V((R, half_chips * HW), lo),
        V((ZN, R, 2 * HW), lo), V((ZN, HR, 2 * HW), lo), V((ZN, HR, 2 * HW), lo),
        V((ZN, R, HW), lo), V((ZN, R, HW), lo), V((2, ZN, R, FS), lo), V((2, ZN, R, FS), lo),
        V((D, TK), lo), V((D, TK), lo), V((D, TK), lo),
        V((CN, TB, D), hi), V((CN, TB, D), lo),
        V((TK, HW), hi), V((TK, HW), hi), V((TK, HW), hi), V((TK, HW), hi),
        V((CN, TB, HW), lo), V((2, TK, HW), lo), V((2, TK, HW), lo),
        V((CN, heads * TB, 2 * TK), hi), V((heads * TB, 2 * TK), hi),
        V((CN, TB, HW), lo), V((CN, TB, D), lo), V((CN, TB, D), lo), V((2 + ZN + CN, 8, 128), hi),
        V((heads, 2 * TK), hi), V((heads * TB, 2 * TK), lo),
        V((CN, TB, D), lo), V((2, CN, TB, FS), hi), V((CN, TB, 2 * FS), lo), V((CN, TB, 2 * FS), lo),
        V((CN, TB, D), lo), V((CN, TB, D), lo), V((TB, D), hi),
        V((CN, TB, D), lo), V((CN, TB, D), lo), V((TB, D), hi),
        V((2, D, FS), lo), V((2, D, FS), lo), V((2, D, FS), hi),
        V((2, ZN, R, FS), lo), V((2, ZN, R, FS), lo), V((2, R, FS), lo),
        V((TB, D), hi), V((CN, TB, D), lo),
        V((CN, TB, HW), hi), V((HW, 2 * TK), hi), V((HW, 2 * TK), hi),
        V((2, HW, TK), lo), V((2, HW, TK), lo), V((TK, HW), lo), V((TK, 2 * HW), lo),
        V((CN, TB, D), lo), V((CN, TB, D), lo), V((TB, D), hi),
        V((2, ZN, HR, 2 * HW), lo), V((2, ZN, HR, 2 * HW), lo), V((2, ZN, HR, 2 * HW), hi),
        V((2, ZN, HR, 2 * HW), lo), V((2, ZN, HR, 2 * HW), lo), V((2, HR, 2 * HW), lo),
        V((3, 8, D // 2 + 256), hi), V((ZN + CN, 8, D // 2 + 256), hi), V((2, TB, D), lo),
        V((R,), lo), V((R,), lo), V((R,), lo), V((R,), lo), V(gain_shape, lo), V(gain_shape, lo),
        V((8, D // 2), hi), V((CN, 8, 256), hi), V((8, 128), hi),
        pltpu.SemaphoreType.DMA((25,)), pltpu.SemaphoreType.DMA((LEAVINGS,)), pltpu.SemaphoreType.DMA((ARRIVALS,)),
    ]
    return pl.pallas_call(
        functools.partial(fused_kernel, sizes),
        out_shape=out_shape,
        in_specs=[any_spec] * 14,
        out_specs=[any_spec] * 8,
        scratch_shapes=scratch,
        compiler_params=pltpu.CompilerParams(
            collective_id=0, has_side_effects=True, vmem_limit_bytes=56 * 2**20
        ),
    )(*operands)


def finish_kernel(
    sizes,
    bo, ig, up_h, dn_h, qkvo_h, lnr_h, qkr_h, peak_h, wq_h, wk_h,
    bo_o, ig_o, l1g_o, l1b_o, l2g_o, l2b_o, qg_o, kg_o, gq_o, gk_o, gv_o, go_o, gu_o, gd_o, cq_o, ck_o,
    upo, dno, qkvo, lnr, qkr, peak, wq, wk, bov, igv, gq, gk, gv, go, gu, gd, cq, ck, l1g, l1b, l2g, l2b, qg, kg, isem, osem,
):
    CN, ZN, TB, D, HW, FS, R = sizes
    half_chips = CN // 2
    s_i, t_i = lax.axis_index("shard"), lax.axis_index("tp")
    ins = [
        pltpu.make_async_copy(src, dst, isem.at[n])
        for n, (src, dst) in enumerate((
            (qkvo_h, qkvo), (up_h, upo), (dn_h, dno), (peak_h, peak), (wq_h, wq), (wk_h, wk),
            (lnr_h, lnr), (qkr_h, qkr), (bo, bov), (ig, igv),
        ))
    ]
    for n in (1, 2, 0, 8, 9, 3, 4, 5, 6, 7):
        ins[n].start()
    outs = []

    def leave(src, dst):
        copy = pltpu.make_async_copy(src, dst, osem.at[len(outs)])
        copy.start()
        outs.append(copy)

    for n, grads, stage, out in ((1, upo, gu, gu_o), (2, dno, gd, gd_o)):
        ins[n].wait()
        for c in range(CN):
            stage[:, c * FS:(c + 1) * FS] = grads[c].astype(full_type)
        leave(stage, out)
    ins[0].wait()
    for n, first, stage, out in ((1, 0, gq, gq_o), (0, 0, gk, gk_o), (0, HW, gv, gv_o), (1, HW, go, go_o)):
        for a in range(2):
            parts = [qkvo[p, a, n][:, first:first + HW] for p in range(half_chips)]
            stage[a * (R // 2):(a + 1) * (R // 2)] = jnp.concatenate(parts, axis=1).astype(full_type)
        leave(stage, out)
    for n, stage, out in ((8, bov, bo_o), (9, igv, ig_o)):
        ins[n].wait()
        leave(stage, out)
    heads = HW // 64
    for n in (3, 4, 5):
        ins[n].wait()
    factor = jnp.sqrt(clip_level / jnp.maximum(peak[0:1], clip_level))
    here = half_chips * heads
    lanes = lax.broadcasted_iota(jnp.int32, (1, here * 64), 1) // 64
    ids = lax.broadcasted_iota(jnp.int32, (1, 128), 1)
    columns = jnp.ones((1, here * 64), full_type)
    for h in range(here):
        one = jnp.sum(jnp.where(ids == t_i * here + h, factor, 0.0), axis=-1, keepdims=True)
        columns = jnp.where(lanes == h, one, columns)
    for weights, stage, out in ((wq, cq, cq_o), (wk, ck, ck_o)):
        stage[...] = (weights[...].astype(full_type) * columns).astype(low_type)
        leave(stage, out)
    ins[6].wait()
    ins[7].wait()
    for k, (stage, out) in enumerate(((l1g, l1g_o), (l1b, l1b_o), (l2g, l2g_o), (l2b, l2b_o))):
        row = jnp.zeros((1, R), full_type)
        for z in range(ZN):
            at = z * R % (D // 2)
            source = 2 * k + z * R // (D // 2)
            row = jnp.where(s_i == z, lnr[source:source + 1, at:at + R], row)
        stage[...] = row.reshape(R)
        leave(stage, out)
    piece = qg.shape[1]
    for p in range(half_chips):
        chip = pltpu.roll(qkr[t_i * half_chips + p], (256 - s_i * piece) % 256, 1)
        for h in range(heads):
            for k, stage in ((0, qg), (1, kg)):
                stage[p * heads + h:p * heads + h + 1] = chip[k:k + 1, h * 64:h * 64 + piece]
    leave(qg, qg_o)
    leave(kg, kg_o)
    for copy in outs:
        copy.wait()


def fused_layer(
    images, cotangent, ln1_gain, ln1_bias, ln2_gain, ln2_bias, q_gain, k_gain,
    w_query, w_key, w_value, w_out, w_up, w_down,
):
    CN, ZN = lax.axis_size("ctx"), lax.axis_size("shard")
    TB = images.shape[1] // 2
    D = images.shape[2]
    R = w_query.shape[0]
    HW = w_query.shape[1] // (CN // 2)
    FS = w_up.shape[1] // CN
    sizes = (CN, ZN, TB, D, HW, FS, R)
    results = fused_call(
        sizes, images, cotangent, ln1_gain, ln1_bias, ln2_gain, ln2_bias, q_gain, k_gain,
        w_query, w_key, w_value, w_out.T, w_up, w_down.T,
    )
    row = jax.ShapeDtypeStruct((R,), full_type)
    gain = jax.ShapeDtypeStruct(q_gain.shape, full_type)
    square = jax.ShapeDtypeStruct(w_query.shape, full_type)
    wide = jax.ShapeDtypeStruct(w_up.shape, full_type)
    tokens = jax.ShapeDtypeStruct(images.shape[1:], low_type)
    clipped = jax.ShapeDtypeStruct(w_query.shape, low_type)
    lo, hi = low_type, full_type
    V = pltpu.VMEM
    any_spec = pl.BlockSpec(memory_space=pl.ANY)
    out = pl.pallas_call(
        functools.partial(finish_kernel, sizes),
        out_shape=[tokens] * 2 + [row] * 4 + [gain] * 2 + [square] * 4 + [wide] * 2 + [clipped] * 2,
        in_specs=[any_spec] * 10,
        out_specs=[any_spec] * 16,
        scratch_shapes=[
            V((CN, R, FS), lo), V((CN, R, FS), lo), V((CN // 2, 2, 2, R // 2, 2 * HW), lo), V((8, D // 2), hi),
            V((CN, 8, 256), hi), V((8, 128), hi), V(w_query.shape, lo), V(w_query.shape, lo),
            V(images.shape[1:], lo), V(images.shape[1:], lo),
        ]
        + [V(w_query.shape, hi)] * 4 + [V(w_up.shape, hi)] * 2 + [V(w_query.shape, lo)] * 2
        + [V((R,), hi)] * 4 + [V(q_gain.shape, hi)] * 2
        + [pltpu.SemaphoreType.DMA((10,)), pltpu.SemaphoreType.DMA((16,))],
        compiler_params=pltpu.CompilerParams(vmem_limit_bytes=60 * 2**20),
    )(*results, w_query, w_key)
    out = list(out)
    out[0], out[1] = out[0].reshape(images.shape), out[1].reshape(images.shape)
    out[11], out[13] = out[11].T, out[13].T
    return tuple(out)


def on_device(images, cotangent, ln1_gain, ln1_bias, ln2_gain, ln2_bias, q_gain, k_gain, *weights):
    fused = fits_fused(images, weights[0], weights[4], q_gain)
    layer = fused_layer if fused else general_layer
    return layer(images, cotangent, ln1_gain, ln1_bias, ln2_gain, ln2_bias, q_gain, k_gain, *weights)


def solution(mesh):
    return jax.shard_map(
        on_device,
        mesh=mesh,
        in_specs=(
            P("shard", "ctx", None),
            P("shard", "ctx", None),
            P("shard"),
            P("shard"),
            P("shard"),
            P("shard"),
            P("tp", "shard"),
            P("tp", "shard"),
            P("shard", "tp"),
            P("shard", "tp"),
            P("shard", "tp"),
            P("tp", "shard"),
            P("shard", "tp"),
            P("tp", "shard"),
        ),
        out_specs=(
            P("shard", "ctx", None),
            P("shard", "ctx", None),
            P("shard"),
            P("shard"),
            P("shard"),
            P("shard"),
            P("tp", "shard"),
            P("tp", "shard"),
            P("shard", "tp"),
            P("shard", "tp"),
            P("shard", "tp"),
            P("tp", "shard"),
            P("shard", "tp"),
            P("tp", "shard"),
            P("shard", "tp"),
            P("shard", "tp"),
        ),
        check_vma=False,
    )
```

```python
import functools
import jax
import jax.numpy as jnp
from jax import lax
from jax.experimental import pallas as pl
from jax.experimental.pallas import tpu as pltpu
from jax.sharding import PartitionSpec as P

norm_eps = 1e-06
clip_level = 0.5


def matmul(left, right):
    return jnp.dot(left, right, preferred_element_type=jnp.float32)


def norm_parts(values):
    center = values - jnp.mean(values, axis=-1, keepdims=True)
    inverse = lax.rsqrt(jnp.mean(center * center, axis=-1, keepdims=True) + norm_eps)
    return (center * inverse, inverse)


def norm_back(grad_hat, normed, inverse):
    return inverse * (
        grad_hat
        - jnp.mean(grad_hat, axis=-1, keepdims=True)
        - normed * jnp.mean(grad_hat * normed, axis=-1, keepdims=True)
    )


def head_scale(values, gain):
    inverse = lax.rsqrt(jnp.mean(values * values, axis=-1, keepdims=True) + norm_eps)
    return values * inverse * gain


def gelu_exact(values):
    return jax.nn.gelu(values, approximate=False)


def general_layer(
    images,
    cotangent,
    ln1_gain,
    ln1_bias,
    ln2_gain,
    ln2_bias,
    q_gain,
    k_gain,
    w_query,
    w_key,
    w_value,
    w_out,
    w_up,
    w_down,
):
    (
        full_query,
        full_key,
        full_value,
        full_up,
        full_out,
        full_down,
        gain_low_one,
        shift_low_one,
        gain_low_two,
        shift_low_two,
        query_gain_low,
        key_gain_low,
    ) = (
        lax.all_gather(w_query, "shard", axis=0, tiled=True),
        lax.all_gather(w_key, "shard", axis=0, tiled=True),
        lax.all_gather(w_value, "shard", axis=0, tiled=True),
        lax.all_gather(w_up, "shard", axis=0, tiled=True),
        lax.all_gather(w_out, "shard", axis=1, tiled=True),
        lax.all_gather(w_down, "shard", axis=1, tiled=True),
        lax.all_gather(ln1_gain, "shard", axis=0, tiled=True),
        lax.all_gather(ln1_bias, "shard", axis=0, tiled=True),
        lax.all_gather(ln2_gain, "shard", axis=0, tiled=True),
        lax.all_gather(ln2_bias, "shard", axis=0, tiled=True),
        lax.all_gather(q_gain, "shard", axis=1, tiled=True),
        lax.all_gather(k_gain, "shard", axis=1, tiled=True),
    )
    gain_one = gain_low_one.astype(jnp.float32)
    shift_one = shift_low_one.astype(jnp.float32)
    gain_two = gain_low_two.astype(jnp.float32)
    shift_two = shift_low_two.astype(jnp.float32)
    query_gain = query_gain_low.astype(jnp.float32)
    key_gain = key_gain_low.astype(jnp.float32)
    count_img, local_len, width = images.shape
    tokens = count_img * local_len
    heads_here, head_size = query_gain.shape
    local_width = heads_here * head_size
    full_len = local_len * lax.axis_size("ctx")
    group = 1
    groups = count_img // group
    scale = head_size ** (-0.5)
    flat = images.reshape(tokens, width).astype(jnp.float32)
    normed_one, inverse_one = norm_parts(flat)
    hidden_one = (normed_one * gain_one + shift_one).astype(jnp.bfloat16)
    query_raw = matmul(hidden_one, full_query).reshape(tokens, heads_here, head_size)
    key_raw = matmul(hidden_one, full_key).reshape(tokens, heads_here, head_size)
    query_norm = head_scale(query_raw, query_gain).astype(jnp.bfloat16)
    key_norm = head_scale(key_raw, key_gain).astype(jnp.bfloat16)
    value_low = matmul(hidden_one, full_value).astype(jnp.bfloat16)
    key_all, value_all = (
        lax.all_gather(
            key_norm.reshape(count_img, local_len, local_width), "ctx", axis=1, tiled=True
        ),
        lax.all_gather(
            value_low.reshape(count_img, local_len, local_width), "ctx", axis=1, tiled=True
        ),
    )
    query_grp = query_norm.reshape(groups, group, local_len, heads_here, head_size)
    key_grp = key_all.reshape(groups, group, full_len, heads_here, head_size)
    value_grp = value_all.reshape(groups, group, full_len, heads_here, head_size)

    def attend(pieces):
        query_blk, key_blk, value_blk = pieces
        scores = (
            jnp.einsum("gqhd,gkhd->ghqk", query_blk, key_blk, preferred_element_type=jnp.float32)
            * scale
        )
        top = jnp.max(scores, axis=-1, keepdims=True)
        expo = jnp.exp(scores - top)
        total = jnp.sum(expo, axis=-1, keepdims=True)
        probs = (expo / total).astype(jnp.bfloat16)
        mixed_blk = jnp.einsum(
            "ghqk,gkhd->gqhd", probs, value_blk, preferred_element_type=jnp.float32
        )
        return (mixed_blk, top + jnp.log(total), jnp.max(top, axis=(0, 2, 3)))

    mixed, log_total, group_peaks = lax.map(attend, (query_grp, key_grp, value_grp))
    local_peak = jnp.max(group_peaks, axis=0)
    peak_all = lax.pmax(local_peak, ("shard", "ctx"))
    attended = mixed.reshape(tokens, local_width).astype(jnp.bfloat16)
    branch_attn = lax.psum(matmul(attended, full_out), "tp")
    resid = flat + branch_attn
    normed_two, inverse_two = norm_parts(resid)
    hidden_two = (normed_two * gain_two + shift_two).astype(jnp.bfloat16)
    up_raw = matmul(hidden_two, full_up)
    active = gelu_exact(up_raw).astype(jnp.bfloat16)
    branch_mlp = lax.psum(matmul(active, full_down).astype(jnp.bfloat16), "tp").astype(jnp.float32)
    block_out = (resid + branch_mlp).astype(jnp.bfloat16).reshape(images.shape)
    grad_out = cotangent.reshape(tokens, width).astype(jnp.float32)
    grad_down = cotangent.reshape(tokens, width)
    grad_w_down = jnp.dot(active.T, grad_down, preferred_element_type=jnp.float32)
    grad_active = matmul(grad_down, full_down.T)
    unused_up, gelu_pull = jax.vjp(gelu_exact, up_raw)
    grad_up = gelu_pull(grad_active)[0].astype(jnp.bfloat16)
    grad_w_up = jnp.dot(hidden_two.T, grad_up, preferred_element_type=jnp.float32)
    grad_two = lax.psum(matmul(grad_up, full_up.T), "tp")
    grad_gain_two = jnp.sum(grad_two * normed_two, axis=0)
    grad_shift_two = jnp.sum(grad_two, axis=0)
    grad_resid = grad_out + norm_back(grad_two * gain_two, normed_two, inverse_two)
    grad_branch = grad_resid.astype(jnp.bfloat16)
    grad_w_out = jnp.dot(attended.T, grad_branch, preferred_element_type=jnp.float32)
    grad_mixed = matmul(grad_branch, full_out.T).astype(jnp.bfloat16)
    grad_grp = grad_mixed.reshape(groups, group, local_len, heads_here, head_size)

    def attend_back(pieces):
        query_blk, key_blk, value_blk, log_blk, grad_blk = pieces
        scores = (
            jnp.einsum("gqhd,gkhd->ghqk", query_blk, key_blk, preferred_element_type=jnp.float32)
            * scale
        )
        probs = jnp.exp(scores - log_blk)
        grad_probs = jnp.einsum(
            "gqhd,gkhd->ghqk", grad_blk, value_blk, preferred_element_type=jnp.float32
        )
        grad_scores = (
            probs * (grad_probs - jnp.sum(probs * grad_probs, axis=-1, keepdims=True))
        ).astype(jnp.bfloat16)
        grad_val = jnp.einsum(
            "ghqk,gqhd->gkhd",
            probs.astype(jnp.bfloat16),
            grad_blk,
            preferred_element_type=jnp.float32,
        )
        grad_qry = (
            jnp.einsum("ghqk,gkhd->gqhd", grad_scores, key_blk, preferred_element_type=jnp.float32)
            * scale
        )
        grad_kys = (
            jnp.einsum(
                "ghqk,gqhd->gkhd", grad_scores, query_blk, preferred_element_type=jnp.float32
            )
            * scale
        )
        return (grad_qry, grad_kys, grad_val)

    grad_query_n, grad_key_full, grad_value_full = lax.map(
        attend_back, (query_grp, key_grp, value_grp, log_total, grad_grp)
    )
    grad_key_n, grad_value_n = (
        lax.psum_scatter(
            grad_key_full.reshape(count_img, full_len, local_width),
            "ctx",
            scatter_dimension=1,
            tiled=True,
        ),
        lax.psum_scatter(
            grad_value_full.reshape(count_img, full_len, local_width),
            "ctx",
            scatter_dimension=1,
            tiled=True,
        ),
    )
    unused_query, query_pull = jax.vjp(head_scale, query_raw, query_gain)
    grad_query_raw, grad_query_gain = query_pull(
        grad_query_n.reshape(tokens, heads_here, head_size)
    )
    unused_key, key_pull = jax.vjp(head_scale, key_raw, key_gain)
    grad_key_raw, grad_key_gain = key_pull(grad_key_n.reshape(tokens, heads_here, head_size))
    grad_query_low = grad_query_raw.reshape(tokens, local_width).astype(jnp.bfloat16)
    grad_key_low = grad_key_raw.reshape(tokens, local_width).astype(jnp.bfloat16)
    grad_value_low = grad_value_n.reshape(tokens, local_width).astype(jnp.bfloat16)
    grad_w_query = jnp.dot(hidden_one.T, grad_query_low, preferred_element_type=jnp.float32)
    grad_w_key = jnp.dot(hidden_one.T, grad_key_low, preferred_element_type=jnp.float32)
    grad_w_value = jnp.dot(hidden_one.T, grad_value_low, preferred_element_type=jnp.float32)
    grad_one_part = (
        matmul(grad_query_low, full_query.T)
        + matmul(grad_key_low, full_key.T)
        + matmul(grad_value_low, full_value.T)
    )
    grad_one = lax.psum(grad_one_part, "tp")
    grad_gain_one = jnp.sum(grad_one * normed_one, axis=0)
    grad_shift_one = jnp.sum(grad_one, axis=0)
    input_grad = (
        (grad_resid + norm_back(grad_one * gain_one, normed_one, inverse_one))
        .astype(jnp.bfloat16)
        .reshape(images.shape)
    )
    (
        sum_query,
        sum_key,
        sum_value,
        sum_up,
        sum_out,
        sum_down,
        sum_gain_one,
        sum_shift_one,
        sum_gain_two,
        sum_shift_two,
        sum_qgain,
        sum_kgain,
    ) = lax.psum(
        (
            grad_w_query,
            grad_w_key,
            grad_w_value,
            grad_w_up,
            grad_w_out,
            grad_w_down,
            grad_gain_one,
            grad_shift_one,
            grad_gain_two,
            grad_shift_two,
            grad_query_gain,
            grad_key_gain,
        ),
        "ctx",
    )
    (
        part_query,
        part_key,
        part_value,
        part_up,
        part_out,
        part_down,
        part_gain_one,
        part_shift_one,
        part_gain_two,
        part_shift_two,
        part_qgain,
        part_kgain,
    ) = (
        lax.psum_scatter(sum_query, "shard", scatter_dimension=0, tiled=True),
        lax.psum_scatter(sum_key, "shard", scatter_dimension=0, tiled=True),
        lax.psum_scatter(sum_value, "shard", scatter_dimension=0, tiled=True),
        lax.psum_scatter(sum_up, "shard", scatter_dimension=0, tiled=True),
        lax.psum_scatter(sum_out, "shard", scatter_dimension=1, tiled=True),
        lax.psum_scatter(sum_down, "shard", scatter_dimension=1, tiled=True),
        lax.psum_scatter(sum_gain_one, "shard", scatter_dimension=0, tiled=True),
        lax.psum_scatter(sum_shift_one, "shard", scatter_dimension=0, tiled=True),
        lax.psum_scatter(sum_gain_two, "shard", scatter_dimension=0, tiled=True),
        lax.psum_scatter(sum_shift_two, "shard", scatter_dimension=0, tiled=True),
        lax.psum_scatter(sum_qgain, "shard", scatter_dimension=1, tiled=True),
        lax.psum_scatter(sum_kgain, "shard", scatter_dimension=1, tiled=True),
    )
    factor = jnp.sqrt(clip_level / jnp.maximum(peak_all, clip_level))
    columns = jnp.repeat(factor, head_size)
    query_clip = (w_query.astype(jnp.float32) * columns).astype(jnp.bfloat16)
    key_clip = (w_key.astype(jnp.float32) * columns).astype(jnp.bfloat16)
    return (
        block_out,
        input_grad,
        part_gain_one,
        part_shift_one,
        part_gain_two,
        part_shift_two,
        part_qgain,
        part_kgain,
        part_query,
        part_key,
        part_value,
        part_out,
        part_up,
        part_down,
        query_clip,
        key_clip,
    )


MESH = pl.DeviceIdType.MESH
NN = (((1,), (0,)), ((), ()))
NT = (((1,), (1,)), ((), ()))
TN = (((0,), (0,)), ((), ()))
low_type = jnp.bfloat16
full_type = jnp.float32


def dot(left, right, dims=NN):
    return lax.dot_general(left, right, dims, preferred_element_type=full_type)


def flip(place, bits, count):
    result = 0
    unit = 1
    while unit < count:
        result = result + ((place // unit + bits // unit) % 2) * unit
        unit *= 2
    return result


def fits_fused(images, w_query, w_up, q_gain):
    count_img, local_len, width = images.shape
    ctx, shard, tp = lax.axis_size("ctx"), lax.axis_size("shard"), lax.axis_size("tp")
    rows = w_query.shape[0]
    return (
        count_img == 1
        and tp == 2
        and ctx == 4
        and shard == 4
        and rows % (16 * ctx) == 0
        and local_len % 32 == 0
        and q_gain.shape[0] % 2 == 0
        and w_up.shape[1] % (128 * ctx) == 0
    )


def fused_kernel(
    sizes,
    img_h, cot_h, g1_a, b1_a, g2_a, b2_a, qg_a, kg_a, wq_h, wk_h, wv_h, wo_h, wup_h, wdn_h,
    bo_o, ig_o, upo, dno, qkvo, lnr_o, qkr_o, peak_o,
    xg, ctg, smalls, wl, wol, wkv, wqp, wop, wqb, wob, wup, wdt, h1_t, h2_t, ct_t,
    xh1, h1, nq, nk, sq, sk, qs, kall, vall, pst, sbuf, attq, brs, brr, pks,
    ptop, dsb,
    h2, ga, act, gu, g2s, g2r, g2own, bos, bor, boown,
    gsib_s, gsib_r, gkeep, gz_s, gz_r, gfin,
    gres, gbg, dqb, dkt, dvt, dks_s, dks_r, dqr, dkv,
    g1s, g1r, g1own, qsib_s, qsib_r, qown, qz_s, qz_r, qfin,
    rows_s, rows_r, obuf, g1_h, b1_h, g2_h, b2_h, qg_h, kg_h, lnr_v, qkr_v, peak_v,
    lsem, ssem, rsem,
):
    CN, ZN, TB, D, HW, FS, R = sizes
    HR = R // 2
    s_i, c_i, t_i = lax.axis_index("shard"), lax.axis_index("ctx"), lax.axis_index("tp")
    o_i = 1 - t_i
    half_chips = CN // 2
    tstar = c_i // half_chips
    place = c_i % half_chips
    TK = CN * TB
    inv_d = 1.0 / D

    def at_ctx(j):
        return (s_i, flip(c_i, j, CN), t_i)

    def at_z(j):
        return (flip(s_i, j, ZN), c_i, t_i)

    sib = (s_i, c_i, o_i)

    outer = (s_i == 0) | (s_i == ZN - 1)
    pair = flip(s_i, 1, ZN)
    far_in = flip(s_i, 3, ZN) * (1 - outer) + flip(s_i, 2, ZN) * outer
    far_out = flip(s_i, 2, ZN) * (1 - outer) + flip(s_i, 3, ZN) * outer

    def plane(z):
        return (z, c_i, t_i)

    arrivals, leavings = {}, {}
    from_one = ("x", "small", "br", "h2", "g2", "qz0", "qz2", "rz", "pkz", "rc", "pkc",
                "ct", "gb", "bo", "g1", "gc0", "gc1")
    apart = ("wd", "wu", "gs", "dk", "qg", "ob")

    def spot(name, count):
        if name not in arrivals:
            first = sum(n for _, n in arrivals.values())
            skip = 1 if name in from_one else 0
            arrivals[name] = (first - skip, count - skip)
        return arrivals[name][0]

    def arrival(name, count, j):
        return rsem.at[spot(name, count) + j]

    def leaving(name, count, j):
        if name not in leavings:
            leavings[name] = (sum(n for _, n in leavings.values()), count if name in apart else 1)
        return ssem.at[leavings[name][0] + (j if name in apart else 0)]

    def put_as(name, count, send, recv, src, dst, dev):
        pltpu.make_async_remote_copy(
            src_ref=src, dst_ref=dst, send_sem=leaving(name, count, send), recv_sem=arrival(name, count, recv),
            device_id=dev, device_id_type=MESH,
        ).start()

    def put(name, count, j, src, dst, dev):
        put_as(name, count, j, j, src, dst, dev)

    def got(name, count, j, dst, dev):
        pltpu.make_async_remote_copy(
            src_ref=dst, dst_ref=dst, send_sem=ssem.at[0], recv_sem=arrival(name, count, j),
            device_id=dev, device_id_type=MESH,
        ).wait_recv()

    def sent(name, count, j, src):
        pltpu.make_async_remote_copy(
            src_ref=src, dst_ref=src, send_sem=leaving(name, count, j), recv_sem=rsem.at[0],
            device_id=sib, device_id_type=MESH,
        ).wait_send()

    x_src = img_h.at[0, pl.ds(t_i * TB, TB)]
    c_src = cot_h.at[0, pl.ds(t_i * TB, TB)]
    locals_ = [
        pltpu.make_async_copy(wk_h, wl.at[1], lsem.at[0]),
        pltpu.make_async_copy(wv_h, wl.at[2], lsem.at[1]),
        pltpu.make_async_copy(wq_h, wl.at[0], lsem.at[2]),
        pltpu.make_async_copy(x_src, xg.at[0], lsem.at[3]),
        pltpu.make_async_copy(wo_h, wol, lsem.at[4]),
        pltpu.make_async_copy(wdn_h.at[:, pl.ds(c_i * FS, FS)], wdt.at[t_i, s_i], lsem.at[5]),
        pltpu.make_async_copy(wup_h.at[:, pl.ds(c_i * FS, FS)], wup.at[t_i, s_i], lsem.at[6]),
        pltpu.make_async_copy(c_src, ctg.at[0], lsem.at[7]),
    ]
    gains = [
        pltpu.make_async_copy(src, dst, lsem.at[16 + n])
        for n, (src, dst) in enumerate((
            (g1_a, g1_h), (b1_a, b1_h), (g2_a, g2_h), (b2_a, b2_h), (qg_a, qg_h), (kg_a, kg_h),
        ))
    ]
    for copy in gains + locals_:
        copy.start()

    barrier = pltpu.get_barrier_semaphore()
    greet = [at_ctx(j) for j in range(1, CN)] + [at_z(j) for j in range(1, ZN)] + [sib]
    for dev in greet:
        pl.semaphore_signal(barrier, inc=1, device_id=dev, device_id_type=MESH)

    for copy in gains:
        copy.wait()
    smalls[t_i, s_i] = jnp.zeros((8, 256), full_type)
    for k, ref in enumerate((g1_h, b1_h, g2_h, b2_h)):
        smalls[t_i, s_i, k:k + 1, :R] = ref[...].astype(full_type).reshape(1, R)
    heads = HW // 64
    piece = qg_h.shape[1]
    lane_of = lax.broadcasted_iota(jnp.int32, (piece, HW), 1)
    spread = (
        (lane_of % piece == lax.broadcasted_iota(jnp.int32, (piece, HW), 0)) & ((lane_of % 64) // piece == s_i)
    ).astype(full_type).astype(low_type)
    head_of = lax.broadcasted_iota(jnp.int32, (qg_h.shape[0], HW), 0)
    wanted = head_of == place * heads + lax.broadcasted_iota(jnp.int32, (qg_h.shape[0], HW), 1) // 64
    wanted = wanted & (t_i == tstar)
    for k, ref in ((4, qg_h), (5, kg_h)):
        row = jnp.sum(jnp.where(wanted, dot(ref[...], spread), 0.0), axis=0, keepdims=True)
        smalls[t_i, s_i, k:k + 1, :HW] = row

    pl.semaphore_wait(barrier, len(greet))

    for j in range(1, CN):
        put("x", CN, j, x_src, xg.at[j], at_ctx(j))
    for j in range(1, ZN):
        put("small", ZN, j, smalls.at[t_i, s_i], smalls.at[t_i, s_i], at_z(j))

    def picker(at, lanes, offset):
        rows = lax.broadcasted_iota(jnp.int32, (half_chips * HW, lanes), 0)
        cols = lax.broadcasted_iota(jnp.int32, (half_chips * HW, lanes), 1) - offset
        return ((rows == cols + at * HW) & (cols >= 0) & (cols < HW)).astype(full_type).astype(low_type)

    projections = (("wkv", wkv), ("wq", wqp), ("wo", wop))

    def send_projection(name, buf):
        for j in range(1, ZN):
            put(name, ZN, j, buf.at[s_i], buf.at[s_i], at_z(j))
        put(name, ZN, 0, buf.at[s_i], buf.at[s_i], sib)

    locals_[4].wait()

    @pl.when(t_i == tstar)
    def _():
        for n in range(3):
            locals_[n].wait()
        wkv[s_i] = (
            dot(wl[1], picker(place, 2 * HW, 0)) + dot(wl[2], picker(place, 2 * HW, HW))
        ).astype(low_type)
        send_projection(*projections[0])
        for source, packed in ((wl.at[0], wqp), (wol, wop)):
            packed[s_i] = (
                dot(source[:HR], picker(place, 2 * HW, 0)) + dot(source[HR:], picker(place, 2 * HW, HW))
            ).astype(low_type)

    @pl.when(t_i != tstar)
    def _():
        for n in range(3):
            locals_[n].wait()

    for j in range(1, ZN):
        got("small", ZN, j, smalls.at[t_i, flip(s_i, j, ZN)], at_z(j))
    put("smallt", 1, 0, smalls.at[t_i], smalls.at[t_i], sib)

    locals_[3].wait()

    def norm_rows(values):
        mean = jnp.sum(values, axis=-1, keepdims=True) * inv_d
        center = values - mean
        inverse = lax.rsqrt(jnp.sum(center * center, axis=-1, keepdims=True) * inv_d + norm_eps)
        return center * inverse, inverse

    ln_rows = jnp.concatenate([smalls[t_i, k][:, :R] for k in range(ZN)], axis=1)
    g1row, b1row, g2row, b2row = (ln_rows[k:k + 1] for k in range(4))

    def first_norm(j, _):
        @pl.when(j > 0)
        def _():
            got("x", CN, j, xg.at[j], at_ctx(j))

        for n in (1, 2):
            @pl.when((j == n) & (t_i == tstar))
            def _():
                send_projection(*projections[n])

        normed, _unused = norm_rows(xg[j].astype(full_type))
        xh1[j] = normed
        hidden = (normed * g1row + b1row).astype(low_type)
        h1[j] = hidden
        h1_t[:, pl.ds(pl.multiple_of(j * TB, TB), TB)] = hidden.T
        return 0

    HB = TB // 2

    def spread(name, src, dst_of):
        for j in (1, 2):
            put(name, 5, j, src, dst_of(j), at_ctx(j))

    def pass_on(name, buf):
        for j in (1, 2):
            got(name, 5, j, buf.at[j], at_ctx(j))
            half = pl.ds((j - 1) * HB, HB)
            put_as(name, 5, 2 + j, 2 + j, buf.at[j, half], buf.at[3, half], at_ctx(3 - j))

    def spread_halves(name, buf):
        for j in (1, 2):
            half = pl.ds((j - 1) * HB, HB)
            put(name, 7, j, buf.at[0, half], buf.at[j, half], at_ctx(j))
        for j in (1, 2):
            half = pl.ds((2 - j) * HB, HB)
            put(name, 7, 4 + j, buf.at[0, half], buf.at[j, half], at_ctx(j))

    def pass_halves(name, buf):
        for j in (1, 2):
            half = pl.ds((j - 1) * HB, HB)
            got(name, 7, j, buf.at[j, half], at_ctx(j))
            put_as(name, 7, 2 + j, 2 + j, buf.at[j, half], buf.at[3, half], at_ctx(3 - j))

    def second_half(name, buf, j):
        got(name, 7, 4 + j, buf.at[j, pl.ds((2 - j) * HB, HB)], at_ctx(j))

    def diagonal_halves(name, buf):
        for j in (1, 2):
            got(name, 7, 2 + j, buf.at[3, pl.ds((j - 1) * HB, HB)], at_ctx(3 - j))

    def send_halves(name, src, land, count=5):
        for j in (1, 2):
            half = pl.ds((j - 1) * HB, HB)
            put_as(name, count, 2 + j, 2 + j, src.at[3, half], land.at[3, half], at_ctx(j))

    def send_plain(name, src, land):
        for j in (1, 2):
            half = pl.ds((j - 1) * HB, HB)
            put_as(name, 7, 4 + j, 4 + j, src.at[j, half], land.at[j, half], at_ctx(j))

    def add_rest(name, src, land):
        for j in (1, 2):
            half = pl.ds((j - 1) * HB, HB)
            got(name, 7, 2 + j, land.at[3, half], at_ctx(j))
            src[3 - j, half] = (src[3 - j, half].astype(full_type) + land[3, half].astype(full_type)).astype(low_type)
        for j in (1, 2):
            half = pl.ds((2 - j) * HB, HB)
            put_as(name, 7, j, j, src.at[j, half], land.at[j, half], at_ctx(j))

    def have_sums(name, land):
        for j in (1, 2):
            got(name, 7, 4 + j, land.at[j, pl.ds((j - 1) * HB, HB)], at_ctx(j))
            got(name, 7, j, land.at[j, pl.ds((2 - j) * HB, HB)], at_ctx(j))

    def add_halves(name, src, land):
        for j in (1, 2):
            half = pl.ds((j - 1) * HB, HB)
            got(name, 5, 2 + j, land.at[3, half], at_ctx(j))
            src[3 - j, half] = (src[3 - j, half].astype(full_type) + land[3, half].astype(full_type)).astype(low_type)
        for j in (1, 2):
            put_as(name, 5, j, j, src.at[j], land.at[j], at_ctx(j))

    def have_rest(name, buf):
        for j in (1, 2):
            half = pl.ds((j - 1) * HB, HB)
            got(name, 5, 2 + j, buf.at[3, half], at_ctx(3 - j))

    spread("ct", c_src, lambda j: ctg.at[j])
    lax.fori_loop(0, CN, first_norm, 0)

    got("smallt", 1, 0, smalls.at[o_i], sib)
    head_rows = smalls[0, 0][4:6, :HW]
    for a in range(2):
        for k in range(ZN):
            if a or k:
                head_rows = head_rows + smalls[a, k][4:6, :HW]
    qgrow, kgrow = head_rows[0:1], head_rows[1:2]

    lane = lax.broadcasted_iota(jnp.int32, (1, HW), 1) // 64
    mask_f = [(lane == h).astype(full_type) for h in range(heads)]
    mask_b = [m.astype(low_type) for m in mask_f]
    same_head = (
        lax.broadcasted_iota(jnp.int32, (HW, HW), 0) // 64
        == lax.broadcasted_iota(jnp.int32, (HW, HW), 1) // 64
    ).astype(full_type).astype(low_type)

    def head_mean(values):
        high = values.astype(low_type)
        rest = (values - high.astype(full_type)).astype(low_type)
        return (dot(high, same_head) + dot(rest, same_head)) * (1.0 / 64)

    def weight_ready(name, buf):
        @pl.when(t_i != tstar)
        def _():
            got(name, ZN, 0, buf.at[s_i], sib)

        for j in range(1, ZN):
            block = buf.at[flip(s_i, j, ZN)]
            got(name, ZN, j, block, sib)

            @pl.when(t_i == tstar)
            def _():
                pltpu.make_async_remote_copy(
                    src_ref=block, dst_ref=block,
                    send_sem=leaving("f" + name, ZN, j), recv_sem=arrival(name, ZN, j),
                    device_id=sib, device_id_type=MESH,
                ).start()

    def unpack(packed, buf):
        for z in range(ZN):
            block = packed[z]
            buf[z, :HR] = block[:, :HW]
            buf[z, HR:] = block[:, HW:]

    h1_all = h1[...].reshape(TK, D)
    weight_ready(*projections[0])
    raw = dot(h1_all, wkv[...].reshape(D, 2 * HW))
    vall[0] = raw[:, HW:].astype(low_type)
    put("v", 1, 0, vall.at[0], vall.at[1], sib)
    raw = raw[:, :HW]
    inverse = lax.rsqrt(head_mean(raw * raw) + norm_eps)
    normed = raw * inverse
    nk[...] = normed
    sk[...] = inverse
    kall[0] = (normed * kgrow).astype(low_type)
    put("k", 1, 0, kall.at[0], kall.at[1], sib)
    weight_ready(*projections[1])
    unpack(wqp, wqb)
    mlp_weights = (("wd", wdt), ("wu", wup))

    def own_mlp(name, buf):
        block = buf.at[t_i, s_i]
        put_as(name, 5, 0, 0, block, block, plane(pair))

        @pl.when(jnp.logical_not(outer))
        def _():
            put_as(name, 5, 1, 1, block, block, plane(far_in))

    def pass_mlp(name, buf, stage):
        source, target = ((pair, far_in), (far_in, pair), (far_out, pair))[stage]
        recv = (2, 1, 2)[stage]

        @pl.when(jnp.logical_not(outer))
        def _():
            block = buf.at[t_i, source]
            got(name, 5, stage, block, plane(pair))
            put_as(name, 5, 2 + stage, recv, block, block, plane(target))

    def have_mlp(name, buf):
        @pl.when(outer)
        def _():
            for n, z in enumerate((pair, far_in, far_out)):
                got(name, 5, n, buf.at[t_i, z], plane(pair))

    locals_[5].wait()
    own_mlp(*mlp_weights[0])
    locals_[6].wait()
    own_mlp(*mlp_weights[1])
    raw = dot(h1_all, wqb[...].reshape(D, HW))
    inverse = lax.rsqrt(head_mean(raw * raw) + norm_eps)
    normed = raw * inverse
    nq[...] = normed
    sq[...] = inverse
    qs[...] = ((normed * qgrow).astype(low_type) * 0.125).astype(low_type).reshape(CN, TB, HW)

    got("k", 1, 0, kall.at[1], sib)
    got("v", 1, 0, vall.at[1], sib)

    def stacked(block):
        return jnp.concatenate([block * m for m in mask_b], axis=0)

    def folded(block):
        total = block[0:TB] * mask_f[0]
        for h in range(1, heads):
            total = total + block[h * TB:(h + 1) * TB] * mask_f[h]
        return total

    ptop[...] = jnp.full(ptop.shape, -3.0e38, full_type)

    def attend(i, _):
        j = CN - 1 - i

        @pl.when(i == CN - 1)
        def _():
            pass_mlp(*mlp_weights[0], 0)
            pass_mlp(*mlp_weights[0], 1)

        sbuf[...] = dot(stacked(qs[j]), kall[...].reshape(2 * TK, HW), NT)
        for h in range(heads):
            rows = slice(h * TB, (h + 1) * TB)
            scores = sbuf[rows]
            ptop[h:h + 1] = jnp.maximum(ptop[h:h + 1], jnp.max(scores, axis=0, keepdims=True))
            expo = jnp.exp(scores)
            pst[j, rows] = expo * (1.0 / jnp.sum(expo, axis=-1, keepdims=True))
        mixed = folded(dot(pst[j].astype(low_type), vall[...].reshape(2 * TK, HW)))
        attq[j] = mixed.astype(low_type)

        @pl.when(i == 0)
        def _():
            weight_ready(*projections[2])
            unpack(wop, wob)

        branch = dot(attq[j], wob[...].reshape(D, HW), NT)

        @pl.when(j > 0)
        def _():
            brs[j] = branch.astype(low_type)
            put("br", CN, j, brs.at[j], brr.at[j], at_ctx(j))

        @pl.when(j == 0)
        def _():
            boown[...] = branch

        return 0

    lax.fori_loop(0, CN, attend, 0)
    pass_mlp(*mlp_weights[1], 0)
    pass_mlp(*mlp_weights[1], 1)
    pass_on("ct", ctg)
    pass_mlp(*mlp_weights[0], 2)
    peak_rows = jnp.max(ptop[...], axis=-1, keepdims=True)
    lane_id = lax.broadcasted_iota(jnp.int32, (8, 128), 1)
    own_peak = jnp.full((8, 128), -3.0e38, full_type)
    for h in range(heads):
        own_peak = jnp.where(lane_id == c_i * heads + h, peak_rows[h:h + 1], own_peak)
    pks[0] = own_peak
    put("pkt", 1, 0, pks.at[0], pks.at[1], sib)

    branch = boown[...]
    for j in (3, 2, 1):
        if j == 1:
            pass_mlp(*mlp_weights[1], 2)
        got("br", CN, j, brr.at[j], at_ctx(j))
        branch = branch + brr[j].astype(full_type)
    resid = xg[0].astype(full_type) + branch
    boown[...] = resid
    xhat2, inv2 = norm_rows(resid)
    h2[0] = (xhat2 * g2row + b2row).astype(low_type)
    spread_halves("h2", h2)

    locals_[7].wait()
    have_rest("ct", ctg)
    ct_t[...] = ctg[...].reshape(TK, D).T
    have_mlp(*mlp_weights[0])
    put("wdt", 1, 0, wdt.at[t_i], wdt.at[t_i], sib)
    ga[t_i] = dot(ctg[...].reshape(TK, D), wdt[t_i].reshape(D, FS)).reshape(CN, TB, FS)
    pass_halves("h2", h2)
    have_mlp(*mlp_weights[1])
    put("wut", 1, 0, wup.at[t_i], wup.at[t_i], sib)
    got("wdt", 1, 0, wdt.at[o_i], sib)
    ga[o_i] = dot(ctg[...].reshape(TK, D), wdt[o_i].reshape(D, FS)).reshape(CN, TB, FS)
    got("wut", 1, 0, wup.at[o_i], sib)

    def mlp(i, _):
        j = ((i + 1) % 3) * (1 - i // 3) + 3 * (i // 3)

        for n in (1, 2):
            @pl.when(j == n)
            def _():
                second_half("h2", h2, n)

        @pl.when(j == 3)
        def _():
            diagonal_halves("h2", h2)

        block = h2[j]
        h2_t[:, pl.ds(pl.multiple_of(j * TB, TB), TB)] = block.T
        for a in range(2):
            up = dot(block, wup[a].reshape(D, FS))
            phi = 0.5 * (1.0 + lax.erf(up * 0.7071067811865476))
            dens = jnp.exp(up * up * -0.5) * 0.3989422804014327
            part = slice(a * FS, (a + 1) * FS)
            act[j, :, part] = (up * phi).astype(low_type)
            gu[j, :, part] = (ga[a, j] * (phi + up * dens)).astype(low_type)
        grad_two = (
            dot(gu[j, :, :FS], wup[0].reshape(D, FS), NT) + dot(gu[j, :, FS:], wup[1].reshape(D, FS), NT)
        )

        @pl.when(j == 0)
        def _():
            g2own[...] = grad_two

        @pl.when(j > 0)
        def _():
            g2s[j] = grad_two.astype(low_type)
            put("g2", CN, j, g2s.at[j], g2r.at[j], at_ctx(j))

        return 0

    lax.fori_loop(0, CN, mlp, 0)

    got("pkt", 1, 0, pks.at[1], sib)
    pks[2] = jnp.maximum(pks[0], pks[1])
    for j in range(1, ZN):
        put("pkz", ZN, j, pks.at[2], pks.at[2 + j], at_z(j))
    own_part = pl.ds(pl.multiple_of(t_i * FS, FS), FS)
    other_part = pl.ds(pl.multiple_of(o_i * FS, FS), FS)
    pairs = ((h2_t, gu), (ct_t, act))
    for k, (left, right) in enumerate(pairs):
        gsib_s[k] = dot(left[...], right[:, :, other_part].reshape(TK, FS)).astype(low_type)
        put("gs", 2, k, gsib_s.at[k], gsib_r.at[k], sib)

    def send_far(k):
        @pl.when(outer)
        def _():
            put("gz%d" % k, 4, 2, gz_s.at[k, far_out], gz_r.at[k, 2], plane(pair))
            put("gz%d" % k, 4, 3, gz_s.at[k, far_in], gz_r.at[k, 3], plane(pair))

    def send_near(k):
        put("gz%d" % k, 4, 0, gz_s.at[k, pair], gz_r.at[k, 0], plane(pair))

    own_grads = [dot(left[...], right[:, :, own_part].reshape(TK, FS)) for left, right in pairs]
    for k in range(2):
        got("gs", 2, k, gsib_r.at[k], sib)
        total = own_grads[k] + gsib_r[k].astype(full_type)
        gkeep[k] = total
        gz_s[k] = total.astype(low_type).reshape(ZN, R, FS)
        send_far(k)
    send_near(0)
    send_near(1)

    def down(j, _):
        part = (
            dot(act[j, :, :FS], wdt[0].reshape(D, FS), NT) + dot(act[j, :, FS:], wdt[1].reshape(D, FS), NT)
        )

        @pl.when(j == 0)
        def _():
            boown[...] += part

        @pl.when(j > 0)
        def _():
            bos[j] = part.astype(low_type)

        return 0

    lax.fori_loop(0, CN, down, 0)

    def relay_mlp(k):
        @pl.when(jnp.logical_not(outer))
        def _():
            for n, z in ((2, far_out), (3, far_in)):
                got("gz%d" % k, 4, n, gz_r.at[k, n], plane(pair))
                mine_part = gkeep[k, pl.ds(pl.multiple_of(z * R, R), R)]
                gz_s[k, z] = (mine_part + gz_r[k, n].astype(full_type)).astype(low_type)
                put_as("gz%d" % k, 4, n, 1, gz_s.at[k, z], gz_r.at[k, 1], plane(z))

    def share_mlp(k, out):
        total = gkeep[k, pl.ds(pl.multiple_of(s_i * R, R), R)]
        for n in range(2):
            got("gz%d" % k, 4, n, gz_r.at[k, n], plane(pair))
            total = total + gz_r[k, n].astype(full_type)
        gfin[k] = total.astype(low_type)
        spread("gc%d" % k, gfin.at[k], lambda j: out.at[c_i])
        pltpu.make_async_copy(gfin.at[k], out.at[c_i], lsem.at[8 + k]).start()

    grad_two = g2own[...]
    for j in range(1, CN):
        got("g2", CN, j, g2r.at[j], at_ctx(j))
        grad_two = grad_two + g2r[j].astype(full_type)
    ln2g = jnp.sum(grad_two * xhat2, axis=0, keepdims=True)
    ln2b = jnp.sum(grad_two, axis=0, keepdims=True)
    hat = grad_two * g2row
    grad_resid = ctg[0].astype(full_type) + inv2 * (
        hat
        - jnp.sum(hat, axis=-1, keepdims=True) * inv_d
        - xhat2 * (jnp.sum(hat * xhat2, axis=-1, keepdims=True) * inv_d)
    )
    gres[...] = grad_resid
    gb = grad_resid.astype(low_type)
    gbg[0] = gb
    spread_halves("gb", gbg)
    send_halves("bo", bos, bor)

    peak = pks[2]
    for j in range(1, ZN):
        got("pkz", ZN, j, pks.at[2 + j], at_z(j))
        peak = jnp.maximum(peak, pks[2 + j])
    first = 2 + ZN
    pks[first] = peak
    for j in range(1, CN):
        put("pkc", CN, j, pks.at[first], pks.at[first + j], at_ctx(j))

    dkt[...] = jnp.zeros_like(dkt)
    dvt[...] = jnp.zeros_like(dvt)

    def attend_back(j, _):
        @pl.when(j == 1)
        def _():
            pass_halves("gb", gbg)
            relay_mlp(0)
            second_half("gb", gbg, 1)

        @pl.when(j == 2)
        def _():
            second_half("gb", gbg, 2)

        @pl.when(j == CN - 1)
        def _():
            add_halves("bo", bos, bor)
            diagonal_halves("gb", gbg)

        grad_rows = stacked(dot(gbg[j], wob[...].reshape(D, HW)).astype(low_type))
        query_rows = stacked(qs[j])
        sbuf[...] = dot(grad_rows, vall[...].reshape(2 * TK, HW), NT)

        for h in range(heads):
            rows = slice(h * TB, (h + 1) * TB)
            probs, grad_probs = pst[j, rows], sbuf[rows]
            inner = jnp.sum(probs * grad_probs, axis=-1, keepdims=True)
            dsb[rows] = (probs * (grad_probs - inner)).astype(low_type)
        grad_scores = dsb[...]
        dqb[j] = folded(dot(grad_scores, kall[...].reshape(2 * TK, HW))) * 0.125
        dvt[...] += dot(grad_rows, pst[j].astype(low_type), TN)
        dkt[...] += dot(query_rows, grad_scores, TN)
        return 0

    lax.fori_loop(0, CN, attend_back, 0)
    dks_s[0] = dvt[:, TK:].astype(low_type)
    dks_s[1] = dkt[:, TK:].astype(low_type)
    for k in range(2):
        put("dk", 2, k, dks_s.at[k], dks_r.at[k], sib)

    for j in range(1, CN):
        got("pkc", CN, j, pks.at[first + j], at_ctx(j))
        peak = jnp.maximum(peak, pks[first + j])
    peak_v[...] = peak
    pltpu.make_async_copy(peak_v, peak_o, lsem.at[22]).start()

    relay_mlp(1)
    def unnorm(grad_n, gain_row, normed, inverse):
        gain_grad = jnp.sum(grad_n * normed, axis=0, keepdims=True)
        e = grad_n * gain_row
        return (inverse * (e - normed * head_mean(e * normed))).astype(low_type), gain_grad

    def share_grad(n, full):
        full = full.reshape(ZN, 2, HR, 2 * HW)
        low_full = full.astype(low_type)
        for k in range(2):
            @pl.when(o_i == k)
            def _():
                qsib_s[n] = low_full[:, k]

            @pl.when(t_i == k)
            def _():
                qown[n] = full[:, k]

        put("qg", 2, n, qsib_s.at[n], qsib_r.at[n], sib)

    pieces = {1: (("qz1", 0, HR),), 0: (("qz0", 0, HR // 2), ("qz2", HR // 2, HR // 2))}

    def reduce_grad(n):
        got("qg", 2, n, qsib_r.at[n], sib)
        total = qown[n] + qsib_r[n].astype(full_type)
        qown[n] = total
        qz_s[n] = total.astype(low_type)
        if n == 1:
            @pl.when(outer)
            def _():
                put("qz1", 4, 2, qz_s.at[1, far_out], qz_r.at[1, 2], plane(pair))
                put("qz1", 4, 3, qz_s.at[1, far_in], qz_r.at[1, 3], plane(pair))

            put("qz1", 4, 0, qz_s.at[1, pair], qz_r.at[1, 0], plane(pair))
            return
        for name, first, count in pieces[n]:
            rows = pl.ds(first, count)
            for j in range(1, ZN):
                put(name, ZN, j, qz_s.at[n, flip(s_i, j, ZN), rows], qz_r.at[n, j, rows], at_z(j))

    def relay_grad():
        @pl.when(jnp.logical_not(outer))
        def _():
            for n, z in ((2, far_out), (3, far_in)):
                got("qz1", 4, n, qz_r.at[1, n], plane(pair))
                qz_s[1, z] = (qown[1, z] + qz_r[1, n].astype(full_type)).astype(low_type)
                put_as("qz1", 4, n, 1, qz_s.at[1, z], qz_r.at[1, 1], plane(z))

    grad_raw, q_gain_row = unnorm(dqb[...].reshape(TK, HW), qgrow, nq[...], sq[...])
    dqr[...] = grad_raw
    empty = jnp.zeros((TK, HW), low_type)
    share_grad(1, (
        dot(h1_t[...], jnp.concatenate([dqr[...], empty], axis=1))
        + dot(gbg[...].reshape(TK, D), jnp.concatenate([empty, attq[...].reshape(TK, HW)], axis=1), TN)
    ))
    share_mlp(0, upo)
    got("dk", 2, 0, dks_r.at[0], sib)
    grad_v = (dvt[:, :TK] + dks_r[0].astype(full_type)).T.astype(low_type)
    got("dk", 2, 1, dks_r.at[1], sib)
    grad_k = (dkt[:, :TK] + dks_r[1].astype(full_type)).T
    grad_raw, k_gain_row = unnorm(grad_k, kgrow, nk[...], sk[...])
    dkv[...] = jnp.concatenate([grad_raw, grad_v], axis=1)
    ln1g = jnp.zeros((1, D), full_type)
    ln1b = jnp.zeros((1, D), full_type)
    for j in range(CN - 1, -1, -1):
        rows = slice(j * TB, (j + 1) * TB)
        part = dot(dqr[rows], wqb[...].reshape(D, HW), NT) + dot(dkv[rows], wkv[...].reshape(D, 2 * HW), NT)
        if j:
            g1s[j] = part.astype(low_type)
        else:
            g1own[...] = part
        if j == 3:
            send_halves("g1", g1s, g1r, 7)
            share_grad(0, dot(h1_t[...], dkv[...]))
            reduce_grad(1)
        ln1g = ln1g + jnp.sum(part * xh1[j], axis=0, keepdims=True)
        ln1b = ln1b + jnp.sum(part, axis=0, keepdims=True)
        if j == 1:
            send_plain("g1", g1s, g1r)
            reduce_grad(0)
    rows_s[0] = jnp.zeros_like(rows_s[0])
    HD2 = D // 2
    for k, row in enumerate((ln1g, ln1b, ln2g, ln2b)):
        rows_s[0, 2 * k:2 * k + 1, :HD2] = row[:, :HD2]
        rows_s[0, 2 * k + 1:2 * k + 2, :HD2] = row[:, HD2:]
    rows_s[0, 0:1, HD2:HD2 + HW] = q_gain_row
    rows_s[0, 1:2, HD2:HD2 + HW] = k_gain_row
    put("rt", 1, 0, rows_s.at[0], rows_r.at[0], sib)
    add_rest("g1", g1s, g1r)
    relay_grad()
    share_mlp(1, dno)
    got("rt", 1, 0, rows_r.at[0], sib)
    rows_s[1] = rows_s[0] + rows_r[0]
    for j in range(1, ZN):
        put("rz", ZN, j, rows_s.at[1], rows_r.at[j], at_z(j))

    total = boown[...]
    for j in (1, 2):
        got("bo", 5, j, bor.at[j], at_ctx(j))
        total = total + bor[j].astype(full_type)
    own_rows = pl.ds(t_i * TB, TB)
    obuf[0] = total.astype(low_type)
    put("ob", 2, 0, obuf.at[0], bo_o.at[own_rows], sib)
    pltpu.make_async_copy(obuf.at[0], bo_o.at[own_rows], lsem.at[10]).start()

    def to_owner(name, first, count, n):
        rows = pl.ds(first, count)
        return qfin.at[n, rows], qkvo.at[place, t_i, n, rows]

    def share_fin(n, which=slice(None)):
        for name, first, count in pieces[n][which]:
            rows = slice(first, first + count)
            total = qown[n, s_i, rows]
            for j in (0, 1) if n == 1 else range(1, ZN):
                got(name, 4, j, qz_r.at[n, j, pl.ds(first, count)], at_z(1))
                total = total + qz_r[n, j, rows].astype(full_type)
            qfin[n, rows] = total.astype(low_type)
            src, dst = to_owner(name, first, count, n)
            slot = spot("r" + name, 2 * half_chips) + place * 2 + t_i
            for j in range(1, CN):
                pltpu.make_async_remote_copy(
                    src_ref=src, dst_ref=dst,
                    send_sem=leaving("s" + name, CN, j), recv_sem=rsem.at[slot],
                    device_id=(s_i, flip(c_i, j, CN), tstar), device_id_type=MESH,
                ).start()

            @pl.when(t_i == tstar)
            def _():
                pltpu.make_async_copy(src, dst, lsem.at[12 + (name == "qz2") * 2 + n]).start()

            @pl.when(t_i != tstar)
            def _():
                pltpu.make_async_remote_copy(
                    src_ref=src, dst_ref=dst,
                    send_sem=leaving("o" + name, 1, 0), recv_sem=rsem.at[slot],
                    device_id=sib, device_id_type=MESH,
                ).start()

    def pass_grad(k, out):
        for j in (1, 2):
            block = out.at[flip(c_i, j, CN)]
            got("gc%d" % k, 5, j, block, at_ctx(j))
            half = block.at[pl.ds((j - 1) * HR, HR)]
            put_as("gc%d" % k, 5, 2 + j, 2 + j, half, half, at_ctx(3 - j))

    pass_grad(0, upo)
    share_fin(0, slice(0, 1))

    xhat1, inv1 = norm_rows(xg[0].astype(full_type))
    grad_one = g1own[...]
    have_sums("g1", g1r)
    for j in (1, 2):
        grad_one = grad_one + g1r[j].astype(full_type)
    hat = grad_one * g1row
    grad_in = gres[...] + inv1 * (
        hat
        - jnp.sum(hat, axis=-1, keepdims=True) * inv_d
        - xhat1 * (jnp.sum(hat * xhat1, axis=-1, keepdims=True) * inv_d)
    )
    obuf[1] = grad_in.astype(low_type)
    put("ob", 2, 1, obuf.at[1], ig_o.at[own_rows], sib)
    pltpu.make_async_copy(obuf.at[1], ig_o.at[own_rows], lsem.at[11]).start()

    pass_grad(1, dno)
    share_fin(0, slice(1, 2))

    rows_sum = rows_s[1]
    for j in range(1, ZN):
        got("rz", ZN, j, rows_r.at[j], at_z(j))
        rows_sum = rows_sum + rows_r[j]
    rows_s[2] = rows_sum
    for j in range(1, CN):
        put("rc", CN, j, rows_s.at[2], rows_r.at[ZN + j], at_ctx(j))
    qkr_v[c_i] = rows_sum[:, HD2:]

    share_fin(1)
    total = rows_sum[:, :HD2]
    for j in range(1, CN):
        got("rc", CN, j, rows_r.at[ZN + j], at_ctx(j))
        block = rows_r[ZN + j]
        total = total + block[:, :HD2]
        qkr_v[flip(c_i, j, CN)] = block[:, HD2:]
    lnr_v[...] = total
    pltpu.make_async_copy(lnr_v, lnr_o, lsem.at[23]).start()
    pltpu.make_async_copy(qkr_v, qkr_o, lsem.at[24]).start()

    for n, (src, dst) in enumerate(((peak_v, peak_o), (lnr_v, lnr_o), (qkr_v, qkr_o))):
        pltpu.make_async_copy(src, dst, lsem.at[22 + n]).wait()
    for k, out in ((0, upo), (1, dno)):
        for j in (1, 2):
            half = out.at[flip(c_i, 3, CN), pl.ds((j - 1) * HR, HR)]
            got("gc%d" % k, 5, 2 + j, half, at_ctx(3 - j))
        pltpu.make_async_copy(gfin.at[k], out.at[c_i], lsem.at[8 + k]).wait()
    other_rows = pl.ds(o_i * TB, TB)
    for k, out in ((0, bo_o), (1, ig_o)):
        got("ob", 2, k, out.at[other_rows], sib)
        pltpu.make_async_copy(obuf.at[k], out.at[own_rows], lsem.at[10 + k]).wait()

    all_pieces = [(name, first, count, n) for n in pieces for name, first, count in pieces[n]]

    @pl.when(t_i == tstar)
    def _():
        for name, first, count, n in all_pieces:
            src, dst = to_owner(name, first, count, n)
            pltpu.make_async_copy(src, dst, lsem.at[12 + (name == "qz2") * 2 + n]).wait()

    for p in range(half_chips):
        for a in range(2):
            @pl.when((t_i != tstar) | (place != p) | (t_i != a))
            def _():
                for name, first, count, n in all_pieces:
                    rows = pl.ds(first, count)
                    pltpu.make_async_remote_copy(
                        src_ref=qfin.at[n, rows], dst_ref=qkvo.at[p, a, n, rows],
                        send_sem=ssem.at[0],
                        recv_sem=rsem.at[spot("r" + name, 2 * half_chips) + p * 2 + a],
                        device_id=sib, device_id_type=MESH,
                    ).wait_recv()

    three = pl.ds(1, 3)
    for name, ref in (
        ("x", xg), ("br", brs), ("h2", h2), ("g2", g2s), ("pkc", pks), ("rc", rows_r), ("small", smalls.at[t_i]),
        ("pkz", pks), ("rz", rows_r), ("ct", ctg), ("gb", gbg), ("bo", bos), ("g1", g1s),
        ("gc0", gz_s.at[0]), ("gc1", gz_s.at[1]), ("gz0", gz_s.at[0]), ("gz1", gz_s.at[1]),
    ):
        sent(name, 5, 0, ref.at[three])
    for name, first, count, n in all_pieces:
        for way in ("", "s"):
            sent(way + name, 4, 0, qz_s.at[n, three, pl.ds(first, count)])
    for name, buf in mlp_weights:
        sent(name, 5, 0, buf.at[t_i, s_i])

        @pl.when(jnp.logical_not(outer))
        def _():
            for n in range(1, 5):
                sent(name, 5, n, buf.at[t_i, s_i])

    for name, ref in (
        ("smallt", smalls.at[t_i]), ("k", kall.at[0]), ("v", vall.at[0]), ("pkt", pks.at[0]),
        ("wdt", wdt.at[t_i]), ("wut", wup.at[t_i]), ("rt", rows_s.at[0]),
    ):
        sent(name, 1, 0, ref)
    for k in range(2):
        sent("gs", 2, k, gsib_s.at[k])
        sent("dk", 2, k, dks_s.at[k])
        sent("ob", 2, k, obuf.at[k])
        sent("qg", 2, k, qsib_s.at[k])

    @pl.when(t_i == tstar)
    def _():
        for name, buf in projections:
            sent(name, ZN, 0, buf)
            sent("f" + name, ZN, 0, buf.at[three])

    @pl.when(t_i != tstar)
    def _():
        for name, first, count, n in all_pieces:
            sent("o" + name, 1, 0, qfin.at[n, pl.ds(first, count)])


ARRIVALS, LEAVINGS = 125, 57


def fused_call(sizes, *operands):
    CN, ZN, TB, D, HW, FS, R = sizes
    TK = CN * TB
    HR = R // 2
    half_chips = CN // 2
    heads = HW // 64
    lo, hi = low_type, full_type
    V = pltpu.VMEM
    any_spec = pl.BlockSpec(memory_space=pl.ANY)
    gain_shape = operands[6].shape
    out_shape = [
        jax.ShapeDtypeStruct((2 * TB, D), lo),
        jax.ShapeDtypeStruct((2 * TB, D), lo),
        jax.ShapeDtypeStruct((CN, R, FS), lo),
        jax.ShapeDtypeStruct((CN, R, FS), lo),
        jax.ShapeDtypeStruct((half_chips, 2, 2, HR, 2 * HW), lo),
        jax.ShapeDtypeStruct((8, D // 2), hi),
        jax.ShapeDtypeStruct((CN, 8, 256), hi),
        jax.ShapeDtypeStruct((8, 128), hi),
    ]
    scratch = [
        V((CN, TB, D), lo), V((CN, TB, D), lo), V((2, ZN, 8, 256), hi),
        V((3, R, half_chips * HW), lo), V((R, half_chips * HW), lo),
        V((ZN, R, 2 * HW), lo), V((ZN, HR, 2 * HW), lo), V((ZN, HR, 2 * HW), lo),
        V((ZN, R, HW), lo), V((ZN, R, HW), lo), V((2, ZN, R, FS), lo), V((2, ZN, R, FS), lo),
        V((D, TK), lo), V((D, TK), lo), V((D, TK), lo),
        V((CN, TB, D), hi), V((CN, TB, D), lo),
        V((TK, HW), hi), V((TK, HW), hi), V((TK, HW), hi), V((TK, HW), hi),
        V((CN, TB, HW), lo), V((2, TK, HW), lo), V((2, TK, HW), lo),
        V((CN, heads * TB, 2 * TK), hi), V((heads * TB, 2 * TK), hi),
        V((CN, TB, HW), lo), V((CN, TB, D), lo), V((CN, TB, D), lo), V((2 + ZN + CN, 8, 128), hi),
        V((heads, 2 * TK), hi), V((heads * TB, 2 * TK), lo),
        V((CN, TB, D), lo), V((2, CN, TB, FS), hi), V((CN, TB, 2 * FS), lo), V((CN, TB, 2 * FS), lo),
        V((CN, TB, D), lo), V((CN, TB, D), lo), V((TB, D), hi),
        V((CN, TB, D), lo), V((CN, TB, D), lo), V((TB, D), hi),
        V((2, D, FS), lo), V((2, D, FS), lo), V((2, D, FS), hi),
        V((2, ZN, R, FS), lo), V((2, ZN, R, FS), lo), V((2, R, FS), lo),
        V((TB, D), hi), V((CN, TB, D), lo),
        V((CN, TB, HW), hi), V((HW, 2 * TK), hi), V((HW, 2 * TK), hi),
        V((2, HW, TK), lo), V((2, HW, TK), lo), V((TK, HW), lo), V((TK, 2 * HW), lo),
        V((CN, TB, D), lo), V((CN, TB, D), lo), V((TB, D), hi),
        V((2, ZN, HR, 2 * HW), lo), V((2, ZN, HR, 2 * HW), lo), V((2, ZN, HR, 2 * HW), hi),
        V((2, ZN, HR, 2 * HW), lo), V((2, ZN, HR, 2 * HW), lo), V((2, HR, 2 * HW), lo),
        V((3, 8, D // 2 + 256), hi), V((ZN + CN, 8, D // 2 + 256), hi), V((2, TB, D), lo),
        V((R,), lo), V((R,), lo), V((R,), lo), V((R,), lo), V(gain_shape, lo), V(gain_shape, lo),
        V((8, D // 2), hi), V((CN, 8, 256), hi), V((8, 128), hi),
        pltpu.SemaphoreType.DMA((25,)), pltpu.SemaphoreType.DMA((LEAVINGS,)), pltpu.SemaphoreType.DMA((ARRIVALS,)),
    ]
    return pl.pallas_call(
        functools.partial(fused_kernel, sizes),
        out_shape=out_shape,
        in_specs=[any_spec] * 14,
        out_specs=[any_spec] * 8,
        scratch_shapes=scratch,
        compiler_params=pltpu.CompilerParams(
            collective_id=0, has_side_effects=True, vmem_limit_bytes=56 * 2**20
        ),
    )(*operands)


def finish_kernel(
    sizes,
    bo, ig, up_h, dn_h, qkvo_h, lnr_h, qkr_h, peak_h, wq_h, wk_h,
    bo_o, ig_o, l1g_o, l1b_o, l2g_o, l2b_o, qg_o, kg_o, gq_o, gk_o, gv_o, go_o, gu_o, gd_o, cq_o, ck_o,
    upo, dno, qkvo, lnr, qkr, peak, wq, wk, bov, igv, gq, gk, gv, go, gu, gd, cq, ck, l1g, l1b, l2g, l2b, qg, kg, isem, osem,
):
    CN, ZN, TB, D, HW, FS, R = sizes
    half_chips = CN // 2
    s_i, t_i = lax.axis_index("shard"), lax.axis_index("tp")
    ins = [
        pltpu.make_async_copy(src, dst, isem.at[n])
        for n, (src, dst) in enumerate((
            (qkvo_h, qkvo), (up_h, upo), (dn_h, dno), (peak_h, peak), (wq_h, wq), (wk_h, wk),
            (lnr_h, lnr), (qkr_h, qkr), (bo, bov), (ig, igv),
        ))
    ]
    for n in (1, 2, 0, 8, 9, 3, 4, 5, 6, 7):
        ins[n].start()
    outs = []

    def leave(src, dst):
        copy = pltpu.make_async_copy(src, dst, osem.at[len(outs)])
        copy.start()
        outs.append(copy)

    for n, grads, stage, out in ((1, upo, gu, gu_o), (2, dno, gd, gd_o)):
        ins[n].wait()
        for c in range(CN):
            stage[:, c * FS:(c + 1) * FS] = grads[c].astype(full_type)
        leave(stage, out)
    ins[0].wait()
    for n, first, stage, out in ((1, 0, gq, gq_o), (0, 0, gk, gk_o), (0, HW, gv, gv_o), (1, HW, go, go_o)):
        for a in range(2):
            parts = [qkvo[p, a, n][:, first:first + HW] for p in range(half_chips)]
            stage[a * (R // 2):(a + 1) * (R // 2)] = jnp.concatenate(parts, axis=1).astype(full_type)
        leave(stage, out)
    for n, stage, out in ((8, bov, bo_o), (9, igv, ig_o)):
        ins[n].wait()
        leave(stage, out)
    heads = HW // 64
    for n in (3, 4, 5):
        ins[n].wait()
    factor = jnp.sqrt(clip_level / jnp.maximum(peak[0:1], clip_level))
    here = half_chips * heads
    lanes = lax.broadcasted_iota(jnp.int32, (1, here * 64), 1) // 64
    ids = lax.broadcasted_iota(jnp.int32, (1, 128), 1)
    columns = jnp.ones((1, here * 64), full_type)
    for h in range(here):
        one = jnp.sum(jnp.where(ids == t_i * here + h, factor, 0.0), axis=-1, keepdims=True)
        columns = jnp.where(lanes == h, one, columns)
    for weights, stage, out in ((wq, cq, cq_o), (wk, ck, ck_o)):
        stage[...] = (weights[...].astype(full_type) * columns).astype(low_type)
        leave(stage, out)
    ins[6].wait()
    ins[7].wait()
    for k, (stage, out) in enumerate(((l1g, l1g_o), (l1b, l1b_o), (l2g, l2g_o), (l2b, l2b_o))):
        row = jnp.zeros((1, R), full_type)
        for z in range(ZN):
            at = z * R % (D // 2)
            source = 2 * k + z * R // (D // 2)
            row = jnp.where(s_i == z, lnr[source:source + 1, at:at + R], row)
        stage[...] = row.reshape(R)
        leave(stage, out)
    piece = qg.shape[1]
    for p in range(half_chips):
        chip = pltpu.roll(qkr[t_i * half_chips + p], (256 - s_i * piece) % 256, 1)
        for h in range(heads):
            for k, stage in ((0, qg), (1, kg)):
                stage[p * heads + h:p * heads + h + 1] = chip[k:k + 1, h * 64:h * 64 + piece]
    leave(qg, qg_o)
    leave(kg, kg_o)
    for copy in outs:
        copy.wait()


def fused_layer(
    images, cotangent, ln1_gain, ln1_bias, ln2_gain, ln2_bias, q_gain, k_gain,
    w_query, w_key, w_value, w_out, w_up, w_down,
):
    CN, ZN = lax.axis_size("ctx"), lax.axis_size("shard")
    TB = images.shape[1] // 2
    D = images.shape[2]
    R = w_query.shape[0]
    HW = w_query.shape[1] // (CN // 2)
    FS = w_up.shape[1] // CN
    sizes = (CN, ZN, TB, D, HW, FS, R)
    results = fused_call(
        sizes, images, cotangent, ln1_gain, ln1_bias, ln2_gain, ln2_bias, q_gain, k_gain,
        w_query, w_key, w_value, w_out.T, w_up, w_down.T,
    )
    row = jax.ShapeDtypeStruct((R,), full_type)
    gain = jax.ShapeDtypeStruct(q_gain.shape, full_type)
    square = jax.ShapeDtypeStruct(w_query.shape, full_type)
    wide = jax.ShapeDtypeStruct(w_up.shape, full_type)
    tokens = jax.ShapeDtypeStruct(images.shape[1:], low_type)
    clipped = jax.ShapeDtypeStruct(w_query.shape, low_type)
    lo, hi = low_type, full_type
    V = pltpu.VMEM
    any_spec = pl.BlockSpec(memory_space=pl.ANY)
    out = pl.pallas_call(
        functools.partial(finish_kernel, sizes),
        out_shape=[tokens] * 2 + [row] * 4 + [gain] * 2 + [square] * 4 + [wide] * 2 + [clipped] * 2,
        in_specs=[any_spec] * 10,
        out_specs=[any_spec] * 16,
        scratch_shapes=[
            V((CN, R, FS), lo), V((CN, R, FS), lo), V((CN // 2, 2, 2, R // 2, 2 * HW), lo), V((8, D // 2), hi),
            V((CN, 8, 256), hi), V((8, 128), hi), V(w_query.shape, lo), V(w_query.shape, lo),
            V(images.shape[1:], lo), V(images.shape[1:], lo),
        ]
        + [V(w_query.shape, hi)] * 4 + [V(w_up.shape, hi)] * 2 + [V(w_query.shape, lo)] * 2
        + [V((R,), hi)] * 4 + [V(q_gain.shape, hi)] * 2
        + [pltpu.SemaphoreType.DMA((10,)), pltpu.SemaphoreType.DMA((16,))],
        compiler_params=pltpu.CompilerParams(vmem_limit_bytes=60 * 2**20),
    )(*results, w_query, w_key)
    out = list(out)
    out[0], out[1] = out[0].reshape(images.shape), out[1].reshape(images.shape)
    out[11], out[13] = out[11].T, out[13].T
    return tuple(out)


def on_device(images, cotangent, ln1_gain, ln1_bias, ln2_gain, ln2_bias, q_gain, k_gain, *weights):
    fused = fits_fused(images, weights[0], weights[4], q_gain)
    layer = fused_layer if fused else general_layer
    return layer(images, cotangent, ln1_gain, ln1_bias, ln2_gain, ln2_bias, q_gain, k_gain, *weights)


def solution(mesh):
    return jax.shard_map(
        on_device,
        mesh=mesh,
        in_specs=(
            P("shard", "ctx", None),
            P("shard", "ctx", None),
            P("shard"),
            P("shard"),
            P("shard"),
            P("shard"),
            P("tp", "shard"),
            P("tp", "shard"),
            P("shard", "tp"),
            P("shard", "tp"),
            P("shard", "tp"),
            P("tp", "shard"),
            P("shard", "tp"),
            P("tp", "shard"),
        ),
        out_specs=(
            P("shard", "ctx", None),
            P("shard", "ctx", None),
            P("shard"),
            P("shard"),
            P("shard"),
            P("shard"),
            P("tp", "shard"),
            P("tp", "shard"),
            P("shard", "tp"),
            P("shard", "tp"),
            P("shard", "tp"),
            P("tp", "shard"),
            P("shard", "tp"),
            P("tp", "shard"),
            P("shard", "tp"),
            P("shard", "tp"),
        ),
        check_vma=False,
    )
```
